32 devices in a mesh: xg: 4 (over x, core), yd: 8 (over z, y).
Axes of the slice: x: 2, y: 2, z: 4, core: 2. Of those that a mesh axis runs over, the one named last changes fastest.
Arguments:
- mobile: float32 [512, 1, 1024], P('yd', None, 'xg'), may hold values from 0 to 2
- dispersion_x: float32 [512, 1, 1024], P('yd', None, 'xg'), may hold values from 0.5 to 200000
- dispersion_y: float32 [512, 1, 1024], P('yd', None, 'xg'), may hold values from 0.5 to 200000
- capacity: float32 [512, 1, 1024], P('yd', None, 'xg'), may hold values from 0.5 to 8
- immobile: float32 [4, 512, 1, 1024], P(None, 'yd', None, 'xg'), may hold values from 0 to 2
- exchange_rates: float32 [4], replicated, may hold values from 0.02 to 50
- rate_shares: float32 [4], replicated, may hold values from 0.1 to 1
Outputs:
- updated: float32 [512, 1, 1024], P('yd', None, 'xg')
The draws below stay inside these ranges and needn't reach their ends.
All inputs are finite; a program needn't handle non-finite values.
Results may differ from the reference program's by a relative error of at most 0.0003.
Values sent between devices are 32-bit elements; how exact they have to be, the bound alone decides.
No kernel may reach another device: no remote copies, remote signals or barrier semaphores. Data moves between devices by JAX's collectives and lax.ppermute only.
A program may use at most 64 MiB of HBM per device.

```python
import math
import jax
import jax.numpy as jnp
from jax import lax

ZS = 1
RATES = 4
NX = 1024
NY = 512


def layered_faces(key, line_shape, lowest):
    key_line = jax.random.fold_in(key, 11)
    key_face = jax.random.fold_in(key, 23)
    line_log = jax.random.uniform(key_line, line_shape, jnp.float32, math.log(lowest), 0.0)
    face_log = jax.random.uniform(key_face, (NY, ZS, NX), jnp.float32, -math.log(2.0), math.log(2.0))
    return 100000.0 * jnp.exp(line_log + face_log)


def draw_dispersion_x(key, part):
    lowest = 1e-05
    return layered_faces(key, (NY, ZS, 1), lowest).astype(jnp.float32)


def draw_dispersion_y(key, part):
    lowest = 1e-05
    return layered_faces(key, (1, ZS, NX), lowest).astype(jnp.float32)


def shard_levels(key, shape, cuts, least, top_value):
    def one(position, parts):
        draws = jax.random.uniform(jax.random.fold_in(jax.random.fold_in(key, 6), position), (parts,), jnp.float32, least / len(cuts), top_value / len(cuts))
        return jnp.repeat(jnp.exp(draws), shape[position] // parts).reshape((-1,) + (1,) * (len(shape) - position - 1))

    loudness = one(*cuts[0])
    for cut in cuts[1:]:
        loudness = loudness * one(*cut)
    return loudness


def setup_inputs(seed: int = 0) -> dict:
    splits = jax.random.split(jax.random.key(seed), 8)
    mobile = jnp.clip(2.0 * jax.random.uniform(splits[0], (NY, ZS, NX), jnp.float32) ** shard_levels(splits[0], (NY, ZS, NX), ((0, 8), (2, 4)), -0.2, 0.2), 0.0, 2.0)
    dispersion_x = draw_dispersion_x(jax.random.fold_in(splits[7], 71), 0)
    dispersion_y = draw_dispersion_y(jax.random.fold_in(splits[7], 71), 0)
    capacity = jnp.clip(jnp.exp(math.log(8.0) - 2.7725887 * jax.random.uniform(splits[3], (NY, ZS, NX), jnp.float32) ** shard_levels(splits[3], (NY, ZS, NX), ((0, 8), (2, 4)), -0.2, 0.2)), 0.5, 8.0)
    immobile = jnp.clip(2.0 * jax.random.uniform(splits[4], (RATES, NY, ZS, NX), jnp.float32) ** shard_levels(splits[4], (RATES, NY, ZS, NX), ((1, 8), (3, 4)), -0.2, 0.2), 0.0, 2.0)
    exchange_rates = jnp.clip(jnp.exp(jax.random.uniform(splits[5], (RATES,), jnp.float32, math.log(0.02), math.log(50.0))), 0.02, 50.0)
    rate_shares = jnp.clip(jnp.exp(jax.random.uniform(splits[6], (RATES,), jnp.float32, math.log(0.1), math.log(1.0))), 0.1, 1.0)
    return dict(mobile=mobile, dispersion_x=dispersion_x, dispersion_y=dispersion_y, capacity=capacity, immobile=immobile, exchange_rates=exchange_rates, rate_shares=rate_shares)


def periodic_solve(face_coef, storage, right_side, axis):
    length = right_side.shape[axis]
    sub_coef = -face_coef
    super_coef = -jnp.roll(face_coef, -1, axis)
    main_coef = storage + face_coef - super_coef
    stride = 1
    while stride < length // 2:
        sub_left = jnp.roll(sub_coef, stride, axis)
        main_left = jnp.roll(main_coef, stride, axis)
        super_left = jnp.roll(super_coef, stride, axis)
        side_left = jnp.roll(right_side, stride, axis)
        sub_right = jnp.roll(sub_coef, -stride, axis)
        main_right = jnp.roll(main_coef, -stride, axis)
        super_right = jnp.roll(super_coef, -stride, axis)
        side_right = jnp.roll(right_side, -stride, axis)
        left_ratio = sub_coef / main_left
        right_ratio = super_coef / main_right
        main_coef = main_coef - left_ratio * super_left - right_ratio * sub_right
        right_side = right_side - left_ratio * side_left - right_ratio * side_right
        sub_coef = -left_ratio * sub_left
        super_coef = -right_ratio * super_right
        stride = stride * 2
    coupling = sub_coef + super_coef
    main_other = jnp.roll(main_coef, stride, axis)
    coupling_other = jnp.roll(coupling, stride, axis)
    side_other = jnp.roll(right_side, stride, axis)
    return (right_side * main_other - coupling * side_other) / (main_coef * main_other - coupling * coupling_other)


def reference(mobile, dispersion_x, dispersion_y, capacity, immobile, exchange_rates, rate_shares):
    weights = rate_shares * exchange_rates / (1.0 + exchange_rates)

    def one_plane(inputs):
        plane_mobile, plane_dx, plane_dy, plane_capacity, plane_immobile = inputs
        gain_terms = plane_capacity[None] * weights[:, None, None]
        storage = 1.0 + jnp.sum(gain_terms, axis=0)
        source = plane_mobile + jnp.sum(gain_terms * plane_immobile, axis=0)
        after_x = periodic_solve(plane_dx, storage, source, 1)
        return periodic_solve(plane_dy, storage, storage * after_x, 0)

    planes = lax.map(one_plane, (mobile.transpose(1, 0, 2), dispersion_x.transpose(1, 0, 2), dispersion_y.transpose(1, 0, 2), capacity.transpose(1, 0, 2), immobile.transpose(2, 0, 1, 3)))
    return planes.transpose(1, 0, 2)
```

```python
import functools

import jax
import jax.numpy as jnp
from jax import lax
from jax.experimental import pallas as pl
from jax.experimental.pallas import tpu as pltpu
from jax.sharding import PartitionSpec as P

LANES = 128
SUBLANES = 8
QUANTITIES = 5
VMEM = pltpu.VMEM


def inverse(value):
    return 1.0 / value


def plus(first, second):
    if first is None:
        return second
    return first + second


def join_coefs(left, right):
    coupling_1, head_1, tail_1 = left
    coupling_2, head_2, tail_2 = right
    middle = plus(head_2, tail_1)
    inv = inverse(coupling_1 + coupling_2 + middle)
    weight_1 = coupling_1 * inv
    weight_2 = coupling_2 * inv
    joined = (coupling_1 * weight_2, plus(head_1, weight_1 * middle), tail_2 + weight_2 * middle)
    return joined, (weight_1, weight_2, inv)


def join_sides(left, right, node):
    head_1, tail_1 = left
    head_2, tail_2 = right
    weight_1, weight_2, inv = node
    side = plus(head_2, tail_1)
    joined = (plus(head_1, weight_1 * side), tail_2 + weight_2 * side)
    return joined, side * inv


def middle_value(node, given, before, after):
    return given + node[0] * before + node[1] * after


def ahead(value, step, axis):
    return pltpu.roll(value, value.shape[axis] - step, axis)


def behind(value, step, axis):
    return pltpu.roll(value, step, axis)


def doubling(count):
    steps = []
    step = 1
    while step < count:
        steps.append(step)
        step *= 2
    return steps


def tree_coefs(leaves, rolls):
    nodes = []
    level = leaves
    while len(level) > 1:
        following = []
        for index in range(0, len(level), 2):
            joined, node = join_coefs(level[index], level[index + 1])
            following.append(joined)
            nodes.append(node)
        level = following
    piece = level[0]
    for step, axis in rolls:
        piece, node = join_coefs(piece, tuple(ahead(part, step, axis) for part in piece))
        nodes.append(node)
    return piece, nodes


def tree_sides(leaves, rolls, nodes):
    givens = []
    level = leaves
    while len(level) > 1:
        following = []
        for index in range(0, len(level), 2):
            joined, given = join_sides(level[index], level[index + 1], nodes[len(givens)])
            following.append(joined)
            givens.append(given)
        level = following
    piece = level[0]
    for step, axis in rolls:
        other = tuple(ahead(part, step, axis) for part in piece)
        piece, given = join_sides(piece, other, nodes[len(givens)])
        givens.append(given)
    return piece, givens


def tree_values(before, after, rolls, count, nodes, givens):
    place = len(nodes)
    for step, axis in reversed(rolls):
        place -= 1
        middle = middle_value(nodes[place], givens[place], before, after)
        upper = (lax.broadcasted_iota(jnp.int32, middle.shape, axis) & step) != 0
        before = jnp.where(upper, behind(middle, step, axis), before)
        after = jnp.where(upper, behind(after, step, axis), middle)
    bounds = [before, after]
    while len(bounds) - 1 < count:
        width = len(bounds) - 1
        place -= width
        following = [bounds[0]]
        for index in range(width):
            following.append(
                middle_value(
                    nodes[place + index], givens[place + index], bounds[index], bounds[index + 1]
                )
            )
            following.append(bounds[index + 1])
        bounds = following
    return bounds[1:]


def ring_ends(slots, index):
    level = slots
    path = []
    bit = 0
    while len(level) > 1:
        upper = ((index >> bit) & 1) == 1
        following = []
        for place in range(0, len(level), 2):
            own, other = level[place], level[place + 1]
            left = [jnp.where(upper, b, a) for a, b in zip(own, other)]
            right = [jnp.where(upper, a, b) for a, b in zip(own, other)]
            coefs, node = join_coefs(left[:3], right[:3])
            sides, given = join_sides(left[3:], right[3:], node)
            if place == 0:
                path.append((node, given, upper))
            following.append(coefs + sides)
        level = following
        bit += 1
    _, head, tail, side_head, side_tail = level[0]
    before = after = (side_head + side_tail) * inverse(head + tail)
    for node, given, upper in reversed(path):
        middle = middle_value(node, given, before, after)
        before = jnp.where(upper, middle, before)
        after = jnp.where(upper, after, middle)
    return before, after


def capacity_weights(rates_ref, shares_ref, zones):
    weights = []
    for zone in range(zones):
        rate = jnp.full((1, LANES), rates_ref[zone], jnp.float32)
        share = jnp.full((1, LANES), shares_ref[zone], jnp.float32)
        weights.append(share * rate / (1.0 + rate))
    return weights


def strided(ref, start, size, stride):
    return ref[pl.ds(start, size, stride=stride), :]


def x_rolls(halves):
    return [(step, 0) for step in doubling(SUBLANES)] + [(step, 1) for step in doubling(halves)]


def y_rolls():
    return [(step, 0) for step in doubling(SUBLANES)]


def x_forward_kernel(
    halves, zones, mobile_ref, faces_ref, capacity_ref, immobile_ref, rates_ref, shares_ref,
    message_ref, state_ref, faces_t, storage_t, source_t,
):
    rows = mobile_ref.shape[0]
    stride = LANES // SUBLANES
    weights = capacity_weights(rates_ref, shares_ref, zones)
    capacity = capacity_ref[...]
    faces_t[...] = faces_ref[...].T
    storage_t[...] = (1.0 + capacity * sum(weights[1:], weights[0])).T
    total = weights[0] * immobile_ref[0:rows, :]
    for zone in range(1, zones):
        total = total + weights[zone] * immobile_ref[zone * rows : (zone + 1) * rows, :]
    source_t[...] = (mobile_ref[...] + capacity * total).T
    coefs, sides = [], []
    for index in range(stride):
        coefs.append((strided(faces_t, index, SUBLANES, stride), None, strided(storage_t, index, SUBLANES, stride)))
        sides.append((None, strided(source_t, index, SUBLANES, stride)))
    rolls = x_rolls(halves)
    piece, nodes = tree_coefs(coefs, rolls)
    side, givens = tree_sides(sides, rolls, nodes)
    for place, (node, given) in enumerate(zip(nodes, givens)):
        state_ref[3 * place] = node[0]
        state_ref[3 * place + 1] = node[1]
        state_ref[3 * place + 2] = given
    for row, value in enumerate(piece + side):
        message_ref[row : row + 1, :] = value[0:1, :]


def y_coefs_kernel(
    halves, zones, faces_ref, capacity_ref, rates_ref, shares_ref, rows_ref, state_ref, storage_ref
):
    rows = faces_ref.shape[0]
    stride = rows // SUBLANES
    weights = capacity_weights(rates_ref, shares_ref, zones)
    storage_ref[...] = 1.0 + capacity_ref[...] * sum(weights[1:], weights[0])
    place = 0
    for half in range(halves):
        coefs = []
        for index in range(half, stride, halves):
            coefs.append((strided(faces_ref, index, SUBLANES, stride), None, strided(storage_ref, index, SUBLANES, stride)))
        piece, nodes = tree_coefs(coefs, y_rolls())
        for node in nodes:
            for part in node:
                state_ref[place] = part
                place += 1
        for number, value in enumerate(piece):
            row = number * halves + half
            rows_ref[row : row + 1, :] = value[0:1, :]


def slot_rows(refs, number, height, quantity_rows):
    slots = []
    for ref in refs:
        for slot in range(ref.shape[0] // height):
            slots.append(
                tuple(
                    ref[slot * height + quantity * quantity_rows : slot * height + (quantity + 1) * quantity_rows, :]
                    for quantity in range(QUANTITIES)
                )
            )
    assert len(slots) == number
    return slots


def x_back_kernel(halves, axis, pieces, *refs):
    message_refs = refs[:pieces]
    x_state, y_state, rows_ref, storage_ref = refs[pieces : pieces + 4]
    message_ref, given_ref = refs[pieces + 4 : pieces + 6]
    values_t, sides_ref = refs[pieces + 6 :]
    rows = storage_ref.shape[0]
    count = lax.axis_size(axis)
    slots = slot_rows(message_refs, count, message_refs[0].shape[0], 1)
    before, after = ring_ends(slots, lax.axis_index(axis))
    before = jnp.broadcast_to(before, (SUBLANES, rows))
    after = jnp.broadcast_to(after, (SUBLANES, rows))
    rolls = x_rolls(halves)
    stride = LANES // SUBLANES
    total = stride - 1 + len(rolls)
    nodes = [(x_state[3 * place], x_state[3 * place + 1]) for place in range(total)]
    givens = [x_state[3 * place + 2] for place in range(total)]
    values = tree_values(before, after, rolls, stride, nodes, givens)
    for index, value in enumerate(values):
        values_t[pl.ds(index, SUBLANES, stride=stride), :] = value
    sides_ref[...] = storage_ref[...] * values_t[...].T
    stride = rows // SUBLANES
    place = 0
    height = 3 * halves
    message_ref[0:height, :] = rows_ref[0:height, :]
    total = stride // halves - 1 + len(y_rolls())
    for half in range(halves):
        sides = [(None, strided(sides_ref, index, SUBLANES, stride)) for index in range(half, stride, halves)]
        nodes = [tuple(y_state[3 * (half * total + node) + part] for part in range(3)) for node in range(total)]
        piece, givens = tree_sides(sides, y_rolls(), nodes)
        for given in givens:
            given_ref[place] = given
            place += 1
        for number, value in enumerate(piece):
            row = height + number * halves + half
            message_ref[row : row + 1, :] = value[0:1, :]


def y_back_kernel(halves, axis, pieces, *refs):
    message_refs = refs[:pieces]
    y_state, given_ref, out_ref = refs[pieces:]
    rows = out_ref.shape[0]
    stride = rows // SUBLANES
    count = lax.axis_size(axis)
    slots = slot_rows(message_refs, count, message_refs[0].shape[0], halves)
    before, after = ring_ends(slots, lax.axis_index(axis))
    total = stride // halves - 1 + len(y_rolls())
    for half in range(halves):
        first = jnp.broadcast_to(before[half : half + 1, :], (SUBLANES, LANES))
        last = jnp.broadcast_to(after[half : half + 1, :], (SUBLANES, LANES))
        nodes = [tuple(y_state[3 * (half * total + node) + part] for part in range(2)) for node in range(total)]
        givens = [given_ref[half * total + node] for node in range(total)]
        values = tree_values(first, last, y_rolls(), stride // halves, nodes, givens)
        for index, value in enumerate(values):
            out_ref[pl.ds(index * halves + half, SUBLANES, stride=stride), :] = value


def exchange(message, axis):
    count = lax.axis_size(axis)
    pieces = [message]
    held = message
    step = 1
    while step < count:
        received = lax.ppermute(held, axis, [(index, index ^ step) for index in range(count)])
        pieces.append(received)
        step *= 2
        if step < count:
            held = jnp.concatenate([held, received], axis=0)
    return pieces


def f32(*shape):
    return jax.ShapeDtypeStruct(shape, jnp.float32)


def held_f32(*shape):
    return VMEM(shape, jnp.float32)


def kernel_call(body, operands, scalars, outputs, scratch):
    spec = pl.BlockSpec(memory_space=VMEM)
    small = pl.BlockSpec(memory_space=pltpu.SMEM)
    return pl.pallas_call(
        body,
        out_shape=outputs,
        in_specs=[spec] * len(operands) + [small] * len(scalars),
        out_specs=[spec] * len(outputs),
        scratch_shapes=scratch,
        compiler_params=pltpu.CompilerParams(vmem_limit_bytes=16 * 1024 * 1024),
    )(*operands, *scalars)


def local(mobile, dispersion_x, dispersion_y, capacity, immobile, exchange_rates, rate_shares):
    shape = mobile.shape
    lines, width = shape[0] * shape[1], shape[2]
    zones = immobile.shape[0]
    halves = width // LANES
    rows = lines * halves
    assert rows == LANES

    def flat(values):
        return values.reshape(-1, LANES)

    mobile, dispersion_x, dispersion_y = flat(mobile), flat(dispersion_x), flat(dispersion_y)
    capacity, immobile = flat(capacity), flat(immobile)
    square = VMEM((rows, LANES), jnp.float32)
    x_nodes = LANES // SUBLANES - 1 + len(x_rolls(halves))
    y_nodes = halves * (rows // SUBLANES // halves - 1 + len(y_rolls()))
    y_height = -(-QUANTITIES * halves // SUBLANES) * SUBLANES
    message, x_state = kernel_call(
        functools.partial(x_forward_kernel, halves, zones),
        (mobile, dispersion_x, capacity, immobile),
        (exchange_rates, rate_shares),
        [f32(SUBLANES, rows), held_f32(3 * x_nodes, SUBLANES, rows)],
        [square] * 3,
    )
    y_rows, y_state, storage = kernel_call(
        functools.partial(y_coefs_kernel, halves, zones),
        (dispersion_y, capacity),
        (exchange_rates, rate_shares),
        [held_f32(SUBLANES, LANES), held_f32(3 * y_nodes, SUBLANES, LANES), held_f32(rows, LANES)],
        [],
    )
    pieces = exchange(message, "xg")
    message, givens = kernel_call(
        functools.partial(x_back_kernel, halves, "xg", len(pieces)),
        (*pieces, x_state, y_state, y_rows, storage),
        (),
        [f32(y_height, LANES), held_f32(y_nodes, SUBLANES, LANES)],
        [square] * 2,
    )
    pieces = exchange(message, "yd")
    (updated,) = kernel_call(
        functools.partial(y_back_kernel, halves, "yd", len(pieces)),
        (*pieces, y_state, givens),
        (),
        [f32(rows, LANES)],
        [],
    )
    return updated.reshape(shape)


def solution(mesh):
    field = P("yd", None, "xg")
    return jax.shard_map(
        local,
        mesh=mesh,
        in_specs=(field, field, field, field, P(None, "yd", None, "xg"), P(), P()),
        out_specs=field,
        check_vma=False,
    )
```

```python
import functools

import jax
import jax.numpy as jnp
from jax import lax
from jax.experimental import pallas as pl
from jax.experimental.pallas import tpu as pltpu
from jax.sharding import PartitionSpec as P

LANES = 128
SUBLANES = 8
QUANTITIES = 5
VMEM = pltpu.VMEM


def inverse(value):
    return 1.0 / value


def plus(first, second):
    if first is None:
        return second
    return first + second


def join_coefs(left, right):
    coupling_1, head_1, tail_1 = left
    coupling_2, head_2, tail_2 = right
    middle = plus(head_2, tail_1)
    inv = inverse(coupling_1 + coupling_2 + middle)
    weight_1 = coupling_1 * inv
    weight_2 = coupling_2 * inv
    joined = (coupling_1 * weight_2, plus(head_1, weight_1 * middle), tail_2 + weight_2 * middle)
    return joined, (weight_1, weight_2, inv)


def join_sides(left, right, node):
    head_1, tail_1 = left
    head_2, tail_2 = right
    weight_1, weight_2, inv = node
    side = plus(head_2, tail_1)
    joined = (plus(head_1, weight_1 * side), tail_2 + weight_2 * side)
    return joined, side * inv


def middle_value(node, given, before, after):
    return given + node[0] * before + node[1] * after


def ahead(value, step, axis):
    return pltpu.roll(value, value.shape[axis] - step, axis)


def behind(value, step, axis):
    return pltpu.roll(value, step, axis)


def doubling(count):
    steps = []
    step = 1
    while step < count:
        steps.append(step)
        step *= 2
    return steps


def tree_coefs(leaves, rolls):
    nodes = []
    level = leaves
    while len(level) > 1:
        following = []
        for index in range(0, len(level), 2):
            joined, node = join_coefs(level[index], level[index + 1])
            following.append(joined)
            nodes.append(node)
        level = following
    piece = level[0]
    for step, axis in rolls:
        piece, node = join_coefs(piece, tuple(ahead(part, step, axis) for part in piece))
        nodes.append(node)
    return piece, nodes


def tree_sides(leaves, rolls, nodes):
    givens = []
    level = leaves
    while len(level) > 1:
        following = []
        for index in range(0, len(level), 2):
            joined, given = join_sides(level[index], level[index + 1], nodes[len(givens)])
            following.append(joined)
            givens.append(given)
        level = following
    piece = level[0]
    for step, axis in rolls:
        other = tuple(ahead(part, step, axis) for part in piece)
        piece, given = join_sides(piece, other, nodes[len(givens)])
        givens.append(given)
    return piece, givens


def tree_values(before, after, rolls, count, nodes, givens):
    place = len(nodes)
    for step, axis in reversed(rolls):
        place -= 1
        middle = middle_value(nodes[place], givens[place], before, after)
        upper = (lax.broadcasted_iota(jnp.int32, middle.shape, axis) & step) != 0
        before = jnp.where(upper, behind(middle, step, axis), before)
        after = jnp.where(upper, behind(after, step, axis), middle)
    bounds = [before, after]
    while len(bounds) - 1 < count:
        width = len(bounds) - 1
        place -= width
        following = [bounds[0]]
        for index in range(width):
            following.append(
                middle_value(
                    nodes[place + index], givens[place + index], bounds[index], bounds[index + 1]
                )
            )
            following.append(bounds[index + 1])
        bounds = following
    return bounds[1:]


def ring_ends(slots, index):
    level = slots
    path = []
    bit = 0
    while len(level) > 1:
        upper = ((index >> bit) & 1) == 1
        following = []
        for place in range(0, len(level), 2):
            own, other = level[place], level[place + 1]
            left = [jnp.where(upper, b, a) for a, b in zip(own, other)]
            right = [jnp.where(upper, a, b) for a, b in zip(own, other)]
            coefs, node = join_coefs(left[:3], right[:3])
            sides, given = join_sides(left[3:], right[3:], node)
            if place == 0:
                path.append((node, given, upper))
            following.append(coefs + sides)
        level = following
        bit += 1
    _, head, tail, side_head, side_tail = level[0]
    before = after = (side_head + side_tail) * inverse(head + tail)
    for node, given, upper in reversed(path):
        middle = middle_value(node, given, before, after)
        before = jnp.where(upper, middle, before)
        after = jnp.where(upper, after, middle)
    return before, after


def capacity_weights(rates, shares):
    weights = shares * rates / (1.0 + rates)
    return [weights[:, zone : zone + 1] for zone in range(weights.shape[1])]


def strided(ref, start, size, stride):
    return ref[pl.ds(start, size, stride=stride), :]


def x_rolls(halves):
    return [(step, 0) for step in doubling(SUBLANES)] + [(step, 1) for step in doubling(halves)]


def y_rolls():
    return [(step, 0) for step in doubling(SUBLANES)]


def x_forward_kernel(
    halves, mobile_hbm, faces_hbm, capacity_hbm, immobile_hbm, rates_hbm, shares_hbm,
    message_ref, state_ref, storage_ref,
    mobile_ref, faces_ref, capacity_ref, immobile_ref, rates_ref, shares_ref, arrived,
    faces_t, storage_t, source_t,
):
    pairs = (
        (rates_hbm, rates_ref), (shares_hbm, shares_ref), (capacity_hbm, capacity_ref),
        (faces_hbm, faces_ref), (immobile_hbm, immobile_ref), (mobile_hbm, mobile_ref),
    )
    copies = [pltpu.make_async_copy(pair[0], pair[1], arrived.at[place]) for place, pair in enumerate(pairs)]
    for copy in copies:
        copy.start()
    rows = mobile_ref.shape[0]
    stride = LANES // SUBLANES
    for copy in copies[:3]:
        copy.wait()
    weights = capacity_weights(rates_ref[...], shares_ref[...])
    capacity = capacity_ref[...]
    storage = 1.0 + capacity * sum(weights[1:], weights[0])
    storage_ref[...] = storage
    storage_t[...] = storage.T
    copies[3].wait()
    faces_t[...] = faces_ref[...].T
    copies[4].wait()
    total = weights[0] * immobile_ref[0:rows, :]
    for zone in range(1, len(weights)):
        total = total + weights[zone] * immobile_ref[zone * rows : (zone + 1) * rows, :]
    copies[5].wait()
    source_t[...] = (mobile_ref[...] + capacity * total).T
    coefs, sides = [], []
    for index in range(stride):
        coefs.append((strided(faces_t, index, SUBLANES, stride), None, strided(storage_t, index, SUBLANES, stride)))
        sides.append((None, strided(source_t, index, SUBLANES, stride)))
    rolls = x_rolls(halves)
    piece, nodes = tree_coefs(coefs, rolls)
    side, givens = tree_sides(sides, rolls, nodes)
    for place, (node, given) in enumerate(zip(nodes, givens)):
        state_ref[3 * place] = node[0]
        state_ref[3 * place + 1] = node[1]
        state_ref[3 * place + 2] = given
    for row, value in enumerate(piece + side):
        message_ref[row : row + 1, :] = value[0:1, :]


def y_coefs_kernel(halves, faces_ref, storage_ref, rows_ref, state_ref):
    rows = faces_ref.shape[0]
    stride = rows // SUBLANES
    place = 0
    for half in range(halves):
        coefs = []
        for index in range(half, stride, halves):
            coefs.append((strided(faces_ref, index, SUBLANES, stride), None, strided(storage_ref, index, SUBLANES, stride)))
        piece, nodes = tree_coefs(coefs, y_rolls())
        for node in nodes:
            for part in node:
                state_ref[place] = part
                place += 1
        for number, value in enumerate(piece):
            row = number * halves + half
            rows_ref[row : row + 1, :] = value[0:1, :]


def slot_rows(refs, number, height, quantity_rows):
    slots = []
    for ref in refs:
        for slot in range(ref.shape[0] // height):
            slots.append(
                tuple(
                    ref[slot * height + quantity * quantity_rows : slot * height + (quantity + 1) * quantity_rows, :]
                    for quantity in range(QUANTITIES)
                )
            )
    assert len(slots) == number
    return slots


def gathered_rows(ref, number, own, quantity_rows):
    height = ref.shape[0] // number
    slots = []
    for slot in range(number):
        start = pl.multiple_of((own ^ slot) * height, height)
        block = ref[pl.ds(start, height), :]
        slots.append(
            tuple(
                block[quantity * quantity_rows : (quantity + 1) * quantity_rows, :]
                for quantity in range(QUANTITIES)
            )
        )
    return slots


def x_back_kernel(halves, axis, pieces, *refs):
    message_refs = refs[:pieces]
    x_state, y_state, rows_ref, storage_ref = refs[pieces : pieces + 4]
    message_ref, given_ref = refs[pieces + 4 : pieces + 6]
    values_t, sides_ref = refs[pieces + 6 :]
    rows = storage_ref.shape[0]
    count = lax.axis_size(axis)
    slots = slot_rows(message_refs, count, message_refs[0].shape[0], 1)
    before, after = ring_ends(slots, lax.axis_index(axis))
    before = jnp.broadcast_to(before, (SUBLANES, rows))
    after = jnp.broadcast_to(after, (SUBLANES, rows))
    rolls = x_rolls(halves)
    stride = LANES // SUBLANES
    total = stride - 1 + len(rolls)
    nodes = [(x_state[3 * place], x_state[3 * place + 1]) for place in range(total)]
    givens = [x_state[3 * place + 2] for place in range(total)]
    values = tree_values(before, after, rolls, stride, nodes, givens)
    for index, value in enumerate(values):
        values_t[pl.ds(index, SUBLANES, stride=stride), :] = value
    sides_ref[...] = storage_ref[...] * values_t[...].T
    stride = rows // SUBLANES
    place = 0
    height = 3 * halves
    message_ref[0:height, :] = rows_ref[0:height, :]
    total = stride // halves - 1 + len(y_rolls())
    for half in range(halves):
        sides = [(None, strided(sides_ref, index, SUBLANES, stride)) for index in range(half, stride, halves)]
        nodes = [tuple(y_state[3 * (half * total + node) + part] for part in range(3)) for node in range(total)]
        piece, givens = tree_sides(sides, y_rolls(), nodes)
        for given in givens:
            given_ref[place] = given
            place += 1
        for number, value in enumerate(piece):
            row = height + number * halves + half
            message_ref[row : row + 1, :] = value[0:1, :]


def y_back_kernel(halves, axis, pieces, *refs):
    message_refs = refs[:pieces]
    y_state, given_ref, out_ref = refs[pieces:]
    rows = out_ref.shape[0]
    stride = rows // SUBLANES
    count = lax.axis_size(axis)
    own = lax.axis_index(axis)
    slots = gathered_rows(message_refs[0], count, own, halves)
    before, after = ring_ends(slots, own)
    total = stride // halves - 1 + len(y_rolls())
    for half in range(halves):
        first = jnp.broadcast_to(before[half : half + 1, :], (SUBLANES, LANES))
        last = jnp.broadcast_to(after[half : half + 1, :], (SUBLANES, LANES))
        nodes = [tuple(y_state[3 * (half * total + node) + part] for part in range(2)) for node in range(total)]
        givens = [given_ref[half * total + node] for node in range(total)]
        values = tree_values(first, last, y_rolls(), stride // halves, nodes, givens)
        for index, value in enumerate(values):
            out_ref[pl.ds(index * halves + half, SUBLANES, stride=stride), :] = value


def exchange(message, axis):
    count = lax.axis_size(axis)
    pieces = [message]
    held = message
    step = 1
    while step < count:
        received = lax.ppermute(held, axis, [(index, index ^ step) for index in range(count)])
        pieces.append(received)
        step *= 2
        if step < count:
            held = jnp.concatenate([held, received], axis=0)
    return pieces


def f32(*shape):
    return jax.ShapeDtypeStruct(shape, jnp.float32)


def held_f32(*shape):
    return VMEM(shape, jnp.float32)


def kernel_call(body, operands, outputs, scratch, space=VMEM):
    return pl.pallas_call(
        body,
        out_shape=outputs,
        in_specs=[pl.BlockSpec(memory_space=space)] * len(operands),
        out_specs=[pl.BlockSpec(memory_space=VMEM)] * len(outputs),
        scratch_shapes=scratch,
        compiler_params=pltpu.CompilerParams(vmem_limit_bytes=16 * 1024 * 1024),
    )(*operands)


def local(mobile, dispersion_x, dispersion_y, capacity, immobile, exchange_rates, rate_shares):
    shape = mobile.shape
    lines, width = shape[0] * shape[1], shape[2]
    zones = immobile.shape[0]
    halves = width // LANES
    rows = lines * halves
    assert rows == LANES

    def flat(values):
        return values.reshape(-1, LANES)

    mobile, dispersion_x, dispersion_y = flat(mobile), flat(dispersion_x), flat(dispersion_y)
    capacity, immobile = flat(capacity), flat(immobile)
    square = VMEM((rows, LANES), jnp.float32)
    x_nodes = LANES // SUBLANES - 1 + len(x_rolls(halves))
    y_nodes = halves * (rows // SUBLANES // halves - 1 + len(y_rolls()))
    y_height = -(-QUANTITIES * halves // SUBLANES) * SUBLANES
    message, x_state, storage = kernel_call(
        functools.partial(x_forward_kernel, halves),
        tuple(
            pltpu.with_memory_space_constraint(value, pltpu.HBM)
            for value in (mobile, dispersion_x, capacity, immobile, exchange_rates[None], rate_shares[None])
        ),
        [f32(SUBLANES, rows), held_f32(3 * x_nodes, SUBLANES, rows), held_f32(rows, LANES)],
        [square] * 3
        + [VMEM((zones * rows, LANES), jnp.float32)]
        + [VMEM((1, zones), jnp.float32)] * 2
        + [pltpu.SemaphoreType.DMA((6,))]
        + [square] * 3,
        pltpu.HBM,
    )
    y_rows, y_state = kernel_call(
        functools.partial(y_coefs_kernel, halves),
        (dispersion_y, storage),
        [held_f32(SUBLANES, LANES), held_f32(3 * y_nodes, SUBLANES, LANES)],
        [],
    )
    pieces = exchange(message, "xg")
    message, givens = kernel_call(
        functools.partial(x_back_kernel, halves, "xg", len(pieces)),
        (*pieces, x_state, y_state, y_rows, storage),
        [f32(y_height, LANES), held_f32(y_nodes, SUBLANES, LANES)],
        [square] * 2,
    )
    pieces = [lax.all_gather(message, "yd", axis=0, tiled=True)]
    (updated,) = kernel_call(
        functools.partial(y_back_kernel, halves, "yd", len(pieces)),
        (*pieces, y_state, givens),
        [f32(rows, LANES)],
        [],
    )
    return updated.reshape(shape)


def solution(mesh):
    field = P("yd", None, "xg")
    return jax.shard_map(
        local,
        mesh=mesh,
        in_specs=(field, field, field, field, P(None, "yd", None, "xg"), P(), P()),
        out_specs=field,
        check_vma=False,
    )
```

```python
import functools

import jax
import jax.numpy as jnp
from jax import lax
from jax.experimental import pallas as pl
from jax.experimental.pallas import tpu as pltpu
from jax.sharding import PartitionSpec as P

LANES = 128
SUBLANES = 8
QUANTITIES = 5
VMEM = pltpu.VMEM


def inverse(value):
    return 1.0 / value


def plus(first, second):
    if first is None:
        return second
    return first + second


def join_coefs(left, right):
    coupling_1, head_1, tail_1 = left
    coupling_2, head_2, tail_2 = right
    middle = plus(head_2, tail_1)
    inv = inverse(coupling_1 + coupling_2 + middle)
    weight_1 = coupling_1 * inv
    weight_2 = coupling_2 * inv
    joined = (coupling_1 * weight_2, plus(head_1, weight_1 * middle), tail_2 + weight_2 * middle)
    return joined, (weight_1, weight_2, inv)


def join_sides(left, right, node):
    head_1, tail_1 = left
    head_2, tail_2 = right
    weight_1, weight_2, inv = node
    side = plus(head_2, tail_1)
    joined = (plus(head_1, weight_1 * side), tail_2 + weight_2 * side)
    return joined, side * inv


def middle_value(node, given, before, after):
    return given + node[0] * before + node[1] * after


def ahead(value, step, axis):
    return pltpu.roll(value, value.shape[axis] - step, axis)


def behind(value, step, axis):
    return pltpu.roll(value, step, axis)


def doubling(count):
    steps = []
    step = 1
    while step < count:
        steps.append(step)
        step *= 2
    return steps


def tree_coefs(leaves, rolls):
    nodes = []
    level = leaves
    while len(level) > 1:
        following = []
        for index in range(0, len(level), 2):
            joined, node = join_coefs(level[index], level[index + 1])
            following.append(joined)
            nodes.append(node)
        level = following
    piece = level[0]
    for step, axis in rolls:
        piece, node = join_coefs(piece, tuple(ahead(part, step, axis) for part in piece))
        nodes.append(node)
    return piece, nodes


def tree_sides(leaves, rolls, nodes):
    givens = []
    level = leaves
    while len(level) > 1:
        following = []
        for index in range(0, len(level), 2):
            joined, given = join_sides(level[index], level[index + 1], nodes[len(givens)])
            following.append(joined)
            givens.append(given)
        level = following
    piece = level[0]
    for step, axis in rolls:
        other = tuple(ahead(part, step, axis) for part in piece)
        piece, given = join_sides(piece, other, nodes[len(givens)])
        givens.append(given)
    return piece, givens


def tree_values(before, after, rolls, count, nodes, givens):
    place = len(nodes)
    for step, axis in reversed(rolls):
        place -= 1
        middle = middle_value(nodes[place], givens[place], before, after)
        upper = (lax.broadcasted_iota(jnp.int32, middle.shape, axis) & step) != 0
        before = jnp.where(upper, behind(middle, step, axis), before)
        after = jnp.where(upper, behind(after, step, axis), middle)
    bounds = [before, after]
    while len(bounds) - 1 < count:
        width = len(bounds) - 1
        place -= width
        following = [bounds[0]]
        for index in range(width):
            following.append(
                middle_value(
                    nodes[place + index], givens[place + index], bounds[index], bounds[index + 1]
                )
            )
            following.append(bounds[index + 1])
        bounds = following
    return bounds[1:]


def ring_ends(slots, index):
    level = slots
    path = []
    bit = 0
    while len(level) > 1:
        upper = ((index >> bit) & 1) == 1
        following = []
        for place in range(0, len(level), 2):
            own, other = level[place], level[place + 1]
            left = [jnp.where(upper, b, a) for a, b in zip(own, other)]
            right = [jnp.where(upper, a, b) for a, b in zip(own, other)]
            coefs, node = join_coefs(left[:3], right[:3])
            sides, given = join_sides(left[3:], right[3:], node)
            if place == 0:
                path.append((node, given, upper))
            following.append(coefs + sides)
        level = following
        bit += 1
    _, head, tail, side_head, side_tail = level[0]
    before = after = (side_head + side_tail) * inverse(head + tail)
    for node, given, upper in reversed(path):
        middle = middle_value(node, given, before, after)
        before = jnp.where(upper, middle, before)
        after = jnp.where(upper, after, middle)
    return before, after


def capacity_weights(rates, shares):
    weights = shares * rates / (1.0 + rates)
    return [weights[:, zone : zone + 1] for zone in range(weights.shape[1])]


def strided(ref, start, size, stride):
    return ref[pl.ds(start, size, stride=stride), :]


def x_rolls(halves):
    return [(step, 0) for step in doubling(SUBLANES)] + [(step, 1) for step in doubling(halves)]


def y_rolls():
    return [(step, 0) for step in doubling(SUBLANES)]


def x_forward_kernel(
    halves, mobile_hbm, faces_hbm, capacity_hbm, immobile_hbm, rates_hbm, shares_hbm,
    message_ref, state_ref, storage_ref,
    mobile_ref, faces_ref, capacity_ref, immobile_ref, rates_ref, shares_ref, arrived,
    faces_t, storage_t, source_t,
):
    pairs = (
        (rates_hbm, rates_ref), (shares_hbm, shares_ref), (capacity_hbm, capacity_ref),
        (faces_hbm, faces_ref), (immobile_hbm, immobile_ref), (mobile_hbm, mobile_ref),
    )
    copies = [pltpu.make_async_copy(pair[0], pair[1], arrived.at[place]) for place, pair in enumerate(pairs)]
    for copy in copies:
        copy.start()
    rows = mobile_ref.shape[0]
    stride = LANES // SUBLANES
    for copy in copies[:3]:
        copy.wait()
    weights = capacity_weights(rates_ref[...], shares_ref[...])
    capacity = capacity_ref[...]
    storage = 1.0 + capacity * sum(weights[1:], weights[0])
    storage_ref[...] = storage
    storage_t[...] = storage.T
    copies[3].wait()
    faces_t[...] = faces_ref[...].T
    copies[4].wait()
    total = weights[0] * immobile_ref[0:rows, :]
    for zone in range(1, len(weights)):
        total = total + weights[zone] * immobile_ref[zone * rows : (zone + 1) * rows, :]
    copies[5].wait()
    source_t[...] = (mobile_ref[...] + capacity * total).T
    coefs, sides = [], []
    for index in range(stride):
        coefs.append((strided(faces_t, index, SUBLANES, stride), None, strided(storage_t, index, SUBLANES, stride)))
        sides.append((None, strided(source_t, index, SUBLANES, stride)))
    rolls = x_rolls(halves)
    piece, nodes = tree_coefs(coefs, rolls)
    side, givens = tree_sides(sides, rolls, nodes)
    for place, (node, given) in enumerate(zip(nodes, givens)):
        state_ref[3 * place] = node[0]
        state_ref[3 * place + 1] = node[1]
        state_ref[3 * place + 2] = given
    for row, value in enumerate(piece + side):
        message_ref[row : row + 1, :] = value[0:1, :]


def y_coefs_kernel(halves, faces_ref, storage_ref, rows_ref, state_ref):
    rows = faces_ref.shape[0]
    stride = rows // SUBLANES
    place = 0
    for half in range(halves):
        coefs = []
        for index in range(half, stride, halves):
            coefs.append((strided(faces_ref, index, SUBLANES, stride), None, strided(storage_ref, index, SUBLANES, stride)))
        piece, nodes = tree_coefs(coefs, y_rolls())
        for node in nodes:
            for part in node:
                state_ref[place] = part
                place += 1
        for number, value in enumerate(piece):
            row = number * halves + half
            rows_ref[row : row + 1, :] = value[0:1, :]


def slot_rows(refs, number, height, quantity_rows):
    slots = []
    for ref in refs:
        for slot in range(ref.shape[0] // height):
            slots.append(
                tuple(
                    ref[slot * height + quantity * quantity_rows : slot * height + (quantity + 1) * quantity_rows, :]
                    for quantity in range(QUANTITIES)
                )
            )
    assert len(slots) == number
    return slots


def x_back_kernel(halves, axis, pieces, *refs):
    message_refs = refs[:pieces]
    x_state, y_state, rows_ref, storage_ref = refs[pieces : pieces + 4]
    message_ref, given_ref = refs[pieces + 4 : pieces + 6]
    values_t, sides_ref = refs[pieces + 6 :]
    rows = storage_ref.shape[0]
    count = lax.axis_size(axis)
    slots = slot_rows(message_refs, count, message_refs[0].shape[0], 1)
    before, after = ring_ends(slots, lax.axis_index(axis))
    before = jnp.broadcast_to(before, (SUBLANES, rows))
    after = jnp.broadcast_to(after, (SUBLANES, rows))
    rolls = x_rolls(halves)
    stride = LANES // SUBLANES
    total = stride - 1 + len(rolls)
    nodes = [(x_state[3 * place], x_state[3 * place + 1]) for place in range(total)]
    givens = [x_state[3 * place + 2] for place in range(total)]
    values = tree_values(before, after, rolls, stride, nodes, givens)
    for index, value in enumerate(values):
        values_t[pl.ds(index, SUBLANES, stride=stride), :] = value
    sides_ref[...] = storage_ref[...] * values_t[...].T
    stride = rows // SUBLANES
    place = 0
    height = 3 * halves
    message_ref[0:height, :] = rows_ref[0:height, :]
    total = stride // halves - 1 + len(y_rolls())
    for half in range(halves):
        sides = [(None, strided(sides_ref, index, SUBLANES, stride)) for index in range(half, stride, halves)]
        nodes = [tuple(y_state[3 * (half * total + node) + part] for part in range(3)) for node in range(total)]
        piece, givens = tree_sides(sides, y_rolls(), nodes)
        for given in givens:
            given_ref[place] = given
            place += 1
        for number, value in enumerate(piece):
            row = height + number * halves + half
            message_ref[row : row + 1, :] = value[0:1, :]


def y_back_kernel(halves, axis, pieces, *refs):
    message_refs = refs[:pieces]
    y_state, given_ref, out_ref = refs[pieces:]
    rows = out_ref.shape[0]
    stride = rows // SUBLANES
    count = lax.axis_size(axis)
    own = lax.axis_index(axis)
    slots = slot_rows(message_refs, count, message_refs[0].shape[0], halves)
    before, after = ring_ends(slots, own)
    total = stride // halves - 1 + len(y_rolls())
    for half in range(halves):
        first = jnp.broadcast_to(before[half : half + 1, :], (SUBLANES, LANES))
        last = jnp.broadcast_to(after[half : half + 1, :], (SUBLANES, LANES))
        nodes = [tuple(y_state[3 * (half * total + node) + part] for part in range(2)) for node in range(total)]
        givens = [given_ref[half * total + node] for node in range(total)]
        values = tree_values(first, last, y_rolls(), stride // halves, nodes, givens)
        for index, value in enumerate(values):
            out_ref[pl.ds(index * halves + half, SUBLANES, stride=stride), :] = value


def exchange(message, axis):
    count = lax.axis_size(axis)
    pieces = [message]
    held = message
    step = 1
    while step < count:
        received = lax.ppermute(held, axis, [(index, index ^ step) for index in range(count)])
        pieces.append(received)
        step *= 2
        if step < count:
            held = jnp.concatenate([held, received], axis=0)
    return pieces


def f32(*shape):
    return jax.ShapeDtypeStruct(shape, jnp.float32)


def held_f32(*shape):
    return VMEM(shape, jnp.float32)


def kernel_call(body, operands, outputs, scratch, space=VMEM):
    return pl.pallas_call(
        body,
        out_shape=outputs,
        in_specs=[pl.BlockSpec(memory_space=space)] * len(operands),
        out_specs=[pl.BlockSpec(memory_space=VMEM)] * len(outputs),
        scratch_shapes=scratch,
        compiler_params=pltpu.CompilerParams(vmem_limit_bytes=16 * 1024 * 1024),
    )(*operands)


def local(mobile, dispersion_x, dispersion_y, capacity, immobile, exchange_rates, rate_shares):
    shape = mobile.shape
    lines, width = shape[0] * shape[1], shape[2]
    zones = immobile.shape[0]
    halves = width // LANES
    rows = lines * halves
    assert rows == LANES

    def flat(values):
        return values.reshape(-1, LANES)

    mobile, dispersion_x, dispersion_y = flat(mobile), flat(dispersion_x), flat(dispersion_y)
    capacity, immobile = flat(capacity), flat(immobile)
    square = VMEM((rows, LANES), jnp.float32)
    x_nodes = LANES // SUBLANES - 1 + len(x_rolls(halves))
    y_nodes = halves * (rows // SUBLANES // halves - 1 + len(y_rolls()))
    y_height = -(-QUANTITIES * halves // SUBLANES) * SUBLANES
    message, x_state, storage = kernel_call(
        functools.partial(x_forward_kernel, halves),
        tuple(
            pltpu.with_memory_space_constraint(value, pltpu.HBM)
            for value in (mobile, dispersion_x, capacity, immobile, exchange_rates[None], rate_shares[None])
        ),
        [f32(SUBLANES, rows), held_f32(3 * x_nodes, SUBLANES, rows), held_f32(rows, LANES)],
        [square] * 3
        + [VMEM((zones * rows, LANES), jnp.float32)]
        + [VMEM((1, zones), jnp.float32)] * 2
        + [pltpu.SemaphoreType.DMA((6,))]
        + [square] * 3,
        pltpu.HBM,
    )
    y_rows, y_state = kernel_call(
        functools.partial(y_coefs_kernel, halves),
        (dispersion_y, storage),
        [held_f32(SUBLANES, LANES), held_f32(3 * y_nodes, SUBLANES, LANES)],
        [],
    )
    pieces = exchange(message, "xg")
    message, givens = kernel_call(
        functools.partial(x_back_kernel, halves, "xg", len(pieces)),
        (*pieces, x_state, y_state, y_rows, storage),
        [f32(y_height, LANES), held_f32(y_nodes, SUBLANES, LANES)],
        [square] * 2,
    )
    pieces = exchange(message, "yd")
    (updated,) = kernel_call(
        functools.partial(y_back_kernel, halves, "yd", len(pieces)),
        (*pieces, y_state, givens),
        [f32(rows, LANES)],
        [],
    )
    return updated.reshape(shape)


def solution(mesh):
    field = P("yd", None, "xg")
    return jax.shard_map(
        local,
        mesh=mesh,
        in_specs=(field, field, field, field, P(None, "yd", None, "xg"), P(), P()),
        out_specs=field,
        check_vma=False,
    )
```

```python
import functools

import jax
import jax.numpy as jnp
from jax import lax
from jax.experimental import pallas as pl
from jax.experimental.pallas import tpu as pltpu
from jax.sharding import PartitionSpec as P

LANES = 128
SUBLANES = 8
QUANTITIES = 5
VMEM = pltpu.VMEM


def inverse(value):
    return 1.0 / value


def plus(first, second):
    if first is None:
        return second
    return first + second


def join_coefs(left, right):
    coupling_1, head_1, tail_1 = left
    coupling_2, head_2, tail_2 = right
    middle = plus(head_2, tail_1)
    inv = inverse(coupling_1 + coupling_2 + middle)
    weight_1 = coupling_1 * inv
    weight_2 = coupling_2 * inv
    joined = (coupling_1 * weight_2, plus(head_1, weight_1 * middle), tail_2 + weight_2 * middle)
    return joined, (weight_1, weight_2, inv)


def join_sides(left, right, node):
    head_1, tail_1 = left
    head_2, tail_2 = right
    weight_1, weight_2, inv = node
    side = plus(head_2, tail_1)
    joined = (plus(head_1, weight_1 * side), tail_2 + weight_2 * side)
    return joined, side * inv


def middle_value(node, given, before, after):
    return given + node[0] * before + node[1] * after


def ahead(value, step, axis):
    return pltpu.roll(value, value.shape[axis] - step, axis)


def behind(value, step, axis):
    return pltpu.roll(value, step, axis)


def doubling(count):
    steps = []
    step = 1
    while step < count:
        steps.append(step)
        step *= 2
    return steps


def tree_coefs(leaves, rolls):
    nodes = []
    level = leaves
    while len(level) > 1:
        following = []
        for index in range(0, len(level), 2):
            joined, node = join_coefs(level[index], level[index + 1])
            following.append(joined)
            nodes.append(node)
        level = following
    piece = level[0]
    for step, axis in rolls:
        piece, node = join_coefs(piece, tuple(ahead(part, step, axis) for part in piece))
        nodes.append(node)
    return piece, nodes


def tree_sides(leaves, rolls, nodes):
    givens = []
    level = leaves
    while len(level) > 1:
        following = []
        for index in range(0, len(level), 2):
            joined, given = join_sides(level[index], level[index + 1], nodes[len(givens)])
            following.append(joined)
            givens.append(given)
        level = following
    piece = level[0]
    for step, axis in rolls:
        other = tuple(ahead(part, step, axis) for part in piece)
        piece, given = join_sides(piece, other, nodes[len(givens)])
        givens.append(given)
    return piece, givens


def tree_values(before, after, rolls, count, nodes, givens):
    place = len(nodes)
    for step, axis in reversed(rolls):
        place -= 1
        middle = middle_value(nodes[place], givens[place], before, after)
        upper = (lax.broadcasted_iota(jnp.int32, middle.shape, axis) & step) != 0
        before = jnp.where(upper, behind(middle, step, axis), before)
        after = jnp.where(upper, behind(after, step, axis), middle)
    bounds = [before, after]
    while len(bounds) - 1 < count:
        width = len(bounds) - 1
        place -= width
        following = [bounds[0]]
        for index in range(width):
            following.append(
                middle_value(
                    nodes[place + index], givens[place + index], bounds[index], bounds[index + 1]
                )
            )
            following.append(bounds[index + 1])
        bounds = following
    return bounds[1:]


def ring_bounds(slots, index):
    level = slots
    rounds = []
    bit = 0
    while len(level) > 1:
        upper = ((index >> bit) & 1) == 1
        following, nodes = [], []
        for place in range(0, len(level), 2):
            own, other = level[place], level[place + 1]
            left = [jnp.where(upper, b, a) for a, b in zip(own, other)]
            right = [jnp.where(upper, a, b) for a, b in zip(own, other)]
            coefs, node = join_coefs(left[:3], right[:3])
            sides, given = join_sides(left[3:], right[3:], node)
            nodes.append((node, given))
            following.append(coefs + sides)
        rounds.append((nodes, upper))
        level = following
        bit += 1
    _, head, tail, side_head, side_tail = level[0]
    last = (side_head + side_tail) * inverse(head + tail)
    bounds = [(last, last)]
    for nodes, upper in reversed(rounds):
        following = []
        for (node, given), (before, after) in zip(nodes, bounds):
            middle = middle_value(node, given, before, after)
            following.append((jnp.where(upper, middle, before), jnp.where(upper, after, middle)))
            following.append((jnp.where(upper, before, middle), jnp.where(upper, middle, after)))
        bounds = following
    return bounds


def capacity_weights(rates, shares):
    weights = shares * rates / (1.0 + rates)
    return [weights[:, zone : zone + 1] for zone in range(weights.shape[1])]


def strided(ref, start, size, stride):
    return ref[pl.ds(start, size, stride=stride), :]


def x_rolls(halves):
    return [(step, 0) for step in doubling(SUBLANES)] + [(step, 1) for step in doubling(halves)]


def y_rolls():
    return [(step, 0) for step in doubling(SUBLANES)]


def x_forward_kernel(
    halves, mobile_hbm, faces_hbm, across_hbm, capacity_hbm, immobile_hbm, rates_hbm, shares_hbm,
    message_ref, block_ref,
    mobile_ref, faces_ref, capacity_ref, immobile_ref, rates_ref, shares_ref, arrived,
    faces_t, storage_t, source_t,
):
    pairs = (
        (rates_hbm, rates_ref), (shares_hbm, shares_ref), (capacity_hbm, capacity_ref),
        (faces_hbm, faces_ref), (immobile_hbm, immobile_ref), (mobile_hbm, mobile_ref),
        (across_hbm, block_ref.at[mobile_ref.shape[0] : 2 * mobile_ref.shape[0], :]),
    )
    copies = [pltpu.make_async_copy(pair[0], pair[1], arrived.at[place]) for place, pair in enumerate(pairs)]
    for copy in copies:
        copy.start()
    rows = mobile_ref.shape[0]
    stride = LANES // SUBLANES
    for copy in copies[:3]:
        copy.wait()
    weights = capacity_weights(rates_ref[...], shares_ref[...])
    capacity = capacity_ref[...]
    storage = 1.0 + capacity * sum(weights[1:], weights[0])
    block_ref[0:rows, :] = storage
    storage_t[...] = storage.T
    copies[3].wait()
    faces_t[...] = faces_ref[...].T
    copies[4].wait()
    total = weights[0] * immobile_ref[0:rows, :]
    for zone in range(1, len(weights)):
        total = total + weights[zone] * immobile_ref[zone * rows : (zone + 1) * rows, :]
    copies[5].wait()
    source_t[...] = (mobile_ref[...] + capacity * total).T
    coefs, sides = [], []
    for index in range(stride):
        coefs.append((strided(faces_t, index, SUBLANES, stride), None, strided(storage_t, index, SUBLANES, stride)))
        sides.append((None, strided(source_t, index, SUBLANES, stride)))
    rolls = x_rolls(halves)
    piece, nodes = tree_coefs(coefs, rolls)
    side, givens = tree_sides(sides, rolls, nodes)
    start = 2 * rows
    for node, given in zip(nodes, givens):
        for part in (node[0], node[1], given):
            block_ref[start : start + SUBLANES, :] = part
            start += SUBLANES
    for row, value in enumerate(piece + side):
        message_ref[row : row + 1, :] = value[0:1, :]
    copies[6].wait()


def y_coefs_kernel(halves, block_ref, rows_ref, state_ref):
    rows = rows_ref.shape[1]
    stride = rows // SUBLANES
    start = 0
    for half in range(halves):
        coefs = []
        for index in range(half, stride, halves):
            storage = strided(block_ref, index, SUBLANES, stride)
            coefs.append((strided(block_ref, rows + index, SUBLANES, stride), None, storage))
        piece, nodes = tree_coefs(coefs, y_rolls())
        for node in nodes:
            for part in node:
                state_ref[start : start + SUBLANES, :] = part
                start += SUBLANES
        for number, value in enumerate(piece):
            row = number * halves + half
            rows_ref[row : row + 1, :] = value[0:1, :]


def state_parts(ref, first, total, parts):
    return [
        tuple(
            ref[(3 * place + part) * SUBLANES : (3 * place + part + 1) * SUBLANES, :]
            for part in range(parts)
        )
        for place in range(first, first + total)
    ]


def message_slots(refs, height, quantity_rows):
    slots = []
    for ref in refs:
        for start in range(0, ref.shape[0], height):
            slots.append(
                tuple(
                    ref[start + quantity * quantity_rows : start + (quantity + 1) * quantity_rows, :]
                    for quantity in range(QUANTITIES)
                )
            )
    return slots


def x_back(halves, bounds, block_ref, values_t, sides_ref):
    rows = values_t.shape[1]
    before, after = (jnp.broadcast_to(bound, (SUBLANES, rows)) for bound in bounds)
    rolls = x_rolls(halves)
    stride = LANES // SUBLANES
    total = stride - 1 + len(rolls)
    parts = state_parts(block_ref.at[2 * rows :, :], 0, total, 3)
    values = tree_values(before, after, rolls, stride, parts, [part[2] for part in parts])
    for index, value in enumerate(values):
        values_t[pl.ds(index, SUBLANES, stride=stride), :] = value
    sides_ref[...] = block_ref[0:rows, :] * values_t[...].T


def x_back_kernel(halves, axis, pieces, *refs):
    slots = message_slots(refs[:pieces], SUBLANES, 1)
    block_refs, rows_refs, state_refs = (refs[pieces + 2 * pair : pieces + 2 * pair + 2] for pair in range(3))
    message_ref, *given_refs = refs[pieces + 6 : pieces + 9]
    scratch = refs[pieces + 9 :]
    bounds = ring_bounds(slots, lax.axis_index(axis))
    rows = scratch[0].shape[1]
    stride = rows // SUBLANES
    total = stride // halves - 1 + len(y_rolls())
    both = 2 * halves
    for block in range(2):
        values_t, sides_ref = scratch[2 * block : 2 * block + 2]
        x_back(halves, bounds[1 - block], block_refs[block], values_t, sides_ref)
        start = 0
        for half in range(halves):
            place = block * halves + half
            sides = [(None, strided(sides_ref, index, SUBLANES, stride)) for index in range(half, stride, halves)]
            nodes = state_parts(state_refs[block], half * total, total, 3)
            piece, givens = tree_sides(sides, y_rolls(), nodes)
            for given in givens:
                given_refs[block][start : start + SUBLANES, :] = given
                start += SUBLANES
            for number in range(3):
                row = number * halves + half
                message_ref[number * both + place : number * both + place + 1, :] = rows_refs[block][row : row + 1, :]
            for number, value in enumerate(piece):
                row = (3 + number) * both + place
                message_ref[row : row + 1, :] = value[0:1, :]


def y_ring_kernel(halves, axis, height, pieces, *refs):
    slots = message_slots(refs[:pieces], height, 2 * halves)
    bounds = ring_bounds(slots, lax.axis_index(axis))
    for ref, (before, after) in zip(refs[pieces:], bounds):
        ref[0 : 2 * halves, :] = before
        ref[2 * halves : 4 * halves, :] = after


def y_back_kernel(halves, axes, hubs, sent, *refs):
    own_ref, *sent_refs = refs[: 1 + sent]
    state_ref, own_given, sent_given, out_ref = refs[1 + sent :]
    rows = out_ref.shape[0]
    stride = rows // SUBLANES
    other = lax.axis_index(axes[0]) % 2 == 0
    place = lax.axis_index(axes[1])
    solved = place == hubs[0]
    for hub in hubs[1:]:
        solved = solved | (place == hub)
    ends = jnp.where(solved & jnp.logical_not(other), own_ref[...], 0.0)
    for ref in sent_refs:
        ends = ends + ref[...]
    total = stride // halves - 1 + len(y_rolls())
    both = 2 * halves
    for half in range(halves):
        bounds = []
        for end in range(2):
            row = end * both + half
            bound = jnp.where(other, ends[row : row + 1, :], ends[row + halves : row + halves + 1, :])
            bounds.append(jnp.broadcast_to(bound, (SUBLANES, LANES)))
        nodes = state_parts(state_ref, half * total, total, 2)
        givens = []
        for node in range(half * total, (half + 1) * total):
            part = slice(node * SUBLANES, (node + 1) * SUBLANES)
            givens.append(jnp.where(other, sent_given[part, :], own_given[part, :]))
        values = tree_values(*bounds, y_rolls(), stride // halves, nodes, givens)
        for index, value in enumerate(values):
            out_ref[pl.ds(index * halves + half, SUBLANES, stride=stride), :] = value


def send(value, pairs):
    width = lax.axis_size("yd")
    flat = [(source[0] * width + source[1], target[0] * width + target[1]) for source, target in pairs]
    return lax.ppermute(value, ("xg", "yd"), flat)


def x_exchange(message, block):
    count, lines = lax.axis_size("xg"), range(lax.axis_size("yd"))
    odd = range(1, count, 2)
    pieces = [message]
    for chip in range(0, count, 2):
        if chip:
            pieces.append(send(message, [((index ^ chip, line), (index, line)) for index in odd for line in lines]))
        pieces.append(send(message, [((index ^ chip ^ 1, line), (index, line)) for index in odd for line in lines]))
    to_odd = [((index - 1, line), (index, line)) for index in odd for line in lines]
    return pieces, send(block, to_odd)


def to_even(value):
    odd = range(1, lax.axis_size("xg"), 2)
    return send(value, [((index, line), (index - 1, line)) for index in odd for line in range(lax.axis_size("yd"))])


def y_hubs(count):
    return [count // 4, count // 2] if 4 <= count <= 8 else list(range(count))


def y_gather(message):
    count = lax.axis_size("yd")
    hubs = y_hubs(count)
    odd = range(1, lax.axis_size("xg"), 2)
    if len(hubs) < count:
        return [message] + [
            send(message, [((index, hub ^ slot), (index, hub)) for index in odd for hub in hubs])
            for slot in range(1, count)
        ]
    pieces = [message]
    held = message
    for step in doubling(count):
        received = send(held, [((index, line ^ step), (index, line)) for index in odd for line in range(count)])
        pieces.append(received)
        held = jnp.concatenate([held, received], axis=0)
    return pieces


def y_spread(bounds):
    hubs = y_hubs(lax.axis_size("yd"))
    odd = range(1, lax.axis_size("xg"), 2)
    sent = []
    for slot, value in enumerate(bounds):
        for step in (1, 0):
            if slot or step:
                sent.append(
                    send(value, [((index, hub), (index - step, hub ^ slot)) for index in odd for hub in hubs])
                )
    return sent


def f32(*shape):
    return jax.ShapeDtypeStruct(shape, jnp.float32)


def held_f32(*shape):
    return VMEM(shape, jnp.float32)


def kernel_call(body, operands, outputs, scratch, space=VMEM):
    return pl.pallas_call(
        body,
        out_shape=outputs,
        in_specs=[pl.BlockSpec(memory_space=space)] * len(operands),
        out_specs=[pl.BlockSpec(memory_space=VMEM)] * len(outputs),
        scratch_shapes=scratch,
        compiler_params=pltpu.CompilerParams(vmem_limit_bytes=16 * 1024 * 1024),
    )(*operands)


def local(mobile, dispersion_x, dispersion_y, capacity, immobile, exchange_rates, rate_shares):
    shape = mobile.shape
    lines, width = shape[0] * shape[1], shape[2]
    zones = immobile.shape[0]
    halves = width // LANES
    rows = lines * halves
    assert rows == LANES

    def flat(values):
        return values.reshape(-1, LANES)

    mobile, dispersion_x, dispersion_y = flat(mobile), flat(dispersion_x), flat(dispersion_y)
    capacity, immobile = flat(capacity), flat(immobile)
    square = VMEM((rows, LANES), jnp.float32)
    x_nodes = LANES // SUBLANES - 1 + len(x_rolls(halves))
    y_nodes = halves * (rows // SUBLANES // halves - 1 + len(y_rolls()))
    message, block = kernel_call(
        functools.partial(x_forward_kernel, halves),
        tuple(
            pltpu.with_memory_space_constraint(value, pltpu.HBM)
            for value in (
                mobile, dispersion_x, dispersion_y, capacity, immobile, exchange_rates[None], rate_shares[None],
            )
        ),
        [f32(SUBLANES, rows), held_f32(2 * rows + 3 * x_nodes * SUBLANES, LANES)],
        [square] * 3
        + [VMEM((zones * rows, LANES), jnp.float32)]
        + [VMEM((1, zones), jnp.float32)] * 2
        + [pltpu.SemaphoreType.DMA((7,))]
        + [square] * 3,
        pltpu.HBM,
    )
    pieces, other_block = x_exchange(message, block)
    y_rows, y_state = zip(
        *(
            kernel_call(
                functools.partial(y_coefs_kernel, halves),
                (part,),
                [held_f32(SUBLANES, LANES), held_f32(3 * y_nodes * SUBLANES, LANES)],
                [],
            )
            for part in (other_block, block)
        )
    )
    height = -(-QUANTITIES * 2 * halves // SUBLANES) * SUBLANES
    message, other_givens, givens = kernel_call(
        functools.partial(x_back_kernel, halves, "xg", len(pieces)),
        (*pieces, other_block, block, *y_rows, *y_state),
        [f32(height, LANES), f32(y_nodes * SUBLANES, LANES), held_f32(y_nodes * SUBLANES, LANES)],
        [square] * 4,
    )
    pieces = y_gather(message)
    sent_givens = to_even(other_givens)
    count = lax.axis_size("yd")
    hubs = y_hubs(count)
    bounds = kernel_call(
        functools.partial(y_ring_kernel, halves, "yd", height, len(pieces)),
        tuple(pieces),
        [f32(4 * halves, LANES)] * (count // len(hubs)),
        [],
    )
    sent = y_spread(bounds)
    (updated,) = kernel_call(
        functools.partial(y_back_kernel, halves, ("xg", "yd"), hubs, len(sent)),
        (bounds[0], *sent, y_state[1], givens, sent_givens),
        [f32(rows, LANES)],
        [],
    )
    return updated.reshape(shape)


def solution(mesh):
    field = P("yd", None, "xg")
    return jax.shard_map(
        local,
        mesh=mesh,
        in_specs=(field, field, field, field, P(None, "yd", None, "xg"), P(), P()),
        out_specs=field,
        check_vma=False,
    )
```

```python
import functools

import jax
import jax.numpy as jnp
from jax import lax
from jax.experimental import pallas as pl
from jax.experimental.pallas import tpu as pltpu
from jax.sharding import PartitionSpec as P

LANES = 128
SUBLANES = 8
QUANTITIES = 5
VMEM = pltpu.VMEM


def inverse(value):
    return 1.0 / value


def plus(first, second):
    if first is None:
        return second
    return first + second


def join_coefs(left, right):
    coupling_1, head_1, tail_1 = left
    coupling_2, head_2, tail_2 = right
    middle = plus(head_2, tail_1)
    inv = inverse(coupling_1 + coupling_2 + middle)
    weight_1 = coupling_1 * inv
    weight_2 = coupling_2 * inv
    joined = (coupling_1 * weight_2, plus(head_1, weight_1 * middle), tail_2 + weight_2 * middle)
    return joined, (weight_1, weight_2, inv)


def join_sides(left, right, node):
    head_1, tail_1 = left
    head_2, tail_2 = right
    weight_1, weight_2, inv = node
    side = plus(head_2, tail_1)
    joined = (plus(head_1, weight_1 * side), tail_2 + weight_2 * side)
    return joined, side * inv


def middle_value(node, given, before, after):
    return given + node[0] * before + node[1] * after


def ahead(value, step, axis):
    return pltpu.roll(value, value.shape[axis] - step, axis)


def behind(value, step, axis):
    return pltpu.roll(value, step, axis)


def doubling(count):
    steps = []
    step = 1
    while step < count:
        steps.append(step)
        step *= 2
    return steps


def tree_coefs(leaves, rolls):
    nodes = []
    level = leaves
    while len(level) > 1:
        following = []
        for index in range(0, len(level), 2):
            joined, node = join_coefs(level[index], level[index + 1])
            following.append(joined)
            nodes.append(node)
        level = following
    piece = level[0]
    for step, axis in rolls:
        piece, node = join_coefs(piece, tuple(ahead(part, step, axis) for part in piece))
        nodes.append(node)
    return piece, nodes


def tree_sides(leaves, rolls, nodes):
    givens = []
    level = leaves
    while len(level) > 1:
        following = []
        for index in range(0, len(level), 2):
            joined, given = join_sides(level[index], level[index + 1], nodes[len(givens)])
            following.append(joined)
            givens.append(given)
        level = following
    piece = level[0]
    for step, axis in rolls:
        other = tuple(ahead(part, step, axis) for part in piece)
        piece, given = join_sides(piece, other, nodes[len(givens)])
        givens.append(given)
    return piece, givens


def tree_values(before, after, rolls, count, nodes, givens):
    place = len(nodes)
    for step, axis in reversed(rolls):
        place -= 1
        middle = middle_value(nodes[place], givens[place], before, after)
        upper = (lax.broadcasted_iota(jnp.int32, middle.shape, axis) & step) != 0
        before = jnp.where(upper, behind(middle, step, axis), before)
        after = jnp.where(upper, behind(after, step, axis), middle)
    bounds = [before, after]
    while len(bounds) - 1 < count:
        width = len(bounds) - 1
        place -= width
        following = [bounds[0]]
        for index in range(width):
            following.append(
                middle_value(
                    nodes[place + index], givens[place + index], bounds[index], bounds[index + 1]
                )
            )
            following.append(bounds[index + 1])
        bounds = following
    return bounds[1:]


def ring_bounds(slots, index):
    level = slots
    rounds = []
    bit = 0
    while len(level) > 1:
        upper = ((index >> bit) & 1) == 1
        following, nodes = [], []
        for place in range(0, len(level), 2):
            own, other = level[place], level[place + 1]
            left = [jnp.where(upper, b, a) for a, b in zip(own, other)]
            right = [jnp.where(upper, a, b) for a, b in zip(own, other)]
            coefs, node = join_coefs(left[:3], right[:3])
            sides, given = join_sides(left[3:], right[3:], node)
            nodes.append((node, given))
            following.append(coefs + sides)
        rounds.append((nodes, upper))
        level = following
        bit += 1
    _, head, tail, side_head, side_tail = level[0]
    last = (side_head + side_tail) * inverse(head + tail)
    bounds = [(last, last)]
    for nodes, upper in reversed(rounds):
        following = []
        for (node, given), (before, after) in zip(nodes, bounds):
            middle = middle_value(node, given, before, after)
            following.append((jnp.where(upper, middle, before), jnp.where(upper, after, middle)))
            following.append((jnp.where(upper, before, middle), jnp.where(upper, middle, after)))
        bounds = following
    return bounds


def capacity_weights(rates, shares):
    weights = shares * rates / (1.0 + rates)
    return [weights[:, zone : zone + 1] for zone in range(weights.shape[1])]


def strided(ref, start, size, stride):
    return ref[pl.ds(start, size, stride=stride), :]


def x_rolls(halves):
    return [(step, 0) for step in doubling(SUBLANES)] + [(step, 1) for step in doubling(halves)]


def y_rolls():
    return [(step, 0) for step in doubling(SUBLANES)]


def x_forward_kernel(
    halves, mobile_hbm, faces_hbm, across_hbm, capacity_hbm, immobile_hbm, rates_hbm, shares_hbm,
    message_ref, block_ref,
    mobile_ref, faces_ref, capacity_ref, immobile_ref, rates_ref, shares_ref, arrived,
    faces_t, storage_t, source_t,
):
    pairs = (
        (rates_hbm, rates_ref), (shares_hbm, shares_ref), (capacity_hbm, capacity_ref),
        (faces_hbm, faces_ref), (immobile_hbm, immobile_ref), (mobile_hbm, mobile_ref),
        (across_hbm, block_ref.at[mobile_ref.shape[0] : 2 * mobile_ref.shape[0], :]),
    )
    copies = [pltpu.make_async_copy(pair[0], pair[1], arrived.at[place]) for place, pair in enumerate(pairs)]
    for copy in copies:
        copy.start()
    rows = mobile_ref.shape[0]
    stride = LANES // SUBLANES
    for copy in copies[:3]:
        copy.wait()
    weights = capacity_weights(rates_ref[...], shares_ref[...])
    capacity = capacity_ref[...]
    storage = 1.0 + capacity * sum(weights[1:], weights[0])
    block_ref[0:rows, :] = storage
    storage_t[...] = storage.T
    copies[3].wait()
    faces_t[...] = faces_ref[...].T
    copies[4].wait()
    total = weights[0] * immobile_ref[0:rows, :]
    for zone in range(1, len(weights)):
        total = total + weights[zone] * immobile_ref[zone * rows : (zone + 1) * rows, :]
    copies[5].wait()
    source_t[...] = (mobile_ref[...] + capacity * total).T
    coefs, sides = [], []
    for index in range(stride):
        coefs.append((strided(faces_t, index, SUBLANES, stride), None, strided(storage_t, index, SUBLANES, stride)))
        sides.append((None, strided(source_t, index, SUBLANES, stride)))
    rolls = x_rolls(halves)
    piece, nodes = tree_coefs(coefs, rolls)
    side, givens = tree_sides(sides, rolls, nodes)
    start = 2 * rows
    for node, given in zip(nodes, givens):
        for part in (node[0], node[1], given):
            block_ref[start : start + SUBLANES, :] = part
            start += SUBLANES
    for row, value in enumerate(piece + side):
        message_ref[row : row + 1, :] = value[0:1, :]
    copies[6].wait()


def y_coefs_kernel(halves, block_ref, rows_ref, state_ref):
    rows = rows_ref.shape[1]
    stride = rows // SUBLANES
    start = 0
    for half in range(halves):
        coefs = []
        for index in range(half, stride, halves):
            storage = strided(block_ref, index, SUBLANES, stride)
            coefs.append((strided(block_ref, rows + index, SUBLANES, stride), None, storage))
        piece, nodes = tree_coefs(coefs, y_rolls())
        for node in nodes:
            for part in node:
                state_ref[start : start + SUBLANES, :] = part
                start += SUBLANES
        for number, value in enumerate(piece):
            row = number * halves + half
            rows_ref[row : row + 1, :] = value[0:1, :]


def state_parts(ref, first, total, parts):
    return [
        tuple(
            ref[(3 * place + part) * SUBLANES : (3 * place + part + 1) * SUBLANES, :]
            for part in range(parts)
        )
        for place in range(first, first + total)
    ]


def message_slots(refs, height, quantity_rows):
    slots = []
    for ref in refs:
        for start in range(0, ref.shape[0], height):
            slots.append(
                tuple(
                    ref[start + quantity * quantity_rows : start + (quantity + 1) * quantity_rows, :]
                    for quantity in range(QUANTITIES)
                )
            )
    return slots


def x_back(halves, bounds, block_ref, values_t, sides_ref):
    rows = values_t.shape[1]
    before, after = (jnp.broadcast_to(bound, (SUBLANES, rows)) for bound in bounds)
    rolls = x_rolls(halves)
    stride = LANES // SUBLANES
    total = stride - 1 + len(rolls)
    parts = state_parts(block_ref.at[2 * rows :, :], 0, total, 3)
    values = tree_values(before, after, rolls, stride, parts, [part[2] for part in parts])
    for index, value in enumerate(values):
        values_t[pl.ds(index, SUBLANES, stride=stride), :] = value
    sides_ref[...] = block_ref[0:rows, :] * values_t[...].T


def x_back_kernel(halves, axis, pieces, *refs):
    slots = message_slots(refs[:pieces], SUBLANES, 1)
    block_refs, rows_refs, state_refs = (refs[pieces + 2 * pair : pieces + 2 * pair + 2] for pair in range(3))
    message_ref, *given_refs = refs[pieces + 6 : pieces + 9]
    scratch = refs[pieces + 9 :]
    bounds = ring_bounds(slots, lax.axis_index(axis))
    rows = scratch[0].shape[1]
    stride = rows // SUBLANES
    total = stride // halves - 1 + len(y_rolls())
    both = 2 * halves
    for block in range(2):
        values_t, sides_ref = scratch[2 * block : 2 * block + 2]
        x_back(halves, bounds[1 - block], block_refs[block], values_t, sides_ref)
        start = 0
        for half in range(halves):
            place = block * halves + half
            sides = [(None, strided(sides_ref, index, SUBLANES, stride)) for index in range(half, stride, halves)]
            nodes = state_parts(state_refs[block], half * total, total, 3)
            piece, givens = tree_sides(sides, y_rolls(), nodes)
            for given in givens:
                given_refs[block][start : start + SUBLANES, :] = given
                start += SUBLANES
            for number in range(3):
                row = number * halves + half
                message_ref[number * both + place : number * both + place + 1, :] = rows_refs[block][row : row + 1, :]
            for number, value in enumerate(piece):
                row = (3 + number) * both + place
                message_ref[row : row + 1, :] = value[0:1, :]


def y_ring_kernel(halves, axis, height, pieces, *refs):
    slots = message_slots(refs[:pieces], height, 2 * halves)
    bounds = ring_bounds(slots, lax.axis_index(axis))
    for ref, (before, after) in zip(refs[pieces:], bounds):
        ref[0 : 2 * halves, :] = before
        ref[2 * halves : 4 * halves, :] = after


def y_back_kernel(halves, axis, own_ref, sent_ref, state_ref, own_given, sent_given, out_ref):
    rows = out_ref.shape[0]
    stride = rows // SUBLANES
    other = lax.axis_index(axis) % 2 == 0
    ends = jnp.where(other, sent_ref[...], own_ref[...])
    total = stride // halves - 1 + len(y_rolls())
    both = 2 * halves
    for half in range(halves):
        bounds = []
        for end in range(2):
            row = end * both + half
            bound = jnp.where(other, ends[row : row + 1, :], ends[row + halves : row + halves + 1, :])
            bounds.append(jnp.broadcast_to(bound, (SUBLANES, LANES)))
        nodes = state_parts(state_ref, half * total, total, 2)
        givens = []
        for node in range(half * total, (half + 1) * total):
            part = slice(node * SUBLANES, (node + 1) * SUBLANES)
            givens.append(jnp.where(other, sent_given[part, :], own_given[part, :]))
        values = tree_values(*bounds, y_rolls(), stride // halves, nodes, givens)
        for index, value in enumerate(values):
            out_ref[pl.ds(index * halves + half, SUBLANES, stride=stride), :] = value


def swap(value, steps):
    width = lax.axis_size("yd")
    pairs = []
    for index in range(lax.axis_size("xg")):
        step = steps(index)
        for line in range(width):
            pairs.append((index * width + line, (index ^ step[0]) * width + (line ^ step[1])))
    return lax.ppermute(value, ("xg", "yd"), pairs)


def swap_cores(value):
    return swap(value, lambda index: (1, 0))


def swap_odd(value, step):
    return swap(value, lambda index: step if index % 2 else (0, 0))


def gather_odd(pieces, held, steps):
    for place, step in enumerate(steps):
        received = swap_odd(held, step)
        pieces.append(received)
        if place < len(steps) - 1:
            held = jnp.concatenate([held, received], axis=0)
    return pieces


def x_exchange(message, block):
    other = swap_cores(message)
    block, other = lax.optimization_barrier((block, other))
    other_block = swap_cores(block)
    steps = [(2 * step, 0) for step in doubling(lax.axis_size("xg") // 2)]
    held = jnp.concatenate([message, other], axis=0)
    return gather_odd([message, other], held, steps), other_block


def y_exchange(message):
    return gather_odd([message], message, [(0, step) for step in doubling(lax.axis_size("yd"))])


def f32(*shape):
    return jax.ShapeDtypeStruct(shape, jnp.float32)


def held_f32(*shape):
    return VMEM(shape, jnp.float32)


def kernel_call(body, operands, outputs, scratch, space=VMEM):
    return pl.pallas_call(
        body,
        out_shape=outputs,
        in_specs=[pl.BlockSpec(memory_space=space)] * len(operands),
        out_specs=[pl.BlockSpec(memory_space=VMEM)] * len(outputs),
        scratch_shapes=scratch,
        compiler_params=pltpu.CompilerParams(vmem_limit_bytes=16 * 1024 * 1024),
    )(*operands)


def local(mobile, dispersion_x, dispersion_y, capacity, immobile, exchange_rates, rate_shares):
    shape = mobile.shape
    lines, width = shape[0] * shape[1], shape[2]
    zones = immobile.shape[0]
    halves = width // LANES
    rows = lines * halves
    assert rows == LANES

    def flat(values):
        return values.reshape(-1, LANES)

    mobile, dispersion_x, dispersion_y = flat(mobile), flat(dispersion_x), flat(dispersion_y)
    capacity, immobile = flat(capacity), flat(immobile)
    square = VMEM((rows, LANES), jnp.float32)
    x_nodes = LANES // SUBLANES - 1 + len(x_rolls(halves))
    y_nodes = halves * (rows // SUBLANES // halves - 1 + len(y_rolls()))
    message, block = kernel_call(
        functools.partial(x_forward_kernel, halves),
        tuple(
            pltpu.with_memory_space_constraint(value, pltpu.HBM)
            for value in (
                mobile, dispersion_x, dispersion_y, capacity, immobile, exchange_rates[None], rate_shares[None],
            )
        ),
        [f32(SUBLANES, rows), held_f32(2 * rows + 3 * x_nodes * SUBLANES, LANES)],
        [square] * 3
        + [VMEM((zones * rows, LANES), jnp.float32)]
        + [VMEM((1, zones), jnp.float32)] * 2
        + [pltpu.SemaphoreType.DMA((7,))]
        + [square] * 3,
        pltpu.HBM,
    )
    pieces, other_block = x_exchange(message, block)
    y_rows, y_state = zip(
        *(
            kernel_call(
                functools.partial(y_coefs_kernel, halves),
                (part,),
                [held_f32(SUBLANES, LANES), held_f32(3 * y_nodes * SUBLANES, LANES)],
                [],
            )
            for part in (other_block, block)
        )
    )
    height = -(-QUANTITIES * 2 * halves // SUBLANES) * SUBLANES
    message, other_givens, givens = kernel_call(
        functools.partial(x_back_kernel, halves, "xg", len(pieces)),
        (*pieces, other_block, block, *y_rows, *y_state),
        [f32(height, LANES), f32(y_nodes * SUBLANES, LANES), held_f32(y_nodes * SUBLANES, LANES)],
        [square] * 4,
    )
    pieces = y_exchange(message)
    sent_givens = swap_cores(other_givens)
    (bounds,) = kernel_call(
        functools.partial(y_ring_kernel, halves, "yd", height, len(pieces)),
        tuple(pieces),
        [f32(4 * halves, LANES)],
        [],
    )
    (updated,) = kernel_call(
        functools.partial(y_back_kernel, halves, "xg"),
        (bounds, swap_cores(bounds), y_state[1], givens, sent_givens),
        [f32(rows, LANES)],
        [],
    )
    return updated.reshape(shape)


def solution(mesh):
    field = P("yd", None, "xg")
    return jax.shard_map(
        local,
        mesh=mesh,
        in_specs=(field, field, field, field, P(None, "yd", None, "xg"), P(), P()),
        out_specs=field,
        check_vma=False,
    )
```

```python
import functools

import jax
import jax.numpy as jnp
from jax import lax
from jax.experimental import pallas as pl
from jax.experimental.pallas import tpu as pltpu
from jax.sharding import PartitionSpec as P

LANES = 128
SUBLANES = 8
QUANTITIES = 5
VMEM = pltpu.VMEM


def inverse(value):
    return 1.0 / value


def plus(first, second):
    if first is None:
        return second
    return first + second


def join_coefs(left, right):
    coupling_1, head_1, tail_1 = left
    coupling_2, head_2, tail_2 = right
    middle = plus(head_2, tail_1)
    inv = inverse(coupling_1 + coupling_2 + middle)
    weight_1 = coupling_1 * inv
    weight_2 = coupling_2 * inv
    joined = (coupling_1 * weight_2, plus(head_1, weight_1 * middle), tail_2 + weight_2 * middle)
    return joined, (weight_1, weight_2, inv)


def join_sides(left, right, node):
    head_1, tail_1 = left
    head_2, tail_2 = right
    weight_1, weight_2, inv = node
    side = plus(head_2, tail_1)
    joined = (plus(head_1, weight_1 * side), tail_2 + weight_2 * side)
    return joined, side * inv


def middle_value(node, given, before, after):
    return given + node[0] * before + node[1] * after


def ahead(value, step, axis):
    return pltpu.roll(value, value.shape[axis] - step, axis)


def behind(value, step, axis):
    return pltpu.roll(value, step, axis)


def doubling(count):
    steps = []
    step = 1
    while step < count:
        steps.append(step)
        step *= 2
    return steps


def tree_coefs(leaves, rolls):
    nodes = []
    level = leaves
    while len(level) > 1:
        following = []
        for index in range(0, len(level), 2):
            joined, node = join_coefs(level[index], level[index + 1])
            following.append(joined)
            nodes.append(node)
        level = following
    piece = level[0]
    for step, axis in rolls:
        piece, node = join_coefs(piece, tuple(ahead(part, step, axis) for part in piece))
        nodes.append(node)
    return piece, nodes


def tree_sides(leaves, rolls, nodes):
    givens = []
    level = leaves
    while len(level) > 1:
        following = []
        for index in range(0, len(level), 2):
            joined, given = join_sides(level[index], level[index + 1], nodes[len(givens)])
            following.append(joined)
            givens.append(given)
        level = following
    piece = level[0]
    for step, axis in rolls:
        other = tuple(ahead(part, step, axis) for part in piece)
        piece, given = join_sides(piece, other, nodes[len(givens)])
        givens.append(given)
    return piece, givens


def tree_values(before, after, rolls, count, nodes, givens):
    place = len(nodes)
    for step, axis in reversed(rolls):
        place -= 1
        middle = middle_value(nodes[place], givens[place], before, after)
        upper = (lax.broadcasted_iota(jnp.int32, middle.shape, axis) & step) != 0
        before = jnp.where(upper, behind(middle, step, axis), before)
        after = jnp.where(upper, behind(after, step, axis), middle)
    bounds = [before, after]
    while len(bounds) - 1 < count:
        width = len(bounds) - 1
        place -= width
        following = [bounds[0]]
        for index in range(width):
            following.append(
                middle_value(
                    nodes[place + index], givens[place + index], bounds[index], bounds[index + 1]
                )
            )
            following.append(bounds[index + 1])
        bounds = following
    return bounds[1:]


def ring_bounds(slots, index):
    level = slots
    rounds = []
    bit = 0
    while len(level) > 1:
        upper = ((index >> bit) & 1) == 1
        following, nodes = [], []
        for place in range(0, len(level), 2):
            own, other = level[place], level[place + 1]
            left = [jnp.where(upper, b, a) for a, b in zip(own, other)]
            right = [jnp.where(upper, a, b) for a, b in zip(own, other)]
            coefs, node = join_coefs(left[:3], right[:3])
            sides, given = join_sides(left[3:], right[3:], node)
            nodes.append((node, given))
            following.append(coefs + sides)
        rounds.append((nodes, upper))
        level = following
        bit += 1
    _, head, tail, side_head, side_tail = level[0]
    last = (side_head + side_tail) * inverse(head + tail)
    bounds = [(last, last)]
    for nodes, upper in reversed(rounds):
        following = []
        for (node, given), (before, after) in zip(nodes, bounds):
            middle = middle_value(node, given, before, after)
            following.append((jnp.where(upper, middle, before), jnp.where(upper, after, middle)))
            following.append((jnp.where(upper, before, middle), jnp.where(upper, middle, after)))
        bounds = following
    return bounds


def capacity_weights(rates, shares):
    weights = shares * rates / (1.0 + rates)
    return [weights[:, zone : zone + 1] for zone in range(weights.shape[1])]


def strided(ref, start, size, stride):
    return ref[pl.ds(start, size, stride=stride), :]


def x_rolls(halves):
    return [(step, 0) for step in doubling(SUBLANES)] + [(step, 1) for step in doubling(halves)]


def y_rolls():
    return [(step, 0) for step in doubling(SUBLANES)]


def x_forward_kernel(
    halves, mobile_hbm, faces_hbm, across_hbm, capacity_hbm, immobile_hbm, rates_hbm, shares_hbm,
    message_ref, block_ref,
    mobile_ref, faces_ref, capacity_ref, immobile_ref, rates_ref, shares_ref, arrived,
    faces_t, storage_t, source_t,
):
    pairs = (
        (rates_hbm, rates_ref), (shares_hbm, shares_ref), (capacity_hbm, capacity_ref),
        (faces_hbm, faces_ref), (immobile_hbm, immobile_ref), (mobile_hbm, mobile_ref),
        (across_hbm, block_ref.at[mobile_ref.shape[0] : 2 * mobile_ref.shape[0], :]),
    )
    copies = [pltpu.make_async_copy(pair[0], pair[1], arrived.at[place]) for place, pair in enumerate(pairs)]
    for copy in copies:
        copy.start()
    rows = mobile_ref.shape[0]
    stride = LANES // SUBLANES
    for copy in copies[:3]:
        copy.wait()
    weights = capacity_weights(rates_ref[...], shares_ref[...])
    capacity = capacity_ref[...]
    storage = 1.0 + capacity * sum(weights[1:], weights[0])
    block_ref[0:rows, :] = storage
    storage_t[...] = storage.T
    copies[3].wait()
    faces_t[...] = faces_ref[...].T
    copies[4].wait()
    total = weights[0] * immobile_ref[0:rows, :]
    for zone in range(1, len(weights)):
        total = total + weights[zone] * immobile_ref[zone * rows : (zone + 1) * rows, :]
    copies[5].wait()
    source_t[...] = (mobile_ref[...] + capacity * total).T
    coefs, sides = [], []
    for index in range(stride):
        coefs.append((strided(faces_t, index, SUBLANES, stride), None, strided(storage_t, index, SUBLANES, stride)))
        sides.append((None, strided(source_t, index, SUBLANES, stride)))
    rolls = x_rolls(halves)
    piece, nodes = tree_coefs(coefs, rolls)
    side, givens = tree_sides(sides, rolls, nodes)
    start = 2 * rows
    for node, given in zip(nodes, givens):
        for part in (node[0], node[1], given):
            block_ref[start : start + SUBLANES, :] = part
            start += SUBLANES
    for row, value in enumerate(piece + side):
        message_ref[row : row + 1, :] = value[0:1, :]
    copies[6].wait()


def y_coefs_kernel(halves, block_ref, rows_ref, state_ref):
    rows = rows_ref.shape[1]
    stride = rows // SUBLANES
    start = 0
    for half in range(halves):
        coefs = []
        for index in range(half, stride, halves):
            storage = strided(block_ref, index, SUBLANES, stride)
            coefs.append((strided(block_ref, rows + index, SUBLANES, stride), None, storage))
        piece, nodes = tree_coefs(coefs, y_rolls())
        for node in nodes:
            for part in node:
                state_ref[start : start + SUBLANES, :] = part
                start += SUBLANES
        for number, value in enumerate(piece):
            row = number * halves + half
            rows_ref[row : row + 1, :] = value[0:1, :]


def state_parts(ref, first, total, parts, pitch=3):
    return [
        tuple(
            ref[(pitch * place + part) * SUBLANES : (pitch * place + part + 1) * SUBLANES, :]
            for part in range(parts)
        )
        for place in range(first, first + total)
    ]


def message_slots(refs, height, pitch, quantity_rows, skips):
    blocks = [(ref, start) for ref in refs for start in range(0, ref.shape[0], height)]
    slots = []
    for (ref, start), skip in zip(blocks, skips):
        rows = [start + quantity * pitch + skip for quantity in range(QUANTITIES)]
        slots.append(tuple(ref[row : row + quantity_rows, :] for row in rows))
    return slots


def x_back(halves, bounds, block_ref, values_t, sides_ref):
    rows = values_t.shape[1]
    before, after = (jnp.broadcast_to(bound, (SUBLANES, rows)) for bound in bounds)
    rolls = x_rolls(halves)
    stride = LANES // SUBLANES
    total = stride - 1 + len(rolls)
    parts = state_parts(block_ref.at[2 * rows :, :], 0, total, 3)
    values = tree_values(before, after, rolls, stride, parts, [part[2] for part in parts])
    for index, value in enumerate(values):
        values_t[pl.ds(index, SUBLANES, stride=stride), :] = value
    sides_ref[...] = block_ref[0:rows, :] * values_t[...].T


def x_back_kernel(halves, axis, order, pieces, *refs):
    slots = message_slots(refs[:pieces], SUBLANES, 1, 1, [0] * len(order))
    slots = [slots[order.index(place)] for place in range(len(order))]
    block_refs, rows_refs, state_refs = (refs[pieces + 2 * pair : pieces + 2 * pair + 2] for pair in range(3))
    message_ref, given_ref = refs[pieces + 6 : pieces + 8]
    scratch = refs[pieces + 8 :]
    bounds = ring_bounds(slots, lax.axis_index(axis))
    rows = scratch[0].shape[1]
    stride = rows // SUBLANES
    total = stride // halves - 1 + len(y_rolls())
    both = 2 * halves
    for block in range(2):
        values_t, sides_ref = scratch[2 * block : 2 * block + 2]
        x_back(halves, bounds[block], block_refs[block], values_t, sides_ref)
        start = 0
        for half in range(halves):
            place = block * halves + half
            sides = [(None, strided(sides_ref, index, SUBLANES, stride)) for index in range(half, stride, halves)]
            nodes = state_parts(state_refs[block], half * total, total, 3)
            piece, givens = tree_sides(sides, y_rolls(), nodes)
            if block == 0:
                for given in givens:
                    given_ref[start : start + SUBLANES, :] = given
                    start += SUBLANES
            for number in range(3):
                row = number * halves + half
                message_ref[number * both + place : number * both + place + 1, :] = rows_refs[block][row : row + 1, :]
            for number, value in enumerate(piece):
                row = (3 + number) * both + place
                message_ref[row : row + 1, :] = value[0:1, :]


def y_back_kernel(halves, axis, height, traded, pieces, *refs):
    state_ref, given_ref, out_ref = refs[pieces:]
    rows = out_ref.shape[0]
    stride = rows // SUBLANES
    slots = message_slots(refs[:pieces], height, 2 * halves, halves, [halves if odd else 0 for odd in traded])
    ends = ring_bounds(slots, lax.axis_index(axis))[0]
    total = stride // halves - 1 + len(y_rolls())
    for half in range(halves):
        bounds = [jnp.broadcast_to(end[half : half + 1, :], (SUBLANES, LANES)) for end in ends]
        nodes = state_parts(state_ref, half * total, total, 2)
        givens = [part[0] for part in state_parts(given_ref, half * total, total, 1, 1)]
        values = tree_values(*bounds, y_rolls(), stride // halves, nodes, givens)
        for index, value in enumerate(values):
            out_ref[pl.ds(index * halves + half, SUBLANES, stride=stride), :] = value


def trade(value, x_step, y_step):
    width = lax.axis_size("yd")
    pairs = []
    for index in range(lax.axis_size("xg")):
        for line in range(width):
            pairs.append((index * width + line, (index ^ x_step) * width + (line ^ y_step)))
    return lax.ppermute(value, ("xg", "yd"), pairs)


def x_exchange(message, block):
    other = trade(message, 1, 0)
    block, other = lax.optimization_barrier((block, other))
    other_block = trade(block, 1, 0)
    pieces = [message, other]
    order = [0, 1]
    held = jnp.concatenate(pieces, axis=0)
    for step in doubling(lax.axis_size("xg") // 2):
        received = trade(held, 2 * step + 1, 0)
        pieces.append(received)
        order += [place ^ (2 * step + 1) for place in order]
        if 4 * step < lax.axis_size("xg"):
            held = jnp.concatenate([held, received], axis=0)
    return pieces, order, other_block


def y_exchange(message):
    count = lax.axis_size("yd")
    stages = [[1], [2, 4, 6]] if count == 8 else [[step] for step in doubling(count)]
    pieces = [message]
    traded = [False]
    held = message
    for stage in stages:
        received = [trade(held, 1, step) for step in stage]
        pieces += received
        traded += [not odd for odd in traded] * len(stage)
        if len(traded) < count:
            held = jnp.concatenate([held] + received, axis=0)
    return pieces, traded


def f32(*shape):
    return jax.ShapeDtypeStruct(shape, jnp.float32)


def held_f32(*shape):
    return VMEM(shape, jnp.float32)


def kernel_call(body, operands, outputs, scratch, space=VMEM):
    return pl.pallas_call(
        body,
        out_shape=outputs,
        in_specs=[pl.BlockSpec(memory_space=space)] * len(operands),
        out_specs=[pl.BlockSpec(memory_space=VMEM)] * len(outputs),
        scratch_shapes=scratch,
        compiler_params=pltpu.CompilerParams(vmem_limit_bytes=16 * 1024 * 1024),
    )(*operands)


def local(mobile, dispersion_x, dispersion_y, capacity, immobile, exchange_rates, rate_shares):
    shape = mobile.shape
    lines, width = shape[0] * shape[1], shape[2]
    zones = immobile.shape[0]
    halves = width // LANES
    rows = lines * halves
    assert rows == LANES

    def flat(values):
        return values.reshape(-1, LANES)

    mobile, dispersion_x, dispersion_y = flat(mobile), flat(dispersion_x), flat(dispersion_y)
    capacity, immobile = flat(capacity), flat(immobile)
    square = VMEM((rows, LANES), jnp.float32)
    x_nodes = LANES // SUBLANES - 1 + len(x_rolls(halves))
    y_nodes = halves * (rows // SUBLANES // halves - 1 + len(y_rolls()))
    message, block = kernel_call(
        functools.partial(x_forward_kernel, halves),
        tuple(
            pltpu.with_memory_space_constraint(value, pltpu.HBM)
            for value in (
                mobile, dispersion_x, dispersion_y, capacity, immobile, exchange_rates[None], rate_shares[None],
            )
        ),
        [f32(SUBLANES, rows), held_f32(2 * rows + 3 * x_nodes * SUBLANES, LANES)],
        [square] * 3
        + [VMEM((zones * rows, LANES), jnp.float32)]
        + [VMEM((1, zones), jnp.float32)] * 2
        + [pltpu.SemaphoreType.DMA((7,))]
        + [square] * 3,
        pltpu.HBM,
    )
    pieces, order, other_block = x_exchange(message, block)
    y_rows, y_state = zip(
        *(
            kernel_call(
                functools.partial(y_coefs_kernel, halves),
                (part,),
                [held_f32(SUBLANES, LANES), held_f32(3 * y_nodes * SUBLANES, LANES)],
                [],
            )
            for part in (block, other_block)
        )
    )
    height = -(-QUANTITIES * 2 * halves // SUBLANES) * SUBLANES
    message, givens = kernel_call(
        functools.partial(x_back_kernel, halves, "xg", order, len(pieces)),
        (*pieces, block, other_block, *y_rows, *y_state),
        [f32(height, LANES), held_f32(y_nodes * SUBLANES, LANES)],
        [square] * 4,
    )
    pieces, traded = y_exchange(message)
    (updated,) = kernel_call(
        functools.partial(y_back_kernel, halves, "yd", height, traded, len(pieces)),
        (*pieces, y_state[0], givens),
        [f32(rows, LANES)],
        [],
    )
    return updated.reshape(shape)


def solution(mesh):
    field = P("yd", None, "xg")
    return jax.shard_map(
        local,
        mesh=mesh,
        in_specs=(field, field, field, field, P(None, "yd", None, "xg"), P(), P()),
        out_specs=field,
        check_vma=False,
    )
```

```python
import functools

import jax
import jax.numpy as jnp
from jax import lax
from jax.experimental import pallas as pl
from jax.experimental.pallas import tpu as pltpu
from jax.sharding import PartitionSpec as P

LANES = 128
SUBLANES = 8
QUANTITIES = 5
VMEM = pltpu.VMEM


def inverse(value):
    return 1.0 / value


def plus(first, second):
    if first is None:
        return second
    return first + second


def join_coefs(left, right):
    coupling_1, head_1, tail_1 = left
    coupling_2, head_2, tail_2 = right
    middle = plus(head_2, tail_1)
    inv = inverse(coupling_1 + coupling_2 + middle)
    weight_1 = coupling_1 * inv
    weight_2 = coupling_2 * inv
    joined = (coupling_1 * weight_2, plus(head_1, weight_1 * middle), tail_2 + weight_2 * middle)
    return joined, (weight_1, weight_2, inv)


def join_sides(left, right, node):
    head_1, tail_1 = left
    head_2, tail_2 = right
    weight_1, weight_2, inv = node
    side = plus(head_2, tail_1)
    joined = (plus(head_1, weight_1 * side), tail_2 + weight_2 * side)
    return joined, side * inv


def middle_value(node, given, before, after):
    return given + node[0] * before + node[1] * after


def ahead(value, step, axis):
    return pltpu.roll(value, value.shape[axis] - step, axis)


def behind(value, step, axis):
    return pltpu.roll(value, step, axis)


def doubling(count):
    steps = []
    step = 1
    while step < count:
        steps.append(step)
        step *= 2
    return steps


def tree_coefs(leaves, rolls):
    nodes = []
    level = leaves
    while len(level) > 1:
        following = []
        for index in range(0, len(level), 2):
            joined, node = join_coefs(level[index], level[index + 1])
            following.append(joined)
            nodes.append(node)
        level = following
    piece = level[0]
    for step, axis in rolls:
        piece, node = join_coefs(piece, tuple(ahead(part, step, axis) for part in piece))
        nodes.append(node)
    return piece, nodes


def tree_sides(leaves, rolls, nodes):
    givens = []
    level = leaves
    while len(level) > 1:
        following = []
        for index in range(0, len(level), 2):
            joined, given = join_sides(level[index], level[index + 1], nodes[len(givens)])
            following.append(joined)
            givens.append(given)
        level = following
    piece = level[0]
    for step, axis in rolls:
        other = tuple(ahead(part, step, axis) for part in piece)
        piece, given = join_sides(piece, other, nodes[len(givens)])
        givens.append(given)
    return piece, givens


def tree_values(before, after, rolls, count, nodes, givens):
    place = len(nodes)
    for step, axis in reversed(rolls):
        place -= 1
        middle = middle_value(nodes[place], givens[place], before, after)
        upper = (lax.broadcasted_iota(jnp.int32, middle.shape, axis) & step) != 0
        before = jnp.where(upper, behind(middle, step, axis), before)
        after = jnp.where(upper, behind(after, step, axis), middle)
    bounds = [before, after]
    while len(bounds) - 1 < count:
        width = len(bounds) - 1
        place -= width
        following = [bounds[0]]
        for index in range(width):
            following.append(
                middle_value(
                    nodes[place + index], givens[place + index], bounds[index], bounds[index + 1]
                )
            )
            following.append(bounds[index + 1])
        bounds = following
    return bounds[1:]


def choose(condition, first, second):
    if isinstance(condition, bool):
        return first if condition else second
    return jnp.where(condition, first, second)


def ring_bounds(slots, index):
    level = slots
    rounds = []
    bit = 0
    while len(level) > 1:
        upper = ((index >> bit) & 1) == 1
        following, nodes = [], []
        for place in range(0, len(level), 2):
            own, other = level[place], level[place + 1]
            left = [choose(upper, b, a) for a, b in zip(own, other)]
            right = [choose(upper, a, b) for a, b in zip(own, other)]
            coefs, node = join_coefs(left[:3], right[:3])
            sides, given = join_sides(left[3:], right[3:], node)
            nodes.append((node, given))
            following.append(coefs + sides)
        rounds.append((nodes, upper))
        level = following
        bit += 1
    _, head, tail, side_head, side_tail = level[0]
    last = (side_head + side_tail) * inverse(head + tail)
    bounds = [(last, last)]
    for nodes, upper in reversed(rounds):
        following = []
        for (node, given), (before, after) in zip(nodes, bounds):
            middle = middle_value(node, given, before, after)
            following.append((choose(upper, middle, before), choose(upper, after, middle)))
            following.append((choose(upper, before, middle), choose(upper, middle, after)))
        bounds = following
    return bounds


def capacity_weights(rates, shares):
    weights = shares * rates / (1.0 + rates)
    return [weights[:, zone : zone + 1] for zone in range(weights.shape[1])]


def strided(ref, start, size, stride):
    return ref[pl.ds(start, size, stride=stride), :]


def x_rolls(halves):
    return [(step, 0) for step in doubling(SUBLANES)] + [(step, 1) for step in doubling(halves)]


def y_rolls():
    return [(step, 0) for step in doubling(SUBLANES)]


def x_forward_kernel(
    halves, mobile_hbm, faces_hbm, across_hbm, capacity_hbm, immobile_hbm, rates_hbm, shares_hbm,
    message_ref, block_ref,
    mobile_ref, faces_ref, capacity_ref, immobile_ref, rates_ref, shares_ref, arrived,
    faces_t, storage_t, source_t,
):
    pairs = (
        (rates_hbm, rates_ref), (shares_hbm, shares_ref), (capacity_hbm, capacity_ref),
        (faces_hbm, faces_ref), (immobile_hbm, immobile_ref), (mobile_hbm, mobile_ref),
        (across_hbm, block_ref.at[mobile_ref.shape[0] : 2 * mobile_ref.shape[0], :]),
    )
    copies = [pltpu.make_async_copy(pair[0], pair[1], arrived.at[place]) for place, pair in enumerate(pairs)]
    for copy in copies:
        copy.start()
    rows = mobile_ref.shape[0]
    stride = LANES // SUBLANES
    for copy in copies[:3]:
        copy.wait()
    weights = capacity_weights(rates_ref[...], shares_ref[...])
    capacity = capacity_ref[...]
    storage = 1.0 + capacity * sum(weights[1:], weights[0])
    block_ref[0:rows, :] = storage
    storage_t[...] = storage.T
    copies[3].wait()
    faces_t[...] = faces_ref[...].T
    copies[4].wait()
    total = weights[0] * immobile_ref[0:rows, :]
    for zone in range(1, len(weights)):
        total = total + weights[zone] * immobile_ref[zone * rows : (zone + 1) * rows, :]
    copies[5].wait()
    source_t[...] = (mobile_ref[...] + capacity * total).T
    coefs, sides = [], []
    for index in range(stride):
        coefs.append((strided(faces_t, index, SUBLANES, stride), None, strided(storage_t, index, SUBLANES, stride)))
        sides.append((None, strided(source_t, index, SUBLANES, stride)))
    rolls = x_rolls(halves)
    piece, nodes = tree_coefs(coefs, rolls)
    side, givens = tree_sides(sides, rolls, nodes)
    start = 2 * rows
    for node, given in zip(nodes, givens):
        for part in (node[0], node[1], given):
            block_ref[start : start + SUBLANES, :] = part
            start += SUBLANES
    for row, value in enumerate(piece + side):
        message_ref[row : row + 1, :] = value[0:1, :]
    copies[6].wait()


def y_coefs_kernel(halves, block_ref, rows_ref, state_ref):
    rows = rows_ref.shape[1]
    stride = rows // SUBLANES
    start = 0
    for half in range(halves):
        coefs = []
        for index in range(half, stride, halves):
            storage = strided(block_ref, index, SUBLANES, stride)
            coefs.append((strided(block_ref, rows + index, SUBLANES, stride), None, storage))
        piece, nodes = tree_coefs(coefs, y_rolls())
        for node in nodes:
            for part in node:
                state_ref[start : start + SUBLANES, :] = part
                start += SUBLANES
        for number, value in enumerate(piece):
            row = number * halves + half
            rows_ref[row : row + 1, :] = value[0:1, :]


def state_parts(ref, first, total, parts, pitch=3):
    return [
        tuple(
            ref[(pitch * place + part) * SUBLANES : (pitch * place + part + 1) * SUBLANES, :]
            for part in range(parts)
        )
        for place in range(first, first + total)
    ]


def message_slots(refs, height, pitch, quantity_rows, skips):
    blocks = [(ref, start) for ref in refs for start in range(0, ref.shape[0], height)]
    slots = []
    for (ref, start), skip in zip(blocks, skips):
        rows = [start + quantity * pitch + skip for quantity in range(QUANTITIES)]
        slots.append(tuple(ref[row : row + quantity_rows, :] for row in rows))
    return slots


def x_back(halves, bounds, block_ref, values_t, sides_ref):
    rows = values_t.shape[1]
    before, after = (jnp.broadcast_to(bound, (SUBLANES, rows)) for bound in bounds)
    rolls = x_rolls(halves)
    stride = LANES // SUBLANES
    total = stride - 1 + len(rolls)
    parts = state_parts(block_ref.at[2 * rows :, :], 0, total, 3)
    values = tree_values(before, after, rolls, stride, parts, [part[2] for part in parts])
    for index, value in enumerate(values):
        values_t[pl.ds(index, SUBLANES, stride=stride), :] = value
    sides_ref[...] = block_ref[0:rows, :] * values_t[...].T


def x_back_kernel(halves, axis, copies, order, pieces, *refs):
    slots = message_slots(refs[:pieces], SUBLANES, 1, 1, [0] * len(order))
    slots = [slots[order.index(place)] for place in range(len(order))]
    block_ref, rows_ref, state_ref, message_ref, given_ref, values_t, sides_ref = refs[pieces:]
    rows = values_t.shape[1]
    stride = rows // SUBLANES
    total = stride // halves - 1 + len(y_rolls())
    height = QUANTITIES * halves

    def put(row, value):
        for copy in range(copies):
            message_ref[copy * height + row : copy * height + row + 1, :] = value

    for row in range(3 * halves):
        put(row, rows_ref[row : row + 1, :])
    x_back(halves, ring_bounds(slots, lax.axis_index(axis))[0], block_ref, values_t, sides_ref)
    start = 0
    for half in range(halves):
        sides = [(None, strided(sides_ref, index, SUBLANES, stride)) for index in range(half, stride, halves)]
        nodes = state_parts(state_ref, half * total, total, 3)
        piece, givens = tree_sides(sides, y_rolls(), nodes)
        for given in givens:
            given_ref[start : start + SUBLANES, :] = given
            start += SUBLANES
        for number, value in enumerate(piece):
            put((3 + number) * halves + half, value[0:1, :])


def y_back_kernel(halves, axis, gathered_ref, state_ref, given_ref, out_ref):
    rows = out_ref.shape[0]
    stride = rows // SUBLANES
    height = QUANTITIES * halves
    count = gathered_ref.shape[0] // height
    slots = message_slots([gathered_ref], height, halves, halves, [0] * count)
    own = lax.axis_index(axis)
    ends = [jnp.zeros((halves, LANES), jnp.float32)] * 2
    for place, bounds in enumerate(ring_bounds(slots, 0)):
        ends = [jnp.where(own == place, bound, end) for bound, end in zip(bounds, ends)]
    total = stride // halves - 1 + len(y_rolls())
    for half in range(halves):
        bounds = [jnp.broadcast_to(end[half : half + 1, :], (SUBLANES, LANES)) for end in ends]
        nodes = state_parts(state_ref, half * total, total, 2)
        givens = [part[0] for part in state_parts(given_ref, half * total, total, 1, 1)]
        values = tree_values(*bounds, y_rolls(), stride // halves, nodes, givens)
        for index, value in enumerate(values):
            out_ref[pl.ds(index * halves + half, SUBLANES, stride=stride), :] = value


def trade(value, x_step, y_step):
    width = lax.axis_size("yd")
    pairs = []
    for index in range(lax.axis_size("xg")):
        for line in range(width):
            pairs.append((index * width + line, (index ^ x_step) * width + (line ^ y_step)))
    return lax.ppermute(value, ("xg", "yd"), pairs)


def x_exchange(message):
    pieces = [message, trade(message, 1, 0)]
    order = [0, 1]
    held = jnp.concatenate(pieces, axis=0)
    for step in doubling(lax.axis_size("xg") // 2):
        received = trade(held, 2 * step + 1, 0)
        pieces.append(received)
        order += [place ^ (2 * step + 1) for place in order]
        if 4 * step < lax.axis_size("xg"):
            held = jnp.concatenate([held, received], axis=0)
    return pieces, order


def y_exchange(copies):
    count = lax.axis_size("yd")
    flat = copies.reshape(count, 1, -1)
    return lax.all_to_all(flat, "yd", split_axis=0, concat_axis=0, tiled=True).reshape(copies.shape)


def f32(*shape):
    return jax.ShapeDtypeStruct(shape, jnp.float32)


def held_f32(*shape):
    return VMEM(shape, jnp.float32)


def kernel_call(body, operands, outputs, scratch, space=VMEM):
    return pl.pallas_call(
        body,
        out_shape=outputs,
        in_specs=[pl.BlockSpec(memory_space=space)] * len(operands),
        out_specs=[pl.BlockSpec(memory_space=VMEM)] * len(outputs),
        scratch_shapes=scratch,
        compiler_params=pltpu.CompilerParams(vmem_limit_bytes=16 * 1024 * 1024),
    )(*operands)


def local(mobile, dispersion_x, dispersion_y, capacity, immobile, exchange_rates, rate_shares):
    shape = mobile.shape
    lines, width = shape[0] * shape[1], shape[2]
    zones = immobile.shape[0]
    halves = width // LANES
    rows = lines * halves
    assert rows == LANES

    def flat(values):
        return values.reshape(-1, LANES)

    mobile, dispersion_x, dispersion_y = flat(mobile), flat(dispersion_x), flat(dispersion_y)
    capacity, immobile = flat(capacity), flat(immobile)
    square = VMEM((rows, LANES), jnp.float32)
    x_nodes = LANES // SUBLANES - 1 + len(x_rolls(halves))
    y_nodes = halves * (rows // SUBLANES // halves - 1 + len(y_rolls()))
    message, block = kernel_call(
        functools.partial(x_forward_kernel, halves),
        tuple(
            pltpu.with_memory_space_constraint(value, pltpu.HBM)
            for value in (
                mobile, dispersion_x, dispersion_y, capacity, immobile, exchange_rates[None], rate_shares[None],
            )
        ),
        [f32(SUBLANES, rows), held_f32(2 * rows + 3 * x_nodes * SUBLANES, LANES)],
        [square] * 3
        + [VMEM((zones * rows, LANES), jnp.float32)]
        + [VMEM((1, zones), jnp.float32)] * 2
        + [pltpu.SemaphoreType.DMA((7,))]
        + [square] * 3,
        pltpu.HBM,
    )
    pieces, order = x_exchange(message)
    y_rows, y_state = kernel_call(
        functools.partial(y_coefs_kernel, halves),
        (block,),
        [held_f32(SUBLANES, LANES), held_f32(3 * y_nodes * SUBLANES, LANES)],
        [],
    )
    count = lax.axis_size("yd")
    copies, givens = kernel_call(
        functools.partial(x_back_kernel, halves, "xg", count, order, len(pieces)),
        (*pieces, block, y_rows, y_state),
        [f32(count * QUANTITIES * halves, LANES), held_f32(y_nodes * SUBLANES, LANES)],
        [square] * 2,
    )
    (updated,) = kernel_call(
        functools.partial(y_back_kernel, halves, "yd"),
        (y_exchange(copies), y_state, givens),
        [f32(rows, LANES)],
        [],
    )
    return updated.reshape(shape)


def solution(mesh):
    field = P("yd", None, "xg")
    return jax.shard_map(
        local,
        mesh=mesh,
        in_specs=(field, field, field, field, P(None, "yd", None, "xg"), P(), P()),
        out_specs=field,
        check_vma=False,
    )
```

```python
import functools

import jax
import jax.numpy as jnp
from jax import lax
from jax.experimental import pallas as pl
from jax.experimental.pallas import tpu as pltpu
from jax.sharding import PartitionSpec as P

LANES = 128
SUBLANES = 8
QUANTITIES = 5
VMEM = pltpu.VMEM


def inverse(value):
    return 1.0 / value


def plus(first, second):
    if first is None:
        return second
    return first + second


def join_coefs(left, right):
    coupling_1, head_1, tail_1 = left
    coupling_2, head_2, tail_2 = right
    middle = plus(head_2, tail_1)
    inv = inverse(coupling_1 + coupling_2 + middle)
    weight_1 = coupling_1 * inv
    weight_2 = coupling_2 * inv
    joined = (coupling_1 * weight_2, plus(head_1, weight_1 * middle), tail_2 + weight_2 * middle)
    return joined, (weight_1, weight_2, inv)


def join_sides(left, right, node):
    head_1, tail_1 = left
    head_2, tail_2 = right
    weight_1, weight_2, inv = node
    side = plus(head_2, tail_1)
    joined = (plus(head_1, weight_1 * side), tail_2 + weight_2 * side)
    return joined, side * inv


def middle_value(node, given, before, after):
    return given + node[0] * before + node[1] * after


def ahead(value, step, axis):
    return pltpu.roll(value, value.shape[axis] - step, axis)


def behind(value, step, axis):
    return pltpu.roll(value, step, axis)


def doubling(count):
    steps = []
    step = 1
    while step < count:
        steps.append(step)
        step *= 2
    return steps


def tree_coefs(leaves, rolls):
    nodes = []
    level = leaves
    while len(level) > 1:
        following = []
        for index in range(0, len(level), 2):
            joined, node = join_coefs(level[index], level[index + 1])
            following.append(joined)
            nodes.append(node)
        level = following
    piece = level[0]
    for step, axis in rolls:
        piece, node = join_coefs(piece, tuple(ahead(part, step, axis) for part in piece))
        nodes.append(node)
    return piece, nodes


def tree_sides(leaves, rolls, nodes):
    givens = []
    level = leaves
    while len(level) > 1:
        following = []
        for index in range(0, len(level), 2):
            joined, given = join_sides(level[index], level[index + 1], nodes[len(givens)])
            following.append(joined)
            givens.append(given)
        level = following
    piece = level[0]
    for step, axis in rolls:
        other = tuple(ahead(part, step, axis) for part in piece)
        piece, given = join_sides(piece, other, nodes[len(givens)])
        givens.append(given)
    return piece, givens


def tree_values(before, after, rolls, count, nodes, givens):
    place = len(nodes)
    for step, axis in reversed(rolls):
        place -= 1
        middle = middle_value(nodes[place], givens[place], before, after)
        upper = (lax.broadcasted_iota(jnp.int32, middle.shape, axis) & step) != 0
        before = jnp.where(upper, behind(middle, step, axis), before)
        after = jnp.where(upper, behind(after, step, axis), middle)
    bounds = [before, after]
    while len(bounds) - 1 < count:
        width = len(bounds) - 1
        place -= width
        following = [bounds[0]]
        for index in range(width):
            following.append(
                middle_value(
                    nodes[place + index], givens[place + index], bounds[index], bounds[index + 1]
                )
            )
            following.append(bounds[index + 1])
        bounds = following
    return bounds[1:]


def choose(condition, first, second):
    if isinstance(condition, bool):
        return first if condition else second
    return jnp.where(condition, first, second)


def ring_bounds(slots, index):
    level = slots
    rounds = []
    bit = 0
    while len(level) > 1:
        upper = ((index >> bit) & 1) == 1
        following, nodes = [], []
        for place in range(0, len(level), 2):
            own, other = level[place], level[place + 1]
            left = [jnp.where(upper, b, a) for a, b in zip(own, other)]
            right = [jnp.where(upper, a, b) for a, b in zip(own, other)]
            coefs, node = join_coefs(left[:3], right[:3])
            sides, given = join_sides(left[3:], right[3:], node)
            nodes.append((node, given))
            following.append(coefs + sides)
        rounds.append((nodes, upper))
        level = following
        bit += 1
    _, head, tail, side_head, side_tail = level[0]
    last = (side_head + side_tail) * inverse(head + tail)
    bounds = [(last, last)]
    for nodes, upper in reversed(rounds):
        following = []
        for (node, given), (before, after) in zip(nodes, bounds):
            middle = middle_value(node, given, before, after)
            following.append((jnp.where(upper, middle, before), jnp.where(upper, after, middle)))
            following.append((jnp.where(upper, before, middle), jnp.where(upper, middle, after)))
        bounds = following
    return bounds


def capacity_weights(rates, shares):
    weights = shares * rates / (1.0 + rates)
    return [weights[:, zone : zone + 1] for zone in range(weights.shape[1])]


def strided(ref, start, size, stride):
    return ref[pl.ds(start, size, stride=stride), :]


def x_rolls(halves):
    return [(step, 0) for step in doubling(SUBLANES)] + [(step, 1) for step in doubling(halves)]


def y_rolls():
    return [(step, 0) for step in doubling(SUBLANES)]


def x_forward_kernel(
    halves, mobile_hbm, faces_hbm, across_hbm, capacity_hbm, immobile_hbm, rates_hbm, shares_hbm,
    message_ref, block_ref,
    mobile_ref, faces_ref, capacity_ref, immobile_ref, rates_ref, shares_ref, arrived,
    faces_t, storage_t, source_t,
):
    pairs = (
        (rates_hbm, rates_ref), (shares_hbm, shares_ref), (capacity_hbm, capacity_ref),
        (faces_hbm, faces_ref), (immobile_hbm, immobile_ref), (mobile_hbm, mobile_ref),
        (across_hbm, block_ref.at[mobile_ref.shape[0] : 2 * mobile_ref.shape[0], :]),
    )
    copies = [pltpu.make_async_copy(pair[0], pair[1], arrived.at[place]) for place, pair in enumerate(pairs)]
    for copy in copies:
        copy.start()
    rows = mobile_ref.shape[0]
    stride = LANES // SUBLANES
    for copy in copies[:3]:
        copy.wait()
    weights = capacity_weights(rates_ref[...], shares_ref[...])
    capacity = capacity_ref[...]
    storage = 1.0 + capacity * sum(weights[1:], weights[0])
    block_ref[0:rows, :] = storage
    storage_t[...] = storage.T
    copies[3].wait()
    faces_t[...] = faces_ref[...].T
    copies[4].wait()
    total = weights[0] * immobile_ref[0:rows, :]
    for zone in range(1, len(weights)):
        total = total + weights[zone] * immobile_ref[zone * rows : (zone + 1) * rows, :]
    copies[5].wait()
    source_t[...] = (mobile_ref[...] + capacity * total).T
    coefs, sides = [], []
    for index in range(stride):
        coefs.append((strided(faces_t, index, SUBLANES, stride), None, strided(storage_t, index, SUBLANES, stride)))
        sides.append((None, strided(source_t, index, SUBLANES, stride)))
    rolls = x_rolls(halves)
    piece, nodes = tree_coefs(coefs, rolls)
    side, givens = tree_sides(sides, rolls, nodes)
    start = 2 * rows
    for node, given in zip(nodes, givens):
        for part in (node[0], node[1], given):
            block_ref[start : start + SUBLANES, :] = part
            start += SUBLANES
    for row, value in enumerate(piece + side):
        message_ref[row : row + 1, :] = value[0:1, :]
    copies[6].wait()


def y_coefs_kernel(halves, block_ref, rows_ref, state_ref):
    rows = rows_ref.shape[1]
    stride = rows // SUBLANES
    start = 0
    for half in range(halves):
        coefs = []
        for index in range(half, stride, halves):
            storage = strided(block_ref, index, SUBLANES, stride)
            coefs.append((strided(block_ref, rows + index, SUBLANES, stride), None, storage))
        piece, nodes = tree_coefs(coefs, y_rolls())
        for node in nodes:
            for part in node:
                state_ref[start : start + SUBLANES, :] = part
                start += SUBLANES
        for number, value in enumerate(piece):
            row = number * halves + half
            rows_ref[row : row + 1, :] = value[0:1, :]


def state_parts(ref, first, total, parts, pitch=3):
    return [
        tuple(
            ref[(pitch * place + part) * SUBLANES : (pitch * place + part + 1) * SUBLANES, :]
            for part in range(parts)
        )
        for place in range(first, first + total)
    ]


def message_slots(refs, height, pitch, quantity_rows, skips):
    blocks = [(ref, start) for ref in refs for start in range(0, ref.shape[0], height)]
    slots = []
    for (ref, start), skip in zip(blocks, skips):
        rows = [start + quantity * pitch + skip for quantity in range(QUANTITIES)]
        slots.append(tuple(ref[row : row + quantity_rows, :] for row in rows))
    return slots


def x_back(halves, bounds, block_ref, values_t, sides_ref):
    rows = values_t.shape[1]
    before, after = (jnp.broadcast_to(bound, (SUBLANES, rows)) for bound in bounds)
    rolls = x_rolls(halves)
    stride = LANES // SUBLANES
    total = stride - 1 + len(rolls)
    parts = state_parts(block_ref.at[2 * rows :, :], 0, total, 3)
    values = tree_values(before, after, rolls, stride, parts, [part[2] for part in parts])
    for index, value in enumerate(values):
        values_t[pl.ds(index, SUBLANES, stride=stride), :] = value
    sides_ref[...] = block_ref[0:rows, :] * values_t[...].T


def quantity(number):
    return slice(number * LANES, (number + 1) * LANES)


def put_traded(ref, row, rows, number, value):
    ref[(row + rows // 2) % rows : (row + rows // 2) % rows + value.shape[0], quantity(number)] = value


def x_back_kernel(halves, axis, order, pieces, *refs):
    slots = message_slots(refs[:pieces], SUBLANES, 1, 1, [0] * len(order))
    slots = [slots[order.index(place)] for place in range(len(order))]
    block_refs, rows_refs, state_refs = (refs[pieces + 2 * pair : pieces + 2 * pair + 2] for pair in range(3))
    kept_ref, sent_ref, given_ref = refs[pieces + 6 : pieces + 9]
    scratch = refs[pieces + 9 :]
    bounds = ring_bounds(slots, lax.axis_index(axis))
    rows = scratch[0].shape[1]
    stride = rows // SUBLANES
    total = stride // halves - 1 + len(y_rolls())

    def put(row, number, value):
        kept_ref[row : row + 1, quantity(number)] = value
        put_traded(sent_ref, row, 2 * halves, number, value)

    for block in range(2):
        values_t, sides_ref = scratch[2 * block : 2 * block + 2]
        x_back(halves, bounds[block], block_refs[block], values_t, sides_ref)
        start = 0
        for half in range(halves):
            place = block * halves + half
            sides = [(None, strided(sides_ref, index, SUBLANES, stride)) for index in range(half, stride, halves)]
            nodes = state_parts(state_refs[block], half * total, total, 3)
            piece, givens = tree_sides(sides, y_rolls(), nodes)
            if block == 0:
                for given in givens:
                    given_ref[start : start + SUBLANES, :] = given
                    start += SUBLANES
            for number in range(3):
                row = number * halves + half
                put(place, number, rows_refs[block][row : row + 1, :])
            for number, value in enumerate(piece):
                put(place, 3 + number, value[0:1, :])


def read_message(ref):
    return [ref[:, quantity(number)] for number in range(QUANTITIES)]


def join_by_bit(own, other, upper):
    left = [choose(upper, b, a) for a, b in zip(own, other)]
    right = [choose(upper, a, b) for a, b in zip(own, other)]
    coefs, node = join_coefs(left[:3], right[:3])
    sides, given = join_sides(left[3:], right[3:], node)
    return coefs + sides, (node[0], node[1], given)


def own_bit(axis, bit):
    return ((lax.axis_index(axis) >> bit) & 1) == 1


def y_join_kernel(axis, bit, own_ref, other_ref, kept_ref, sent_ref, path_ref):
    joined, path = join_by_bit(read_message(own_ref), read_message(other_ref), own_bit(axis, bit))
    rows = own_ref.shape[0]
    for number, value in enumerate(joined):
        kept_ref[:, quantity(number)] = value
        for row in (0, rows // 2):
            put_traded(sent_ref, row, rows, number, value[row : row + rows // 2, :])
    for number, value in enumerate(path):
        path_ref[:, quantity(number)] = value


def y_back_kernel(halves, axis, rounds, own_ref, other_ref, *refs):
    path_refs = refs[: rounds - 1]
    state_ref, given_ref, out_ref = refs[rounds - 1 :]
    rows = out_ref.shape[0]
    stride = rows // SUBLANES
    joined, path = join_by_bit(read_message(own_ref), read_message(other_ref), own_bit(axis, rounds - 1))
    _, head, tail, side_head, side_tail = joined
    before = after = (side_head + side_tail) * inverse(head + tail)
    paths = [[ref[:, quantity(number)] for number in range(3)] for ref in path_refs] + [path]
    for bit in reversed(range(rounds)):
        node = paths[bit]
        middle = middle_value(node, node[2], before, after)
        upper = own_bit(axis, bit)
        before = jnp.where(upper, middle, before)
        after = jnp.where(upper, after, middle)
    total = stride // halves - 1 + len(y_rolls())
    for half in range(halves):
        bounds = [jnp.broadcast_to(end[half : half + 1, :], (SUBLANES, LANES)) for end in (before, after)]
        nodes = state_parts(state_ref, half * total, total, 2)
        givens = [part[0] for part in state_parts(given_ref, half * total, total, 1, 1)]
        values = tree_values(*bounds, y_rolls(), stride // halves, nodes, givens)
        for index, value in enumerate(values):
            out_ref[pl.ds(index * halves + half, SUBLANES, stride=stride), :] = value


def trade(value, x_step, y_step):
    width = lax.axis_size("yd")
    pairs = []
    for index in range(lax.axis_size("xg")):
        for line in range(width):
            pairs.append((index * width + line, (index ^ x_step) * width + (line ^ y_step)))
    return lax.ppermute(value, ("xg", "yd"), pairs)


def x_exchange(message, block):
    other = trade(message, 1, 0)
    block, other = lax.optimization_barrier((block, other))
    other_block = trade(block, 1, 0)
    pieces = [message, other]
    order = [0, 1]
    held = jnp.concatenate(pieces, axis=0)
    for step in doubling(lax.axis_size("xg") // 2):
        received = trade(held, 2 * step + 1, 0)
        pieces.append(received)
        order += [place ^ (2 * step + 1) for place in order]
        if 4 * step < lax.axis_size("xg"):
            held = jnp.concatenate([held, received], axis=0)
    return pieces, order, other_block


def y_exchange(kept, sent):
    rows = kept.shape[0]
    paths = []
    steps = doubling(lax.axis_size("yd"))
    for bit, step in enumerate(steps):
        received = trade(sent, 1, step)
        if bit < len(steps) - 1:
            kept, sent, path = kernel_call(
                functools.partial(y_join_kernel, "yd", bit),
                (kept, received),
                [held_f32(*kept.shape), f32(*kept.shape), held_f32(rows, 3 * LANES)],
                [],
            )
            paths.append(path)
    return [kept, received] + paths, len(steps)


def f32(*shape):
    return jax.ShapeDtypeStruct(shape, jnp.float32)


def held_f32(*shape):
    return VMEM(shape, jnp.float32)


def kernel_call(body, operands, outputs, scratch, space=VMEM):
    return pl.pallas_call(
        body,
        out_shape=outputs,
        in_specs=[pl.BlockSpec(memory_space=space)] * len(operands),
        out_specs=[pl.BlockSpec(memory_space=VMEM)] * len(outputs),
        scratch_shapes=scratch,
        compiler_params=pltpu.CompilerParams(vmem_limit_bytes=16 * 1024 * 1024),
    )(*operands)


def local(mobile, dispersion_x, dispersion_y, capacity, immobile, exchange_rates, rate_shares):
    shape = mobile.shape
    lines, width = shape[0] * shape[1], shape[2]
    zones = immobile.shape[0]
    halves = width // LANES
    rows = lines * halves
    assert rows == LANES

    def flat(values):
        return values.reshape(-1, LANES)

    mobile, dispersion_x, dispersion_y = flat(mobile), flat(dispersion_x), flat(dispersion_y)
    capacity, immobile = flat(capacity), flat(immobile)
    square = VMEM((rows, LANES), jnp.float32)
    x_nodes = LANES // SUBLANES - 1 + len(x_rolls(halves))
    y_nodes = halves * (rows // SUBLANES // halves - 1 + len(y_rolls()))
    message, block = kernel_call(
        functools.partial(x_forward_kernel, halves),
        tuple(
            pltpu.with_memory_space_constraint(value, pltpu.HBM)
            for value in (
                mobile, dispersion_x, dispersion_y, capacity, immobile, exchange_rates[None], rate_shares[None],
            )
        ),
        [f32(SUBLANES, rows), held_f32(2 * rows + 3 * x_nodes * SUBLANES, LANES)],
        [square] * 3
        + [VMEM((zones * rows, LANES), jnp.float32)]
        + [VMEM((1, zones), jnp.float32)] * 2
        + [pltpu.SemaphoreType.DMA((7,))]
        + [square] * 3,
        pltpu.HBM,
    )
    pieces, order, other_block = x_exchange(message, block)
    y_rows, y_state = zip(
        *(
            kernel_call(
                functools.partial(y_coefs_kernel, halves),
                (part,),
                [held_f32(SUBLANES, LANES), held_f32(3 * y_nodes * SUBLANES, LANES)],
                [],
            )
            for part in (block, other_block)
        )
    )
    kept, sent, givens = kernel_call(
        functools.partial(x_back_kernel, halves, "xg", order, len(pieces)),
        (*pieces, block, other_block, *y_rows, *y_state),
        [
            held_f32(2 * halves, QUANTITIES * LANES),
            f32(2 * halves, QUANTITIES * LANES),
            held_f32(y_nodes * SUBLANES, LANES),
        ],
        [square] * 4,
    )
    pieces, rounds = y_exchange(kept, sent)
    (updated,) = kernel_call(
        functools.partial(y_back_kernel, halves, "yd", rounds),
        (*pieces, y_state[0], givens),
        [f32(rows, LANES)],
        [],
    )
    return updated.reshape(shape)


def solution(mesh):
    field = P("yd", None, "xg")
    return jax.shard_map(
        local,
        mesh=mesh,
        in_specs=(field, field, field, field, P(None, "yd", None, "xg"), P(), P()),
        out_specs=field,
        check_vma=False,
    )
```

```python
import functools

import jax
import jax.numpy as jnp
from jax import lax
from jax.experimental import pallas as pl
from jax.experimental.pallas import tpu as pltpu
from jax.sharding import PartitionSpec as P

LANES = 128
SUBLANES = 8
QUANTITIES = 5
VMEM = pltpu.VMEM


def inverse(value):
    return 1.0 / value


def plus(first, second):
    if first is None:
        return second
    return first + second


def join_coefs(left, right):
    coupling_1, head_1, tail_1 = left
    coupling_2, head_2, tail_2 = right
    middle = plus(head_2, tail_1)
    inv = inverse(coupling_1 + coupling_2 + middle)
    weight_1 = coupling_1 * inv
    weight_2 = coupling_2 * inv
    joined = (coupling_1 * weight_2, plus(head_1, weight_1 * middle), tail_2 + weight_2 * middle)
    return joined, (weight_1, weight_2, inv)


def join_sides(left, right, node):
    head_1, tail_1 = left
    head_2, tail_2 = right
    weight_1, weight_2, inv = node
    side = plus(head_2, tail_1)
    joined = (plus(head_1, weight_1 * side), tail_2 + weight_2 * side)
    return joined, side * inv


def middle_value(node, given, before, after):
    return given + node[0] * before + node[1] * after


def ahead(value, step, axis):
    return pltpu.roll(value, value.shape[axis] - step, axis)


def behind(value, step, axis):
    return pltpu.roll(value, step, axis)


def doubling(count):
    steps = []
    step = 1
    while step < count:
        steps.append(step)
        step *= 2
    return steps


def tree_coefs(leaves, rolls):
    nodes = []
    level = leaves
    while len(level) > 1:
        following = []
        for index in range(0, len(level), 2):
            joined, node = join_coefs(level[index], level[index + 1])
            following.append(joined)
            nodes.append(node)
        level = following
    piece = level[0]
    for step, axis in rolls:
        piece, node = join_coefs(piece, tuple(ahead(part, step, axis) for part in piece))
        nodes.append(node)
    return piece, nodes


def tree_sides(leaves, rolls, nodes):
    givens = []
    level = leaves
    while len(level) > 1:
        following = []
        for index in range(0, len(level), 2):
            joined, given = join_sides(level[index], level[index + 1], nodes[len(givens)])
            following.append(joined)
            givens.append(given)
        level = following
    piece = level[0]
    for step, axis in rolls:
        other = tuple(ahead(part, step, axis) for part in piece)
        piece, given = join_sides(piece, other, nodes[len(givens)])
        givens.append(given)
    return piece, givens


def tree_values(before, after, rolls, count, nodes, givens):
    place = len(nodes)
    for step, axis in reversed(rolls):
        place -= 1
        middle = middle_value(nodes[place], givens[place], before, after)
        upper = (lax.broadcasted_iota(jnp.int32, middle.shape, axis) & step) != 0
        before = jnp.where(upper, behind(middle, step, axis), before)
        after = jnp.where(upper, behind(after, step, axis), middle)
    bounds = [before, after]
    while len(bounds) - 1 < count:
        width = len(bounds) - 1
        place -= width
        following = [bounds[0]]
        for index in range(width):
            following.append(
                middle_value(
                    nodes[place + index], givens[place + index], bounds[index], bounds[index + 1]
                )
            )
            following.append(bounds[index + 1])
        bounds = following
    return bounds[1:]


def choose(condition, first, second):
    if isinstance(condition, bool):
        return first if condition else second
    return jnp.where(condition, first, second)


def ring_bounds(slots, index):
    level = slots
    rounds = []
    bit = 0
    while len(level) > 1:
        upper = ((index >> bit) & 1) == 1
        following, nodes = [], []
        for place in range(0, len(level), 2):
            own, other = level[place], level[place + 1]
            left = [jnp.where(upper, b, a) for a, b in zip(own, other)]
            right = [jnp.where(upper, a, b) for a, b in zip(own, other)]
            coefs, node = join_coefs(left[:3], right[:3])
            sides, given = join_sides(left[3:], right[3:], node)
            nodes.append((node, given))
            following.append(coefs + sides)
        rounds.append((nodes, upper))
        level = following
        bit += 1
    _, head, tail, side_head, side_tail = level[0]
    last = (side_head + side_tail) * inverse(head + tail)
    bounds = [(last, last)]
    for nodes, upper in reversed(rounds):
        following = []
        for (node, given), (before, after) in zip(nodes, bounds):
            middle = middle_value(node, given, before, after)
            following.append((jnp.where(upper, middle, before), jnp.where(upper, after, middle)))
            following.append((jnp.where(upper, before, middle), jnp.where(upper, middle, after)))
        bounds = following
    return bounds


def capacity_weights(rates, shares):
    weights = shares * rates / (1.0 + rates)
    return [weights[:, zone : zone + 1] for zone in range(weights.shape[1])]


def strided(ref, start, size, stride):
    return ref[pl.ds(start, size, stride=stride), :]


def x_rolls(halves):
    return [(step, 0) for step in doubling(SUBLANES)] + [(step, 1) for step in doubling(halves)]


def y_rolls():
    return [(step, 0) for step in doubling(SUBLANES)]


def x_forward_kernel(
    halves, mobile_hbm, faces_hbm, across_hbm, capacity_hbm, immobile_hbm, rates_hbm, shares_hbm,
    message_ref, block_ref,
    mobile_ref, faces_ref, capacity_ref, immobile_ref, rates_ref, shares_ref, arrived,
    faces_t, storage_t, source_t,
):
    pairs = (
        (rates_hbm, rates_ref), (shares_hbm, shares_ref), (capacity_hbm, capacity_ref),
        (faces_hbm, faces_ref), (immobile_hbm, immobile_ref), (mobile_hbm, mobile_ref),
        (across_hbm, block_ref.at[mobile_ref.shape[0] : 2 * mobile_ref.shape[0], :]),
    )
    copies = [pltpu.make_async_copy(pair[0], pair[1], arrived.at[place]) for place, pair in enumerate(pairs)]
    for copy in copies:
        copy.start()
    rows = mobile_ref.shape[0]
    stride = LANES // SUBLANES
    for copy in copies[:3]:
        copy.wait()
    weights = capacity_weights(rates_ref[...], shares_ref[...])
    capacity = capacity_ref[...]
    storage = 1.0 + capacity * sum(weights[1:], weights[0])
    block_ref[0:rows, :] = storage
    storage_t[...] = storage.T
    copies[3].wait()
    faces_t[...] = faces_ref[...].T
    copies[4].wait()
    total = weights[0] * immobile_ref[0:rows, :]
    for zone in range(1, len(weights)):
        total = total + weights[zone] * immobile_ref[zone * rows : (zone + 1) * rows, :]
    copies[5].wait()
    source_t[...] = (mobile_ref[...] + capacity * total).T
    coefs, sides = [], []
    for index in range(stride):
        coefs.append((strided(faces_t, index, SUBLANES, stride), None, strided(storage_t, index, SUBLANES, stride)))
        sides.append((None, strided(source_t, index, SUBLANES, stride)))
    rolls = x_rolls(halves)
    piece, nodes = tree_coefs(coefs, rolls)
    side, givens = tree_sides(sides, rolls, nodes)
    start = 2 * rows
    for node, given in zip(nodes, givens):
        for part in (node[0], node[1], given):
            block_ref[start : start + SUBLANES, :] = part
            start += SUBLANES
    for row, value in enumerate(piece + side):
        message_ref[row : row + 1, :] = value[0:1, :]
    copies[6].wait()


def y_coefs_kernel(halves, block_ref, rows_ref, state_ref):
    rows = rows_ref.shape[1]
    stride = rows // SUBLANES
    start = 0
    for half in range(halves):
        coefs = []
        for index in range(half, stride, halves):
            storage = strided(block_ref, index, SUBLANES, stride)
            coefs.append((strided(block_ref, rows + index, SUBLANES, stride), None, storage))
        piece, nodes = tree_coefs(coefs, y_rolls())
        for node in nodes:
            for part in node:
                state_ref[start : start + SUBLANES, :] = part
                start += SUBLANES
        for number, value in enumerate(piece):
            row = number * halves + half
            rows_ref[row : row + 1, :] = value[0:1, :]


def state_parts(ref, first, total, parts, pitch=3):
    return [
        tuple(
            ref[(pitch * place + part) * SUBLANES : (pitch * place + part + 1) * SUBLANES, :]
            for part in range(parts)
        )
        for place in range(first, first + total)
    ]


def message_slots(refs, height, pitch, quantity_rows, skips):
    blocks = [(ref, start) for ref in refs for start in range(0, ref.shape[0], height)]
    slots = []
    for (ref, start), skip in zip(blocks, skips):
        rows = [start + quantity * pitch + skip for quantity in range(QUANTITIES)]
        slots.append(tuple(ref[row : row + quantity_rows, :] for row in rows))
    return slots


def x_back(halves, bounds, block_ref, values_t, sides_ref):
    rows = values_t.shape[1]
    before, after = (jnp.broadcast_to(bound, (SUBLANES, rows)) for bound in bounds)
    rolls = x_rolls(halves)
    stride = LANES // SUBLANES
    total = stride - 1 + len(rolls)
    parts = state_parts(block_ref.at[2 * rows :, :], 0, total, 3)
    values = tree_values(before, after, rolls, stride, parts, [part[2] for part in parts])
    for index, value in enumerate(values):
        values_t[pl.ds(index, SUBLANES, stride=stride), :] = value
    sides_ref[...] = block_ref[0:rows, :] * values_t[...].T


def quantity(number):
    return slice(number * LANES, (number + 1) * LANES)


def put_traded(ref, row, rows, number, value):
    ref[(row + rows // 2) % rows : (row + rows // 2) % rows + value.shape[0], quantity(number)] = value


def x_back_kernel(halves, axis, order, pieces, *refs):
    slots = message_slots(refs[:pieces], SUBLANES, 1, 1, [0] * len(order))
    slots = [slots[order.index(place)] for place in range(len(order))]
    block_refs, rows_refs, state_refs = (refs[pieces + 2 * pair : pieces + 2 * pair + 2] for pair in range(3))
    kept_ref, sent_ref, given_ref = refs[pieces + 6 : pieces + 9]
    scratch = refs[pieces + 9 :]
    bounds = ring_bounds(slots, lax.axis_index(axis))
    rows = scratch[0].shape[1]
    stride = rows // SUBLANES
    total = stride // halves - 1 + len(y_rolls())

    def put(row, number, value):
        kept_ref[row : row + 1, quantity(number)] = value
        put_traded(sent_ref, row, 2 * halves, number, value)

    for block in range(2):
        values_t, sides_ref = scratch[2 * block : 2 * block + 2]
        x_back(halves, bounds[block], block_refs[block], values_t, sides_ref)
        start = 0
        for half in range(halves):
            place = block * halves + half
            sides = [(None, strided(sides_ref, index, SUBLANES, stride)) for index in range(half, stride, halves)]
            nodes = state_parts(state_refs[block], half * total, total, 3)
            piece, givens = tree_sides(sides, y_rolls(), nodes)
            if block == 0:
                for given in givens:
                    given_ref[start : start + SUBLANES, :] = given
                    start += SUBLANES
            for number in range(3):
                row = number * halves + half
                put(place, number, rows_refs[block][row : row + 1, :])
            for number, value in enumerate(piece):
                put(place, 3 + number, value[0:1, :])


def read_message(ref):
    return [ref[:, quantity(number)] for number in range(QUANTITIES)]


def join_by_bit(own, other, upper):
    left = [choose(upper, b, a) for a, b in zip(own, other)]
    right = [choose(upper, a, b) for a, b in zip(own, other)]
    coefs, node = join_coefs(left[:3], right[:3])
    sides, given = join_sides(left[3:], right[3:], node)
    return coefs + sides, (node[0], node[1], given)


def own_bit(axis, bit):
    return ((lax.axis_index(axis) >> bit) & 1) == 1


def y_join_kernel(axis, bit, own_ref, other_ref, kept_ref, sent_ref, path_ref):
    joined, path = join_by_bit(read_message(own_ref), read_message(other_ref), own_bit(axis, bit))
    rows = own_ref.shape[0]
    for number, value in enumerate(joined):
        kept_ref[:, quantity(number)] = value
        for row in (0, rows // 2):
            put_traded(sent_ref, row, rows, number, value[row : row + rows // 2, :])
    for number, value in enumerate(path):
        path_ref[:, quantity(number)] = value


def y_back_kernel(halves, axis, rounds, own_ref, other_ref, *refs):
    path_refs = refs[: rounds - 1]
    state_ref, given_ref, out_ref = refs[rounds - 1 :]
    rows = out_ref.shape[0]
    stride = rows // SUBLANES
    joined, path = join_by_bit(read_message(own_ref), read_message(other_ref), own_bit(axis, rounds - 1))
    _, head, tail, side_head, side_tail = joined
    before = after = (side_head + side_tail) * inverse(head + tail)
    paths = [[ref[:, quantity(number)] for number in range(3)] for ref in path_refs] + [path]
    for bit in reversed(range(rounds)):
        node = paths[bit]
        middle = middle_value(node, node[2], before, after)
        upper = own_bit(axis, bit)
        before = jnp.where(upper, middle, before)
        after = jnp.where(upper, after, middle)
    total = stride // halves - 1 + len(y_rolls())
    for half in range(halves):
        bounds = [jnp.broadcast_to(end[half : half + 1, :], (SUBLANES, LANES)) for end in (before, after)]
        nodes = state_parts(state_ref, half * total, total, 2)
        givens = [part[0] for part in state_parts(given_ref, half * total, total, 1, 1)]
        values = tree_values(*bounds, y_rolls(), stride // halves, nodes, givens)
        for index, value in enumerate(values):
            out_ref[pl.ds(index * halves + half, SUBLANES, stride=stride), :] = value


def trade(value, x_step, y_step):
    width = lax.axis_size("yd")
    pairs = []
    for index in range(lax.axis_size("xg")):
        for line in range(width):
            pairs.append((index * width + line, (index ^ x_step) * width + (line ^ y_step)))
    return lax.ppermute(value, ("xg", "yd"), pairs)


def x_exchange(message):
    held = message
    pieces = [message]
    order = [0]
    for step in doubling(lax.axis_size("xg") // 2):
        received = trade(held, 2 * step + 1, 0)
        pieces.append(received)
        order += [place ^ (2 * step + 1) for place in order]
        held = jnp.concatenate([held, received], axis=0)
    pieces.append(trade(held, 1, 0))
    order += [place ^ 1 for place in order]
    return pieces, order


def y_exchange(kept, sent):
    rows = kept.shape[0]
    paths = []
    steps = doubling(lax.axis_size("yd"))
    for bit, step in enumerate(steps):
        received = trade(sent, 1, step)
        if bit < len(steps) - 1:
            kept, sent, path = kernel_call(
                functools.partial(y_join_kernel, "yd", bit),
                (kept, received),
                [held_f32(*kept.shape), f32(*kept.shape), held_f32(rows, 3 * LANES)],
                [],
            )
            paths.append(path)
    return [kept, received] + paths, len(steps)


def f32(*shape):
    return jax.ShapeDtypeStruct(shape, jnp.float32)


def held_f32(*shape):
    return VMEM(shape, jnp.float32)


def kernel_call(body, operands, outputs, scratch, space=VMEM):
    return pl.pallas_call(
        body,
        out_shape=outputs,
        in_specs=[pl.BlockSpec(memory_space=space)] * len(operands),
        out_specs=[pl.BlockSpec(memory_space=VMEM)] * len(outputs),
        scratch_shapes=scratch,
        compiler_params=pltpu.CompilerParams(vmem_limit_bytes=16 * 1024 * 1024),
    )(*operands)


def local(mobile, dispersion_x, dispersion_y, capacity, immobile, exchange_rates, rate_shares):
    shape = mobile.shape
    lines, width = shape[0] * shape[1], shape[2]
    zones = immobile.shape[0]
    halves = width // LANES
    rows = lines * halves
    assert rows == LANES

    def flat(values):
        return values.reshape(-1, LANES)

    mobile, dispersion_x, dispersion_y = flat(mobile), flat(dispersion_x), flat(dispersion_y)
    capacity, immobile = flat(capacity), flat(immobile)
    square = VMEM((rows, LANES), jnp.float32)
    x_nodes = LANES // SUBLANES - 1 + len(x_rolls(halves))
    y_nodes = halves * (rows // SUBLANES // halves - 1 + len(y_rolls()))
    message, block = kernel_call(
        functools.partial(x_forward_kernel, halves),
        tuple(
            pltpu.with_memory_space_constraint(value, pltpu.HBM)
            for value in (
                mobile, dispersion_x, dispersion_y, capacity, immobile, exchange_rates[None], rate_shares[None],
            )
        ),
        [f32(SUBLANES, rows), held_f32(2 * rows + 3 * x_nodes * SUBLANES, LANES)],
        [square] * 3
        + [VMEM((zones * rows, LANES), jnp.float32)]
        + [VMEM((1, zones), jnp.float32)] * 2
        + [pltpu.SemaphoreType.DMA((7,))]
        + [square] * 3,
        pltpu.HBM,
    )
    def y_coefs(part):
        return kernel_call(
            functools.partial(y_coefs_kernel, halves),
            (part,),
            [held_f32(SUBLANES, LANES), held_f32(3 * y_nodes * SUBLANES, LANES)],
            [],
        )

    pieces, order = x_exchange(message)
    y_rows, y_state = y_coefs(block)
    other_block = trade(block, 1, 0)
    other_rows, other_state = y_coefs(other_block)
    kept, sent, givens = kernel_call(
        functools.partial(x_back_kernel, halves, "xg", order, len(pieces)),
        (*pieces, block, other_block, y_rows, other_rows, y_state, other_state),
        [
            held_f32(2 * halves, QUANTITIES * LANES),
            f32(2 * halves, QUANTITIES * LANES),
            held_f32(y_nodes * SUBLANES, LANES),
        ],
        [square] * 4,
    )
    pieces, rounds = y_exchange(kept, sent)
    (updated,) = kernel_call(
        functools.partial(y_back_kernel, halves, "yd", rounds),
        (*pieces, y_state, givens),
        [f32(rows, LANES)],
        [],
    )
    return updated.reshape(shape)


def solution(mesh):
    field = P("yd", None, "xg")
    return jax.shard_map(
        local,
        mesh=mesh,
        in_specs=(field, field, field, field, P(None, "yd", None, "xg"), P(), P()),
        out_specs=field,
        check_vma=False,
    )
```

```python
import functools

import jax
import jax.numpy as jnp
from jax import lax
from jax.experimental import pallas as pl
from jax.experimental.pallas import tpu as pltpu
from jax.sharding import PartitionSpec as P

LANES = 128
SUBLANES = 8
QUANTITIES = 5
VMEM = pltpu.VMEM


def inverse(value):
    return 1.0 / value


def plus(first, second):
    if first is None:
        return second
    return first + second


def join_coefs(left, right):
    coupling_1, head_1, tail_1 = left
    coupling_2, head_2, tail_2 = right
    middle = plus(head_2, tail_1)
    inv = inverse(coupling_1 + coupling_2 + middle)
    weight_1 = coupling_1 * inv
    weight_2 = coupling_2 * inv
    joined = (coupling_1 * weight_2, plus(head_1, weight_1 * middle), tail_2 + weight_2 * middle)
    return joined, (weight_1, weight_2, inv)


def join_sides(left, right, node):
    head_1, tail_1 = left
    head_2, tail_2 = right
    weight_1, weight_2, inv = node
    side = plus(head_2, tail_1)
    joined = (plus(head_1, weight_1 * side), tail_2 + weight_2 * side)
    return joined, side * inv


def middle_value(node, given, before, after):
    return given + node[0] * before + node[1] * after


def ahead(value, step, axis):
    return pltpu.roll(value, value.shape[axis] - step, axis)


def behind(value, step, axis):
    return pltpu.roll(value, step, axis)


def doubling(count):
    steps = []
    step = 1
    while step < count:
        steps.append(step)
        step *= 2
    return steps


def tree_coefs(leaves, rolls):
    nodes = []
    level = leaves
    while len(level) > 1:
        following = []
        for index in range(0, len(level), 2):
            joined, node = join_coefs(level[index], level[index + 1])
            following.append(joined)
            nodes.append(node)
        level = following
    piece = level[0]
    for step, axis in rolls:
        piece, node = join_coefs(piece, tuple(ahead(part, step, axis) for part in piece))
        nodes.append(node)
    return piece, nodes


def tree_sides(leaves, rolls, nodes):
    givens = []
    level = leaves
    while len(level) > 1:
        following = []
        for index in range(0, len(level), 2):
            joined, given = join_sides(level[index], level[index + 1], nodes[len(givens)])
            following.append(joined)
            givens.append(given)
        level = following
    piece = level[0]
    for step, axis in rolls:
        other = tuple(ahead(part, step, axis) for part in piece)
        piece, given = join_sides(piece, other, nodes[len(givens)])
        givens.append(given)
    return piece, givens


def tree_values(before, after, rolls, count, nodes, givens):
    place = len(nodes)
    for step, axis in reversed(rolls):
        place -= 1
        middle = middle_value(nodes[place], givens[place], before, after)
        upper = (lax.broadcasted_iota(jnp.int32, middle.shape, axis) & step) != 0
        before = jnp.where(upper, behind(middle, step, axis), before)
        after = jnp.where(upper, behind(after, step, axis), middle)
    bounds = [before, after]
    while len(bounds) - 1 < count:
        width = len(bounds) - 1
        place -= width
        following = [bounds[0]]
        for index in range(width):
            following.append(
                middle_value(
                    nodes[place + index], givens[place + index], bounds[index], bounds[index + 1]
                )
            )
            following.append(bounds[index + 1])
        bounds = following
    return bounds[1:]


def choose(condition, first, second):
    if isinstance(condition, bool):
        return first if condition else second
    return jnp.where(condition, first, second)


def ring_bounds(slots, index):
    level = slots
    rounds = []
    bit = 0
    while len(level) > 1:
        upper = ((index >> bit) & 1) == 1
        following, nodes = [], []
        for place in range(0, len(level), 2):
            own, other = level[place], level[place + 1]
            left = [jnp.where(upper, b, a) for a, b in zip(own, other)]
            right = [jnp.where(upper, a, b) for a, b in zip(own, other)]
            coefs, node = join_coefs(left[:3], right[:3])
            sides, given = join_sides(left[3:], right[3:], node)
            nodes.append((node, given))
            following.append(coefs + sides)
        rounds.append((nodes, upper))
        level = following
        bit += 1
    _, head, tail, side_head, side_tail = level[0]
    last = (side_head + side_tail) * inverse(head + tail)
    bounds = [(last, last)]
    for nodes, upper in reversed(rounds):
        following = []
        for (node, given), (before, after) in zip(nodes, bounds):
            middle = middle_value(node, given, before, after)
            following.append((jnp.where(upper, middle, before), jnp.where(upper, after, middle)))
            following.append((jnp.where(upper, before, middle), jnp.where(upper, middle, after)))
        bounds = following
    return bounds


def capacity_weights(rates, shares):
    weights = shares * rates / (1.0 + rates)
    return [weights[:, zone : zone + 1] for zone in range(weights.shape[1])]


def strided(ref, start, size, stride):
    return ref[pl.ds(start, size, stride=stride), :]


def x_rolls(halves):
    return [(step, 0) for step in doubling(SUBLANES)] + [(step, 1) for step in doubling(halves)]


def y_rolls():
    return [(step, 0) for step in doubling(SUBLANES)]


def x_forward_kernel(
    halves, mobile_hbm, faces_hbm, across_hbm, capacity_hbm, immobile_hbm, rates_hbm, shares_hbm,
    message_ref, block_ref,
    mobile_ref, faces_ref, capacity_ref, immobile_ref, rates_ref, shares_ref, arrived,
    faces_t, storage_t, source_t,
):
    rows = mobile_ref.shape[0]
    zones = [slice(start, start + rows) for start in range(0, immobile_ref.shape[0], rows)]
    pairs = [
        (rates_hbm, rates_ref), (shares_hbm, shares_ref), (capacity_hbm, capacity_ref), (faces_hbm, faces_ref),
        *((immobile_hbm.at[zone, :], immobile_ref.at[zone, :]) for zone in zones),
        (mobile_hbm, mobile_ref), (across_hbm, block_ref.at[rows : 2 * rows, :]),
    ]
    copies = [pltpu.make_async_copy(pair[0], pair[1], arrived.at[place]) for place, pair in enumerate(pairs)]
    for copy in copies:
        copy.start()
    stride = LANES // SUBLANES
    for copy in copies[:3]:
        copy.wait()
    weights = capacity_weights(rates_ref[...], shares_ref[...])
    capacity = capacity_ref[...]
    storage = 1.0 + capacity * sum(weights[1:], weights[0])
    block_ref[0:rows, :] = storage
    storage_t[...] = storage.T
    copies[3].wait()
    faces_t[...] = faces_ref[...].T
    total = None
    for copy, weight, zone in zip(copies[4:], weights, zones):
        copy.wait()
        total = plus(total, weight * immobile_ref[zone, :])
    copies[-2].wait()
    source_t[...] = (mobile_ref[...] + capacity * total).T
    coefs, sides = [], []
    for index in range(stride):
        coefs.append((strided(faces_t, index, SUBLANES, stride), None, strided(storage_t, index, SUBLANES, stride)))
        sides.append((None, strided(source_t, index, SUBLANES, stride)))
    rolls = x_rolls(halves)
    piece, nodes = tree_coefs(coefs, rolls)
    side, givens = tree_sides(sides, rolls, nodes)
    start = 2 * rows
    for node, given in zip(nodes, givens):
        for part in (node[0], node[1], given):
            block_ref[start : start + SUBLANES, :] = part
            start += SUBLANES
    for row, value in enumerate(piece + side):
        message_ref[row : row + 1, :] = value[0:1, :]
    copies[-1].wait()


def y_coefs_kernel(halves, block_ref, rows_ref, state_ref):
    rows = rows_ref.shape[1]
    stride = rows // SUBLANES
    start = 0
    for half in range(halves):
        coefs = []
        for index in range(half, stride, halves):
            storage = strided(block_ref, index, SUBLANES, stride)
            coefs.append((strided(block_ref, rows + index, SUBLANES, stride), None, storage))
        piece, nodes = tree_coefs(coefs, y_rolls())
        for node in nodes:
            for part in node:
                state_ref[start : start + SUBLANES, :] = part
                start += SUBLANES
        for number, value in enumerate(piece):
            row = number * halves + half
            rows_ref[row : row + 1, :] = value[0:1, :]


def state_parts(ref, first, total, parts, pitch=3):
    return [
        tuple(
            ref[(pitch * place + part) * SUBLANES : (pitch * place + part + 1) * SUBLANES, :]
            for part in range(parts)
        )
        for place in range(first, first + total)
    ]


def message_slots(refs, height, pitch, quantity_rows, skips):
    blocks = [(ref, start) for ref in refs for start in range(0, ref.shape[0], height)]
    slots = []
    for (ref, start), skip in zip(blocks, skips):
        rows = [start + quantity * pitch + skip for quantity in range(QUANTITIES)]
        slots.append(tuple(ref[row : row + quantity_rows, :] for row in rows))
    return slots


def x_back(halves, bounds, block_ref, values_t, sides_ref):
    rows = values_t.shape[1]
    before, after = (jnp.broadcast_to(bound, (SUBLANES, rows)) for bound in bounds)
    rolls = x_rolls(halves)
    stride = LANES // SUBLANES
    total = stride - 1 + len(rolls)
    parts = state_parts(block_ref.at[2 * rows :, :], 0, total, 3)
    values = tree_values(before, after, rolls, stride, parts, [part[2] for part in parts])
    for index, value in enumerate(values):
        values_t[pl.ds(index, SUBLANES, stride=stride), :] = value
    sides_ref[...] = block_ref[0:rows, :] * values_t[...].T


def quantity(number):
    return slice(number * LANES, (number + 1) * LANES)


def put_traded(ref, row, rows, number, value):
    ref[(row + rows // 2) % rows : (row + rows // 2) % rows + value.shape[0], quantity(number)] = value


def x_back_kernel(halves, axis, order, pieces, *refs):
    slots = message_slots(refs[:pieces], SUBLANES, 1, 1, [0] * len(order))
    slots = [slots[order.index(place)] for place in range(len(order))]
    block_refs, rows_refs, state_refs = (refs[pieces + 2 * pair : pieces + 2 * pair + 2] for pair in range(3))
    kept_ref, sent_ref, given_ref = refs[pieces + 6 : pieces + 9]
    scratch = refs[pieces + 9 :]
    bounds = ring_bounds(slots, lax.axis_index(axis))
    rows = scratch[0].shape[1]
    stride = rows // SUBLANES
    total = stride // halves - 1 + len(y_rolls())

    def put(row, number, value):
        kept_ref[row : row + 1, quantity(number)] = value
        put_traded(sent_ref, row, 2 * halves, number, value)

    for block in range(2):
        values_t, sides_ref = scratch[2 * block : 2 * block + 2]
        x_back(halves, bounds[block], block_refs[block], values_t, sides_ref)
        start = 0
        for half in range(halves):
            place = block * halves + half
            sides = [(None, strided(sides_ref, index, SUBLANES, stride)) for index in range(half, stride, halves)]
            nodes = state_parts(state_refs[block], half * total, total, 3)
            piece, givens = tree_sides(sides, y_rolls(), nodes)
            if block == 0:
                for given in givens:
                    given_ref[start : start + SUBLANES, :] = given
                    start += SUBLANES
            for number in range(3):
                row = number * halves + half
                put(place, number, rows_refs[block][row : row + 1, :])
            for number, value in enumerate(piece):
                put(place, 3 + number, value[0:1, :])


def read_message(ref):
    return [ref[:, quantity(number)] for number in range(QUANTITIES)]


def join_by_bit(own, other, upper):
    left = [choose(upper, b, a) for a, b in zip(own, other)]
    right = [choose(upper, a, b) for a, b in zip(own, other)]
    coefs, node = join_coefs(left[:3], right[:3])
    sides, given = join_sides(left[3:], right[3:], node)
    return coefs + sides, (node[0], node[1], given)


def own_bit(axis, bit):
    return ((lax.axis_index(axis) >> bit) & 1) == 1


def y_join_kernel(axis, bit, own_ref, other_ref, kept_ref, sent_ref, path_ref):
    joined, path = join_by_bit(read_message(own_ref), read_message(other_ref), own_bit(axis, bit))
    rows = own_ref.shape[0]
    for number, value in enumerate(joined):
        kept_ref[:, quantity(number)] = value
        for row in (0, rows // 2):
            put_traded(sent_ref, row, rows, number, value[row : row + rows // 2, :])
    for number, value in enumerate(path):
        path_ref[:, quantity(number)] = value


def y_back_kernel(halves, axis, rounds, own_ref, other_ref, *refs):
    path_refs = refs[: rounds - 1]
    state_ref, given_ref, out_ref = refs[rounds - 1 :]
    rows = out_ref.shape[0]
    stride = rows // SUBLANES
    joined, path = join_by_bit(read_message(own_ref), read_message(other_ref), own_bit(axis, rounds - 1))
    _, head, tail, side_head, side_tail = joined
    before = after = (side_head + side_tail) * inverse(head + tail)
    paths = [[ref[:, quantity(number)] for number in range(3)] for ref in path_refs] + [path]
    for bit in reversed(range(rounds)):
        node = paths[bit]
        middle = middle_value(node, node[2], before, after)
        upper = own_bit(axis, bit)
        before = jnp.where(upper, middle, before)
        after = jnp.where(upper, after, middle)
    total = stride // halves - 1 + len(y_rolls())
    for half in range(halves):
        bounds = [jnp.broadcast_to(end[half : half + 1, :], (SUBLANES, LANES)) for end in (before, after)]
        nodes = state_parts(state_ref, half * total, total, 2)
        givens = [part[0] for part in state_parts(given_ref, half * total, total, 1, 1)]
        values = tree_values(*bounds, y_rolls(), stride // halves, nodes, givens)
        for index, value in enumerate(values):
            out_ref[pl.ds(index * halves + half, SUBLANES, stride=stride), :] = value


def trade(value, x_step, y_step):
    width = lax.axis_size("yd")
    pairs = []
    for index in range(lax.axis_size("xg")):
        for line in range(width):
            pairs.append((index * width + line, (index ^ x_step) * width + (line ^ y_step)))
    return lax.ppermute(value, ("xg", "yd"), pairs)


def pack_kernel(first_ref, second_ref, out_ref):
    height = first_ref.shape[0]
    out_ref[0:height, :] = first_ref[...]
    out_ref[height:, :] = second_ref[...]


def pack(first, second):
    (packed,) = kernel_call(
        pack_kernel, (first, second), [f32(first.shape[0] + second.shape[0], first.shape[1])], [], cost=10000000000
    )
    return packed


def x_exchange(message):
    held = message
    pieces = [message]
    order = [0]
    for step in doubling(lax.axis_size("xg") // 2):
        received = trade(held, 2 * step + 1, 0)
        pieces.append(received)
        order += [place ^ (2 * step + 1) for place in order]
        held = pack(held, received)
    pieces.append(trade(held, 1, 0))
    order += [place ^ 1 for place in order]
    return pieces, order


def y_exchange(kept, sent):
    rows = kept.shape[0]
    paths = []
    steps = doubling(lax.axis_size("yd"))
    for bit, step in enumerate(steps):
        received = trade(sent, 1, step)
        if bit < len(steps) - 1:
            kept, sent, path = kernel_call(
                functools.partial(y_join_kernel, "yd", bit),
                (kept, received),
                [held_f32(*kept.shape), f32(*kept.shape), held_f32(rows, 3 * LANES)],
                [],
            )
            paths.append(path)
    return [kept, received] + paths, len(steps)


def f32(*shape):
    return jax.ShapeDtypeStruct(shape, jnp.float32)


def held_f32(*shape):
    return VMEM(shape, jnp.float32)


def kernel_call(body, operands, outputs, scratch, space=VMEM, cost=500000):
    return pl.pallas_call(
        body,
        out_shape=outputs,
        in_specs=[pl.BlockSpec(memory_space=space)] * len(operands),
        out_specs=[pl.BlockSpec(memory_space=VMEM)] * len(outputs),
        scratch_shapes=scratch,
        cost_estimate=pl.CostEstimate(flops=cost, bytes_accessed=cost, transcendentals=0),
        compiler_params=pltpu.CompilerParams(vmem_limit_bytes=16 * 1024 * 1024),
    )(*operands)


def local(mobile, dispersion_x, dispersion_y, capacity, immobile, exchange_rates, rate_shares):
    shape = mobile.shape
    lines, width = shape[0] * shape[1], shape[2]
    zones = immobile.shape[0]
    halves = width // LANES
    rows = lines * halves
    assert rows == LANES

    def flat(values):
        return values.reshape(-1, LANES)

    mobile, dispersion_x, dispersion_y = flat(mobile), flat(dispersion_x), flat(dispersion_y)
    capacity, immobile = flat(capacity), flat(immobile)
    square = VMEM((rows, LANES), jnp.float32)
    x_nodes = LANES // SUBLANES - 1 + len(x_rolls(halves))
    y_nodes = halves * (rows // SUBLANES // halves - 1 + len(y_rolls()))
    message, block = kernel_call(
        functools.partial(x_forward_kernel, halves),
        tuple(
            pltpu.with_memory_space_constraint(value, pltpu.HBM)
            for value in (
                mobile, dispersion_x, dispersion_y, capacity, immobile, exchange_rates[None], rate_shares[None],
            )
        ),
        [f32(SUBLANES, rows), held_f32(2 * rows + 3 * x_nodes * SUBLANES, LANES)],
        [square] * 3
        + [VMEM((zones * rows, LANES), jnp.float32)]
        + [VMEM((1, zones), jnp.float32)] * 2
        + [pltpu.SemaphoreType.DMA((6 + zones,))]
        + [square] * 3,
        pltpu.HBM,
    )
    def y_coefs(part):
        return kernel_call(
            functools.partial(y_coefs_kernel, halves),
            (part,),
            [held_f32(SUBLANES, LANES), held_f32(3 * y_nodes * SUBLANES, LANES)],
            [],
        )

    pieces, order = x_exchange(message)
    y_rows, y_state = y_coefs(block)
    other_block = trade(block, 1, 0)
    other_rows, other_state = y_coefs(other_block)
    kept, sent, givens = kernel_call(
        functools.partial(x_back_kernel, halves, "xg", order, len(pieces)),
        (*pieces, block, other_block, y_rows, other_rows, y_state, other_state),
        [
            held_f32(2 * halves, QUANTITIES * LANES),
            f32(2 * halves, QUANTITIES * LANES),
            held_f32(y_nodes * SUBLANES, LANES),
        ],
        [square] * 4,
    )
    pieces, rounds = y_exchange(kept, sent)
    (updated,) = kernel_call(
        functools.partial(y_back_kernel, halves, "yd", rounds),
        (*pieces, y_state, givens),
        [f32(rows, LANES)],
        [],
    )
    return updated.reshape(shape)


def solution(mesh):
    field = P("yd", None, "xg")
    return jax.shard_map(
        local,
        mesh=mesh,
        in_specs=(field, field, field, field, P(None, "yd", None, "xg"), P(), P()),
        out_specs=field,
        check_vma=False,
    )
```

```python
import functools

import jax
import jax.numpy as jnp
from jax import lax
from jax.experimental import pallas as pl
from jax.experimental.pallas import tpu as pltpu
from jax.sharding import PartitionSpec as P

LANES = 128
SUBLANES = 8
QUANTITIES = 5
VMEM = pltpu.VMEM


def inverse(value):
    return 1.0 / value


def plus(first, second):
    if first is None:
        return second
    return first + second


def join_coefs(left, right):
    coupling_1, head_1, tail_1 = left
    coupling_2, head_2, tail_2 = right
    middle = plus(head_2, tail_1)
    inv = inverse(coupling_1 + coupling_2 + middle)
    weight_1 = coupling_1 * inv
    weight_2 = coupling_2 * inv
    joined = (coupling_1 * weight_2, plus(head_1, weight_1 * middle), tail_2 + weight_2 * middle)
    return joined, (weight_1, weight_2, inv)


def join_sides(left, right, node):
    head_1, tail_1 = left
    head_2, tail_2 = right
    weight_1, weight_2, inv = node
    side = plus(head_2, tail_1)
    joined = (plus(head_1, weight_1 * side), tail_2 + weight_2 * side)
    return joined, side * inv


def middle_value(node, given, before, after):
    return given + node[0] * before + node[1] * after


def ahead(value, step, axis):
    return pltpu.roll(value, value.shape[axis] - step, axis)


def behind(value, step, axis):
    return pltpu.roll(value, step, axis)


def doubling(count):
    steps = []
    step = 1
    while step < count:
        steps.append(step)
        step *= 2
    return steps


def tree_coefs(leaves, rolls):
    nodes = []
    level = leaves
    while len(level) > 1:
        following = []
        for index in range(0, len(level), 2):
            joined, node = join_coefs(level[index], level[index + 1])
            following.append(joined)
            nodes.append(node)
        level = following
    piece = level[0]
    for step, axis in rolls:
        piece, node = join_coefs(piece, tuple(ahead(part, step, axis) for part in piece))
        nodes.append(node)
    return piece, nodes


def tree_sides(leaves, rolls, nodes):
    givens = []
    level = leaves
    while len(level) > 1:
        following = []
        for index in range(0, len(level), 2):
            joined, given = join_sides(level[index], level[index + 1], nodes[len(givens)])
            following.append(joined)
            givens.append(given)
        level = following
    piece = level[0]
    for step, axis in rolls:
        other = tuple(ahead(part, step, axis) for part in piece)
        piece, given = join_sides(piece, other, nodes[len(givens)])
        givens.append(given)
    return piece, givens


def tree_values(before, after, rolls, count, nodes, givens):
    place = len(nodes)
    for step, axis in reversed(rolls):
        place -= 1
        middle = middle_value(nodes[place], givens[place], before, after)
        upper = (lax.broadcasted_iota(jnp.int32, middle.shape, axis) & step) != 0
        before = jnp.where(upper, behind(middle, step, axis), before)
        after = jnp.where(upper, behind(after, step, axis), middle)
    bounds = [before, after]
    while len(bounds) - 1 < count:
        width = len(bounds) - 1
        place -= width
        following = [bounds[0]]
        for index in range(width):
            following.append(
                middle_value(
                    nodes[place + index], givens[place + index], bounds[index], bounds[index + 1]
                )
            )
            following.append(bounds[index + 1])
        bounds = following
    return bounds[1:]


def choose(condition, first, second):
    if isinstance(condition, bool):
        return first if condition else second
    return jnp.where(condition, first, second)


def ring_bounds(slots, index):
    level = slots
    rounds = []
    bit = 0
    while len(level) > 1:
        upper = ((index >> bit) & 1) == 1
        following, nodes = [], []
        for place in range(0, len(level), 2):
            own, other = level[place], level[place + 1]
            left = [jnp.where(upper, b, a) for a, b in zip(own, other)]
            right = [jnp.where(upper, a, b) for a, b in zip(own, other)]
            coefs, node = join_coefs(left[:3], right[:3])
            sides, given = join_sides(left[3:], right[3:], node)
            nodes.append((node, given))
            following.append(coefs + sides)
        rounds.append((nodes, upper))
        level = following
        bit += 1
    _, head, tail, side_head, side_tail = level[0]
    last = (side_head + side_tail) * inverse(head + tail)
    bounds = [(last, last)]
    for nodes, upper in reversed(rounds):
        following = []
        for (node, given), (before, after) in zip(nodes, bounds):
            middle = middle_value(node, given, before, after)
            following.append((jnp.where(upper, middle, before), jnp.where(upper, after, middle)))
            following.append((jnp.where(upper, before, middle), jnp.where(upper, middle, after)))
        bounds = following
    return bounds


def capacity_weights(rates, shares):
    weights = shares * rates / (1.0 + rates)
    return [weights[:, zone : zone + 1] for zone in range(weights.shape[1])]


def strided(ref, start, size, stride):
    return ref[pl.ds(start, size, stride=stride), :]


def x_rolls(halves):
    return [(step, 0) for step in doubling(SUBLANES)] + [(step, 1) for step in doubling(halves)]


def y_rolls():
    return [(step, 0) for step in doubling(SUBLANES)]


def x_forward_kernel(
    halves, mobile_hbm, faces_hbm, across_hbm, capacity_hbm, immobile_hbm, rates_hbm, shares_hbm,
    message_ref, block_ref,
    mobile_ref, faces_ref, capacity_ref, immobile_ref, rates_ref, shares_ref, arrived,
    faces_t, storage_t, source_t,
):
    rows = mobile_ref.shape[0]
    pairs = (
        (immobile_hbm, immobile_ref), (capacity_hbm, capacity_ref), (mobile_hbm, mobile_ref), (faces_hbm, faces_ref),
        (rates_hbm, rates_ref), (shares_hbm, shares_ref), (across_hbm, block_ref.at[rows : 2 * rows, :]),
    )
    copies = [pltpu.make_async_copy(pair[0], pair[1], arrived.at[place]) for place, pair in enumerate(pairs)]
    for copy in copies:
        copy.start()
    immobile_copy, capacity_copy, mobile_copy, faces_copy, rates_copy, shares_copy, across_copy = copies
    stride = LANES // SUBLANES
    faces_copy.wait()
    faces_t[...] = faces_ref[...].T
    rates_copy.wait()
    shares_copy.wait()
    capacity_copy.wait()
    weights = capacity_weights(rates_ref[...], shares_ref[...])
    capacity = capacity_ref[...]
    storage = 1.0 + capacity * sum(weights[1:], weights[0])
    block_ref[0:rows, :] = storage
    storage_t[...] = storage.T
    immobile_copy.wait()
    total = None
    for zone, weight in enumerate(weights):
        total = plus(total, weight * immobile_ref[zone * rows : (zone + 1) * rows, :])
    mobile_copy.wait()
    source_t[...] = (mobile_ref[...] + capacity * total).T
    coefs, sides = [], []
    for index in range(stride):
        coefs.append((strided(faces_t, index, SUBLANES, stride), None, strided(storage_t, index, SUBLANES, stride)))
        sides.append((None, strided(source_t, index, SUBLANES, stride)))
    rolls = x_rolls(halves)
    piece, nodes = tree_coefs(coefs, rolls)
    side, givens = tree_sides(sides, rolls, nodes)
    start = 2 * rows
    for node, given in zip(nodes, givens):
        for part in (node[0], node[1], given):
            block_ref[start : start + SUBLANES, :] = part
            start += SUBLANES
    for row, value in enumerate(piece + side):
        message_ref[row : row + 1, :] = value[0:1, :]
    across_copy.wait()


def ends_responses(shape):
    one, nothing = jnp.ones(shape, jnp.float32), jnp.zeros(shape, jnp.float32)
    return ((one, nothing), (nothing, one))


def prepare_kernel(halves, block_ref, rows_ref, lines_ref, sums_ref, state_ref, spread_ref):
    rows = rows_ref.shape[1]
    stride = LANES // SUBLANES
    rolls = x_rolls(halves)
    total = stride - 1 + len(rolls)
    nodes = state_parts(block_ref.at[2 * rows :, :], 0, total, 3)
    nothing = jnp.zeros((SUBLANES, rows), jnp.float32)
    cases = [((nothing, nothing), [node[2] for node in nodes])]
    cases += [(ends, [0.0] * total) for ends in ends_responses((SUBLANES, rows))]
    for case, (ends, givens) in enumerate(cases):
        for index, value in enumerate(tree_values(*ends, rolls, stride, nodes, givens)):
            lines_ref[pl.ds(case * LANES + index, SUBLANES, stride=stride), :] = value
    stride = rows // SUBLANES
    start = 0
    for half in range(halves):
        storage = [strided(block_ref, index, SUBLANES, stride) for index in range(half, stride, halves)]
        faces = [strided(block_ref, rows + index, SUBLANES, stride) for index in range(half, stride, halves)]
        piece, nodes = tree_coefs([(face, None, held) for face, held in zip(faces, storage)], y_rolls())
        for node in nodes:
            for part in node:
                state_ref[start : start + SUBLANES, :] = part
                start += SUBLANES
        for number, value in enumerate(piece):
            row = number * halves + half
            rows_ref[row : row + 1, :] = value[0:1, :]
        for case, ends in enumerate(ends_responses((SUBLANES, LANES))):
            values = tree_values(*ends, y_rolls(), len(storage), nodes, [0.0] * len(nodes))
            for index, (value, held) in enumerate(zip(values, storage)):
                place = pl.ds(case * rows + index * halves + half, SUBLANES, stride=stride)
                spread_ref[place, :] = value
                sums_ref[place, :] = value * held


def state_parts(ref, first, total, parts, pitch=3):
    return [
        tuple(
            ref[(pitch * place + part) * SUBLANES : (pitch * place + part + 1) * SUBLANES, :]
            for part in range(parts)
        )
        for place in range(first, first + total)
    ]


def message_slots(refs, height, pitch, quantity_rows, skips):
    blocks = [(ref, start) for ref in refs for start in range(0, ref.shape[0], height)]
    slots = []
    for (ref, start), skip in zip(blocks, skips):
        rows = [start + quantity * pitch + skip for quantity in range(QUANTITIES)]
        slots.append(tuple(ref[row : row + quantity_rows, :] for row in rows))
    return slots


def quantity(number):
    return slice(number * LANES, (number + 1) * LANES)


def put_traded(ref, row, rows, number, value):
    ref[(row + rows // 2) % rows : (row + rows // 2) % rows + value.shape[0], quantity(number)] = value


def along_line(bound, halves, rows):
    value = jnp.broadcast_to(bound, (SUBLANES, rows))
    lane = lax.broadcasted_iota(jnp.int32, value.shape, 1)
    for step in doubling(halves):
        value = jnp.where((lane & step) != 0, behind(value, step, 1), value)
    return value[0:1, :]


def x_back_kernel(halves, axis, order, pieces, *refs):
    slots = message_slots(refs[:pieces], SUBLANES, 1, 1, [0] * len(order))
    slots = [slots[order.index(place)] for place in range(len(order))]
    lines_refs, sums_refs, rows_refs = (refs[pieces + 2 * pair : pieces + 2 * pair + 2] for pair in range(3))
    kept_ref, sent_ref, values_ref = refs[pieces + 6 :]
    bounds = ring_bounds(slots, lax.axis_index(axis))
    rows = values_ref.shape[0]

    def put(row, number, value):
        kept_ref[row : row + 1, quantity(number)] = value
        put_traded(sent_ref, row, 2 * halves, number, value)

    for block in range(2):
        for half in range(halves):
            for number in range(3):
                row = number * halves + half
                put(block * halves + half, number, rows_refs[block][row : row + 1, :])
    for block in range(2):
        lines_ref, sums_ref = lines_refs[block], sums_refs[block]
        before, after = (along_line(bound, halves, rows) for bound in bounds[block])
        values = lines_ref[0:LANES, :] + lines_ref[LANES : 2 * LANES, :] * before + lines_ref[2 * LANES :, :] * after
        values = values.T
        if block == 0:
            values_ref[...] = values
        for end in range(2):
            parts = (values * sums_ref[end * rows : (end + 1) * rows, :]).reshape(-1, SUBLANES, LANES)
            side = jnp.sum(parts, axis=0)
            for step in doubling(SUBLANES // halves):
                side = side + behind(side, step * halves, 0)
            for half in range(halves):
                put(block * halves + half, 3 + end, side[half : half + 1, :])


def y_given_kernel(halves, block_ref, values_ref, state_ref, given_ref):
    rows = values_ref.shape[0]
    stride = rows // SUBLANES
    total = stride // halves - 1 + len(y_rolls())
    nothing = jnp.zeros((SUBLANES, LANES), jnp.float32)
    for half in range(halves):
        places = [pl.ds(index, SUBLANES, stride=stride) for index in range(half, stride, halves)]
        sides = [(None, block_ref[place, :] * values_ref[place, :]) for place in places]
        nodes = state_parts(state_ref, half * total, total, 3)
        _, givens = tree_sides(sides, y_rolls(), nodes)
        for place, value in zip(places, tree_values(nothing, nothing, y_rolls(), len(places), nodes, givens)):
            given_ref[place, :] = value


def read_message(ref):
    return [ref[:, quantity(number)] for number in range(QUANTITIES)]


def join_by_bit(own, other, upper):
    left = [choose(upper, b, a) for a, b in zip(own, other)]
    right = [choose(upper, a, b) for a, b in zip(own, other)]
    coefs, node = join_coefs(left[:3], right[:3])
    sides, given = join_sides(left[3:], right[3:], node)
    return coefs + sides, (node[0], node[1], given)


def own_bit(axis, bit):
    return ((lax.axis_index(axis) >> bit) & 1) == 1


def y_join_kernel(axis, bit, own_ref, other_ref, kept_ref, sent_ref, path_ref):
    joined, path = join_by_bit(read_message(own_ref), read_message(other_ref), own_bit(axis, bit))
    rows = own_ref.shape[0]
    for number, value in enumerate(joined):
        kept_ref[:, quantity(number)] = value
        for row in (0, rows // 2):
            put_traded(sent_ref, row, rows, number, value[row : row + rows // 2, :])
    for number, value in enumerate(path):
        path_ref[:, quantity(number)] = value


def y_back_kernel(halves, axis, rounds, own_ref, other_ref, *refs):
    path_refs = refs[: rounds - 1]
    given_ref, spread_ref, out_ref = refs[rounds - 1 :]
    rows = out_ref.shape[0]
    joined, path = join_by_bit(read_message(own_ref), read_message(other_ref), own_bit(axis, rounds - 1))
    _, head, tail, side_head, side_tail = joined
    before = after = (side_head + side_tail) * inverse(head + tail)
    paths = [[ref[:, quantity(number)] for number in range(3)] for ref in path_refs] + [path]
    for bit in reversed(range(rounds)):
        node = paths[bit]
        middle = middle_value(node, node[2], before, after)
        upper = own_bit(axis, bit)
        before = jnp.where(upper, middle, before)
        after = jnp.where(upper, after, middle)
    sublane = lax.broadcasted_iota(jnp.int32, (SUBLANES, LANES), 0) % halves
    ends = []
    for end in (before, after):
        value = jnp.broadcast_to(end[0:1, :], (SUBLANES, LANES))
        for half in range(1, halves):
            value = jnp.where(sublane == half, jnp.broadcast_to(end[half : half + 1, :], value.shape), value)
        ends.append(value)
    for start in range(0, rows, SUBLANES):
        part = slice(start, start + SUBLANES)
        late = slice(rows + start, rows + start + SUBLANES)
        out_ref[part, :] = given_ref[part, :] + spread_ref[part, :] * ends[0] + spread_ref[late, :] * ends[1]


def trade(value, x_step, y_step):
    width = lax.axis_size("yd")
    pairs = []
    for index in range(lax.axis_size("xg")):
        for line in range(width):
            pairs.append((index * width + line, (index ^ x_step) * width + (line ^ y_step)))
    return lax.ppermute(value, ("xg", "yd"), pairs)


def pack_kernel(first_ref, second_ref, out_ref):
    height = first_ref.shape[0]
    out_ref[0:height, :] = first_ref[...]
    out_ref[height:, :] = second_ref[...]


def pack(first, second):
    (packed,) = kernel_call(
        pack_kernel, (first, second), [f32(first.shape[0] + second.shape[0], first.shape[1])], [], cost=10000000000
    )
    return packed


def x_exchange(message):
    held = message
    pieces = [message]
    order = [0]
    for step in doubling(lax.axis_size("xg") // 2):
        received = trade(held, 2 * step + 1, 0)
        pieces.append(received)
        order += [place ^ (2 * step + 1) for place in order]
        held = pack(held, received)
    pieces.append(trade(held, 1, 0))
    order += [place ^ 1 for place in order]
    return pieces, order


def y_exchange(kept, sent):
    rows = kept.shape[0]
    paths = []
    steps = doubling(lax.axis_size("yd"))
    for bit, step in enumerate(steps):
        received = trade(sent, 1, step)
        if bit < len(steps) - 1:
            kept, sent, path = kernel_call(
                functools.partial(y_join_kernel, "yd", bit),
                (kept, received),
                [held_f32(*kept.shape), f32(*kept.shape), held_f32(rows, 3 * LANES)],
                [],
            )
            paths.append(path)
    return [kept, received] + paths, len(steps)


def f32(*shape):
    return jax.ShapeDtypeStruct(shape, jnp.float32)


def held_f32(*shape):
    return VMEM(shape, jnp.float32)


def kernel_call(body, operands, outputs, scratch, space=VMEM, cost=500000):
    return pl.pallas_call(
        body,
        out_shape=outputs,
        in_specs=[pl.BlockSpec(memory_space=space)] * len(operands),
        out_specs=[pl.BlockSpec(memory_space=VMEM)] * len(outputs),
        scratch_shapes=scratch,
        cost_estimate=pl.CostEstimate(flops=cost, bytes_accessed=cost, transcendentals=0),
        compiler_params=pltpu.CompilerParams(vmem_limit_bytes=16 * 1024 * 1024),
    )(*operands)


def local(mobile, dispersion_x, dispersion_y, capacity, immobile, exchange_rates, rate_shares):
    shape = mobile.shape
    lines, width = shape[0] * shape[1], shape[2]
    zones = immobile.shape[0]
    halves = width // LANES
    rows = lines * halves
    assert rows == LANES

    def flat(values):
        return values.reshape(-1, LANES)

    mobile, dispersion_x, dispersion_y = flat(mobile), flat(dispersion_x), flat(dispersion_y)
    capacity, immobile = flat(capacity), flat(immobile)
    square = VMEM((rows, LANES), jnp.float32)
    x_nodes = LANES // SUBLANES - 1 + len(x_rolls(halves))
    y_nodes = halves * (rows // SUBLANES // halves - 1 + len(y_rolls()))
    message, block = kernel_call(
        functools.partial(x_forward_kernel, halves),
        tuple(
            pltpu.with_memory_space_constraint(value, pltpu.HBM)
            for value in (
                mobile, dispersion_x, dispersion_y, capacity, immobile, exchange_rates[None], rate_shares[None],
            )
        ),
        [f32(SUBLANES, rows), held_f32(2 * rows + 3 * x_nodes * SUBLANES, LANES)],
        [square] * 3
        + [VMEM((zones * rows, LANES), jnp.float32)]
        + [VMEM((1, zones), jnp.float32)] * 2
        + [pltpu.SemaphoreType.DMA((7,))]
        + [square] * 3,
        pltpu.HBM,
    )
    def prepare(part):
        return kernel_call(
            functools.partial(prepare_kernel, halves),
            (part,),
            [
                held_f32(SUBLANES, LANES),
                held_f32(3 * LANES, rows),
                held_f32(2 * rows, LANES),
                held_f32(3 * y_nodes * SUBLANES, LANES),
                held_f32(2 * rows, LANES),
            ],
            [],
        )

    pieces, order = x_exchange(message)
    y_rows, lines_x, sums, y_state, spread = prepare(block)
    other_rows, other_lines, other_sums, _, _ = prepare(trade(block, 1, 0))
    kept, sent, values = kernel_call(
        functools.partial(x_back_kernel, halves, "xg", order, len(pieces)),
        (*pieces, lines_x, other_lines, sums, other_sums, y_rows, other_rows),
        [
            held_f32(2 * halves, QUANTITIES * LANES),
            f32(2 * halves, QUANTITIES * LANES),
            held_f32(rows, LANES),
        ],
        [],
    )
    (given,) = kernel_call(
        functools.partial(y_given_kernel, halves), (block, values, y_state), [held_f32(rows, LANES)], []
    )
    pieces, rounds = y_exchange(kept, sent)
    (updated,) = kernel_call(
        functools.partial(y_back_kernel, halves, "yd", rounds),
        (*pieces, given, spread),
        [f32(rows, LANES)],
        [],
    )
    return updated.reshape(shape)


def solution(mesh):
    field = P("yd", None, "xg")
    return jax.shard_map(
        local,
        mesh=mesh,
        in_specs=(field, field, field, field, P(None, "yd", None, "xg"), P(), P()),
        out_specs=field,
        check_vma=False,
    )
```

```python
import functools

import jax
import jax.numpy as jnp
from jax import lax
from jax.experimental import pallas as pl
from jax.experimental.pallas import tpu as pltpu
from jax.sharding import PartitionSpec as P

LANES = 128
SUBLANES = 8
QUANTITIES = 5
VMEM = pltpu.VMEM


def inverse(value):
    return 1.0 / value


def plus(first, second):
    if first is None:
        return second
    return first + second


def join_coefs(left, right):
    coupling_1, head_1, tail_1 = left
    coupling_2, head_2, tail_2 = right
    middle = plus(head_2, tail_1)
    inv = inverse(coupling_1 + coupling_2 + middle)
    weight_1 = coupling_1 * inv
    weight_2 = coupling_2 * inv
    joined = (coupling_1 * weight_2, plus(head_1, weight_1 * middle), tail_2 + weight_2 * middle)
    return joined, (weight_1, weight_2, inv)


def join_sides(left, right, node):
    head_1, tail_1 = left
    head_2, tail_2 = right
    weight_1, weight_2, inv = node
    side = plus(head_2, tail_1)
    joined = (plus(head_1, weight_1 * side), tail_2 + weight_2 * side)
    return joined, side * inv


def middle_value(node, given, before, after):
    return given + node[0] * before + node[1] * after


def ahead(value, step, axis):
    return pltpu.roll(value, value.shape[axis] - step, axis)


def behind(value, step, axis):
    return pltpu.roll(value, step, axis)


def doubling(count):
    steps = []
    step = 1
    while step < count:
        steps.append(step)
        step *= 2
    return steps


def tree_coefs(leaves, rolls):
    nodes = []
    level = leaves
    while len(level) > 1:
        following = []
        for index in range(0, len(level), 2):
            joined, node = join_coefs(level[index], level[index + 1])
            following.append(joined)
            nodes.append(node)
        level = following
    piece = level[0]
    for step, axis in rolls:
        piece, node = join_coefs(piece, tuple(ahead(part, step, axis) for part in piece))
        nodes.append(node)
    return piece, nodes


def tree_sides(leaves, rolls, nodes):
    givens = []
    level = leaves
    while len(level) > 1:
        following = []
        for index in range(0, len(level), 2):
            joined, given = join_sides(level[index], level[index + 1], nodes[len(givens)])
            following.append(joined)
            givens.append(given)
        level = following
    piece = level[0]
    for step, axis in rolls:
        other = tuple(ahead(part, step, axis) for part in piece)
        piece, given = join_sides(piece, other, nodes[len(givens)])
        givens.append(given)
    return piece, givens


def tree_values(before, after, rolls, count, nodes, givens):
    place = len(nodes)
    for step, axis in reversed(rolls):
        place -= 1
        middle = middle_value(nodes[place], givens[place], before, after)
        upper = (lax.broadcasted_iota(jnp.int32, middle.shape, axis) & step) != 0
        before = jnp.where(upper, behind(middle, step, axis), before)
        after = jnp.where(upper, behind(after, step, axis), middle)
    bounds = [before, after]
    while len(bounds) - 1 < count:
        width = len(bounds) - 1
        place -= width
        following = [bounds[0]]
        for index in range(width):
            following.append(
                middle_value(
                    nodes[place + index], givens[place + index], bounds[index], bounds[index + 1]
                )
            )
            following.append(bounds[index + 1])
        bounds = following
    return bounds[1:]


def choose(condition, first, second):
    if isinstance(condition, bool):
        return first if condition else second
    return jnp.where(condition, first, second)


def ring_bounds(slots, index):
    level = slots
    rounds = []
    bit = 0
    while len(level) > 1:
        upper = ((index >> bit) & 1) == 1
        following, nodes = [], []
        for place in range(0, len(level), 2):
            own, other = level[place], level[place + 1]
            left = [jnp.where(upper, b, a) for a, b in zip(own, other)]
            right = [jnp.where(upper, a, b) for a, b in zip(own, other)]
            coefs, node = join_coefs(left[:3], right[:3])
            sides, given = join_sides(left[3:], right[3:], node)
            nodes.append((node, given))
            following.append(coefs + sides)
        rounds.append((nodes, upper))
        level = following
        bit += 1
    _, head, tail, side_head, side_tail = level[0]
    last = (side_head + side_tail) * inverse(head + tail)
    bounds = [(last, last)]
    for nodes, upper in reversed(rounds):
        following = []
        for (node, given), (before, after) in zip(nodes, bounds):
            middle = middle_value(node, given, before, after)
            following.append((jnp.where(upper, middle, before), jnp.where(upper, after, middle)))
            following.append((jnp.where(upper, before, middle), jnp.where(upper, middle, after)))
        bounds = following
    return bounds


def capacity_weights(rates, shares):
    weights = shares * rates / (1.0 + rates)
    return [weights[:, zone : zone + 1] for zone in range(weights.shape[1])]


def strided(ref, start, size, stride):
    return ref[pl.ds(start, size, stride=stride), :]


def x_rolls(halves):
    return [(step, 0) for step in doubling(SUBLANES)] + [(step, 1) for step in doubling(halves)]


def y_rolls():
    return [(step, 0) for step in doubling(SUBLANES)]


def x_forward_kernel(
    halves, mobile_hbm, faces_hbm, across_hbm, capacity_hbm, immobile_hbm, rates_hbm, shares_hbm,
    message_ref, block_ref,
    mobile_ref, faces_ref, capacity_ref, immobile_ref, rates_ref, shares_ref, arrived,
    faces_t, storage_t, source_t,
):
    rows = mobile_ref.shape[0]
    pairs = (
        (rates_hbm, rates_ref), (shares_hbm, shares_ref), (capacity_hbm, capacity_ref), (faces_hbm, faces_ref),
        (immobile_hbm, immobile_ref), (mobile_hbm, mobile_ref), (across_hbm, block_ref.at[rows : 2 * rows, :]),
    )
    copies = [pltpu.make_async_copy(pair[0], pair[1], arrived.at[place]) for place, pair in enumerate(pairs)]
    for copy in copies:
        copy.start()
    stride = LANES // SUBLANES
    for copy in copies[:3]:
        copy.wait()
    weights = capacity_weights(rates_ref[...], shares_ref[...])
    capacity = capacity_ref[...]
    storage = 1.0 + capacity * sum(weights[1:], weights[0])
    block_ref[0:rows, :] = storage
    storage_t[...] = storage.T
    copies[3].wait()
    faces_t[...] = faces_ref[...].T
    copies[4].wait()
    total = None
    for zone, weight in enumerate(weights):
        total = plus(total, weight * immobile_ref[zone * rows : (zone + 1) * rows, :])
    copies[5].wait()
    source_t[...] = (mobile_ref[...] + capacity * total).T
    coefs, sides = [], []
    for index in range(stride):
        coefs.append((strided(faces_t, index, SUBLANES, stride), None, strided(storage_t, index, SUBLANES, stride)))
        sides.append((None, strided(source_t, index, SUBLANES, stride)))
    rolls = x_rolls(halves)
    piece, nodes = tree_coefs(coefs, rolls)
    side, givens = tree_sides(sides, rolls, nodes)
    start = 2 * rows
    for node, given in zip(nodes, givens):
        for part in (node[0], node[1], given):
            block_ref[start : start + SUBLANES, :] = part
            start += SUBLANES
    for row, value in enumerate(piece + side):
        message_ref[row : row + 1, :] = value[0:1, :]
    copies[6].wait()


def ends_responses(shape):
    one, nothing = jnp.ones(shape, jnp.float32), jnp.zeros(shape, jnp.float32)
    return ((one, nothing), (nothing, one))


def prepare_kernel(halves, block_ref, rows_ref, lines_ref, sums_ref, *own_refs):
    rows = rows_ref.shape[1]
    stride = LANES // SUBLANES
    rolls = x_rolls(halves)
    total = stride - 1 + len(rolls)
    nodes = state_parts(block_ref.at[2 * rows :, :], 0, total, 3)
    nothing = jnp.zeros((SUBLANES, rows), jnp.float32)
    cases = [((nothing, nothing), [node[2] for node in nodes])]
    cases += [(ends, [0.0] * total) for ends in ends_responses((SUBLANES, rows))]
    for case, (ends, givens) in enumerate(cases):
        for index, value in enumerate(tree_values(*ends, rolls, stride, nodes, givens)):
            lines_ref[pl.ds(case * LANES + index, SUBLANES, stride=stride), :] = value
    stride = rows // SUBLANES
    start = 0
    for half in range(halves):
        storage = [strided(block_ref, index, SUBLANES, stride) for index in range(half, stride, halves)]
        faces = [strided(block_ref, rows + index, SUBLANES, stride) for index in range(half, stride, halves)]
        piece, nodes = tree_coefs([(face, None, held) for face, held in zip(faces, storage)], y_rolls())
        for part in [part for node in nodes for part in node] if own_refs else []:
            own_refs[0][start : start + SUBLANES, :] = part
            start += SUBLANES
        for number, value in enumerate(piece):
            row = number * halves + half
            rows_ref[row : row + 1, :] = value[0:1, :]
        for case, ends in enumerate(ends_responses((SUBLANES, LANES))):
            values = tree_values(*ends, y_rolls(), len(storage), nodes, [0.0] * len(nodes))
            for index, (value, held) in enumerate(zip(values, storage)):
                place = pl.ds(case * rows + index * halves + half, SUBLANES, stride=stride)
                sums_ref[place, :] = value * held
                if own_refs:
                    own_refs[1][place, :] = value


def state_parts(ref, first, total, parts, pitch=3):
    return [
        tuple(
            ref[(pitch * place + part) * SUBLANES : (pitch * place + part + 1) * SUBLANES, :]
            for part in range(parts)
        )
        for place in range(first, first + total)
    ]


def message_slots(refs, height, pitch, quantity_rows, skips):
    blocks = [(ref, start) for ref in refs for start in range(0, ref.shape[0], height)]
    slots = []
    for (ref, start), skip in zip(blocks, skips):
        rows = [start + quantity * pitch + skip for quantity in range(QUANTITIES)]
        slots.append(tuple(ref[row : row + quantity_rows, :] for row in rows))
    return slots


def quantity(number):
    return slice(number * LANES, (number + 1) * LANES)


def put_traded(ref, row, rows, number, value):
    ref[(row + rows // 2) % rows : (row + rows // 2) % rows + value.shape[0], quantity(number)] = value


def along_line(bound, halves, rows):
    value = jnp.broadcast_to(bound, (SUBLANES, rows))
    lane = lax.broadcasted_iota(jnp.int32, value.shape, 1)
    for step in doubling(halves):
        value = jnp.where((lane & step) != 0, behind(value, step, 1), value)
    return value[0:1, :]


def x_back_kernel(halves, axis, order, pieces, *refs):
    slots = message_slots(refs[:pieces], SUBLANES, 1, 1, [0] * len(order))
    slots = [slots[order.index(place)] for place in range(len(order))]
    lines_refs, sums_refs, rows_refs = (refs[pieces + 2 * pair : pieces + 2 * pair + 2] for pair in range(3))
    kept_ref, sent_ref, values_ref = refs[pieces + 6 :]
    bounds = ring_bounds(slots, lax.axis_index(axis))
    rows = values_ref.shape[0]

    def put(row, number, value):
        kept_ref[row : row + 1, quantity(number)] = value
        put_traded(sent_ref, row, 2 * halves, number, value)

    for block in range(2):
        for half in range(halves):
            for number in range(3):
                row = number * halves + half
                put(block * halves + half, number, rows_refs[block][row : row + 1, :])
    for block in range(2):
        lines_ref, sums_ref = lines_refs[block], sums_refs[block]
        before, after = (along_line(bound, halves, rows) for bound in bounds[block])
        values = lines_ref[0:LANES, :] + lines_ref[LANES : 2 * LANES, :] * before + lines_ref[2 * LANES :, :] * after
        values = values.T
        if block == 0:
            values_ref[...] = values
        for end in range(2):
            parts = (values * sums_ref[end * rows : (end + 1) * rows, :]).reshape(-1, SUBLANES, LANES)
            side = jnp.sum(parts, axis=0)
            for step in doubling(SUBLANES // halves):
                side = side + behind(side, step * halves, 0)
            for half in range(halves):
                put(block * halves + half, 3 + end, side[half : half + 1, :])


def y_given_kernel(halves, block_ref, values_ref, state_ref, given_ref):
    rows = values_ref.shape[0]
    stride = rows // SUBLANES
    total = stride // halves - 1 + len(y_rolls())
    nothing = jnp.zeros((SUBLANES, LANES), jnp.float32)
    for half in range(halves):
        places = [pl.ds(index, SUBLANES, stride=stride) for index in range(half, stride, halves)]
        sides = [(None, block_ref[place, :] * values_ref[place, :]) for place in places]
        nodes = state_parts(state_ref, half * total, total, 3)
        _, givens = tree_sides(sides, y_rolls(), nodes)
        for place, value in zip(places, tree_values(nothing, nothing, y_rolls(), len(places), nodes, givens)):
            given_ref[place, :] = value


def read_message(ref):
    return [ref[:, quantity(number)] for number in range(QUANTITIES)]


def join_by_bit(own, other, upper):
    left = [choose(upper, b, a) for a, b in zip(own, other)]
    right = [choose(upper, a, b) for a, b in zip(own, other)]
    coefs, node = join_coefs(left[:3], right[:3])
    sides, given = join_sides(left[3:], right[3:], node)
    return coefs + sides, (node[0], node[1], given)


def own_bit(axis, bit):
    return ((lax.axis_index(axis) >> bit) & 1) == 1


def y_join_kernel(axis, bit, own_ref, other_ref, kept_ref, sent_ref, path_ref):
    joined, path = join_by_bit(read_message(own_ref), read_message(other_ref), own_bit(axis, bit))
    rows = own_ref.shape[0]
    for number, value in enumerate(joined):
        kept_ref[:, quantity(number)] = value
        for row in (0, rows // 2):
            put_traded(sent_ref, row, rows, number, value[row : row + rows // 2, :])
    for number, value in enumerate(path):
        path_ref[:, quantity(number)] = value


def y_back_kernel(halves, axis, rounds, own_ref, other_ref, *refs):
    path_refs = refs[: rounds - 1]
    given_ref, spread_ref, out_ref = refs[rounds - 1 :]
    rows = out_ref.shape[0]
    joined, path = join_by_bit(read_message(own_ref), read_message(other_ref), own_bit(axis, rounds - 1))
    _, head, tail, side_head, side_tail = joined
    before = after = (side_head + side_tail) * inverse(head + tail)
    paths = [[ref[:, quantity(number)] for number in range(3)] for ref in path_refs] + [path]
    for bit in reversed(range(rounds)):
        node = paths[bit]
        middle = middle_value(node, node[2], before, after)
        upper = own_bit(axis, bit)
        before = jnp.where(upper, middle, before)
        after = jnp.where(upper, after, middle)
    sublane = lax.broadcasted_iota(jnp.int32, (SUBLANES, LANES), 0) % halves
    ends = []
    for end in (before, after):
        value = jnp.broadcast_to(end[0:1, :], (SUBLANES, LANES))
        for half in range(1, halves):
            value = jnp.where(sublane == half, jnp.broadcast_to(end[half : half + 1, :], value.shape), value)
        ends.append(value)
    for start in range(0, rows, SUBLANES):
        part = slice(start, start + SUBLANES)
        late = slice(rows + start, rows + start + SUBLANES)
        out_ref[part, :] = given_ref[part, :] + spread_ref[part, :] * ends[0] + spread_ref[late, :] * ends[1]


def trade(value, x_step, y_step):
    width = lax.axis_size("yd")
    pairs = []
    for index in range(lax.axis_size("xg")):
        for line in range(width):
            pairs.append((index * width + line, (index ^ x_step) * width + (line ^ y_step)))
    return lax.ppermute(value, ("xg", "yd"), pairs)


def pack_kernel(first_ref, second_ref, out_ref):
    height = first_ref.shape[0]
    out_ref[0:height, :] = first_ref[...]
    out_ref[height:, :] = second_ref[...]


def pack(first, second):
    (packed,) = kernel_call(
        pack_kernel, (first, second), [f32(first.shape[0] + second.shape[0], first.shape[1])], [], cost=10000000000
    )
    return packed


def x_exchange(message):
    held = message
    pieces = [message]
    order = [0]
    for step in doubling(lax.axis_size("xg") // 2):
        received = trade(held, 2 * step + 1, 0)
        pieces.append(received)
        order += [place ^ (2 * step + 1) for place in order]
        held = pack(held, received)
    pieces.append(trade(held, 1, 0))
    order += [place ^ 1 for place in order]
    return pieces, order


def y_exchange(kept, sent):
    rows = kept.shape[0]
    paths = []
    steps = doubling(lax.axis_size("yd"))
    for bit, step in enumerate(steps):
        received = trade(sent, 1, step)
        if bit < len(steps) - 1:
            kept, sent, path = kernel_call(
                functools.partial(y_join_kernel, "yd", bit),
                (kept, received),
                [held_f32(*kept.shape), f32(*kept.shape), held_f32(rows, 3 * LANES)],
                [],
            )
            paths.append(path)
    return [kept, received] + paths, len(steps)


def f32(*shape):
    return jax.ShapeDtypeStruct(shape, jnp.float32)


def held_f32(*shape):
    return VMEM(shape, jnp.float32)


def kernel_call(body, operands, outputs, scratch, space=VMEM, cost=500000):
    return pl.pallas_call(
        body,
        out_shape=outputs,
        in_specs=[pl.BlockSpec(memory_space=space)] * len(operands),
        out_specs=[pl.BlockSpec(memory_space=VMEM)] * len(outputs),
        scratch_shapes=scratch,
        cost_estimate=pl.CostEstimate(flops=cost, bytes_accessed=cost, transcendentals=0),
        compiler_params=pltpu.CompilerParams(vmem_limit_bytes=16 * 1024 * 1024),
    )(*operands)


def local(mobile, dispersion_x, dispersion_y, capacity, immobile, exchange_rates, rate_shares):
    shape = mobile.shape
    lines, width = shape[0] * shape[1], shape[2]
    zones = immobile.shape[0]
    halves = width // LANES
    rows = lines * halves
    assert rows == LANES

    def flat(values):
        return values.reshape(-1, LANES)

    mobile, dispersion_x, dispersion_y = flat(mobile), flat(dispersion_x), flat(dispersion_y)
    capacity, immobile = flat(capacity), flat(immobile)
    square = VMEM((rows, LANES), jnp.float32)
    x_nodes = LANES // SUBLANES - 1 + len(x_rolls(halves))
    y_nodes = halves * (rows // SUBLANES // halves - 1 + len(y_rolls()))
    message, block = kernel_call(
        functools.partial(x_forward_kernel, halves),
        tuple(
            pltpu.with_memory_space_constraint(value, pltpu.HBM)
            for value in (
                mobile, dispersion_x, dispersion_y, capacity, immobile, exchange_rates[None], rate_shares[None],
            )
        ),
        [f32(SUBLANES, rows), held_f32(2 * rows + 3 * x_nodes * SUBLANES, LANES)],
        [square] * 3
        + [VMEM((zones * rows, LANES), jnp.float32)]
        + [VMEM((1, zones), jnp.float32)] * 2
        + [pltpu.SemaphoreType.DMA((7,))]
        + [square] * 3,
        pltpu.HBM,
    )
    def prepare(part, own):
        outputs = [held_f32(SUBLANES, LANES), held_f32(3 * LANES, rows), held_f32(2 * rows, LANES)]
        if own:
            outputs += [held_f32(3 * y_nodes * SUBLANES, LANES), held_f32(2 * rows, LANES)]
        return kernel_call(functools.partial(prepare_kernel, halves), (part,), outputs, [])

    pieces, order = x_exchange(message)
    y_rows, lines_x, sums, y_state, spread = prepare(block, True)
    other_rows, other_lines, other_sums = prepare(trade(block, 1, 0), False)
    kept, sent, values = kernel_call(
        functools.partial(x_back_kernel, halves, "xg", order, len(pieces)),
        (*pieces, lines_x, other_lines, sums, other_sums, y_rows, other_rows),
        [
            held_f32(2 * halves, QUANTITIES * LANES),
            f32(2 * halves, QUANTITIES * LANES),
            held_f32(rows, LANES),
        ],
        [],
    )
    (given,) = kernel_call(
        functools.partial(y_given_kernel, halves), (block, values, y_state), [held_f32(rows, LANES)], []
    )
    pieces, rounds = y_exchange(kept, sent)
    (updated,) = kernel_call(
        functools.partial(y_back_kernel, halves, "yd", rounds),
        (*pieces, given, spread),
        [f32(rows, LANES)],
        [],
    )
    return updated.reshape(shape)


def solution(mesh):
    field = P("yd", None, "xg")
    return jax.shard_map(
        local,
        mesh=mesh,
        in_specs=(field, field, field, field, P(None, "yd", None, "xg"), P(), P()),
        out_specs=field,
        check_vma=False,
    )
```

```python
import functools

import jax
import jax.numpy as jnp
from jax import lax
from jax.experimental import pallas as pl
from jax.experimental.pallas import tpu as pltpu
from jax.sharding import PartitionSpec as P

LANES = 128
SUBLANES = 8
QUANTITIES = 5
VMEM = pltpu.VMEM


def inverse(value):
    return 1.0 / value


def plus(first, second):
    if first is None:
        return second
    return first + second


def join_coefs(left, right):
    coupling_1, head_1, tail_1 = left
    coupling_2, head_2, tail_2 = right
    middle = plus(head_2, tail_1)
    inv = inverse(coupling_1 + coupling_2 + middle)
    weight_1 = coupling_1 * inv
    weight_2 = coupling_2 * inv
    joined = (coupling_1 * weight_2, plus(head_1, weight_1 * middle), tail_2 + weight_2 * middle)
    return joined, (weight_1, weight_2, inv)


def join_sides(left, right, node):
    head_1, tail_1 = left
    head_2, tail_2 = right
    weight_1, weight_2, inv = node
    side = plus(head_2, tail_1)
    joined = (plus(head_1, weight_1 * side), tail_2 + weight_2 * side)
    return joined, side * inv


def middle_value(node, given, before, after):
    return given + node[0] * before + node[1] * after


def ahead(value, step, axis):
    return pltpu.roll(value, value.shape[axis] - step, axis)


def behind(value, step, axis):
    return pltpu.roll(value, step, axis)


def doubling(count):
    steps = []
    step = 1
    while step < count:
        steps.append(step)
        step *= 2
    return steps


def tree_coefs(leaves, rolls):
    nodes = []
    level = leaves
    while len(level) > 1:
        following = []
        for index in range(0, len(level), 2):
            joined, node = join_coefs(level[index], level[index + 1])
            following.append(joined)
            nodes.append(node)
        level = following
    piece = level[0]
    for step, axis in rolls:
        piece, node = join_coefs(piece, tuple(ahead(part, step, axis) for part in piece))
        nodes.append(node)
    return piece, nodes


def tree_sides(leaves, rolls, nodes):
    givens = []
    level = leaves
    while len(level) > 1:
        following = []
        for index in range(0, len(level), 2):
            joined, given = join_sides(level[index], level[index + 1], nodes[len(givens)])
            following.append(joined)
            givens.append(given)
        level = following
    piece = level[0]
    for step, axis in rolls:
        other = tuple(ahead(part, step, axis) for part in piece)
        piece, given = join_sides(piece, other, nodes[len(givens)])
        givens.append(given)
    return piece, givens


def tree_values(before, after, rolls, count, nodes, givens):
    place = len(nodes)
    for step, axis in reversed(rolls):
        place -= 1
        middle = middle_value(nodes[place], givens[place], before, after)
        upper = (lax.broadcasted_iota(jnp.int32, middle.shape, axis) & step) != 0
        before = jnp.where(upper, behind(middle, step, axis), before)
        after = jnp.where(upper, behind(after, step, axis), middle)
    bounds = [before, after]
    while len(bounds) - 1 < count:
        width = len(bounds) - 1
        place -= width
        following = [bounds[0]]
        for index in range(width):
            following.append(
                middle_value(
                    nodes[place + index], givens[place + index], bounds[index], bounds[index + 1]
                )
            )
            following.append(bounds[index + 1])
        bounds = following
    return bounds[1:]


def choose(condition, first, second):
    if isinstance(condition, bool):
        return first if condition else second
    return jnp.where(condition, first, second)


def ring_bounds(slots, index):
    level = slots
    rounds = []
    bit = 0
    while len(level) > 1:
        upper = ((index >> bit) & 1) == 1
        following, nodes = [], []
        for place in range(0, len(level), 2):
            own, other = level[place], level[place + 1]
            left = [jnp.where(upper, b, a) for a, b in zip(own, other)]
            right = [jnp.where(upper, a, b) for a, b in zip(own, other)]
            coefs, node = join_coefs(left[:3], right[:3])
            sides, given = join_sides(left[3:], right[3:], node)
            nodes.append((node, given))
            following.append(coefs + sides)
        rounds.append((nodes, upper))
        level = following
        bit += 1
    _, head, tail, side_head, side_tail = level[0]
    last = (side_head + side_tail) * inverse(head + tail)
    bounds = [(last, last)]
    for nodes, upper in reversed(rounds):
        following = []
        for (node, given), (before, after) in zip(nodes, bounds):
            middle = middle_value(node, given, before, after)
            following.append((jnp.where(upper, middle, before), jnp.where(upper, after, middle)))
            following.append((jnp.where(upper, before, middle), jnp.where(upper, middle, after)))
        bounds = following
    return bounds


def capacity_weights(rates, shares):
    weights = shares * rates / (1.0 + rates)
    return [weights[:, zone : zone + 1] for zone in range(weights.shape[1])]


def strided(ref, start, size, stride):
    return ref[pl.ds(start, size, stride=stride), :]


def x_rolls(halves):
    return [(step, 0) for step in doubling(SUBLANES)] + [(step, 1) for step in doubling(halves)]


def y_rolls():
    return [(step, 0) for step in doubling(SUBLANES)]


def x_forward_kernel(
    halves, mobile_hbm, faces_hbm, across_hbm, capacity_hbm, immobile_hbm, rates_hbm, shares_hbm,
    message_ref, block_ref,
    mobile_ref, faces_ref, capacity_ref, immobile_ref, rates_ref, shares_ref, arrived,
    faces_t, storage_t, source_t,
):
    rows = mobile_ref.shape[0]
    pairs = (
        (rates_hbm, rates_ref), (shares_hbm, shares_ref), (capacity_hbm, capacity_ref), (faces_hbm, faces_ref),
        (immobile_hbm, immobile_ref), (mobile_hbm, mobile_ref), (across_hbm, block_ref.at[rows : 2 * rows, :]),
    )
    copies = [pltpu.make_async_copy(pair[0], pair[1], arrived.at[place]) for place, pair in enumerate(pairs)]
    for copy in copies:
        copy.start()
    stride = LANES // SUBLANES
    for copy in copies[:6]:
        copy.wait()
    faces_t[...] = faces_ref[...].T
    weights = capacity_weights(rates_ref[...], shares_ref[...])
    capacity = capacity_ref[...]
    storage = 1.0 + capacity * sum(weights[1:], weights[0])
    storage_t[...] = storage.T
    total = None
    for zone, weight in enumerate(weights):
        total = plus(total, weight * immobile_ref[zone * rows : (zone + 1) * rows, :])
    source_t[...] = (mobile_ref[...] + capacity * total).T
    block_ref[0:rows, :] = storage
    coefs, sides = [], []
    for index in range(stride):
        coefs.append((strided(faces_t, index, SUBLANES, stride), None, strided(storage_t, index, SUBLANES, stride)))
        sides.append((None, strided(source_t, index, SUBLANES, stride)))
    rolls = x_rolls(halves)
    piece, nodes = tree_coefs(coefs, rolls)
    side, givens = tree_sides(sides, rolls, nodes)
    start = 2 * rows
    for node, given in zip(nodes, givens):
        for part in (node[0], node[1], given):
            block_ref[start : start + SUBLANES, :] = part
            start += SUBLANES
    for row, value in enumerate(piece + side):
        message_ref[row : row + 1, :] = value[0:1, :]
    copies[6].wait()


def ends_responses(shape):
    one, nothing = jnp.ones(shape, jnp.float32), jnp.zeros(shape, jnp.float32)
    return ((one, nothing), (nothing, one))


def prepare_kernel(halves, block_ref, rows_ref, lines_ref, sums_ref, *own_refs):
    rows = rows_ref.shape[1]
    stride = LANES // SUBLANES
    rolls = x_rolls(halves)
    total = stride - 1 + len(rolls)
    nodes = state_parts(block_ref.at[2 * rows :, :], 0, total, 3)
    nothing = jnp.zeros((SUBLANES, rows), jnp.float32)
    cases = [((nothing, nothing), [node[2] for node in nodes])]
    cases += [(ends, [0.0] * total) for ends in ends_responses((SUBLANES, rows))]
    for case, (ends, givens) in enumerate(cases):
        for index, value in enumerate(tree_values(*ends, rolls, stride, nodes, givens)):
            lines_ref[pl.ds(case * LANES + index, SUBLANES, stride=stride), :] = value
    stride = rows // SUBLANES
    start = 0
    for half in range(halves):
        storage = [strided(block_ref, index, SUBLANES, stride) for index in range(half, stride, halves)]
        faces = [strided(block_ref, rows + index, SUBLANES, stride) for index in range(half, stride, halves)]
        piece, nodes = tree_coefs([(face, None, held) for face, held in zip(faces, storage)], y_rolls())
        for part in [part for node in nodes for part in node] if own_refs else []:
            own_refs[0][start : start + SUBLANES, :] = part
            start += SUBLANES
        for number, value in enumerate(piece):
            row = number * halves + half
            rows_ref[row : row + 1, :] = value[0:1, :]
        for case, ends in enumerate(ends_responses((SUBLANES, LANES))):
            values = tree_values(*ends, y_rolls(), len(storage), nodes, [0.0] * len(nodes))
            for index, (value, held) in enumerate(zip(values, storage)):
                place = pl.ds(case * rows + index * halves + half, SUBLANES, stride=stride)
                sums_ref[place, :] = value * held
                if own_refs:
                    own_refs[1][place, :] = value


def state_parts(ref, first, total, parts, pitch=3):
    return [
        tuple(
            ref[(pitch * place + part) * SUBLANES : (pitch * place + part + 1) * SUBLANES, :]
            for part in range(parts)
        )
        for place in range(first, first + total)
    ]


def message_slots(refs, height, pitch, quantity_rows, skips):
    blocks = [(ref, start) for ref in refs for start in range(0, ref.shape[0], height)]
    slots = []
    for (ref, start), skip in zip(blocks, skips):
        rows = [start + quantity * pitch + skip for quantity in range(QUANTITIES)]
        slots.append(tuple(ref[row : row + quantity_rows, :] for row in rows))
    return slots


def quantity(number):
    return slice(number * LANES, (number + 1) * LANES)


def put_traded(ref, row, rows, number, value):
    ref[(row + rows // 2) % rows : (row + rows // 2) % rows + value.shape[0], quantity(number)] = value


def along_line(bound, halves, rows):
    value = jnp.broadcast_to(bound, (SUBLANES, rows))
    lane = lax.broadcasted_iota(jnp.int32, value.shape, 1)
    for step in doubling(halves):
        value = jnp.where((lane & step) != 0, behind(value, step, 1), value)
    return value[0:1, :]


def x_back_kernel(halves, axis, order, pieces, *refs):
    slots = message_slots(refs[:pieces], SUBLANES, 1, 1, [0] * len(order))
    slots = [slots[order.index(place)] for place in range(len(order))]
    lines_refs, sums_refs, rows_refs = (refs[pieces + 2 * pair : pieces + 2 * pair + 2] for pair in range(3))
    kept_ref, sent_ref, values_ref = refs[pieces + 6 :]
    bounds = ring_bounds(slots, lax.axis_index(axis))
    rows = values_ref.shape[0]

    def put(row, number, value):
        kept_ref[row : row + 1, quantity(number)] = value
        put_traded(sent_ref, row, 2 * halves, number, value)

    for block in range(2):
        for half in range(halves):
            for number in range(3):
                row = number * halves + half
                put(block * halves + half, number, rows_refs[block][row : row + 1, :])
    for block in range(2):
        lines_ref, sums_ref = lines_refs[block], sums_refs[block]
        before, after = (along_line(bound, halves, rows) for bound in bounds[block])
        values = lines_ref[0:LANES, :] + lines_ref[LANES : 2 * LANES, :] * before + lines_ref[2 * LANES :, :] * after
        values = values.T
        if block == 0:
            values_ref[...] = values
        for end in range(2):
            parts = (values * sums_ref[end * rows : (end + 1) * rows, :]).reshape(-1, SUBLANES, LANES)
            side = jnp.sum(parts, axis=0)
            for step in doubling(SUBLANES // halves):
                side = side + behind(side, step * halves, 0)
            for half in range(halves):
                put(block * halves + half, 3 + end, side[half : half + 1, :])


def y_given_kernel(halves, block_ref, values_ref, state_ref, given_ref):
    rows = values_ref.shape[0]
    stride = rows // SUBLANES
    total = stride // halves - 1 + len(y_rolls())
    nothing = jnp.zeros((SUBLANES, LANES), jnp.float32)
    for half in range(halves):
        places = [pl.ds(index, SUBLANES, stride=stride) for index in range(half, stride, halves)]
        sides = [(None, block_ref[place, :] * values_ref[place, :]) for place in places]
        nodes = state_parts(state_ref, half * total, total, 3)
        _, givens = tree_sides(sides, y_rolls(), nodes)
        for place, value in zip(places, tree_values(nothing, nothing, y_rolls(), len(places), nodes, givens)):
            given_ref[place, :] = value


def read_message(ref):
    return [ref[:, quantity(number)] for number in range(QUANTITIES)]


def join_by_bit(own, other, upper):
    left = [choose(upper, b, a) for a, b in zip(own, other)]
    right = [choose(upper, a, b) for a, b in zip(own, other)]
    coefs, node = join_coefs(left[:3], right[:3])
    sides, given = join_sides(left[3:], right[3:], node)
    return coefs + sides, (node[0], node[1], given)


def own_bit(axis, bit):
    return ((lax.axis_index(axis) >> bit) & 1) == 1


def y_join_kernel(axis, bit, own_ref, other_ref, kept_ref, sent_ref, path_ref):
    joined, path = join_by_bit(read_message(own_ref), read_message(other_ref), own_bit(axis, bit))
    rows = own_ref.shape[0]
    for number, value in enumerate(joined):
        kept_ref[:, quantity(number)] = value
        for row in (0, rows // 2):
            put_traded(sent_ref, row, rows, number, value[row : row + rows // 2, :])
    for number, value in enumerate(path):
        path_ref[:, quantity(number)] = value


def y_back_kernel(halves, axis, rounds, own_ref, other_ref, *refs):
    path_refs = refs[: rounds - 1]
    given_ref, spread_ref, out_ref = refs[rounds - 1 :]
    rows = out_ref.shape[0]
    joined, path = join_by_bit(read_message(own_ref), read_message(other_ref), own_bit(axis, rounds - 1))
    _, head, tail, side_head, side_tail = joined
    before = after = (side_head + side_tail) * inverse(head + tail)
    paths = [[ref[:, quantity(number)] for number in range(3)] for ref in path_refs] + [path]
    for bit in reversed(range(rounds)):
        node = paths[bit]
        middle = middle_value(node, node[2], before, after)
        upper = own_bit(axis, bit)
        before = jnp.where(upper, middle, before)
        after = jnp.where(upper, after, middle)
    sublane = lax.broadcasted_iota(jnp.int32, (SUBLANES, LANES), 0) % halves
    ends = []
    for end in (before, after):
        value = jnp.broadcast_to(end[0:1, :], (SUBLANES, LANES))
        for half in range(1, halves):
            value = jnp.where(sublane == half, jnp.broadcast_to(end[half : half + 1, :], value.shape), value)
        ends.append(value)
    for start in range(0, rows, SUBLANES):
        part = slice(start, start + SUBLANES)
        late = slice(rows + start, rows + start + SUBLANES)
        out_ref[part, :] = given_ref[part, :] + spread_ref[part, :] * ends[0] + spread_ref[late, :] * ends[1]


def trade(value, x_step, y_step):
    width = lax.axis_size("yd")
    pairs = []
    for index in range(lax.axis_size("xg")):
        for line in range(width):
            pairs.append((index * width + line, (index ^ x_step) * width + (line ^ y_step)))
    return lax.ppermute(value, ("xg", "yd"), pairs)


def pack_kernel(first_ref, second_ref, out_ref):
    height = first_ref.shape[0]
    out_ref[0:height, :] = first_ref[...]
    out_ref[height:, :] = second_ref[...]


def pack(first, second):
    (packed,) = kernel_call(
        pack_kernel, (first, second), [f32(first.shape[0] + second.shape[0], first.shape[1])], [], cost=10000000000
    )
    return packed


def x_exchange(message):
    held = message
    pieces = [message]
    order = [0]
    for step in doubling(lax.axis_size("xg") // 2):
        received = trade(held, 2 * step + 1, 0)
        pieces.append(received)
        order += [place ^ (2 * step + 1) for place in order]
        held = pack(held, received)
    pieces.append(trade(held, 1, 0))
    order += [place ^ 1 for place in order]
    return pieces, order


def y_exchange(kept, sent):
    rows = kept.shape[0]
    paths = []
    steps = doubling(lax.axis_size("yd"))
    for bit, step in enumerate(steps):
        received = trade(sent, 1, step)
        if bit < len(steps) - 1:
            kept, sent, path = kernel_call(
                functools.partial(y_join_kernel, "yd", bit),
                (kept, received),
                [held_f32(*kept.shape), f32(*kept.shape), held_f32(rows, 3 * LANES)],
                [],
            )
            paths.append(path)
    return [kept, received] + paths, len(steps)


def f32(*shape):
    return jax.ShapeDtypeStruct(shape, jnp.float32)


def held_f32(*shape):
    return VMEM(shape, jnp.float32)


def kernel_call(body, operands, outputs, scratch, space=VMEM, cost=500000):
    return pl.pallas_call(
        body,
        out_shape=outputs,
        in_specs=[pl.BlockSpec(memory_space=space)] * len(operands),
        out_specs=[pl.BlockSpec(memory_space=VMEM)] * len(outputs),
        scratch_shapes=scratch,
        cost_estimate=pl.CostEstimate(flops=cost, bytes_accessed=cost, transcendentals=0),
        compiler_params=pltpu.CompilerParams(vmem_limit_bytes=16 * 1024 * 1024),
    )(*operands)


def local(mobile, dispersion_x, dispersion_y, capacity, immobile, exchange_rates, rate_shares):
    shape = mobile.shape
    lines, width = shape[0] * shape[1], shape[2]
    zones = immobile.shape[0]
    halves = width // LANES
    rows = lines * halves
    assert rows == LANES

    def flat(values):
        return values.reshape(-1, LANES)

    mobile, dispersion_x, dispersion_y = flat(mobile), flat(dispersion_x), flat(dispersion_y)
    capacity, immobile = flat(capacity), flat(immobile)
    square = VMEM((rows, LANES), jnp.float32)
    x_nodes = LANES // SUBLANES - 1 + len(x_rolls(halves))
    y_nodes = halves * (rows // SUBLANES // halves - 1 + len(y_rolls()))
    message, block = kernel_call(
        functools.partial(x_forward_kernel, halves),
        tuple(
            pltpu.with_memory_space_constraint(value, pltpu.HBM)
            for value in (
                mobile, dispersion_x, dispersion_y, capacity, immobile, exchange_rates[None], rate_shares[None],
            )
        ),
        [f32(SUBLANES, rows), held_f32(2 * rows + 3 * x_nodes * SUBLANES, LANES)],
        [square] * 3
        + [VMEM((zones * rows, LANES), jnp.float32)]
        + [VMEM((1, zones), jnp.float32)] * 2
        + [pltpu.SemaphoreType.DMA((7,))]
        + [square] * 3,
        pltpu.HBM,
    )
    def prepare(part, own):
        outputs = [held_f32(SUBLANES, LANES), held_f32(3 * LANES, rows), held_f32(2 * rows, LANES)]
        if own:
            outputs += [held_f32(3 * y_nodes * SUBLANES, LANES), held_f32(2 * rows, LANES)]
        return kernel_call(functools.partial(prepare_kernel, halves), (part,), outputs, [])

    pieces, order = x_exchange(message)
    y_rows, lines_x, sums, y_state, spread = prepare(block, True)
    other_rows, other_lines, other_sums = prepare(trade(block, 1, 0), False)
    kept, sent, values = kernel_call(
        functools.partial(x_back_kernel, halves, "xg", order, len(pieces)),
        (*pieces, lines_x, other_lines, sums, other_sums, y_rows, other_rows),
        [
            held_f32(2 * halves, QUANTITIES * LANES),
            f32(2 * halves, QUANTITIES * LANES),
            held_f32(rows, LANES),
        ],
        [],
    )
    (given,) = kernel_call(
        functools.partial(y_given_kernel, halves), (block, values, y_state), [held_f32(rows, LANES)], []
    )
    pieces, rounds = y_exchange(kept, sent)
    (updated,) = kernel_call(
        functools.partial(y_back_kernel, halves, "yd", rounds),
        (*pieces, given, spread),
        [f32(rows, LANES)],
        [],
    )
    return updated.reshape(shape)


def solution(mesh):
    field = P("yd", None, "xg")
    return jax.shard_map(
        local,
        mesh=mesh,
        in_specs=(field, field, field, field, P(None, "yd", None, "xg"), P(), P()),
        out_specs=field,
        check_vma=False,
    )
```

```python
import functools

import jax
import jax.numpy as jnp
from jax import lax
from jax.experimental import pallas as pl
from jax.experimental.pallas import tpu as pltpu
from jax.sharding import PartitionSpec as P

LANES = 128
SUBLANES = 8
QUANTITIES = 5
VMEM = pltpu.VMEM


def inverse(value):
    return 1.0 / value


def plus(first, second):
    if first is None:
        return second
    return first + second


def join_coefs(left, right):
    coupling_1, head_1, tail_1 = left
    coupling_2, head_2, tail_2 = right
    middle = plus(head_2, tail_1)
    inv = inverse(coupling_1 + coupling_2 + middle)
    weight_1 = coupling_1 * inv
    weight_2 = coupling_2 * inv
    joined = (coupling_1 * weight_2, plus(head_1, weight_1 * middle), tail_2 + weight_2 * middle)
    return joined, (weight_1, weight_2, inv)


def join_sides(left, right, node):
    head_1, tail_1 = left
    head_2, tail_2 = right
    weight_1, weight_2, inv = node
    side = plus(head_2, tail_1)
    joined = (plus(head_1, weight_1 * side), tail_2 + weight_2 * side)
    return joined, side * inv


def middle_value(node, given, before, after):
    return given + node[0] * before + node[1] * after


def ahead(value, step, axis):
    return pltpu.roll(value, value.shape[axis] - step, axis)


def behind(value, step, axis):
    return pltpu.roll(value, step, axis)


def doubling(count):
    steps = []
    step = 1
    while step < count:
        steps.append(step)
        step *= 2
    return steps


def tree_coefs(leaves, rolls):
    nodes = []
    level = leaves
    while len(level) > 1:
        following = []
        for index in range(0, len(level), 2):
            joined, node = join_coefs(level[index], level[index + 1])
            following.append(joined)
            nodes.append(node)
        level = following
    piece = level[0]
    for step, axis in rolls:
        piece, node = join_coefs(piece, tuple(ahead(part, step, axis) for part in piece))
        nodes.append(node)
    return piece, nodes


def tree_sides(leaves, rolls, nodes):
    givens = []
    level = leaves
    while len(level) > 1:
        following = []
        for index in range(0, len(level), 2):
            joined, given = join_sides(level[index], level[index + 1], nodes[len(givens)])
            following.append(joined)
            givens.append(given)
        level = following
    piece = level[0]
    for step, axis in rolls:
        other = tuple(ahead(part, step, axis) for part in piece)
        piece, given = join_sides(piece, other, nodes[len(givens)])
        givens.append(given)
    return piece, givens


def tree_values(before, after, rolls, count, nodes, givens):
    place = len(nodes)
    for step, axis in reversed(rolls):
        place -= 1
        middle = middle_value(nodes[place], givens[place], before, after)
        upper = (lax.broadcasted_iota(jnp.int32, middle.shape, axis) & step) != 0
        before = jnp.where(upper, behind(middle, step, axis), before)
        after = jnp.where(upper, behind(after, step, axis), middle)
    bounds = [before, after]
    while len(bounds) - 1 < count:
        width = len(bounds) - 1
        place -= width
        following = [bounds[0]]
        for index in range(width):
            following.append(
                middle_value(
                    nodes[place + index], givens[place + index], bounds[index], bounds[index + 1]
                )
            )
            following.append(bounds[index + 1])
        bounds = following
    return bounds[1:]


def choose(condition, first, second):
    if isinstance(condition, bool):
        return first if condition else second
    return jnp.where(condition, first, second)


def ring_bounds(slots, index):
    level = slots
    rounds = []
    bit = 0
    while len(level) > 1:
        upper = ((index >> bit) & 1) == 1
        following, nodes = [], []
        for place in range(0, len(level), 2):
            own, other = level[place], level[place + 1]
            left = [jnp.where(upper, b, a) for a, b in zip(own, other)]
            right = [jnp.where(upper, a, b) for a, b in zip(own, other)]
            coefs, node = join_coefs(left[:3], right[:3])
            sides, given = join_sides(left[3:], right[3:], node)
            nodes.append((node, given))
            following.append(coefs + sides)
        rounds.append((nodes, upper))
        level = following
        bit += 1
    _, head, tail, side_head, side_tail = level[0]
    last = (side_head + side_tail) * inverse(head + tail)
    bounds = [(last, last)]
    for nodes, upper in reversed(rounds):
        following = []
        for (node, given), (before, after) in zip(nodes, bounds):
            middle = middle_value(node, given, before, after)
            following.append((jnp.where(upper, middle, before), jnp.where(upper, after, middle)))
            following.append((jnp.where(upper, before, middle), jnp.where(upper, middle, after)))
        bounds = following
    return bounds


def capacity_weights(rates, shares):
    weights = shares * rates / (1.0 + rates)
    return [weights[:, zone : zone + 1] for zone in range(weights.shape[1])]


def strided(ref, start, size, stride):
    return ref[pl.ds(start, size, stride=stride), :]


def x_rolls(halves):
    return [(step, 0) for step in doubling(SUBLANES)] + [(step, 1) for step in doubling(halves)]


def y_rolls():
    return [(step, 0) for step in doubling(SUBLANES)]


def x_forward_kernel(
    halves, mobile_hbm, faces_hbm, across_hbm, capacity_hbm, immobile_hbm, rates_hbm, shares_hbm,
    message_ref, block_ref,
    mobile_ref, faces_ref, capacity_ref, immobile_ref, rates_ref, shares_ref, arrived,
    faces_t, storage_t, source_t,
):
    rows = mobile_ref.shape[0]
    pairs = (
        (rates_hbm, rates_ref), (shares_hbm, shares_ref), (capacity_hbm, capacity_ref), (faces_hbm, faces_ref),
        (immobile_hbm, immobile_ref), (mobile_hbm, mobile_ref), (across_hbm, block_ref.at[rows : 2 * rows, :]),
    )
    copies = [pltpu.make_async_copy(pair[0], pair[1], arrived.at[place]) for place, pair in enumerate(pairs)]
    for place, copy in enumerate(copies):
        copy.start(priority=int(place in (4, 6)))
    stride = LANES // SUBLANES
    for copy in copies[:3]:
        copy.wait()
    weights = capacity_weights(rates_ref[...], shares_ref[...])
    capacity = capacity_ref[...]
    storage = 1.0 + capacity * sum(weights[1:], weights[0])
    block_ref[0:rows, :] = storage
    storage_t[...] = storage.T
    copies[3].wait()
    faces_t[...] = faces_ref[...].T
    copies[4].wait()
    total = None
    for zone, weight in enumerate(weights):
        total = plus(total, weight * immobile_ref[zone * rows : (zone + 1) * rows, :])
    copies[5].wait()
    source_t[...] = (mobile_ref[...] + capacity * total).T
    coefs, sides = [], []
    for index in range(stride):
        coefs.append((strided(faces_t, index, SUBLANES, stride), None, strided(storage_t, index, SUBLANES, stride)))
        sides.append((None, strided(source_t, index, SUBLANES, stride)))
    rolls = x_rolls(halves)
    piece, nodes = tree_coefs(coefs, rolls)
    side, givens = tree_sides(sides, rolls, nodes)
    start = 2 * rows
    for node, given in zip(nodes, givens):
        for part in (node[0], node[1], given):
            block_ref[start : start + SUBLANES, :] = part
            start += SUBLANES
    for row, value in enumerate(piece + side):
        message_ref[row : row + 1, :] = value[0:1, :]
    copies[6].wait()


def ends_responses(shape):
    one, nothing = jnp.ones(shape, jnp.float32), jnp.zeros(shape, jnp.float32)
    return ((one, nothing), (nothing, one))


def prepare_kernel(halves, block_ref, rows_ref, lines_ref, sums_ref, *own_refs):
    rows = rows_ref.shape[1]
    stride = LANES // SUBLANES
    rolls = x_rolls(halves)
    total = stride - 1 + len(rolls)
    nodes = state_parts(block_ref.at[2 * rows :, :], 0, total, 3)
    nothing = jnp.zeros((SUBLANES, rows), jnp.float32)
    cases = [((nothing, nothing), [node[2] for node in nodes])]
    cases += [(ends, [0.0] * total) for ends in ends_responses((SUBLANES, rows))]
    for case, (ends, givens) in enumerate(cases):
        for index, value in enumerate(tree_values(*ends, rolls, stride, nodes, givens)):
            lines_ref[pl.ds(case * LANES + index, SUBLANES, stride=stride), :] = value
    stride = rows // SUBLANES
    start = 0
    for half in range(halves):
        storage = [strided(block_ref, index, SUBLANES, stride) for index in range(half, stride, halves)]
        faces = [strided(block_ref, rows + index, SUBLANES, stride) for index in range(half, stride, halves)]
        piece, nodes = tree_coefs([(face, None, held) for face, held in zip(faces, storage)], y_rolls())
        for part in [part for node in nodes for part in node] if own_refs else []:
            own_refs[0][start : start + SUBLANES, :] = part
            start += SUBLANES
        for number, value in enumerate(piece):
            row = number * halves + half
            rows_ref[row : row + 1, :] = value[0:1, :]
        for case, ends in enumerate(ends_responses((SUBLANES, LANES))):
            values = tree_values(*ends, y_rolls(), len(storage), nodes, [0.0] * len(nodes))
            for index, (value, held) in enumerate(zip(values, storage)):
                place = pl.ds(case * rows + index * halves + half, SUBLANES, stride=stride)
                sums_ref[place, :] = value * held
                if own_refs:
                    own_refs[1][place, :] = value


def state_parts(ref, first, total, parts, pitch=3):
    return [
        tuple(
            ref[(pitch * place + part) * SUBLANES : (pitch * place + part + 1) * SUBLANES, :]
            for part in range(parts)
        )
        for place in range(first, first + total)
    ]


def message_slots(refs, height, pitch, quantity_rows, skips):
    blocks = [(ref, start) for ref in refs for start in range(0, ref.shape[0], height)]
    slots = []
    for (ref, start), skip in zip(blocks, skips):
        rows = [start + quantity * pitch + skip for quantity in range(QUANTITIES)]
        slots.append(tuple(ref[row : row + quantity_rows, :] for row in rows))
    return slots


def quantity(number):
    return slice(number * LANES, (number + 1) * LANES)


def put_traded(ref, row, rows, number, value):
    ref[(row + rows // 2) % rows : (row + rows // 2) % rows + value.shape[0], quantity(number)] = value


def along_line(bound, halves, rows):
    value = jnp.broadcast_to(bound, (SUBLANES, rows))
    lane = lax.broadcasted_iota(jnp.int32, value.shape, 1)
    for step in doubling(halves):
        value = jnp.where((lane & step) != 0, behind(value, step, 1), value)
    return value[0:1, :]


def x_back_kernel(halves, axis, order, pieces, *refs):
    slots = message_slots(refs[:pieces], SUBLANES, 1, 1, [0] * len(order))
    slots = [slots[order.index(place)] for place in range(len(order))]
    lines_refs, sums_refs, rows_refs = (refs[pieces + 2 * pair : pieces + 2 * pair + 2] for pair in range(3))
    kept_ref, sent_ref, values_ref = refs[pieces + 6 :]
    bounds = ring_bounds(slots, lax.axis_index(axis))
    rows = values_ref.shape[0]

    def put(row, number, value):
        kept_ref[row : row + 1, quantity(number)] = value
        put_traded(sent_ref, row, 2 * halves, number, value)

    for block in range(2):
        for half in range(halves):
            for number in range(3):
                row = number * halves + half
                put(block * halves + half, number, rows_refs[block][row : row + 1, :])
    for block in range(2):
        lines_ref, sums_ref = lines_refs[block], sums_refs[block]
        before, after = (along_line(bound, halves, rows) for bound in bounds[block])
        values = lines_ref[0:LANES, :] + lines_ref[LANES : 2 * LANES, :] * before + lines_ref[2 * LANES :, :] * after
        values = values.T
        if block == 0:
            values_ref[...] = values
        for end in range(2):
            parts = (values * sums_ref[end * rows : (end + 1) * rows, :]).reshape(-1, SUBLANES, LANES)
            side = jnp.sum(parts, axis=0)
            for step in doubling(SUBLANES // halves):
                side = side + behind(side, step * halves, 0)
            for half in range(halves):
                put(block * halves + half, 3 + end, side[half : half + 1, :])


def y_given_kernel(halves, block_ref, values_ref, state_ref, given_ref):
    rows = values_ref.shape[0]
    stride = rows // SUBLANES
    total = stride // halves - 1 + len(y_rolls())
    nothing = jnp.zeros((SUBLANES, LANES), jnp.float32)
    for half in range(halves):
        places = [pl.ds(index, SUBLANES, stride=stride) for index in range(half, stride, halves)]
        sides = [(None, block_ref[place, :] * values_ref[place, :]) for place in places]
        nodes = state_parts(state_ref, half * total, total, 3)
        _, givens = tree_sides(sides, y_rolls(), nodes)
        for place, value in zip(places, tree_values(nothing, nothing, y_rolls(), len(places), nodes, givens)):
            given_ref[place, :] = value


def read_message(ref):
    return [ref[:, quantity(number)] for number in range(QUANTITIES)]


def join_by_bit(own, other, upper):
    left = [choose(upper, b, a) for a, b in zip(own, other)]
    right = [choose(upper, a, b) for a, b in zip(own, other)]
    coefs, node = join_coefs(left[:3], right[:3])
    sides, given = join_sides(left[3:], right[3:], node)
    return coefs + sides, (node[0], node[1], given)


def own_bit(axis, bit):
    return ((lax.axis_index(axis) >> bit) & 1) == 1


def y_join_kernel(axis, bit, own_ref, other_ref, kept_ref, sent_ref, path_ref):
    joined, path = join_by_bit(read_message(own_ref), read_message(other_ref), own_bit(axis, bit))
    rows = own_ref.shape[0]
    for number, value in enumerate(joined):
        kept_ref[:, quantity(number)] = value
        for row in (0, rows // 2):
            put_traded(sent_ref, row, rows, number, value[row : row + rows // 2, :])
    for number, value in enumerate(path):
        path_ref[:, quantity(number)] = value


def y_back_kernel(halves, axis, rounds, own_ref, other_ref, *refs):
    path_refs = refs[: rounds - 1]
    given_ref, spread_ref, out_ref = refs[rounds - 1 :]
    rows = out_ref.shape[0]
    joined, path = join_by_bit(read_message(own_ref), read_message(other_ref), own_bit(axis, rounds - 1))
    _, head, tail, side_head, side_tail = joined
    before = after = (side_head + side_tail) * inverse(head + tail)
    paths = [[ref[:, quantity(number)] for number in range(3)] for ref in path_refs] + [path]
    for bit in reversed(range(rounds)):
        node = paths[bit]
        middle = middle_value(node, node[2], before, after)
        upper = own_bit(axis, bit)
        before = jnp.where(upper, middle, before)
        after = jnp.where(upper, after, middle)
    sublane = lax.broadcasted_iota(jnp.int32, (SUBLANES, LANES), 0) % halves
    ends = []
    for end in (before, after):
        value = jnp.broadcast_to(end[0:1, :], (SUBLANES, LANES))
        for half in range(1, halves):
            value = jnp.where(sublane == half, jnp.broadcast_to(end[half : half + 1, :], value.shape), value)
        ends.append(value)
    for start in range(0, rows, SUBLANES):
        part = slice(start, start + SUBLANES)
        late = slice(rows + start, rows + start + SUBLANES)
        out_ref[part, :] = given_ref[part, :] + spread_ref[part, :] * ends[0] + spread_ref[late, :] * ends[1]


def trade(value, x_step, y_step):
    width = lax.axis_size("yd")
    pairs = []
    for index in range(lax.axis_size("xg")):
        for line in range(width):
            pairs.append((index * width + line, (index ^ x_step) * width + (line ^ y_step)))
    return lax.ppermute(value, ("xg", "yd"), pairs)


def pack_kernel(first_ref, second_ref, out_ref):
    height = first_ref.shape[0]
    out_ref[0:height, :] = first_ref[...]
    out_ref[height:, :] = second_ref[...]


def pack(first, second):
    (packed,) = kernel_call(
        pack_kernel, (first, second), [f32(first.shape[0] + second.shape[0], first.shape[1])], [], cost=10000000000
    )
    return packed


def x_exchange(message):
    held = message
    pieces = [message]
    order = [0]
    for step in doubling(lax.axis_size("xg") // 2):
        received = trade(held, 2 * step + 1, 0)
        pieces.append(received)
        order += [place ^ (2 * step + 1) for place in order]
        held = pack(held, received)
    pieces.append(trade(held, 1, 0))
    order += [place ^ 1 for place in order]
    return pieces, order


def y_exchange(kept, sent):
    rows = kept.shape[0]
    paths = []
    steps = doubling(lax.axis_size("yd"))
    for bit, step in enumerate(steps):
        received = trade(sent, 1, step)
        if bit < len(steps) - 1:
            kept, sent, path = kernel_call(
                functools.partial(y_join_kernel, "yd", bit),
                (kept, received),
                [held_f32(*kept.shape), f32(*kept.shape), held_f32(rows, 3 * LANES)],
                [],
            )
            paths.append(path)
    return [kept, received] + paths, len(steps)


def f32(*shape):
    return jax.ShapeDtypeStruct(shape, jnp.float32)


def held_f32(*shape):
    return VMEM(shape, jnp.float32)


def kernel_call(body, operands, outputs, scratch, space=VMEM, cost=500000):
    return pl.pallas_call(
        body,
        out_shape=outputs,
        in_specs=[pl.BlockSpec(memory_space=space)] * len(operands),
        out_specs=[pl.BlockSpec(memory_space=VMEM)] * len(outputs),
        scratch_shapes=scratch,
        cost_estimate=pl.CostEstimate(flops=cost, bytes_accessed=cost, transcendentals=0),
        compiler_params=pltpu.CompilerParams(vmem_limit_bytes=16 * 1024 * 1024),
    )(*operands)


def local(mobile, dispersion_x, dispersion_y, capacity, immobile, exchange_rates, rate_shares):
    shape = mobile.shape
    lines, width = shape[0] * shape[1], shape[2]
    zones = immobile.shape[0]
    halves = width // LANES
    rows = lines * halves
    assert rows == LANES

    def flat(values):
        return values.reshape(-1, LANES)

    mobile, dispersion_x, dispersion_y = flat(mobile), flat(dispersion_x), flat(dispersion_y)
    capacity, immobile = flat(capacity), flat(immobile)
    square = VMEM((rows, LANES), jnp.float32)
    x_nodes = LANES // SUBLANES - 1 + len(x_rolls(halves))
    y_nodes = halves * (rows // SUBLANES // halves - 1 + len(y_rolls()))
    message, block = kernel_call(
        functools.partial(x_forward_kernel, halves),
        tuple(
            pltpu.with_memory_space_constraint(value, pltpu.HBM)
            for value in (
                mobile, dispersion_x, dispersion_y, capacity, immobile, exchange_rates[None], rate_shares[None],
            )
        ),
        [f32(SUBLANES, rows), held_f32(2 * rows + 3 * x_nodes * SUBLANES, LANES)],
        [square] * 3
        + [VMEM((zones * rows, LANES), jnp.float32)]
        + [VMEM((1, zones), jnp.float32)] * 2
        + [pltpu.SemaphoreType.DMA((7,))]
        + [square] * 3,
        pltpu.HBM,
    )
    def prepare(part, own):
        outputs = [held_f32(SUBLANES, LANES), held_f32(3 * LANES, rows), held_f32(2 * rows, LANES)]
        if own:
            outputs += [held_f32(3 * y_nodes * SUBLANES, LANES), held_f32(2 * rows, LANES)]
        return kernel_call(functools.partial(prepare_kernel, halves), (part,), outputs, [])

    pieces, order = x_exchange(message)
    y_rows, lines_x, sums, y_state, spread = prepare(block, True)
    other_rows, other_lines, other_sums = prepare(trade(block, 1, 0), False)
    kept, sent, values = kernel_call(
        functools.partial(x_back_kernel, halves, "xg", order, len(pieces)),
        (*pieces, lines_x, other_lines, sums, other_sums, y_rows, other_rows),
        [
            held_f32(2 * halves, QUANTITIES * LANES),
            f32(2 * halves, QUANTITIES * LANES),
            held_f32(rows, LANES),
        ],
        [],
    )
    (given,) = kernel_call(
        functools.partial(y_given_kernel, halves), (block, values, y_state), [held_f32(rows, LANES)], []
    )
    pieces, rounds = y_exchange(kept, sent)
    (updated,) = kernel_call(
        functools.partial(y_back_kernel, halves, "yd", rounds),
        (*pieces, given, spread),
        [f32(rows, LANES)],
        [],
    )
    return updated.reshape(shape)


def solution(mesh):
    field = P("yd", None, "xg")
    return jax.shard_map(
        local,
        mesh=mesh,
        in_specs=(field, field, field, field, P(None, "yd", None, "xg"), P(), P()),
        out_specs=field,
        check_vma=False,
    )
```

```python
import functools

import jax
import jax.numpy as jnp
from jax import lax
from jax.experimental import pallas as pl
from jax.experimental.pallas import tpu as pltpu
from jax.sharding import PartitionSpec as P

LANES = 128
SUBLANES = 8
QUANTITIES = 5
VMEM = pltpu.VMEM


def inverse(value):
    return 1.0 / value


def plus(first, second):
    if first is None:
        return second
    return first + second


def join_coefs(left, right):
    coupling_1, head_1, tail_1 = left
    coupling_2, head_2, tail_2 = right
    middle = plus(head_2, tail_1)
    inv = inverse(coupling_1 + coupling_2 + middle)
    weight_1 = coupling_1 * inv
    weight_2 = coupling_2 * inv
    joined = (coupling_1 * weight_2, plus(head_1, weight_1 * middle), tail_2 + weight_2 * middle)
    return joined, (weight_1, weight_2, inv)


def join_sides(left, right, node):
    head_1, tail_1 = left
    head_2, tail_2 = right
    weight_1, weight_2, inv = node
    side = plus(head_2, tail_1)
    joined = (plus(head_1, weight_1 * side), tail_2 + weight_2 * side)
    return joined, side * inv


def middle_value(node, given, before, after):
    return given + node[0] * before + node[1] * after


def ahead(value, step, axis):
    return pltpu.roll(value, value.shape[axis] - step, axis)


def behind(value, step, axis):
    return pltpu.roll(value, step, axis)


def doubling(count):
    steps = []
    step = 1
    while step < count:
        steps.append(step)
        step *= 2
    return steps


def tree_coefs(leaves, rolls):
    nodes = []
    level = leaves
    while len(level) > 1:
        following = []
        for index in range(0, len(level), 2):
            joined, node = join_coefs(level[index], level[index + 1])
            following.append(joined)
            nodes.append(node)
        level = following
    piece = level[0]
    for step, axis in rolls:
        piece, node = join_coefs(piece, tuple(ahead(part, step, axis) for part in piece))
        nodes.append(node)
    return piece, nodes


def tree_sides(leaves, rolls, nodes):
    givens = []
    level = leaves
    while len(level) > 1:
        following = []
        for index in range(0, len(level), 2):
            joined, given = join_sides(level[index], level[index + 1], nodes[len(givens)])
            following.append(joined)
            givens.append(given)
        level = following
    piece = level[0]
    for step, axis in rolls:
        other = tuple(ahead(part, step, axis) for part in piece)
        piece, given = join_sides(piece, other, nodes[len(givens)])
        givens.append(given)
    return piece, givens


def tree_values(before, after, rolls, count, nodes, givens):
    place = len(nodes)
    for step, axis in reversed(rolls):
        place -= 1
        middle = middle_value(nodes[place], givens[place], before, after)
        upper = (lax.broadcasted_iota(jnp.int32, middle.shape, axis) & step) != 0
        before = jnp.where(upper, behind(middle, step, axis), before)
        after = jnp.where(upper, behind(after, step, axis), middle)
    bounds = [before, after]
    while len(bounds) - 1 < count:
        width = len(bounds) - 1
        place -= width
        following = [bounds[0]]
        for index in range(width):
            following.append(
                middle_value(
                    nodes[place + index], givens[place + index], bounds[index], bounds[index + 1]
                )
            )
            following.append(bounds[index + 1])
        bounds = following
    return bounds[1:]


def choose(condition, first, second):
    if isinstance(condition, bool):
        return first if condition else second
    return jnp.where(condition, first, second)


def ring_bounds(slots, index):
    level = slots
    rounds = []
    bit = 0
    while len(level) > 1:
        upper = ((index >> bit) & 1) == 1
        following, nodes = [], []
        for place in range(0, len(level), 2):
            own, other = level[place], level[place + 1]
            left = [jnp.where(upper, b, a) for a, b in zip(own, other)]
            right = [jnp.where(upper, a, b) for a, b in zip(own, other)]
            coefs, node = join_coefs(left[:3], right[:3])
            sides, given = join_sides(left[3:], right[3:], node)
            nodes.append((node, given))
            following.append(coefs + sides)
        rounds.append((nodes, upper))
        level = following
        bit += 1
    _, head, tail, side_head, side_tail = level[0]
    last = (side_head + side_tail) * inverse(head + tail)
    bounds = [(last, last)]
    for nodes, upper in reversed(rounds):
        following = []
        for (node, given), (before, after) in zip(nodes, bounds):
            middle = middle_value(node, given, before, after)
            following.append((jnp.where(upper, middle, before), jnp.where(upper, after, middle)))
            following.append((jnp.where(upper, before, middle), jnp.where(upper, middle, after)))
        bounds = following
    return bounds


def capacity_weights(rates, shares):
    weights = shares * rates / (1.0 + rates)
    return [weights[:, zone : zone + 1] for zone in range(weights.shape[1])]


def strided(ref, start, size, stride):
    return ref[pl.ds(start, size, stride=stride), :]


def x_rolls(halves):
    return [(step, 0) for step in doubling(SUBLANES)] + [(step, 1) for step in doubling(halves)]


def y_rolls():
    return [(step, 0) for step in doubling(SUBLANES)]


def x_forward_kernel(
    halves, mobile_hbm, faces_hbm, across_hbm, capacity_hbm, immobile_hbm, rates_hbm, shares_hbm,
    message_ref, block_ref,
    mobile_ref, faces_ref, capacity_ref, immobile_ref, rates_ref, shares_ref, arrived,
    faces_t, storage_t, source_t,
):
    rows = mobile_ref.shape[0]
    pairs = (
        (rates_hbm, rates_ref), (shares_hbm, shares_ref), (capacity_hbm, capacity_ref), (faces_hbm, faces_ref),
        (immobile_hbm, immobile_ref), (mobile_hbm, mobile_ref), (across_hbm, block_ref.at[rows : 2 * rows, :]),
    )
    copies = [pltpu.make_async_copy(pair[0], pair[1], arrived.at[place]) for place, pair in enumerate(pairs)]
    for place, copy in enumerate(copies):
        copy.start(priority=int(place in (4, 6)))
    stride = LANES // SUBLANES
    for copy in copies[:3]:
        copy.wait()
    weights = capacity_weights(rates_ref[...], shares_ref[...])
    capacity = capacity_ref[...]
    storage = 1.0 + capacity * sum(weights[1:], weights[0])
    block_ref[0:rows, :] = storage
    storage_t[...] = storage.T
    copies[3].wait()
    faces_t[...] = faces_ref[...].T
    copies[4].wait()
    total = None
    for zone, weight in enumerate(weights):
        total = plus(total, weight * immobile_ref[zone * rows : (zone + 1) * rows, :])
    copies[5].wait()
    source_t[...] = (mobile_ref[...] + capacity * total).T
    coefs, sides = [], []
    for index in range(stride):
        coefs.append((strided(faces_t, index, SUBLANES, stride), None, strided(storage_t, index, SUBLANES, stride)))
        sides.append((None, strided(source_t, index, SUBLANES, stride)))
    rolls = x_rolls(halves)
    piece, nodes = tree_coefs(coefs, rolls)
    side, givens = tree_sides(sides, rolls, nodes)
    start = 2 * rows
    for node, given in zip(nodes, givens):
        for part in (node[0], node[1], given):
            block_ref[start : start + SUBLANES, :] = part
            start += SUBLANES
    for row, value in enumerate(piece + side):
        message_ref[row : row + 1, :] = value[0:1, :]
    copies[6].wait()


def ends_responses(shape):
    one, nothing = jnp.ones(shape, jnp.float32), jnp.zeros(shape, jnp.float32)
    return ((one, nothing), (nothing, one))


def prepare_kernel(halves, block_ref, rows_ref, lines_ref, sums_ref, *own_refs):
    rows = rows_ref.shape[1]
    stride = LANES // SUBLANES
    rolls = x_rolls(halves)
    total = stride - 1 + len(rolls)
    nodes = state_parts(block_ref.at[2 * rows :, :], 0, total, 3)
    nothing = jnp.zeros((SUBLANES, rows), jnp.float32)
    cases = [((nothing, nothing), [node[2] for node in nodes])]
    cases += [(ends, [0.0] * total) for ends in ends_responses((SUBLANES, rows))]
    for case, (ends, givens) in enumerate(cases):
        for index, value in enumerate(tree_values(*ends, rolls, stride, nodes, givens)):
            lines_ref[pl.ds(case * LANES + index, SUBLANES, stride=stride), :] = value
    stride = rows // SUBLANES
    start = 0
    for half in range(halves):
        storage = [strided(block_ref, index, SUBLANES, stride) for index in range(half, stride, halves)]
        faces = [strided(block_ref, rows + index, SUBLANES, stride) for index in range(half, stride, halves)]
        piece, nodes = tree_coefs([(face, None, held) for face, held in zip(faces, storage)], y_rolls())
        for part in [part for node in nodes for part in node] if own_refs else []:
            own_refs[0][start : start + SUBLANES, :] = part
            start += SUBLANES
        for number, value in enumerate(piece):
            row = number * halves + half
            rows_ref[row : row + 1, :] = value[0:1, :]
        for case, ends in enumerate(ends_responses((SUBLANES, LANES))):
            values = tree_values(*ends, y_rolls(), len(storage), nodes, [0.0] * len(nodes))
            for index, (value, held) in enumerate(zip(values, storage)):
                place = pl.ds(case * rows + index * halves + half, SUBLANES, stride=stride)
                sums_ref[place, :] = value * held
                if own_refs:
                    own_refs[1][place, :] = value


def state_parts(ref, first, total, parts, pitch=3):
    return [
        tuple(
            ref[(pitch * place + part) * SUBLANES : (pitch * place + part + 1) * SUBLANES, :]
            for part in range(parts)
        )
        for place in range(first, first + total)
    ]


def message_slots(refs, height, pitch, quantity_rows, skips):
    blocks = [(ref, start) for ref in refs for start in range(0, ref.shape[0], height)]
    slots = []
    for (ref, start), skip in zip(blocks, skips):
        rows = [start + quantity * pitch + skip for quantity in range(QUANTITIES)]
        slots.append(tuple(ref[row : row + quantity_rows, :] for row in rows))
    return slots


def quantity(number):
    return slice(number * LANES, (number + 1) * LANES)


def put_traded(ref, row, rows, number, value):
    ref[(row + rows // 2) % rows : (row + rows // 2) % rows + value.shape[0], quantity(number)] = value


def along_line(bound, halves, rows):
    value = jnp.broadcast_to(bound, (SUBLANES, rows))
    lane = lax.broadcasted_iota(jnp.int32, value.shape, 1)
    for step in doubling(halves):
        value = jnp.where((lane & step) != 0, behind(value, step, 1), value)
    return value[0:1, :]


def x_back_kernel(halves, axis, order, pieces, *refs):
    slots = message_slots(refs[:pieces], SUBLANES, 1, 1, [0] * len(order))
    slots = [slots[order.index(place)] for place in range(len(order))]
    lines_refs, sums_refs, rows_refs = (refs[pieces + 2 * pair : pieces + 2 * pair + 2] for pair in range(3))
    kept_ref, sent_ref, values_ref = refs[pieces + 6 :]
    bounds = ring_bounds(slots, lax.axis_index(axis))
    rows = values_ref.shape[0]

    def put(row, number, value):
        kept_ref[row : row + 1, quantity(number)] = value
        put_traded(sent_ref, row, 2 * halves, number, value)

    for block in range(2):
        for half in range(halves):
            for number in range(3):
                row = number * halves + half
                put(block * halves + half, number, rows_refs[block][row : row + 1, :])
    for block in range(2):
        lines_ref, sums_ref = lines_refs[block], sums_refs[block]
        before, after = (along_line(bound, halves, rows) for bound in bounds[block])
        values = lines_ref[0:LANES, :] + lines_ref[LANES : 2 * LANES, :] * before + lines_ref[2 * LANES :, :] * after
        values = values.T
        if block == 0:
            values_ref[...] = values
        for end in range(2):
            parts = (values * sums_ref[end * rows : (end + 1) * rows, :]).reshape(-1, SUBLANES, LANES)
            side = jnp.sum(parts, axis=0)
            for step in doubling(SUBLANES // halves):
                side = side + behind(side, step * halves, 0)
            for half in range(halves):
                put(block * halves + half, 3 + end, side[half : half + 1, :])


def y_given_kernel(halves, block_ref, values_ref, state_ref, given_ref):
    rows = values_ref.shape[0]
    stride = rows // SUBLANES
    total = stride // halves - 1 + len(y_rolls())
    nothing = jnp.zeros((SUBLANES, LANES), jnp.float32)
    for half in range(halves):
        places = [pl.ds(index, SUBLANES, stride=stride) for index in range(half, stride, halves)]
        sides = [(None, block_ref[place, :] * values_ref[place, :]) for place in places]
        nodes = state_parts(state_ref, half * total, total, 3)
        _, givens = tree_sides(sides, y_rolls(), nodes)
        for place, value in zip(places, tree_values(nothing, nothing, y_rolls(), len(places), nodes, givens)):
            given_ref[place, :] = value


def read_message(ref):
    return [ref[:, quantity(number)] for number in range(QUANTITIES)]


def join_by_bit(own, other, upper):
    left = [choose(upper, b, a) for a, b in zip(own, other)]
    right = [choose(upper, a, b) for a, b in zip(own, other)]
    coefs, node = join_coefs(left[:3], right[:3])
    sides, given = join_sides(left[3:], right[3:], node)
    return coefs + sides, (node[0], node[1], given)


def own_bit(axis, bit):
    return ((lax.axis_index(axis) >> bit) & 1) == 1


def y_join_kernel(axis, bit, own_ref, other_ref, kept_ref, sent_ref, path_ref):
    joined, path = join_by_bit(read_message(own_ref), read_message(other_ref), own_bit(axis, bit))
    rows = own_ref.shape[0]
    for number, value in enumerate(joined):
        kept_ref[:, quantity(number)] = value
        for row in (0, rows // 2):
            put_traded(sent_ref, row, rows, number, value[row : row + rows // 2, :])
    for number, value in enumerate(path):
        path_ref[:, quantity(number)] = value


def y_back_kernel(halves, axis, rounds, own_ref, other_ref, *refs):
    path_refs = refs[: rounds - 1]
    given_ref, spread_ref, out_ref = refs[rounds - 1 :]
    rows = out_ref.shape[0]
    joined, path = join_by_bit(read_message(own_ref), read_message(other_ref), own_bit(axis, rounds - 1))
    _, head, tail, side_head, side_tail = joined
    before = after = (side_head + side_tail) * inverse(head + tail)
    paths = [[ref[:, quantity(number)] for number in range(3)] for ref in path_refs] + [path]
    for bit in reversed(range(rounds)):
        node = paths[bit]
        middle = middle_value(node, node[2], before, after)
        upper = own_bit(axis, bit)
        before = jnp.where(upper, middle, before)
        after = jnp.where(upper, after, middle)
    sublane = lax.broadcasted_iota(jnp.int32, (SUBLANES, LANES), 0) % halves
    ends = []
    for end in (before, after):
        value = jnp.broadcast_to(end[0:1, :], (SUBLANES, LANES))
        for half in range(1, halves):
            value = jnp.where(sublane == half, jnp.broadcast_to(end[half : half + 1, :], value.shape), value)
        ends.append(value)
    for start in range(0, rows, SUBLANES):
        part = slice(start, start + SUBLANES)
        late = slice(rows + start, rows + start + SUBLANES)
        out_ref[part, :] = given_ref[part, :] + spread_ref[part, :] * ends[0] + spread_ref[late, :] * ends[1]


def trade(value, x_step, y_step):
    width = lax.axis_size("yd")
    pairs = []
    for index in range(lax.axis_size("xg")):
        for line in range(width):
            pairs.append((index * width + line, (index ^ x_step) * width + (line ^ y_step)))
    return lax.ppermute(value, ("xg", "yd"), pairs)


def x_exchange(message):
    order = [0] + list(range(1, lax.axis_size("xg")))
    return [message] + [trade(message, step, 0) for step in order[1:]], order


def y_exchange(kept, sent):
    rows = kept.shape[0]
    paths = []
    steps = doubling(lax.axis_size("yd"))
    for bit, step in enumerate(steps):
        received = trade(sent, 1, step)
        if bit < len(steps) - 1:
            kept, sent, path = kernel_call(
                functools.partial(y_join_kernel, "yd", bit),
                (kept, received),
                [held_f32(*kept.shape), f32(*kept.shape), held_f32(rows, 3 * LANES)],
                [],
            )
            paths.append(path)
    return [kept, received] + paths, len(steps)


def f32(*shape):
    return jax.ShapeDtypeStruct(shape, jnp.float32)


def held_f32(*shape):
    return VMEM(shape, jnp.float32)


def kernel_call(body, operands, outputs, scratch, space=VMEM, cost=500000):
    return pl.pallas_call(
        body,
        out_shape=outputs,
        in_specs=[pl.BlockSpec(memory_space=space)] * len(operands),
        out_specs=[pl.BlockSpec(memory_space=VMEM)] * len(outputs),
        scratch_shapes=scratch,
        cost_estimate=pl.CostEstimate(flops=cost, bytes_accessed=cost, transcendentals=0),
        compiler_params=pltpu.CompilerParams(vmem_limit_bytes=16 * 1024 * 1024),
    )(*operands)


def local(mobile, dispersion_x, dispersion_y, capacity, immobile, exchange_rates, rate_shares):
    shape = mobile.shape
    lines, width = shape[0] * shape[1], shape[2]
    zones = immobile.shape[0]
    halves = width // LANES
    rows = lines * halves
    assert rows == LANES

    def flat(values):
        return values.reshape(-1, LANES)

    mobile, dispersion_x, dispersion_y = flat(mobile), flat(dispersion_x), flat(dispersion_y)
    capacity, immobile = flat(capacity), flat(immobile)
    square = VMEM((rows, LANES), jnp.float32)
    x_nodes = LANES // SUBLANES - 1 + len(x_rolls(halves))
    y_nodes = halves * (rows // SUBLANES // halves - 1 + len(y_rolls()))
    message, block = kernel_call(
        functools.partial(x_forward_kernel, halves),
        tuple(
            pltpu.with_memory_space_constraint(value, pltpu.HBM)
            for value in (
                mobile, dispersion_x, dispersion_y, capacity, immobile, exchange_rates[None], rate_shares[None],
            )
        ),
        [f32(SUBLANES, rows), held_f32(2 * rows + 3 * x_nodes * SUBLANES, LANES)],
        [square] * 3
        + [VMEM((zones * rows, LANES), jnp.float32)]
        + [VMEM((1, zones), jnp.float32)] * 2
        + [pltpu.SemaphoreType.DMA((7,))]
        + [square] * 3,
        pltpu.HBM,
    )
    def prepare(part, own):
        outputs = [held_f32(SUBLANES, LANES), held_f32(3 * LANES, rows), held_f32(2 * rows, LANES)]
        if own:
            outputs += [held_f32(3 * y_nodes * SUBLANES, LANES), held_f32(2 * rows, LANES)]
        return kernel_call(functools.partial(prepare_kernel, halves), (part,), outputs, [], cost=10000000000 if own else 500000)

    pieces, order = x_exchange(message)
    y_rows, lines_x, sums, y_state, spread = prepare(block, True)
    other_rows, other_lines, other_sums = prepare(trade(block, 1, 0), False)
    kept, sent, values = kernel_call(
        functools.partial(x_back_kernel, halves, "xg", order, len(pieces)),
        (*pieces, lines_x, other_lines, sums, other_sums, y_rows, other_rows),
        [
            held_f32(2 * halves, QUANTITIES * LANES),
            f32(2 * halves, QUANTITIES * LANES),
            held_f32(rows, LANES),
        ],
        [],
    )
    (given,) = kernel_call(
        functools.partial(y_given_kernel, halves), (block, values, y_state), [held_f32(rows, LANES)], []
    )
    pieces, rounds = y_exchange(kept, sent)
    (updated,) = kernel_call(
        functools.partial(y_back_kernel, halves, "yd", rounds),
        (*pieces, given, spread),
        [f32(rows, LANES)],
        [],
    )
    return updated.reshape(shape)


def solution(mesh):
    field = P("yd", None, "xg")
    return jax.shard_map(
        local,
        mesh=mesh,
        in_specs=(field, field, field, field, P(None, "yd", None, "xg"), P(), P()),
        out_specs=field,
        check_vma=False,
    )
```

```python
import functools

import jax
import jax.numpy as jnp
from jax import lax
from jax.experimental import pallas as pl
from jax.experimental.pallas import tpu as pltpu
from jax.sharding import PartitionSpec as P

LANES = 128
SUBLANES = 8
QUANTITIES = 5
VMEM = pltpu.VMEM


def inverse(value):
    return 1.0 / value


def plus(first, second):
    if first is None:
        return second
    return first + second


def join_coefs(left, right):
    coupling_1, head_1, tail_1 = left
    coupling_2, head_2, tail_2 = right
    middle = plus(head_2, tail_1)
    inv = inverse(coupling_1 + coupling_2 + middle)
    weight_1 = coupling_1 * inv
    weight_2 = coupling_2 * inv
    joined = (coupling_1 * weight_2, plus(head_1, weight_1 * middle), tail_2 + weight_2 * middle)
    return joined, (weight_1, weight_2, inv)


def join_sides(left, right, node):
    head_1, tail_1 = left
    head_2, tail_2 = right
    weight_1, weight_2, inv = node
    side = plus(head_2, tail_1)
    joined = (plus(head_1, weight_1 * side), tail_2 + weight_2 * side)
    return joined, side * inv


def middle_value(node, given, before, after):
    return given + node[0] * before + node[1] * after


def ahead(value, step, axis):
    return pltpu.roll(value, value.shape[axis] - step, axis)


def behind(value, step, axis):
    return pltpu.roll(value, step, axis)


def doubling(count):
    steps = []
    step = 1
    while step < count:
        steps.append(step)
        step *= 2
    return steps


def tree_coefs(leaves, rolls):
    nodes = []
    level = leaves
    while len(level) > 1:
        following = []
        for index in range(0, len(level), 2):
            joined, node = join_coefs(level[index], level[index + 1])
            following.append(joined)
            nodes.append(node)
        level = following
    piece = level[0]
    for step, axis in rolls:
        piece, node = join_coefs(piece, tuple(ahead(part, step, axis) for part in piece))
        nodes.append(node)
    return piece, nodes


def tree_sides(leaves, rolls, nodes):
    givens = []
    level = leaves
    while len(level) > 1:
        following = []
        for index in range(0, len(level), 2):
            joined, given = join_sides(level[index], level[index + 1], nodes[len(givens)])
            following.append(joined)
            givens.append(given)
        level = following
    piece = level[0]
    for step, axis in rolls:
        other = tuple(ahead(part, step, axis) for part in piece)
        piece, given = join_sides(piece, other, nodes[len(givens)])
        givens.append(given)
    return piece, givens


def tree_values(before, after, rolls, count, nodes, givens):
    place = len(nodes)
    for step, axis in reversed(rolls):
        place -= 1
        middle = middle_value(nodes[place], givens[place], before, after)
        upper = (lax.broadcasted_iota(jnp.int32, middle.shape, axis) & step) != 0
        before = jnp.where(upper, behind(middle, step, axis), before)
        after = jnp.where(upper, behind(after, step, axis), middle)
    bounds = [before, after]
    while len(bounds) - 1 < count:
        width = len(bounds) - 1
        place -= width
        following = [bounds[0]]
        for index in range(width):
            following.append(
                middle_value(
                    nodes[place + index], givens[place + index], bounds[index], bounds[index + 1]
                )
            )
            following.append(bounds[index + 1])
        bounds = following
    return bounds[1:]


def choose(condition, first, second):
    if isinstance(condition, bool):
        return first if condition else second
    return jnp.where(condition, first, second)


def ring_bounds(slots, index):
    level = slots
    rounds = []
    bit = 0
    while len(level) > 1:
        upper = ((index >> bit) & 1) == 1
        following, nodes = [], []
        for place in range(0, len(level), 2):
            own, other = level[place], level[place + 1]
            left = [jnp.where(upper, b, a) for a, b in zip(own, other)]
            right = [jnp.where(upper, a, b) for a, b in zip(own, other)]
            coefs, node = join_coefs(left[:3], right[:3])
            sides, given = join_sides(left[3:], right[3:], node)
            nodes.append((node, given))
            following.append(coefs + sides)
        rounds.append((nodes, upper))
        level = following
        bit += 1
    _, head, tail, side_head, side_tail = level[0]
    last = (side_head + side_tail) * inverse(head + tail)
    bounds = [(last, last)]
    for nodes, upper in reversed(rounds):
        following = []
        for (node, given), (before, after) in zip(nodes, bounds):
            middle = middle_value(node, given, before, after)
            following.append((jnp.where(upper, middle, before), jnp.where(upper, after, middle)))
            following.append((jnp.where(upper, before, middle), jnp.where(upper, middle, after)))
        bounds = following
    return bounds


def capacity_weights(rates, shares):
    weights = shares * rates / (1.0 + rates)
    return [weights[:, zone : zone + 1] for zone in range(weights.shape[1])]


def strided(ref, start, size, stride):
    return ref[pl.ds(start, size, stride=stride), :]


def x_rolls(halves):
    return [(step, 0) for step in doubling(SUBLANES)] + [(step, 1) for step in doubling(halves)]


def y_rolls():
    return [(step, 0) for step in doubling(SUBLANES)]


def x_forward_kernel(
    halves, mobile_hbm, faces_hbm, across_hbm, capacity_hbm, immobile_hbm, rates_hbm, shares_hbm,
    message_ref, block_ref,
    mobile_ref, faces_ref, capacity_ref, immobile_ref, rates_ref, shares_ref, arrived,
    faces_t, storage_t, source_t,
):
    rows = mobile_ref.shape[0]
    pairs = (
        (rates_hbm, rates_ref), (shares_hbm, shares_ref), (capacity_hbm, capacity_ref), (faces_hbm, faces_ref),
        (immobile_hbm, immobile_ref), (mobile_hbm, mobile_ref), (across_hbm, block_ref.at[rows : 2 * rows, :]),
    )
    copies = [pltpu.make_async_copy(pair[0], pair[1], arrived.at[place]) for place, pair in enumerate(pairs)]
    for place, copy in enumerate(copies):
        copy.start(priority=int(place in (4, 6)))
    stride = LANES // SUBLANES
    for copy in copies[:3]:
        copy.wait()
    weights = capacity_weights(rates_ref[...], shares_ref[...])
    capacity = capacity_ref[...]
    storage = 1.0 + capacity * sum(weights[1:], weights[0])
    block_ref[0:rows, :] = storage
    storage_t[...] = storage.T
    copies[3].wait()
    faces_t[...] = faces_ref[...].T
    copies[4].wait()
    total = None
    for zone, weight in enumerate(weights):
        total = plus(total, weight * immobile_ref[zone * rows : (zone + 1) * rows, :])
    copies[5].wait()
    source_t[...] = (mobile_ref[...] + capacity * total).T
    coefs, sides = [], []
    for index in range(stride):
        coefs.append((strided(faces_t, index, SUBLANES, stride), None, strided(storage_t, index, SUBLANES, stride)))
        sides.append((None, strided(source_t, index, SUBLANES, stride)))
    rolls = x_rolls(halves)
    piece, nodes = tree_coefs(coefs, rolls)
    side, givens = tree_sides(sides, rolls, nodes)
    start = 2 * rows
    for node, given in zip(nodes, givens):
        for part in (node[0], node[1], given):
            block_ref[start : start + SUBLANES, :] = part
            start += SUBLANES
    for row, value in enumerate(piece + side):
        message_ref[row : row + 1, :] = value[0:1, :]
        block_ref[start + row : start + row + 1, :] = value[0:1, :]
    copies[6].wait()


def ends_responses(shape):
    one, nothing = jnp.ones(shape, jnp.float32), jnp.zeros(shape, jnp.float32)
    return ((one, nothing), (nothing, one))


def prepare_kernel(halves, own, block_ref, rows_ref, lines_ref, sums_ref, *extra_refs):
    rows = rows_ref.shape[1]
    stride = LANES // SUBLANES
    rolls = x_rolls(halves)
    total = stride - 1 + len(rolls)
    nodes = state_parts(block_ref.at[2 * rows :, :], 0, total, 3)
    own_refs = extra_refs if own else ()
    if not own:
        extra_refs[0][...] = block_ref[-SUBLANES:, :]
    nothing = jnp.zeros((SUBLANES, rows), jnp.float32)
    cases = [((nothing, nothing), [node[2] for node in nodes])]
    cases += [(ends, [0.0] * total) for ends in ends_responses((SUBLANES, rows))]
    for case, (ends, givens) in enumerate(cases):
        for index, value in enumerate(tree_values(*ends, rolls, stride, nodes, givens)):
            lines_ref[pl.ds(case * LANES + index, SUBLANES, stride=stride), :] = value
    stride = rows // SUBLANES
    start = 0
    for half in range(halves):
        storage = [strided(block_ref, index, SUBLANES, stride) for index in range(half, stride, halves)]
        faces = [strided(block_ref, rows + index, SUBLANES, stride) for index in range(half, stride, halves)]
        piece, nodes = tree_coefs([(face, None, held) for face, held in zip(faces, storage)], y_rolls())
        for part in [part for node in nodes for part in node] if own_refs else []:
            own_refs[0][start : start + SUBLANES, :] = part
            start += SUBLANES
        for number, value in enumerate(piece):
            row = number * halves + half
            rows_ref[row : row + 1, :] = value[0:1, :]
        for case, ends in enumerate(ends_responses((SUBLANES, LANES))):
            values = tree_values(*ends, y_rolls(), len(storage), nodes, [0.0] * len(nodes))
            for index, (value, held) in enumerate(zip(values, storage)):
                place = pl.ds(case * rows + index * halves + half, SUBLANES, stride=stride)
                sums_ref[place, :] = value * held
                if own_refs:
                    own_refs[1][place, :] = value


def state_parts(ref, first, total, parts, pitch=3):
    return [
        tuple(
            ref[(pitch * place + part) * SUBLANES : (pitch * place + part + 1) * SUBLANES, :]
            for part in range(parts)
        )
        for place in range(first, first + total)
    ]


def message_slots(refs, height, pitch, quantity_rows, skips):
    blocks = [(ref, start) for ref in refs for start in range(0, ref.shape[0], height)]
    slots = []
    for (ref, start), skip in zip(blocks, skips):
        rows = [start + quantity * pitch + skip for quantity in range(QUANTITIES)]
        slots.append(tuple(ref[row : row + quantity_rows, :] for row in rows))
    return slots


def quantity(number):
    return slice(number * LANES, (number + 1) * LANES)


def put_traded(ref, row, rows, number, value):
    ref[(row + rows // 2) % rows : (row + rows // 2) % rows + value.shape[0], quantity(number)] = value


def along_line(bound, halves, rows):
    value = jnp.broadcast_to(bound, (SUBLANES, rows))
    lane = lax.broadcasted_iota(jnp.int32, value.shape, 1)
    for step in doubling(halves):
        value = jnp.where((lane & step) != 0, behind(value, step, 1), value)
    return value[0:1, :]


def x_back_kernel(halves, axis, order, pieces, *refs):
    lines_refs, sums_refs, rows_refs = (refs[pieces + 2 * pair : pieces + 2 * pair + 2] for pair in range(3))
    last_ref, kept_ref, sent_ref, values_ref = refs[pieces + 6 :]
    slots = message_slots([*refs[:pieces], last_ref], SUBLANES, 1, 1, [0] * len(order))
    slots = [slots[order.index(place)] for place in range(len(order))]
    bounds = ring_bounds(slots, lax.axis_index(axis))
    rows = values_ref.shape[0]

    def put(row, number, value):
        kept_ref[row : row + 1, quantity(number)] = value
        put_traded(sent_ref, row, 2 * halves, number, value)

    for block in range(2):
        for half in range(halves):
            for number in range(3):
                row = number * halves + half
                put(block * halves + half, number, rows_refs[block][row : row + 1, :])
    for block in range(2):
        lines_ref, sums_ref = lines_refs[block], sums_refs[block]
        before, after = (along_line(bound, halves, rows) for bound in bounds[block])
        values = lines_ref[0:LANES, :] + lines_ref[LANES : 2 * LANES, :] * before + lines_ref[2 * LANES :, :] * after
        values = values.T
        if block == 0:
            values_ref[...] = values
        for end in range(2):
            parts = (values * sums_ref[end * rows : (end + 1) * rows, :]).reshape(-1, SUBLANES, LANES)
            side = jnp.sum(parts, axis=0)
            for step in doubling(SUBLANES // halves):
                side = side + behind(side, step * halves, 0)
            for half in range(halves):
                put(block * halves + half, 3 + end, side[half : half + 1, :])


def y_given_kernel(halves, block_ref, values_ref, state_ref, given_ref):
    rows = values_ref.shape[0]
    stride = rows // SUBLANES
    total = stride // halves - 1 + len(y_rolls())
    nothing = jnp.zeros((SUBLANES, LANES), jnp.float32)
    for half in range(halves):
        places = [pl.ds(index, SUBLANES, stride=stride) for index in range(half, stride, halves)]
        sides = [(None, block_ref[place, :] * values_ref[place, :]) for place in places]
        nodes = state_parts(state_ref, half * total, total, 3)
        _, givens = tree_sides(sides, y_rolls(), nodes)
        for place, value in zip(places, tree_values(nothing, nothing, y_rolls(), len(places), nodes, givens)):
            given_ref[place, :] = value


def read_message(ref):
    return [ref[:, quantity(number)] for number in range(QUANTITIES)]


def join_by_bit(own, other, upper):
    left = [choose(upper, b, a) for a, b in zip(own, other)]
    right = [choose(upper, a, b) for a, b in zip(own, other)]
    coefs, node = join_coefs(left[:3], right[:3])
    sides, given = join_sides(left[3:], right[3:], node)
    return coefs + sides, (node[0], node[1], given)


def own_bit(axis, bit):
    return ((lax.axis_index(axis) >> bit) & 1) == 1


def y_join_kernel(axis, bit, own_ref, other_ref, kept_ref, sent_ref, path_ref):
    joined, path = join_by_bit(read_message(own_ref), read_message(other_ref), own_bit(axis, bit))
    rows = own_ref.shape[0]
    for number, value in enumerate(joined):
        kept_ref[:, quantity(number)] = value
        for row in (0, rows // 2):
            put_traded(sent_ref, row, rows, number, value[row : row + rows // 2, :])
    for number, value in enumerate(path):
        path_ref[:, quantity(number)] = value


def y_back_kernel(halves, axis, rounds, own_ref, other_ref, *refs):
    path_refs = refs[: rounds - 1]
    given_ref, spread_ref, out_ref = refs[rounds - 1 :]
    rows = out_ref.shape[0]
    joined, path = join_by_bit(read_message(own_ref), read_message(other_ref), own_bit(axis, rounds - 1))
    _, head, tail, side_head, side_tail = joined
    before = after = (side_head + side_tail) * inverse(head + tail)
    paths = [[ref[:, quantity(number)] for number in range(3)] for ref in path_refs] + [path]
    for bit in reversed(range(rounds)):
        node = paths[bit]
        middle = middle_value(node, node[2], before, after)
        upper = own_bit(axis, bit)
        before = jnp.where(upper, middle, before)
        after = jnp.where(upper, after, middle)
    sublane = lax.broadcasted_iota(jnp.int32, (SUBLANES, LANES), 0) % halves
    ends = []
    for end in (before, after):
        value = jnp.broadcast_to(end[0:1, :], (SUBLANES, LANES))
        for half in range(1, halves):
            value = jnp.where(sublane == half, jnp.broadcast_to(end[half : half + 1, :], value.shape), value)
        ends.append(value)
    for start in range(0, rows, SUBLANES):
        part = slice(start, start + SUBLANES)
        late = slice(rows + start, rows + start + SUBLANES)
        out_ref[part, :] = given_ref[part, :] + spread_ref[part, :] * ends[0] + spread_ref[late, :] * ends[1]


def trade(value, x_step, y_step):
    width = lax.axis_size("yd")
    pairs = []
    for index in range(lax.axis_size("xg")):
        for line in range(width):
            pairs.append((index * width + line, (index ^ x_step) * width + (line ^ y_step)))
    return lax.ppermute(value, ("xg", "yd"), pairs)


def x_exchange(message, block):
    count = lax.axis_size("xg")
    held = message
    pieces = [message]
    order = [0]
    other_block = trade(block, 1, 0)
    for step in doubling(count // 2):
        received = trade(held, 2 * step + 1, 0)
        pieces.append(received)
        order += [place ^ (2 * step + 1) for place in order]
        if 4 * step < count:
            held = jnp.concatenate([held, received], axis=0)
    received = pieces[1] if len(pieces) == 2 else jnp.concatenate(pieces[1:], axis=0)
    pieces.append(trade(received, 1, 0))
    order += [place ^ 1 for place in order[1:]] + [1]
    return pieces, order, other_block


def y_exchange(kept, sent):
    rows = kept.shape[0]
    paths = []
    steps = doubling(lax.axis_size("yd"))
    for bit, step in enumerate(steps):
        received = trade(sent, 1, step)
        if bit < len(steps) - 1:
            kept, sent, path = kernel_call(
                functools.partial(y_join_kernel, "yd", bit),
                (kept, received),
                [held_f32(*kept.shape), f32(*kept.shape), held_f32(rows, 3 * LANES)],
                [],
            )
            paths.append(path)
    return [kept, received] + paths, len(steps)


def f32(*shape):
    return jax.ShapeDtypeStruct(shape, jnp.float32)


def held_f32(*shape):
    return VMEM(shape, jnp.float32)


def kernel_call(body, operands, outputs, scratch, space=VMEM, cost=500000):
    return pl.pallas_call(
        body,
        out_shape=outputs,
        in_specs=[pl.BlockSpec(memory_space=space)] * len(operands),
        out_specs=[pl.BlockSpec(memory_space=VMEM)] * len(outputs),
        scratch_shapes=scratch,
        cost_estimate=pl.CostEstimate(flops=cost, bytes_accessed=cost, transcendentals=0),
        compiler_params=pltpu.CompilerParams(vmem_limit_bytes=16 * 1024 * 1024),
    )(*operands)


def local(mobile, dispersion_x, dispersion_y, capacity, immobile, exchange_rates, rate_shares):
    shape = mobile.shape
    lines, width = shape[0] * shape[1], shape[2]
    zones = immobile.shape[0]
    halves = width // LANES
    rows = lines * halves
    assert rows == LANES

    def flat(values):
        return values.reshape(-1, LANES)

    mobile, dispersion_x, dispersion_y = flat(mobile), flat(dispersion_x), flat(dispersion_y)
    capacity, immobile = flat(capacity), flat(immobile)
    square = VMEM((rows, LANES), jnp.float32)
    x_nodes = LANES // SUBLANES - 1 + len(x_rolls(halves))
    y_nodes = halves * (rows // SUBLANES // halves - 1 + len(y_rolls()))
    message, block = kernel_call(
        functools.partial(x_forward_kernel, halves),
        tuple(
            pltpu.with_memory_space_constraint(value, pltpu.HBM)
            for value in (
                mobile, dispersion_x, dispersion_y, capacity, immobile, exchange_rates[None], rate_shares[None],
            )
        ),
        [f32(SUBLANES, rows), held_f32(2 * rows + (3 * x_nodes + 1) * SUBLANES, LANES)],
        [square] * 3
        + [VMEM((zones * rows, LANES), jnp.float32)]
        + [VMEM((1, zones), jnp.float32)] * 2
        + [pltpu.SemaphoreType.DMA((7,))]
        + [square] * 3,
        pltpu.HBM,
    )
    def prepare(part, own):
        outputs = [held_f32(SUBLANES, LANES), held_f32(3 * LANES, rows), held_f32(2 * rows, LANES)]
        if own:
            outputs += [held_f32(3 * y_nodes * SUBLANES, LANES), held_f32(2 * rows, LANES)]
        else:
            outputs += [held_f32(SUBLANES, rows)]
        return kernel_call(functools.partial(prepare_kernel, halves, own), (part,), outputs, [], cost=10000000000)

    pieces, order, other_block = x_exchange(message, block)
    y_rows, lines_x, sums, y_state, spread = prepare(block, True)
    other_rows, other_lines, other_sums, other_message = prepare(other_block, False)
    kept, sent, values = kernel_call(
        functools.partial(x_back_kernel, halves, "xg", order, len(pieces)),
        (*pieces, lines_x, other_lines, sums, other_sums, y_rows, other_rows, other_message),
        [
            held_f32(2 * halves, QUANTITIES * LANES),
            f32(2 * halves, QUANTITIES * LANES),
            held_f32(rows, LANES),
        ],
        [],
    )
    (given,) = kernel_call(
        functools.partial(y_given_kernel, halves), (block, values, y_state), [held_f32(rows, LANES)], []
    )
    pieces, rounds = y_exchange(kept, sent)
    (updated,) = kernel_call(
        functools.partial(y_back_kernel, halves, "yd", rounds),
        (*pieces, given, spread),
        [f32(rows, LANES)],
        [],
    )
    return updated.reshape(shape)


def solution(mesh):
    field = P("yd", None, "xg")
    return jax.shard_map(
        local,
        mesh=mesh,
        in_specs=(field, field, field, field, P(None, "yd", None, "xg"), P(), P()),
        out_specs=field,
        check_vma=False,
    )
```

```python
import functools

import jax
import jax.numpy as jnp
from jax import lax
from jax.experimental import pallas as pl
from jax.experimental.pallas import tpu as pltpu
from jax.sharding import PartitionSpec as P

LANES = 128
SUBLANES = 8
QUANTITIES = 5
VMEM = pltpu.VMEM


def inverse(value):
    return 1.0 / value


def plus(first, second):
    if first is None:
        return second
    return first + second


def join_coefs(left, right):
    coupling_1, head_1, tail_1 = left
    coupling_2, head_2, tail_2 = right
    middle = plus(head_2, tail_1)
    inv = inverse(coupling_1 + coupling_2 + middle)
    weight_1 = coupling_1 * inv
    weight_2 = coupling_2 * inv
    joined = (coupling_1 * weight_2, plus(head_1, weight_1 * middle), tail_2 + weight_2 * middle)
    return joined, (weight_1, weight_2, inv)


def join_sides(left, right, node):
    head_1, tail_1 = left
    head_2, tail_2 = right
    weight_1, weight_2, inv = node
    side = plus(head_2, tail_1)
    joined = (plus(head_1, weight_1 * side), tail_2 + weight_2 * side)
    return joined, side * inv


def middle_value(node, given, before, after):
    return given + node[0] * before + node[1] * after


def ahead(value, step, axis):
    return pltpu.roll(value, value.shape[axis] - step, axis)


def behind(value, step, axis):
    return pltpu.roll(value, step, axis)


def doubling(count):
    steps = []
    step = 1
    while step < count:
        steps.append(step)
        step *= 2
    return steps


def tree_coefs(leaves, rolls):
    nodes = []
    level = leaves
    while len(level) > 1:
        following = []
        for index in range(0, len(level), 2):
            joined, node = join_coefs(level[index], level[index + 1])
            following.append(joined)
            nodes.append(node)
        level = following
    piece = level[0]
    for step, axis in rolls:
        piece, node = join_coefs(piece, tuple(ahead(part, step, axis) for part in piece))
        nodes.append(node)
    return piece, nodes


def tree_sides(leaves, rolls, nodes):
    givens = []
    level = leaves
    while len(level) > 1:
        following = []
        for index in range(0, len(level), 2):
            joined, given = join_sides(level[index], level[index + 1], nodes[len(givens)])
            following.append(joined)
            givens.append(given)
        level = following
    piece = level[0]
    for step, axis in rolls:
        other = tuple(ahead(part, step, axis) for part in piece)
        piece, given = join_sides(piece, other, nodes[len(givens)])
        givens.append(given)
    return piece, givens


def tree_values(before, after, rolls, count, nodes, givens):
    place = len(nodes)
    for step, axis in reversed(rolls):
        place -= 1
        middle = middle_value(nodes[place], givens[place], before, after)
        upper = (lax.broadcasted_iota(jnp.int32, middle.shape, axis) & step) != 0
        before = jnp.where(upper, behind(middle, step, axis), before)
        after = jnp.where(upper, behind(after, step, axis), middle)
    bounds = [before, after]
    while len(bounds) - 1 < count:
        width = len(bounds) - 1
        place -= width
        following = [bounds[0]]
        for index in range(width):
            following.append(
                middle_value(
                    nodes[place + index], givens[place + index], bounds[index], bounds[index + 1]
                )
            )
            following.append(bounds[index + 1])
        bounds = following
    return bounds[1:]


def choose(condition, first, second):
    if isinstance(condition, bool):
        return first if condition else second
    return jnp.where(condition, first, second)


def ring_bounds(slots, index):
    level = slots
    rounds = []
    bit = 0
    while len(level) > 1:
        upper = ((index >> bit) & 1) == 1
        following, nodes = [], []
        for place in range(0, len(level), 2):
            own, other = level[place], level[place + 1]
            left = [jnp.where(upper, b, a) for a, b in zip(own, other)]
            right = [jnp.where(upper, a, b) for a, b in zip(own, other)]
            coefs, node = join_coefs(left[:3], right[:3])
            sides, given = join_sides(left[3:], right[3:], node)
            nodes.append((node, given))
            following.append(coefs + sides)
        rounds.append((nodes, upper))
        level = following
        bit += 1
    _, head, tail, side_head, side_tail = level[0]
    last = (side_head + side_tail) * inverse(head + tail)
    bounds = [(last, last)]
    for nodes, upper in reversed(rounds):
        following = []
        for (node, given), (before, after) in zip(nodes, bounds):
            middle = middle_value(node, given, before, after)
            following.append((jnp.where(upper, middle, before), jnp.where(upper, after, middle)))
            following.append((jnp.where(upper, before, middle), jnp.where(upper, middle, after)))
        bounds = following
    return bounds


def capacity_weights(rates_ref, shares_ref):
    weights = []
    for zone in range(rates_ref.shape[1]):
        rate = jnp.full((SUBLANES, LANES), rates_ref[0, zone], jnp.float32)
        share = jnp.full((SUBLANES, LANES), shares_ref[0, zone], jnp.float32)
        weights.append((share * rate / (1.0 + rate))[0:1, :])
    return weights


def strided(ref, start, size, stride):
    return ref[pl.ds(start, size, stride=stride), :]


def x_rolls(halves):
    return [(step, 0) for step in doubling(SUBLANES)] + [(step, 1) for step in doubling(halves)]


def y_rolls():
    return [(step, 0) for step in doubling(SUBLANES)]


def x_forward_kernel(
    halves, mobile_hbm, faces_hbm, across_hbm, capacity_hbm, immobile_hbm, rates_hbm, shares_hbm,
    message_ref, block_ref,
    mobile_ref, faces_ref, capacity_ref, immobile_ref, rates_ref, shares_ref, arrived,
    faces_t, storage_t, source_t,
):
    rows = mobile_ref.shape[0]
    pairs = (
        (rates_hbm, rates_ref), (shares_hbm, shares_ref), (capacity_hbm, capacity_ref), (faces_hbm, faces_ref),
        (immobile_hbm, immobile_ref), (mobile_hbm, mobile_ref), (across_hbm, block_ref.at[rows : 2 * rows, :]),
    )
    copies = [pltpu.make_async_copy(pair[0], pair[1], arrived.at[place]) for place, pair in enumerate(pairs)]
    for place, copy in enumerate(copies):
        copy.start(priority=int(place in (4, 6)))
    stride = LANES // SUBLANES
    for copy in copies[:3]:
        copy.wait()
    weights = capacity_weights(rates_ref, shares_ref)
    capacity = capacity_ref[...]
    storage = 1.0 + capacity * sum(weights[1:], weights[0])
    block_ref[0:rows, :] = storage
    storage_t[...] = storage.T
    copies[3].wait()
    faces_t[...] = faces_ref[...].T
    copies[4].wait()
    total = None
    for zone, weight in enumerate(weights):
        total = plus(total, weight * immobile_ref[zone * rows : (zone + 1) * rows, :])
    copies[5].wait()
    source_t[...] = (mobile_ref[...] + capacity * total).T
    coefs, sides = [], []
    for index in range(stride):
        coefs.append((strided(faces_t, index, SUBLANES, stride), None, strided(storage_t, index, SUBLANES, stride)))
        sides.append((None, strided(source_t, index, SUBLANES, stride)))
    rolls = x_rolls(halves)
    piece, nodes = tree_coefs(coefs, rolls)
    side, givens = tree_sides(sides, rolls, nodes)
    start = 2 * rows
    for node, given in zip(nodes, givens):
        for part in (node[0], node[1], given):
            block_ref[start : start + SUBLANES, :] = part
            start += SUBLANES
    for row, value in enumerate(piece + side):
        message_ref[row : row + 1, :] = value[0:1, :]
        block_ref[start + row : start + row + 1, :] = value[0:1, :]
    copies[6].wait()


def ends_responses(shape):
    one, nothing = jnp.ones(shape, jnp.float32), jnp.zeros(shape, jnp.float32)
    return ((one, nothing), (nothing, one))


def prepare_kernel(halves, own, block_ref, rows_ref, lines_ref, sums_ref, *extra_refs):
    rows = lines_ref.shape[1]
    stride = LANES // SUBLANES
    rolls = x_rolls(halves)
    total = stride - 1 + len(rolls)
    nodes = state_parts(block_ref.at[2 * rows :, :], 0, total, 3)
    own_refs = extra_refs if own else ()
    if not own:
        extra_refs[0][...] = block_ref[-SUBLANES:, :]
    nothing = jnp.zeros((SUBLANES, rows), jnp.float32)
    cases = [((nothing, nothing), [node[2] for node in nodes])]
    cases += [(ends, [0.0] * total) for ends in ends_responses((SUBLANES, rows))]
    for case, (ends, givens) in enumerate(cases):
        for index, value in enumerate(tree_values(*ends, rolls, stride, nodes, givens)):
            lines_ref[pl.ds(case * LANES + index, SUBLANES, stride=stride), :] = value
    stride = rows // SUBLANES
    start = 0
    sublane = lax.broadcasted_iota(jnp.int32, (SUBLANES, LANES), 0) % halves
    tiles = None
    for half in range(halves):
        storage = [strided(block_ref, index, SUBLANES, stride) for index in range(half, stride, halves)]
        faces = [strided(block_ref, rows + index, SUBLANES, stride) for index in range(half, stride, halves)]
        piece, nodes = tree_coefs([(face, None, held) for face, held in zip(faces, storage)], y_rolls())
        for part in [part for node in nodes for part in node] if own_refs else []:
            own_refs[0][start : start + SUBLANES, :] = part
            start += SUBLANES
        values = [jnp.broadcast_to(value[0:1, :], value.shape) for value in piece]
        tiles = [jnp.where(sublane == half, new, old) for new, old in zip(values, tiles or values)]
        for case, ends in enumerate(ends_responses((SUBLANES, LANES))):
            values = tree_values(*ends, y_rolls(), len(storage), nodes, [0.0] * len(nodes))
            for index, (value, held) in enumerate(zip(values, storage)):
                place = pl.ds(case * rows + index * halves + half, SUBLANES, stride=stride)
                sums_ref[place, :] = value * held
                if own_refs:
                    own_refs[1][place, :] = value
    for number, tile in enumerate(tiles):
        rows_ref[:, quantity(number)] = tile


def state_parts(ref, first, total, parts, pitch=3):
    return [
        tuple(
            ref[(pitch * place + part) * SUBLANES : (pitch * place + part + 1) * SUBLANES, :]
            for part in range(parts)
        )
        for place in range(first, first + total)
    ]


def message_slots(refs, height, pitch, quantity_rows, skips):
    blocks = [(ref, start) for ref in refs for start in range(0, ref.shape[0], height)]
    slots = []
    for (ref, start), skip in zip(blocks, skips):
        rows = [start + quantity * pitch + skip for quantity in range(QUANTITIES)]
        slots.append(tuple(ref[row : row + quantity_rows, :] for row in rows))
    return slots


def quantity(number):
    return slice(number * LANES, (number + 1) * LANES)


def put_traded(ref, row, rows, number, value):
    ref[(row + rows // 2) % rows : (row + rows // 2) % rows + value.shape[0], quantity(number)] = value


def along_line(bound, halves, rows):
    value = jnp.broadcast_to(bound, (SUBLANES, rows))
    lane = lax.broadcasted_iota(jnp.int32, value.shape, 1)
    for step in doubling(halves):
        value = jnp.where((lane & step) != 0, behind(value, step, 1), value)
    return value[0:1, :]


def x_back_kernel(halves, axis, order, pieces, *refs):
    lines_refs, sums_refs, rows_refs = (refs[pieces + 2 * pair : pieces + 2 * pair + 2] for pair in range(3))
    last_ref, kept_ref, sent_ref, values_ref = refs[pieces + 6 :]
    slots = message_slots([*refs[:pieces], last_ref], SUBLANES, 1, 1, [0] * len(order))
    slots = [slots[order.index(place)] for place in range(len(order))]
    bounds = ring_bounds(slots, lax.axis_index(axis))
    rows = values_ref.shape[0]

    height = 2 * halves
    first = lax.broadcasted_iota(jnp.int32, (SUBLANES, LANES), 0) < halves

    def put(number, own, other):
        kept_ref[:, quantity(number)] = jnp.where(first, own, other)[0:height, :]
        sent_ref[:, quantity(number)] = jnp.where(first, other, own)[0:height, :]

    for number in range(3):
        put(number, *(ref[:, quantity(number)] for ref in rows_refs))
    sides = []
    for block in range(2):
        lines_ref, sums_ref = lines_refs[block], sums_refs[block]
        before, after = (along_line(bound, halves, rows) for bound in bounds[block])
        values = lines_ref[0:LANES, :] + lines_ref[LANES : 2 * LANES, :] * before + lines_ref[2 * LANES :, :] * after
        values = values.T
        if block == 0:
            values_ref[...] = values
        for end in range(2):
            parts = (values * sums_ref[end * rows : (end + 1) * rows, :]).reshape(-1, SUBLANES, LANES)
            side = jnp.sum(parts, axis=0)
            for step in doubling(SUBLANES // halves):
                side = side + behind(side, step * halves, 0)
            sides.append(side)
    for end in range(2):
        put(3 + end, sides[end], sides[2 + end])


def y_given_kernel(halves, block_ref, values_ref, state_ref, given_ref):
    rows = values_ref.shape[0]
    stride = rows // SUBLANES
    total = stride // halves - 1 + len(y_rolls())
    nothing = jnp.zeros((SUBLANES, LANES), jnp.float32)
    for half in range(halves):
        places = [pl.ds(index, SUBLANES, stride=stride) for index in range(half, stride, halves)]
        sides = [(None, block_ref[place, :] * values_ref[place, :]) for place in places]
        nodes = state_parts(state_ref, half * total, total, 3)
        _, givens = tree_sides(sides, y_rolls(), nodes)
        for place, value in zip(places, tree_values(nothing, nothing, y_rolls(), len(places), nodes, givens)):
            given_ref[place, :] = value


def read_message(ref):
    return [ref[:, quantity(number)] for number in range(QUANTITIES)]


def join_by_bit(own, other, upper):
    left = [choose(upper, b, a) for a, b in zip(own, other)]
    right = [choose(upper, a, b) for a, b in zip(own, other)]
    coefs, node = join_coefs(left[:3], right[:3])
    sides, given = join_sides(left[3:], right[3:], node)
    return coefs + sides, (node[0], node[1], given)


def own_bit(axis, bit):
    return ((lax.axis_index(axis) >> bit) & 1) == 1


def y_join_kernel(axis, bit, own_ref, other_ref, kept_ref, sent_ref, path_ref):
    joined, path = join_by_bit(read_message(own_ref), read_message(other_ref), own_bit(axis, bit))
    rows = own_ref.shape[0]
    for number, value in enumerate(joined):
        kept_ref[:, quantity(number)] = value
        for row in (0, rows // 2):
            put_traded(sent_ref, row, rows, number, value[row : row + rows // 2, :])
    for number, value in enumerate(path):
        path_ref[:, quantity(number)] = value


def y_back_kernel(halves, axis, rounds, own_ref, other_ref, *refs):
    path_refs = refs[: rounds - 1]
    given_ref, spread_ref, out_ref = refs[rounds - 1 :]
    rows = out_ref.shape[0]
    joined, path = join_by_bit(read_message(own_ref), read_message(other_ref), own_bit(axis, rounds - 1))
    _, head, tail, side_head, side_tail = joined
    before = after = (side_head + side_tail) * inverse(head + tail)
    paths = [[ref[:, quantity(number)] for number in range(3)] for ref in path_refs] + [path]
    for bit in reversed(range(rounds)):
        node = paths[bit]
        middle = middle_value(node, node[2], before, after)
        upper = own_bit(axis, bit)
        before = jnp.where(upper, middle, before)
        after = jnp.where(upper, after, middle)
    sublane = lax.broadcasted_iota(jnp.int32, (SUBLANES, LANES), 0) % halves
    ends = []
    for end in (before, after):
        value = jnp.broadcast_to(end[0:1, :], (SUBLANES, LANES))
        for half in range(1, halves):
            value = jnp.where(sublane == half, jnp.broadcast_to(end[half : half + 1, :], value.shape), value)
        ends.append(value)
    for start in range(0, rows, SUBLANES):
        part = slice(start, start + SUBLANES)
        late = slice(rows + start, rows + start + SUBLANES)
        out_ref[part, :] = given_ref[part, :] + spread_ref[part, :] * ends[0] + spread_ref[late, :] * ends[1]


def trade(value, x_step, y_step):
    width = lax.axis_size("yd")
    pairs = []
    for index in range(lax.axis_size("xg")):
        for line in range(width):
            pairs.append((index * width + line, (index ^ x_step) * width + (line ^ y_step)))
    return lax.ppermute(value, ("xg", "yd"), pairs)


def x_exchange(message, block):
    count = lax.axis_size("xg")
    held = message
    pieces = [message]
    order = [0]
    other_block = trade(block, 1, 0)
    for step in doubling(count // 2):
        received = trade(held, 2 * step + 1, 0)
        pieces.append(received)
        order += [place ^ (2 * step + 1) for place in order]
        if 4 * step < count:
            held = jnp.concatenate([held, received], axis=0)
    received = pieces[1] if len(pieces) == 2 else jnp.concatenate(pieces[1:], axis=0)
    pieces.append(trade(received, 1, 0))
    order += [place ^ 1 for place in order[1:]] + [1]
    return pieces, order, other_block


def y_exchange(kept, sent):
    rows = kept.shape[0]
    paths = []
    steps = doubling(lax.axis_size("yd"))
    for bit, step in enumerate(steps):
        received = trade(sent, 1, step)
        if bit < len(steps) - 1:
            kept, sent, path = kernel_call(
                functools.partial(y_join_kernel, "yd", bit),
                (kept, received),
                [held_f32(*kept.shape), f32(*kept.shape), held_f32(rows, 3 * LANES)],
                [],
            )
            paths.append(path)
    return [kept, received] + paths, len(steps)


def f32(*shape):
    return jax.ShapeDtypeStruct(shape, jnp.float32)


def held_f32(*shape):
    return VMEM(shape, jnp.float32)


def kernel_call(body, operands, outputs, scratch, space=VMEM, cost=500000):
    return pl.pallas_call(
        body,
        out_shape=outputs,
        in_specs=[pl.BlockSpec(memory_space=space)] * len(operands),
        out_specs=[pl.BlockSpec(memory_space=VMEM)] * len(outputs),
        scratch_shapes=scratch,
        cost_estimate=pl.CostEstimate(flops=cost, bytes_accessed=cost, transcendentals=0),
        compiler_params=pltpu.CompilerParams(vmem_limit_bytes=16 * 1024 * 1024),
    )(*operands)


def local(mobile, dispersion_x, dispersion_y, capacity, immobile, exchange_rates, rate_shares):
    shape = mobile.shape
    lines, width = shape[0] * shape[1], shape[2]
    zones = immobile.shape[0]
    halves = width // LANES
    rows = lines * halves
    assert rows == LANES

    def flat(values):
        return values.reshape(-1, LANES)

    mobile, dispersion_x, dispersion_y = flat(mobile), flat(dispersion_x), flat(dispersion_y)
    capacity, immobile = flat(capacity), flat(immobile)
    square = VMEM((rows, LANES), jnp.float32)
    x_nodes = LANES // SUBLANES - 1 + len(x_rolls(halves))
    y_nodes = halves * (rows // SUBLANES // halves - 1 + len(y_rolls()))
    message, block = kernel_call(
        functools.partial(x_forward_kernel, halves),
        tuple(
            pltpu.with_memory_space_constraint(value, pltpu.HBM)
            for value in (
                mobile, dispersion_x, dispersion_y, capacity, immobile, exchange_rates[None], rate_shares[None],
            )
        ),
        [f32(SUBLANES, rows), held_f32(2 * rows + (3 * x_nodes + 1) * SUBLANES, LANES)],
        [square] * 3
        + [VMEM((zones * rows, LANES), jnp.float32)]
        + [pltpu.SMEM((1, zones), jnp.float32)] * 2
        + [pltpu.SemaphoreType.DMA((7,))]
        + [square] * 3,
        pltpu.HBM,
    )
    def prepare(part, own):
        outputs = [held_f32(SUBLANES, 3 * LANES), held_f32(3 * LANES, rows), held_f32(2 * rows, LANES)]
        if own:
            outputs += [held_f32(3 * y_nodes * SUBLANES, LANES), held_f32(2 * rows, LANES)]
        else:
            outputs += [held_f32(SUBLANES, rows)]
        return kernel_call(functools.partial(prepare_kernel, halves, own), (part,), outputs, [], cost=10000000000)

    pieces, order, other_block = x_exchange(message, block)
    y_rows, lines_x, sums, y_state, spread = prepare(block, True)
    other_rows, other_lines, other_sums, other_message = prepare(other_block, False)
    kept, sent, values = kernel_call(
        functools.partial(x_back_kernel, halves, "xg", order, len(pieces)),
        (*pieces, lines_x, other_lines, sums, other_sums, y_rows, other_rows, other_message),
        [
            held_f32(2 * halves, QUANTITIES * LANES),
            f32(2 * halves, QUANTITIES * LANES),
            held_f32(rows, LANES),
        ],
        [],
    )
    (given,) = kernel_call(
        functools.partial(y_given_kernel, halves), (block, values, y_state), [held_f32(rows, LANES)], []
    )
    pieces, rounds = y_exchange(kept, sent)
    (updated,) = kernel_call(
        functools.partial(y_back_kernel, halves, "yd", rounds),
        (*pieces, given, spread),
        [f32(rows, LANES)],
        [],
    )
    return updated.reshape(shape)


def solution(mesh):
    field = P("yd", None, "xg")
    return jax.shard_map(
        local,
        mesh=mesh,
        in_specs=(field, field, field, field, P(None, "yd", None, "xg"), P(), P()),
        out_specs=field,
        check_vma=False,
    )
```

```python
import functools

import jax
import jax.numpy as jnp
from jax import lax
from jax.experimental import pallas as pl
from jax.experimental.pallas import tpu as pltpu
from jax.sharding import PartitionSpec as P

LANES = 128
SUBLANES = 8
QUANTITIES = 5
VMEM = pltpu.VMEM


def inverse(value):
    return 1.0 / value


def plus(first, second):
    if first is None:
        return second
    return first + second


def join_coefs(left, right):
    coupling_1, head_1, tail_1 = left
    coupling_2, head_2, tail_2 = right
    middle = plus(head_2, tail_1)
    inv = inverse(coupling_1 + coupling_2 + middle)
    weight_1 = coupling_1 * inv
    weight_2 = coupling_2 * inv
    joined = (coupling_1 * weight_2, plus(head_1, weight_1 * middle), tail_2 + weight_2 * middle)
    return joined, (weight_1, weight_2, inv)


def join_sides(left, right, node):
    head_1, tail_1 = left
    head_2, tail_2 = right
    weight_1, weight_2, inv = node
    side = plus(head_2, tail_1)
    joined = (plus(head_1, weight_1 * side), tail_2 + weight_2 * side)
    return joined, side * inv


def middle_value(node, given, before, after):
    return given + node[0] * before + node[1] * after


def ahead(value, step, axis):
    return pltpu.roll(value, value.shape[axis] - step, axis)


def behind(value, step, axis):
    return pltpu.roll(value, step, axis)


def doubling(count):
    steps = []
    step = 1
    while step < count:
        steps.append(step)
        step *= 2
    return steps


def tree_coefs(leaves, rolls):
    nodes = []
    level = leaves
    while len(level) > 1:
        following = []
        for index in range(0, len(level), 2):
            joined, node = join_coefs(level[index], level[index + 1])
            following.append(joined)
            nodes.append(node)
        level = following
    piece = level[0]
    for step, axis in rolls:
        piece, node = join_coefs(piece, tuple(ahead(part, step, axis) for part in piece))
        nodes.append(node)
    return piece, nodes


def tree_sides(leaves, rolls, nodes):
    givens = []
    level = leaves
    while len(level) > 1:
        following = []
        for index in range(0, len(level), 2):
            joined, given = join_sides(level[index], level[index + 1], nodes[len(givens)])
            following.append(joined)
            givens.append(given)
        level = following
    piece = level[0]
    for step, axis in rolls:
        other = tuple(ahead(part, step, axis) for part in piece)
        piece, given = join_sides(piece, other, nodes[len(givens)])
        givens.append(given)
    return piece, givens


def tree_values(before, after, rolls, count, nodes, givens):
    place = len(nodes)
    for step, axis in reversed(rolls):
        place -= 1
        middle = middle_value(nodes[place], givens[place], before, after)
        upper = (lax.broadcasted_iota(jnp.int32, middle.shape, axis) & step) != 0
        before = jnp.where(upper, behind(middle, step, axis), before)
        after = jnp.where(upper, behind(after, step, axis), middle)
    bounds = [before, after]
    while len(bounds) - 1 < count:
        width = len(bounds) - 1
        place -= width
        following = [bounds[0]]
        for index in range(width):
            following.append(
                middle_value(
                    nodes[place + index], givens[place + index], bounds[index], bounds[index + 1]
                )
            )
            following.append(bounds[index + 1])
        bounds = following
    return bounds[1:]


def choose(condition, first, second):
    if isinstance(condition, bool):
        return first if condition else second
    return jnp.where(condition, first, second)


def ring_bounds(slots, index):
    level = slots
    rounds = []
    bit = 0
    while len(level) > 1:
        upper = ((index >> bit) & 1) == 1
        following, nodes = [], []
        for place in range(0, len(level), 2):
            own, other = level[place], level[place + 1]
            left = [jnp.where(upper, b, a) for a, b in zip(own, other)]
            right = [jnp.where(upper, a, b) for a, b in zip(own, other)]
            coefs, node = join_coefs(left[:3], right[:3])
            sides, given = join_sides(left[3:], right[3:], node)
            nodes.append((node, given))
            following.append(coefs + sides)
        rounds.append((nodes, upper))
        level = following
        bit += 1
    _, head, tail, side_head, side_tail = level[0]
    last = (side_head + side_tail) * inverse(head + tail)
    bounds = [(last, last)]
    for nodes, upper in reversed(rounds):
        following = []
        for (node, given), (before, after) in zip(nodes, bounds):
            middle = middle_value(node, given, before, after)
            following.append((jnp.where(upper, middle, before), jnp.where(upper, after, middle)))
            following.append((jnp.where(upper, before, middle), jnp.where(upper, middle, after)))
        bounds = following
    return bounds


def capacity_weights(rates_ref, shares_ref):
    weights = []
    for zone in range(rates_ref.shape[1]):
        rate = jnp.full((SUBLANES, LANES), rates_ref[0, zone], jnp.float32)
        share = jnp.full((SUBLANES, LANES), shares_ref[0, zone], jnp.float32)
        weights.append(share * rate / (1.0 + rate))
    return weights


def strided(ref, start, size, stride):
    return ref[pl.ds(start, size, stride=stride), :]


def x_rolls(halves):
    return [(step, 0) for step in doubling(SUBLANES)] + [(step, 1) for step in doubling(halves)]


def y_rolls():
    return [(step, 0) for step in doubling(SUBLANES)]


def x_forward_kernel(
    halves, mobile_hbm, faces_hbm, across_hbm, capacity_hbm, immobile_hbm, rates_hbm, shares_hbm,
    message_ref, block_ref,
    mobile_ref, faces_ref, capacity_ref, immobile_ref, rates_ref, shares_ref, arrived,
    faces_t, storage_t, source_t,
):
    rows = mobile_ref.shape[0]
    pairs = (
        (rates_hbm, rates_ref), (shares_hbm, shares_ref), (capacity_hbm, capacity_ref), (faces_hbm, faces_ref),
        (immobile_hbm, immobile_ref), (mobile_hbm, mobile_ref), (across_hbm, block_ref.at[rows : 2 * rows, :]),
    )
    copies = [pltpu.make_async_copy(pair[0], pair[1], arrived.at[place]) for place, pair in enumerate(pairs)]
    for place, copy in enumerate(copies):
        copy.start(priority=int(place in (4, 6)))
    stride = LANES // SUBLANES
    for copy in copies[:3]:
        copy.wait()
    weights = capacity_weights(rates_ref, shares_ref)

    def tiles(ref, start=0):
        return ref[start : start + rows, :].reshape(-1, SUBLANES, LANES)

    capacity = tiles(capacity_ref)
    storage = (1.0 + capacity * sum(weights[1:], weights[0])).reshape(rows, LANES)
    block_ref[0:rows, :] = storage
    storage_t[...] = storage.T
    copies[3].wait()
    faces_t[...] = faces_ref[...].T
    coefs = []
    for index in range(stride):
        coefs.append((strided(faces_t, index, SUBLANES, stride), None, strided(storage_t, index, SUBLANES, stride)))
    rolls = x_rolls(halves)
    piece, nodes = tree_coefs(coefs, rolls)
    start = 2 * rows
    for part in [part for node in nodes for part in node]:
        block_ref[start : start + SUBLANES, :] = part
        start += SUBLANES
    copies[4].wait()
    total = None
    for zone, weight in enumerate(weights):
        total = plus(total, weight * tiles(immobile_ref, zone * rows))
    copies[5].wait()
    source_t[...] = (tiles(mobile_ref) + capacity * total).reshape(rows, LANES).T
    sides = [(None, strided(source_t, index, SUBLANES, stride)) for index in range(stride)]
    nodes = state_parts(block_ref.at[2 * rows :, :], 0, len(nodes), 3)
    side, givens = tree_sides(sides, rolls, nodes)
    for row, value in enumerate(piece + side):
        message_ref[row : row + 1, :] = value[0:1, :]
        block_ref[start + row : start + row + 1, :] = value[0:1, :]
    for place, given in enumerate(givens):
        last = 2 * rows + (3 * place + 2) * SUBLANES
        block_ref[last : last + SUBLANES, :] = given
    copies[6].wait()


def ends_responses(shape):
    one, nothing = jnp.ones(shape, jnp.float32), jnp.zeros(shape, jnp.float32)
    return ((one, nothing), (nothing, one))


def prepare_kernel(halves, own, block_ref, rows_ref, lines_ref, sums_ref, *extra_refs):
    rows = lines_ref.shape[1]
    stride = LANES // SUBLANES
    rolls = x_rolls(halves)
    total = stride - 1 + len(rolls)
    nodes = state_parts(block_ref.at[2 * rows :, :], 0, total, 3)
    own_refs = extra_refs if own else ()
    if not own:
        extra_refs[0][...] = block_ref[-SUBLANES:, :]
    nothing = jnp.zeros((SUBLANES, rows), jnp.float32)
    cases = [((nothing, nothing), [node[2] for node in nodes])]
    cases += [(ends, [0.0] * total) for ends in ends_responses((SUBLANES, rows))]
    for case, (ends, givens) in enumerate(cases):
        for index, value in enumerate(tree_values(*ends, rolls, stride, nodes, givens)):
            lines_ref[pl.ds(case * LANES + index, SUBLANES, stride=stride), :] = value
    stride = rows // SUBLANES
    start = 0
    sublane = lax.broadcasted_iota(jnp.int32, (SUBLANES, LANES), 0) % halves
    tiles = None
    for half in range(halves):
        storage = [strided(block_ref, index, SUBLANES, stride) for index in range(half, stride, halves)]
        faces = [strided(block_ref, rows + index, SUBLANES, stride) for index in range(half, stride, halves)]
        piece, nodes = tree_coefs([(face, None, held) for face, held in zip(faces, storage)], y_rolls())
        for part in [part for node in nodes for part in node] if own_refs else []:
            own_refs[0][start : start + SUBLANES, :] = part
            start += SUBLANES
        values = [jnp.broadcast_to(value[0:1, :], value.shape) for value in piece]
        tiles = [jnp.where(sublane == half, new, old) for new, old in zip(values, tiles or values)]
        for case, ends in enumerate(ends_responses((SUBLANES, LANES))):
            values = tree_values(*ends, y_rolls(), len(storage), nodes, [0.0] * len(nodes))
            for index, (value, held) in enumerate(zip(values, storage)):
                place = pl.ds(case * rows + index * halves + half, SUBLANES, stride=stride)
                sums_ref[place, :] = value * held
                if own_refs:
                    own_refs[1][place, :] = value
    for number, tile in enumerate(tiles):
        rows_ref[:, quantity(number)] = tile


def state_parts(ref, first, total, parts, pitch=3):
    return [
        tuple(
            ref[(pitch * place + part) * SUBLANES : (pitch * place + part + 1) * SUBLANES, :]
            for part in range(parts)
        )
        for place in range(first, first + total)
    ]


def message_slots(refs, height, pitch, quantity_rows, skips):
    blocks = [(ref, start) for ref in refs for start in range(0, ref.shape[0], height)]
    slots = []
    for (ref, start), skip in zip(blocks, skips):
        rows = [start + quantity * pitch + skip for quantity in range(QUANTITIES)]
        slots.append(tuple(ref[row : row + quantity_rows, :] for row in rows))
    return slots


def quantity(number):
    return slice(number * LANES, (number + 1) * LANES)


def put_traded(ref, row, rows, number, value):
    ref[(row + rows // 2) % rows : (row + rows // 2) % rows + value.shape[0], quantity(number)] = value


def along_line(bound, halves, rows):
    value = jnp.broadcast_to(bound, (SUBLANES, rows))
    lane = lax.broadcasted_iota(jnp.int32, value.shape, 1)
    for step in doubling(halves):
        value = jnp.where((lane & step) != 0, behind(value, step, 1), value)
    return value[0:1, :]


def x_back_kernel(halves, axis, order, pieces, *refs):
    lines_refs, sums_refs, rows_refs = (refs[pieces + 2 * pair : pieces + 2 * pair + 2] for pair in range(3))
    last_ref, kept_ref, sent_ref, values_ref = refs[pieces + 6 :]
    slots = message_slots([*refs[:pieces], last_ref], SUBLANES, 1, 1, [0] * len(order))
    slots = [slots[order.index(place)] for place in range(len(order))]
    bounds = ring_bounds(slots, lax.axis_index(axis))
    rows = values_ref.shape[0]

    height = 2 * halves
    first = lax.broadcasted_iota(jnp.int32, (SUBLANES, LANES), 0) < halves

    def put(number, own, other):
        kept_ref[:, quantity(number)] = jnp.where(first, own, other)[0:height, :]
        sent_ref[:, quantity(number)] = jnp.where(first, other, own)[0:height, :]

    for number in range(3):
        put(number, *(ref[:, quantity(number)] for ref in rows_refs))
    sides = []
    for block in range(2):
        lines_ref, sums_ref = lines_refs[block], sums_refs[block]
        before, after = (along_line(bound, halves, rows) for bound in bounds[block])
        values = lines_ref[0:LANES, :] + lines_ref[LANES : 2 * LANES, :] * before + lines_ref[2 * LANES :, :] * after
        values = values.T
        if block == 0:
            values_ref[...] = values
        for end in range(2):
            parts = (values * sums_ref[end * rows : (end + 1) * rows, :]).reshape(-1, SUBLANES, LANES)
            side = jnp.sum(parts, axis=0)
            for step in doubling(SUBLANES // halves):
                side = side + behind(side, step * halves, 0)
            sides.append(side)
    for end in range(2):
        put(3 + end, sides[end], sides[2 + end])


def y_given_kernel(halves, block_ref, values_ref, state_ref, given_ref):
    rows = values_ref.shape[0]
    stride = rows // SUBLANES
    total = stride // halves - 1 + len(y_rolls())
    nothing = jnp.zeros((SUBLANES, LANES), jnp.float32)
    for half in range(halves):
        places = [pl.ds(index, SUBLANES, stride=stride) for index in range(half, stride, halves)]
        sides = [(None, block_ref[place, :] * values_ref[place, :]) for place in places]
        nodes = state_parts(state_ref, half * total, total, 3)
        _, givens = tree_sides(sides, y_rolls(), nodes)
        for place, value in zip(places, tree_values(nothing, nothing, y_rolls(), len(places), nodes, givens)):
            given_ref[place, :] = value


def read_message(ref):
    return [ref[:, quantity(number)] for number in range(QUANTITIES)]


def join_by_bit(own, other, upper):
    left = [choose(upper, b, a) for a, b in zip(own, other)]
    right = [choose(upper, a, b) for a, b in zip(own, other)]
    coefs, node = join_coefs(left[:3], right[:3])
    sides, given = join_sides(left[3:], right[3:], node)
    return coefs + sides, (node[0], node[1], given)


def own_bit(axis, bit):
    return ((lax.axis_index(axis) >> bit) & 1) == 1


def y_join_kernel(axis, bit, own_ref, other_ref, kept_ref, sent_ref, path_ref):
    joined, path = join_by_bit(read_message(own_ref), read_message(other_ref), own_bit(axis, bit))
    rows = own_ref.shape[0]
    for number, value in enumerate(joined):
        kept_ref[:, quantity(number)] = value
        for row in (0, rows // 2):
            put_traded(sent_ref, row, rows, number, value[row : row + rows // 2, :])
    for number, value in enumerate(path):
        path_ref[:, quantity(number)] = value


def y_back_kernel(halves, axis, rounds, own_ref, other_ref, *refs):
    path_refs = refs[: rounds - 1]
    given_ref, spread_ref, out_ref = refs[rounds - 1 :]
    rows = out_ref.shape[0]
    joined, path = join_by_bit(read_message(own_ref), read_message(other_ref), own_bit(axis, rounds - 1))
    _, head, tail, side_head, side_tail = joined
    before = after = (side_head + side_tail) * inverse(head + tail)
    paths = [[ref[:, quantity(number)] for number in range(3)] for ref in path_refs] + [path]
    for bit in reversed(range(rounds)):
        node = paths[bit]
        middle = middle_value(node, node[2], before, after)
        upper = own_bit(axis, bit)
        before = jnp.where(upper, middle, before)
        after = jnp.where(upper, after, middle)
    sublane = lax.broadcasted_iota(jnp.int32, (SUBLANES, LANES), 0) % halves
    ends = []
    for end in (before, after):
        value = jnp.broadcast_to(end[0:1, :], (SUBLANES, LANES))
        for half in range(1, halves):
            value = jnp.where(sublane == half, jnp.broadcast_to(end[half : half + 1, :], value.shape), value)
        ends.append(value)
    for start in range(0, rows, SUBLANES):
        part = slice(start, start + SUBLANES)
        late = slice(rows + start, rows + start + SUBLANES)
        out_ref[part, :] = given_ref[part, :] + spread_ref[part, :] * ends[0] + spread_ref[late, :] * ends[1]


def trade(value, x_step, y_step):
    width = lax.axis_size("yd")
    pairs = []
    for index in range(lax.axis_size("xg")):
        for line in range(width):
            pairs.append((index * width + line, (index ^ x_step) * width + (line ^ y_step)))
    return lax.ppermute(value, ("xg", "yd"), pairs)


def x_exchange(message, block):
    count = lax.axis_size("xg")
    held = message
    pieces = [message]
    order = [0]
    other_block = trade(block, 1, 0)
    for step in doubling(count // 2):
        received = trade(held, 2 * step + 1, 0)
        pieces.append(received)
        order += [place ^ (2 * step + 1) for place in order]
        if 4 * step < count:
            held = jnp.concatenate([held, received], axis=0)
    received = pieces[1] if len(pieces) == 2 else jnp.concatenate(pieces[1:], axis=0)
    pieces.append(trade(received, 1, 0))
    order += [place ^ 1 for place in order[1:]] + [1]
    return pieces, order, other_block


def y_exchange(kept, sent):
    rows = kept.shape[0]
    paths = []
    steps = doubling(lax.axis_size("yd"))
    for bit, step in enumerate(steps):
        received = trade(sent, 1, step)
        if bit < len(steps) - 1:
            kept, sent, path = kernel_call(
                functools.partial(y_join_kernel, "yd", bit),
                (kept, received),
                [held_f32(*kept.shape), f32(*kept.shape), held_f32(rows, 3 * LANES)],
                [],
            )
            paths.append(path)
    return [kept, received] + paths, len(steps)


def f32(*shape):
    return jax.ShapeDtypeStruct(shape, jnp.float32)


def held_f32(*shape):
    return VMEM(shape, jnp.float32)


def kernel_call(body, operands, outputs, scratch, space=VMEM, cost=500000):
    return pl.pallas_call(
        body,
        out_shape=outputs,
        in_specs=[pl.BlockSpec(memory_space=space)] * len(operands),
        out_specs=[pl.BlockSpec(memory_space=VMEM)] * len(outputs),
        scratch_shapes=scratch,
        cost_estimate=pl.CostEstimate(flops=cost, bytes_accessed=cost, transcendentals=0),
        compiler_params=pltpu.CompilerParams(vmem_limit_bytes=16 * 1024 * 1024),
    )(*operands)


def local(mobile, dispersion_x, dispersion_y, capacity, immobile, exchange_rates, rate_shares):
    shape = mobile.shape
    lines, width = shape[0] * shape[1], shape[2]
    zones = immobile.shape[0]
    halves = width // LANES
    rows = lines * halves
    assert rows == LANES

    def flat(values):
        return values.reshape(-1, LANES)

    mobile, dispersion_x, dispersion_y = flat(mobile), flat(dispersion_x), flat(dispersion_y)
    capacity, immobile = flat(capacity), flat(immobile)
    square = VMEM((rows, LANES), jnp.float32)
    x_nodes = LANES // SUBLANES - 1 + len(x_rolls(halves))
    y_nodes = halves * (rows // SUBLANES // halves - 1 + len(y_rolls()))
    message, block = kernel_call(
        functools.partial(x_forward_kernel, halves),
        tuple(
            pltpu.with_memory_space_constraint(value, pltpu.HBM)
            for value in (
                mobile, dispersion_x, dispersion_y, capacity, immobile, exchange_rates[None], rate_shares[None],
            )
        ),
        [f32(SUBLANES, rows), held_f32(2 * rows + (3 * x_nodes + 1) * SUBLANES, LANES)],
        [square] * 3
        + [VMEM((zones * rows, LANES), jnp.float32)]
        + [pltpu.SMEM((1, zones), jnp.float32)] * 2
        + [pltpu.SemaphoreType.DMA((7,))]
        + [square] * 3,
        pltpu.HBM,
    )
    def prepare(part, own):
        outputs = [held_f32(SUBLANES, 3 * LANES), held_f32(3 * LANES, rows), held_f32(2 * rows, LANES)]
        if own:
            outputs += [held_f32(3 * y_nodes * SUBLANES, LANES), held_f32(2 * rows, LANES)]
        else:
            outputs += [held_f32(SUBLANES, rows)]
        return kernel_call(functools.partial(prepare_kernel, halves, own), (part,), outputs, [], cost=10000000000)

    pieces, order, other_block = x_exchange(message, block)
    y_rows, lines_x, sums, y_state, spread = prepare(block, True)
    other_rows, other_lines, other_sums, other_message = prepare(other_block, False)
    kept, sent, values = kernel_call(
        functools.partial(x_back_kernel, halves, "xg", order, len(pieces)),
        (*pieces, lines_x, other_lines, sums, other_sums, y_rows, other_rows, other_message),
        [
            held_f32(2 * halves, QUANTITIES * LANES),
            f32(2 * halves, QUANTITIES * LANES),
            held_f32(rows, LANES),
        ],
        [],
    )
    (given,) = kernel_call(
        functools.partial(y_given_kernel, halves), (block, values, y_state), [held_f32(rows, LANES)], []
    )
    pieces, rounds = y_exchange(kept, sent)
    (updated,) = kernel_call(
        functools.partial(y_back_kernel, halves, "yd", rounds),
        (*pieces, given, spread),
        [f32(rows, LANES)],
        [],
    )
    return updated.reshape(shape)


def solution(mesh):
    field = P("yd", None, "xg")
    return jax.shard_map(
        local,
        mesh=mesh,
        in_specs=(field, field, field, field, P(None, "yd", None, "xg"), P(), P()),
        out_specs=field,
        check_vma=False,
    )
```

```python
import functools

import jax
import jax.numpy as jnp
from jax import lax
from jax.experimental import pallas as pl
from jax.experimental.pallas import tpu as pltpu
from jax.sharding import PartitionSpec as P

LANES = 128
SUBLANES = 8
QUANTITIES = 5
VMEM = pltpu.VMEM


def inverse(value):
    return 1.0 / value


def plus(first, second):
    if first is None:
        return second
    return first + second


def join_coefs(left, right):
    coupling_1, head_1, tail_1 = left
    coupling_2, head_2, tail_2 = right
    middle = plus(head_2, tail_1)
    inv = inverse(coupling_1 + coupling_2 + middle)
    weight_1 = coupling_1 * inv
    weight_2 = coupling_2 * inv
    joined = (coupling_1 * weight_2, plus(head_1, weight_1 * middle), tail_2 + weight_2 * middle)
    return joined, (weight_1, weight_2, inv)


def join_sides(left, right, node):
    head_1, tail_1 = left
    head_2, tail_2 = right
    weight_1, weight_2, inv = node
    side = plus(head_2, tail_1)
    joined = (plus(head_1, weight_1 * side), tail_2 + weight_2 * side)
    return joined, side * inv


def middle_value(node, given, before, after):
    return given + node[0] * before + node[1] * after


def ahead(value, step, axis):
    return pltpu.roll(value, value.shape[axis] - step, axis)


def behind(value, step, axis):
    return pltpu.roll(value, step, axis)


def doubling(count):
    steps = []
    step = 1
    while step < count:
        steps.append(step)
        step *= 2
    return steps


def tree_coefs(leaves, rolls):
    nodes = []
    level = leaves
    while len(level) > 1:
        following = []
        for index in range(0, len(level), 2):
            joined, node = join_coefs(level[index], level[index + 1])
            following.append(joined)
            nodes.append(node)
        level = following
    piece = level[0]
    for step, axis in rolls:
        piece, node = join_coefs(piece, tuple(ahead(part, step, axis) for part in piece))
        nodes.append(node)
    return piece, nodes


def tree_sides(leaves, rolls, nodes):
    givens = []
    level = leaves
    while len(level) > 1:
        following = []
        for index in range(0, len(level), 2):
            joined, given = join_sides(level[index], level[index + 1], nodes[len(givens)])
            following.append(joined)
            givens.append(given)
        level = following
    piece = level[0]
    for step, axis in rolls:
        other = tuple(ahead(part, step, axis) for part in piece)
        piece, given = join_sides(piece, other, nodes[len(givens)])
        givens.append(given)
    return piece, givens


def tree_values(before, after, rolls, count, nodes, givens):
    place = len(nodes)
    for step, axis in reversed(rolls):
        place -= 1
        middle = middle_value(nodes[place], givens[place], before, after)
        upper = (lax.broadcasted_iota(jnp.int32, middle.shape, axis) & step) != 0
        before = jnp.where(upper, behind(middle, step, axis), before)
        after = jnp.where(upper, behind(after, step, axis), middle)
    bounds = [before, after]
    while len(bounds) - 1 < count:
        width = len(bounds) - 1
        place -= width
        following = [bounds[0]]
        for index in range(width):
            following.append(
                middle_value(
                    nodes[place + index], givens[place + index], bounds[index], bounds[index + 1]
                )
            )
            following.append(bounds[index + 1])
        bounds = following
    return bounds[1:]


def choose(condition, first, second):
    if isinstance(condition, bool):
        return first if condition else second
    return jnp.where(condition, first, second)


def ring_bounds(slots, index):
    level = slots
    rounds = []
    bit = 0
    while len(level) > 1:
        upper = ((index >> bit) & 1) == 1
        following, nodes = [], []
        for place in range(0, len(level), 2):
            own, other = level[place], level[place + 1]
            left = [jnp.where(upper, b, a) for a, b in zip(own, other)]
            right = [jnp.where(upper, a, b) for a, b in zip(own, other)]
            coefs, node = join_coefs(left[:3], right[:3])
            sides, given = join_sides(left[3:], right[3:], node)
            nodes.append((node, given))
            following.append(coefs + sides)
        rounds.append((nodes, upper))
        level = following
        bit += 1
    _, head, tail, side_head, side_tail = level[0]
    last = (side_head + side_tail) * inverse(head + tail)
    bounds = [(last, last)]
    for nodes, upper in reversed(rounds):
        following = []
        for (node, given), (before, after) in zip(nodes, bounds):
            middle = middle_value(node, given, before, after)
            following.append((jnp.where(upper, middle, before), jnp.where(upper, after, middle)))
            following.append((jnp.where(upper, before, middle), jnp.where(upper, middle, after)))
        bounds = following
    return bounds


def capacity_weights(rates_ref, shares_ref):
    weights = []
    for zone in range(rates_ref.shape[1]):
        rate = jnp.full((SUBLANES, LANES), rates_ref[0, zone], jnp.float32)
        share = jnp.full((SUBLANES, LANES), shares_ref[0, zone], jnp.float32)
        weights.append((share * rate / (1.0 + rate))[0:1, :])
    return weights


def flipped(value):
    rows = value.shape[1]
    row, column = (lax.broadcasted_iota(jnp.int32, (rows, rows), axis) for axis in range(2))
    unit = (row == column).astype(jnp.bfloat16)
    total = None
    for _ in range(3):
        part = value.astype(jnp.bfloat16)
        value = value - part.astype(jnp.float32)
        moved = lax.dot_general(unit, part, (((1,), (1,)), ((), ())), preferred_element_type=jnp.float32)
        total = plus(total, moved)
    return total


def strided(ref, start, size, stride):
    return ref[pl.ds(start, size, stride=stride), :]


def x_rolls(halves):
    return [(step, 0) for step in doubling(SUBLANES)] + [(step, 1) for step in doubling(halves)]


def y_rolls():
    return [(step, 0) for step in doubling(SUBLANES)]


def x_forward_kernel(
    halves, mobile_hbm, faces_hbm, across_hbm, capacity_hbm, immobile_hbm, rates_hbm, shares_hbm,
    message_ref, block_ref,
    mobile_ref, faces_ref, capacity_ref, immobile_ref, rates_ref, shares_ref, arrived,
    faces_t, storage_t, source_t,
):
    rows = mobile_ref.shape[0]
    pairs = (
        (rates_hbm, rates_ref), (shares_hbm, shares_ref), (capacity_hbm, capacity_ref), (faces_hbm, faces_ref),
        (immobile_hbm, immobile_ref), (mobile_hbm, mobile_ref), (across_hbm, block_ref.at[rows : 2 * rows, :]),
    )
    copies = [pltpu.make_async_copy(pair[0], pair[1], arrived.at[place]) for place, pair in enumerate(pairs)]
    for place, copy in enumerate(copies):
        copy.start(priority=int(place in (4, 6)))
    stride = LANES // SUBLANES
    for copy in copies[:3]:
        copy.wait()
    weights = capacity_weights(rates_ref, shares_ref)
    capacity = capacity_ref[...]
    storage = 1.0 + capacity * sum(weights[1:], weights[0])
    block_ref[0:rows, :] = storage
    storage_t[...] = storage.T
    copies[3].wait()
    faces_t[...] = faces_ref[...].T
    copies[4].wait()
    total = None
    for zone, weight in enumerate(weights):
        total = plus(total, weight * immobile_ref[zone * rows : (zone + 1) * rows, :])
    copies[5].wait()
    source_t[...] = flipped(mobile_ref[...] + capacity * total)
    coefs, sides = [], []
    for index in range(stride):
        coefs.append((strided(faces_t, index, SUBLANES, stride), None, strided(storage_t, index, SUBLANES, stride)))
        sides.append((None, strided(source_t, index, SUBLANES, stride)))
    rolls = x_rolls(halves)
    piece, nodes = tree_coefs(coefs, rolls)
    side, givens = tree_sides(sides, rolls, nodes)
    start = 2 * rows
    for node, given in zip(nodes, givens):
        for part in (node[0], node[1], given):
            block_ref[start : start + SUBLANES, :] = part
            start += SUBLANES
    for row, value in enumerate(piece + side):
        message_ref[row : row + 1, :] = value[0:1, :]
        block_ref[start + row : start + row + 1, :] = value[0:1, :]
    copies[6].wait()


def ends_responses(shape):
    one, nothing = jnp.ones(shape, jnp.float32), jnp.zeros(shape, jnp.float32)
    return ((one, nothing), (nothing, one))


def prepare_kernel(halves, own, block_ref, rows_ref, lines_ref, sums_ref, *extra_refs):
    rows = lines_ref.shape[1]
    stride = LANES // SUBLANES
    rolls = x_rolls(halves)
    total = stride - 1 + len(rolls)
    nodes = state_parts(block_ref.at[2 * rows :, :], 0, total, 3)
    own_refs = extra_refs if own else ()
    if not own:
        extra_refs[0][...] = block_ref[-SUBLANES:, :]
    nothing = jnp.zeros((SUBLANES, rows), jnp.float32)
    cases = [((nothing, nothing), [node[2] for node in nodes])]
    cases += [(ends, [0.0] * total) for ends in ends_responses((SUBLANES, rows))]
    for case, (ends, givens) in enumerate(cases):
        for index, value in enumerate(tree_values(*ends, rolls, stride, nodes, givens)):
            lines_ref[pl.ds(case * LANES + index, SUBLANES, stride=stride), :] = value
    stride = rows // SUBLANES
    start = 0
    sublane = lax.broadcasted_iota(jnp.int32, (SUBLANES, LANES), 0) % halves
    tiles = None
    for half in range(halves):
        storage = [strided(block_ref, index, SUBLANES, stride) for index in range(half, stride, halves)]
        faces = [strided(block_ref, rows + index, SUBLANES, stride) for index in range(half, stride, halves)]
        piece, nodes = tree_coefs([(face, None, held) for face, held in zip(faces, storage)], y_rolls())
        for part in [part for node in nodes for part in node] if own_refs else []:
            own_refs[0][start : start + SUBLANES, :] = part
            start += SUBLANES
        values = [jnp.broadcast_to(value[0:1, :], value.shape) for value in piece]
        tiles = [jnp.where(sublane == half, new, old) for new, old in zip(values, tiles or values)]
        for case, ends in enumerate(ends_responses((SUBLANES, LANES))):
            values = tree_values(*ends, y_rolls(), len(storage), nodes, [0.0] * len(nodes))
            for index, (value, held) in enumerate(zip(values, storage)):
                place = pl.ds(case * rows + index * halves + half, SUBLANES, stride=stride)
                sums_ref[place, :] = value * held
                if own_refs:
                    own_refs[1][place, :] = value
    for number, tile in enumerate(tiles):
        rows_ref[:, quantity(number)] = tile


def state_parts(ref, first, total, parts, pitch=3):
    return [
        tuple(
            ref[(pitch * place + part) * SUBLANES : (pitch * place + part + 1) * SUBLANES, :]
            for part in range(parts)
        )
        for place in range(first, first + total)
    ]


def message_slots(refs, height, pitch, quantity_rows, skips):
    blocks = [(ref, start) for ref in refs for start in range(0, ref.shape[0], height)]
    slots = []
    for (ref, start), skip in zip(blocks, skips):
        rows = [start + quantity * pitch + skip for quantity in range(QUANTITIES)]
        slots.append(tuple(ref[row : row + quantity_rows, :] for row in rows))
    return slots


def quantity(number):
    return slice(number * LANES, (number + 1) * LANES)


def put_traded(ref, row, rows, number, value):
    ref[(row + rows // 2) % rows : (row + rows // 2) % rows + value.shape[0], quantity(number)] = value


def along_line(bound, halves, rows):
    value = jnp.broadcast_to(bound, (SUBLANES, rows))
    lane = lax.broadcasted_iota(jnp.int32, value.shape, 1)
    for step in doubling(halves):
        value = jnp.where((lane & step) != 0, behind(value, step, 1), value)
    return value[0:1, :]


def x_back_kernel(halves, axis, order, pieces, *refs):
    lines_refs, sums_refs, rows_refs = (refs[pieces + 2 * pair : pieces + 2 * pair + 2] for pair in range(3))
    last_ref, kept_ref, sent_ref, values_ref = refs[pieces + 6 :]
    slots = message_slots([*refs[:pieces], last_ref], SUBLANES, 1, 1, [0] * len(order))
    slots = [slots[order.index(place)] for place in range(len(order))]
    bounds = ring_bounds(slots, lax.axis_index(axis))
    rows = values_ref.shape[0]

    height = 2 * halves
    first = lax.broadcasted_iota(jnp.int32, (SUBLANES, LANES), 0) < halves

    def put(number, own, other):
        kept_ref[:, quantity(number)] = jnp.where(first, own, other)[0:height, :]
        sent_ref[:, quantity(number)] = jnp.where(first, other, own)[0:height, :]

    for number in range(3):
        put(number, *(ref[:, quantity(number)] for ref in rows_refs))
    sides = []
    for block in range(2):
        lines_ref, sums_ref = lines_refs[block], sums_refs[block]
        before, after = (along_line(bound, halves, rows) for bound in bounds[block])
        values = lines_ref[0:LANES, :] + lines_ref[LANES : 2 * LANES, :] * before + lines_ref[2 * LANES :, :] * after
        values = flipped(values)
        if block == 0:
            values_ref[...] = values
        for end in range(2):
            parts = (values * sums_ref[end * rows : (end + 1) * rows, :]).reshape(-1, SUBLANES, LANES)
            side = jnp.sum(parts, axis=0)
            for step in doubling(SUBLANES // halves):
                side = side + behind(side, step * halves, 0)
            sides.append(side)
    for end in range(2):
        put(3 + end, sides[end], sides[2 + end])


def y_given_kernel(halves, block_ref, values_ref, state_ref, given_ref):
    rows = values_ref.shape[0]
    stride = rows // SUBLANES
    total = stride // halves - 1 + len(y_rolls())
    nothing = jnp.zeros((SUBLANES, LANES), jnp.float32)
    for half in range(halves):
        places = [pl.ds(index, SUBLANES, stride=stride) for index in range(half, stride, halves)]
        sides = [(None, block_ref[place, :] * values_ref[place, :]) for place in places]
        nodes = state_parts(state_ref, half * total, total, 3)
        _, givens = tree_sides(sides, y_rolls(), nodes)
        for place, value in zip(places, tree_values(nothing, nothing, y_rolls(), len(places), nodes, givens)):
            given_ref[place, :] = value


def read_message(ref):
    return [ref[:, quantity(number)] for number in range(QUANTITIES)]


def join_by_bit(own, other, upper):
    left = [choose(upper, b, a) for a, b in zip(own, other)]
    right = [choose(upper, a, b) for a, b in zip(own, other)]
    coefs, node = join_coefs(left[:3], right[:3])
    sides, given = join_sides(left[3:], right[3:], node)
    return coefs + sides, (node[0], node[1], given)


def own_bit(axis, bit):
    return ((lax.axis_index(axis) >> bit) & 1) == 1


def y_join_kernel(axis, bit, own_ref, other_ref, kept_ref, sent_ref, path_ref):
    joined, path = join_by_bit(read_message(own_ref), read_message(other_ref), own_bit(axis, bit))
    rows = own_ref.shape[0]
    for number, value in enumerate(joined):
        kept_ref[:, quantity(number)] = value
        for row in (0, rows // 2):
            put_traded(sent_ref, row, rows, number, value[row : row + rows // 2, :])
    for number, value in enumerate(path):
        path_ref[:, quantity(number)] = value


def y_back_kernel(halves, axis, rounds, own_ref, other_ref, *refs):
    path_refs = refs[: rounds - 1]
    given_ref, spread_ref, out_ref = refs[rounds - 1 :]
    rows = out_ref.shape[0]
    joined, path = join_by_bit(read_message(own_ref), read_message(other_ref), own_bit(axis, rounds - 1))
    _, head, tail, side_head, side_tail = joined
    before = after = (side_head + side_tail) * inverse(head + tail)
    paths = [[ref[:, quantity(number)] for number in range(3)] for ref in path_refs] + [path]
    for bit in reversed(range(rounds)):
        node = paths[bit]
        middle = middle_value(node, node[2], before, after)
        upper = own_bit(axis, bit)
        before = jnp.where(upper, middle, before)
        after = jnp.where(upper, after, middle)
    sublane = lax.broadcasted_iota(jnp.int32, (SUBLANES, LANES), 0) % halves
    ends = []
    for end in (before, after):
        value = jnp.broadcast_to(end[0:1, :], (SUBLANES, LANES))
        for half in range(1, halves):
            value = jnp.where(sublane == half, jnp.broadcast_to(end[half : half + 1, :], value.shape), value)
        ends.append(value)
    for start in range(0, rows, SUBLANES):
        part = slice(start, start + SUBLANES)
        late = slice(rows + start, rows + start + SUBLANES)
        out_ref[part, :] = given_ref[part, :] + spread_ref[part, :] * ends[0] + spread_ref[late, :] * ends[1]


def trade(value, x_step, y_step):
    width = lax.axis_size("yd")
    pairs = []
    for index in range(lax.axis_size("xg")):
        for line in range(width):
            pairs.append((index * width + line, (index ^ x_step) * width + (line ^ y_step)))
    return lax.ppermute(value, ("xg", "yd"), pairs)


def x_exchange(message, block):
    count = lax.axis_size("xg")
    held = message
    pieces = [message]
    order = [0]
    other_block = trade(block, 1, 0)
    for step in doubling(count // 2):
        received = trade(held, 2 * step + 1, 0)
        pieces.append(received)
        order += [place ^ (2 * step + 1) for place in order]
        if 4 * step < count:
            held = jnp.concatenate([held, received], axis=0)
    received = pieces[1] if len(pieces) == 2 else jnp.concatenate(pieces[1:], axis=0)
    pieces.append(trade(received, 1, 0))
    order += [place ^ 1 for place in order[1:]] + [1]
    return pieces, order, other_block


def y_exchange(kept, sent):
    rows = kept.shape[0]
    paths = []
    steps = doubling(lax.axis_size("yd"))
    for bit, step in enumerate(steps):
        received = trade(sent, 1, step)
        if bit < len(steps) - 1:
            kept, sent, path = kernel_call(
                functools.partial(y_join_kernel, "yd", bit),
                (kept, received),
                [held_f32(*kept.shape), f32(*kept.shape), held_f32(rows, 3 * LANES)],
                [],
            )
            paths.append(path)
    return [kept, received] + paths, len(steps)


def f32(*shape):
    return jax.ShapeDtypeStruct(shape, jnp.float32)


def held_f32(*shape):
    return VMEM(shape, jnp.float32)


def kernel_call(body, operands, outputs, scratch, space=VMEM, cost=500000):
    return pl.pallas_call(
        body,
        out_shape=outputs,
        in_specs=[pl.BlockSpec(memory_space=space)] * len(operands),
        out_specs=[pl.BlockSpec(memory_space=VMEM)] * len(outputs),
        scratch_shapes=scratch,
        cost_estimate=pl.CostEstimate(flops=cost, bytes_accessed=cost, transcendentals=0),
        compiler_params=pltpu.CompilerParams(vmem_limit_bytes=16 * 1024 * 1024),
    )(*operands)


def local(mobile, dispersion_x, dispersion_y, capacity, immobile, exchange_rates, rate_shares):
    shape = mobile.shape
    lines, width = shape[0] * shape[1], shape[2]
    zones = immobile.shape[0]
    halves = width // LANES
    rows = lines * halves
    assert rows == LANES

    def flat(values):
        return values.reshape(-1, LANES)

    mobile, dispersion_x, dispersion_y = flat(mobile), flat(dispersion_x), flat(dispersion_y)
    capacity, immobile = flat(capacity), flat(immobile)
    square = VMEM((rows, LANES), jnp.float32)
    x_nodes = LANES // SUBLANES - 1 + len(x_rolls(halves))
    y_nodes = halves * (rows // SUBLANES // halves - 1 + len(y_rolls()))
    message, block = kernel_call(
        functools.partial(x_forward_kernel, halves),
        tuple(
            pltpu.with_memory_space_constraint(value, pltpu.HBM)
            for value in (
                mobile, dispersion_x, dispersion_y, capacity, immobile, exchange_rates[None], rate_shares[None],
            )
        ),
        [f32(SUBLANES, rows), held_f32(2 * rows + (3 * x_nodes + 1) * SUBLANES, LANES)],
        [square] * 3
        + [VMEM((zones * rows, LANES), jnp.float32)]
        + [pltpu.SMEM((1, zones), jnp.float32)] * 2
        + [pltpu.SemaphoreType.DMA((7,))]
        + [square] * 3,
        pltpu.HBM,
    )
    def prepare(part, own):
        outputs = [held_f32(SUBLANES, 3 * LANES), held_f32(3 * LANES, rows), held_f32(2 * rows, LANES)]
        if own:
            outputs += [held_f32(3 * y_nodes * SUBLANES, LANES), held_f32(2 * rows, LANES)]
        else:
            outputs += [held_f32(SUBLANES, rows)]
        return kernel_call(functools.partial(prepare_kernel, halves, own), (part,), outputs, [], cost=10000000000)

    pieces, order, other_block = x_exchange(message, block)
    y_rows, lines_x, sums, y_state, spread = prepare(block, True)
    other_rows, other_lines, other_sums, other_message = prepare(other_block, False)
    kept, sent, values = kernel_call(
        functools.partial(x_back_kernel, halves, "xg", order, len(pieces)),
        (*pieces, lines_x, other_lines, sums, other_sums, y_rows, other_rows, other_message),
        [
            held_f32(2 * halves, QUANTITIES * LANES),
            f32(2 * halves, QUANTITIES * LANES),
            held_f32(rows, LANES),
        ],
        [],
    )
    (given,) = kernel_call(
        functools.partial(y_given_kernel, halves), (block, values, y_state), [held_f32(rows, LANES)], []
    )
    pieces, rounds = y_exchange(kept, sent)
    (updated,) = kernel_call(
        functools.partial(y_back_kernel, halves, "yd", rounds),
        (*pieces, given, spread),
        [f32(rows, LANES)],
        [],
    )
    return updated.reshape(shape)


def solution(mesh):
    field = P("yd", None, "xg")
    return jax.shard_map(
        local,
        mesh=mesh,
        in_specs=(field, field, field, field, P(None, "yd", None, "xg"), P(), P()),
        out_specs=field,
        check_vma=False,
    )
```

```python
import functools

import jax
import jax.numpy as jnp
from jax import lax
from jax.experimental import pallas as pl
from jax.experimental.pallas import tpu as pltpu
from jax.sharding import PartitionSpec as P

LANES = 128
SUBLANES = 8
QUANTITIES = 5
VMEM = pltpu.VMEM


def inverse(value):
    return 1.0 / value


def plus(first, second):
    if first is None:
        return second
    return first + second


def join_coefs(left, right):
    coupling_1, head_1, tail_1 = left
    coupling_2, head_2, tail_2 = right
    middle = plus(head_2, tail_1)
    inv = inverse(coupling_1 + coupling_2 + middle)
    weight_1 = coupling_1 * inv
    weight_2 = coupling_2 * inv
    joined = (coupling_1 * weight_2, plus(head_1, weight_1 * middle), tail_2 + weight_2 * middle)
    return joined, (weight_1, weight_2, inv)


def join_sides(left, right, node):
    head_1, tail_1 = left
    head_2, tail_2 = right
    weight_1, weight_2, inv = node
    side = plus(head_2, tail_1)
    joined = (plus(head_1, weight_1 * side), tail_2 + weight_2 * side)
    return joined, side * inv


def middle_value(node, given, before, after):
    return given + node[0] * before + node[1] * after


def ahead(value, step, axis):
    return pltpu.roll(value, value.shape[axis] - step, axis)


def behind(value, step, axis):
    return pltpu.roll(value, step, axis)


def doubling(count):
    steps = []
    step = 1
    while step < count:
        steps.append(step)
        step *= 2
    return steps


def tree_coefs(leaves, rolls):
    nodes = []
    level = leaves
    while len(level) > 1:
        following = []
        for index in range(0, len(level), 2):
            joined, node = join_coefs(level[index], level[index + 1])
            following.append(joined)
            nodes.append(node)
        level = following
    piece = level[0]
    for step, axis in rolls:
        piece, node = join_coefs(piece, tuple(ahead(part, step, axis) for part in piece))
        nodes.append(node)
    return piece, nodes


def tree_sides(leaves, rolls, nodes):
    givens = []
    level = leaves
    while len(level) > 1:
        following = []
        for index in range(0, len(level), 2):
            joined, given = join_sides(level[index], level[index + 1], nodes[len(givens)])
            following.append(joined)
            givens.append(given)
        level = following
    piece = level[0]
    for step, axis in rolls:
        other = tuple(ahead(part, step, axis) for part in piece)
        piece, given = join_sides(piece, other, nodes[len(givens)])
        givens.append(given)
    return piece, givens


def tree_values(before, after, rolls, count, nodes, givens):
    place = len(nodes)
    for step, axis in reversed(rolls):
        place -= 1
        middle = middle_value(nodes[place], givens[place], before, after)
        upper = (lax.broadcasted_iota(jnp.int32, middle.shape, axis) & step) != 0
        before = jnp.where(upper, behind(middle, step, axis), before)
        after = jnp.where(upper, behind(after, step, axis), middle)
    bounds = [before, after]
    while len(bounds) - 1 < count:
        width = len(bounds) - 1
        place -= width
        following = [bounds[0]]
        for index in range(width):
            following.append(
                middle_value(
                    nodes[place + index], givens[place + index], bounds[index], bounds[index + 1]
                )
            )
            following.append(bounds[index + 1])
        bounds = following
    return bounds[1:]


def choose(condition, first, second):
    if isinstance(condition, bool):
        return first if condition else second
    return jnp.where(condition, first, second)


def ring_bounds(slots, index):
    level = slots
    rounds = []
    bit = 0
    while len(level) > 1:
        upper = ((index >> bit) & 1) == 1
        following, nodes = [], []
        for place in range(0, len(level), 2):
            own, other = level[place], level[place + 1]
            left = [jnp.where(upper, b, a) for a, b in zip(own, other)]
            right = [jnp.where(upper, a, b) for a, b in zip(own, other)]
            coefs, node = join_coefs(left[:3], right[:3])
            sides, given = join_sides(left[3:], right[3:], node)
            nodes.append((node, given))
            following.append(coefs + sides)
        rounds.append((nodes, upper))
        level = following
        bit += 1
    _, head, tail, side_head, side_tail = level[0]
    last = (side_head + side_tail) * inverse(head + tail)
    bounds = [(last, last)]
    for nodes, upper in reversed(rounds):
        following = []
        for (node, given), (before, after) in zip(nodes, bounds):
            middle = middle_value(node, given, before, after)
            following.append((jnp.where(upper, middle, before), jnp.where(upper, after, middle)))
            following.append((jnp.where(upper, before, middle), jnp.where(upper, middle, after)))
        bounds = following
    return bounds


def capacity_weights(rates_ref, shares_ref):
    weights = []
    for zone in range(rates_ref.shape[1]):
        rate = jnp.full((SUBLANES, LANES), rates_ref[0, zone], jnp.float32)
        share = jnp.full((SUBLANES, LANES), shares_ref[0, zone], jnp.float32)
        weights.append((share * rate / (1.0 + rate))[0:1, :])
    return weights


def strided(ref, start, size, stride):
    return ref[pl.ds(start, size, stride=stride), :]


def x_rolls(halves):
    return [(step, 0) for step in doubling(SUBLANES)] + [(step, 1) for step in doubling(halves)]


def y_rolls():
    return [(step, 0) for step in doubling(SUBLANES)]


def x_forward_kernel(
    halves, mobile_hbm, faces_hbm, across_hbm, capacity_hbm, immobile_hbm, rates_hbm, shares_hbm,
    message_ref, block_ref,
    mobile_ref, faces_ref, capacity_ref, immobile_ref, rates_ref, shares_ref, arrived,
    faces_t, storage_t, source_t,
):
    rows = mobile_ref.shape[0]
    pairs = (
        (rates_hbm, rates_ref), (shares_hbm, shares_ref), (capacity_hbm, capacity_ref), (faces_hbm, faces_ref),
        (immobile_hbm, immobile_ref), (mobile_hbm, mobile_ref), (across_hbm, block_ref.at[rows : 2 * rows, :]),
    )
    copies = [pltpu.make_async_copy(pair[0], pair[1], arrived.at[place]) for place, pair in enumerate(pairs)]
    for place, copy in enumerate(copies):
        copy.start(priority=int(place in (4, 6)))
    stride = LANES // SUBLANES
    for copy in copies[:6]:
        copy.wait()
    weights = capacity_weights(rates_ref, shares_ref)
    capacity = capacity_ref[...]
    storage = 1.0 + capacity * sum(weights[1:], weights[0])
    storage_t[...] = storage.T
    faces_t[...] = faces_ref[...].T
    total = None
    for zone, weight in enumerate(weights):
        total = plus(total, weight * immobile_ref[zone * rows : (zone + 1) * rows, :])
    source_t[...] = (mobile_ref[...] + capacity * total).T
    block_ref[0:rows, :] = storage
    coefs, sides = [], []
    for index in range(stride):
        coefs.append((strided(faces_t, index, SUBLANES, stride), None, strided(storage_t, index, SUBLANES, stride)))
        sides.append((None, strided(source_t, index, SUBLANES, stride)))
    rolls = x_rolls(halves)
    piece, nodes = tree_coefs(coefs, rolls)
    side, givens = tree_sides(sides, rolls, nodes)
    start = 2 * rows
    for node, given in zip(nodes, givens):
        for part in (node[0], node[1], given):
            block_ref[start : start + SUBLANES, :] = part
            start += SUBLANES
    for row, value in enumerate(piece + side):
        message_ref[row : row + 1, :] = value[0:1, :]
        block_ref[start + row : start + row + 1, :] = value[0:1, :]
    copies[6].wait()


def ends_responses(shape):
    one, nothing = jnp.ones(shape, jnp.float32), jnp.zeros(shape, jnp.float32)
    return ((one, nothing), (nothing, one))


def prepare_kernel(halves, own, block_ref, rows_ref, lines_ref, sums_ref, *extra_refs):
    rows = lines_ref.shape[1]
    stride = LANES // SUBLANES
    rolls = x_rolls(halves)
    total = stride - 1 + len(rolls)
    nodes = state_parts(block_ref.at[2 * rows :, :], 0, total, 3)
    own_refs = extra_refs if own else ()
    if not own:
        extra_refs[0][...] = block_ref[-SUBLANES:, :]
    nothing = jnp.zeros((SUBLANES, rows), jnp.float32)
    cases = [((nothing, nothing), [node[2] for node in nodes])]
    cases += [(ends, [0.0] * total) for ends in ends_responses((SUBLANES, rows))]
    for case, (ends, givens) in enumerate(cases):
        for index, value in enumerate(tree_values(*ends, rolls, stride, nodes, givens)):
            lines_ref[pl.ds(case * LANES + index, SUBLANES, stride=stride), :] = value
    stride = rows // SUBLANES
    start = 0
    sublane = lax.broadcasted_iota(jnp.int32, (SUBLANES, LANES), 0) % halves
    tiles = None
    for half in range(halves):
        storage = [strided(block_ref, index, SUBLANES, stride) for index in range(half, stride, halves)]
        faces = [strided(block_ref, rows + index, SUBLANES, stride) for index in range(half, stride, halves)]
        piece, nodes = tree_coefs([(face, None, held) for face, held in zip(faces, storage)], y_rolls())
        for part in [part for node in nodes for part in node] if own_refs else []:
            own_refs[0][start : start + SUBLANES, :] = part
            start += SUBLANES
        values = [jnp.broadcast_to(value[0:1, :], value.shape) for value in piece]
        tiles = [jnp.where(sublane == half, new, old) for new, old in zip(values, tiles or values)]
        for case, ends in enumerate(ends_responses((SUBLANES, LANES))):
            values = tree_values(*ends, y_rolls(), len(storage), nodes, [0.0] * len(nodes))
            for index, (value, held) in enumerate(zip(values, storage)):
                place = pl.ds(case * rows + index * halves + half, SUBLANES, stride=stride)
                sums_ref[place, :] = value * held
                if own_refs:
                    own_refs[1][place, :] = value
    for number, tile in enumerate(tiles):
        rows_ref[:, quantity(number)] = tile


def state_parts(ref, first, total, parts, pitch=3):
    return [
        tuple(
            ref[(pitch * place + part) * SUBLANES : (pitch * place + part + 1) * SUBLANES, :]
            for part in range(parts)
        )
        for place in range(first, first + total)
    ]


def message_slots(refs, height, pitch, quantity_rows, skips):
    blocks = [(ref, start) for ref in refs for start in range(0, ref.shape[0], height)]
    slots = []
    for (ref, start), skip in zip(blocks, skips):
        rows = [start + quantity * pitch + skip for quantity in range(QUANTITIES)]
        slots.append(tuple(ref[row : row + quantity_rows, :] for row in rows))
    return slots


def quantity(number):
    return slice(number * LANES, (number + 1) * LANES)


def put_traded(ref, row, rows, number, value):
    ref[(row + rows // 2) % rows : (row + rows // 2) % rows + value.shape[0], quantity(number)] = value


def along_line(bound, halves, rows):
    value = jnp.broadcast_to(bound, (SUBLANES, rows))
    lane = lax.broadcasted_iota(jnp.int32, value.shape, 1)
    for step in doubling(halves):
        value = jnp.where((lane & step) != 0, behind(value, step, 1), value)
    return value[0:1, :]


def x_back_kernel(halves, axis, order, pieces, *refs):
    lines_refs, sums_refs, rows_refs = (refs[pieces + 2 * pair : pieces + 2 * pair + 2] for pair in range(3))
    last_ref, kept_ref, sent_ref, values_ref = refs[pieces + 6 :]
    slots = message_slots([*refs[:pieces], last_ref], SUBLANES, 1, 1, [0] * len(order))
    slots = [slots[order.index(place)] for place in range(len(order))]
    bounds = ring_bounds(slots, lax.axis_index(axis))
    rows = values_ref.shape[0]

    height = 2 * halves
    first = lax.broadcasted_iota(jnp.int32, (SUBLANES, LANES), 0) < halves

    def put(number, own, other):
        kept_ref[:, quantity(number)] = jnp.where(first, own, other)[0:height, :]
        sent_ref[:, quantity(number)] = jnp.where(first, other, own)[0:height, :]

    for number in range(3):
        put(number, *(ref[:, quantity(number)] for ref in rows_refs))
    sides = []
    for block in range(2):
        lines_ref, sums_ref = lines_refs[block], sums_refs[block]
        before, after = (along_line(bound, halves, rows) for bound in bounds[block])
        values = lines_ref[0:LANES, :] + lines_ref[LANES : 2 * LANES, :] * before + lines_ref[2 * LANES :, :] * after
        values = values.T
        if block == 0:
            values_ref[...] = values
        for end in range(2):
            parts = (values * sums_ref[end * rows : (end + 1) * rows, :]).reshape(-1, SUBLANES, LANES)
            side = jnp.sum(parts, axis=0)
            for step in doubling(SUBLANES // halves):
                side = side + behind(side, step * halves, 0)
            sides.append(side)
    for end in range(2):
        put(3 + end, sides[end], sides[2 + end])


def y_given_kernel(halves, block_ref, values_ref, state_ref, given_ref):
    rows = values_ref.shape[0]
    stride = rows // SUBLANES
    total = stride // halves - 1 + len(y_rolls())
    nothing = jnp.zeros((SUBLANES, LANES), jnp.float32)
    for half in range(halves):
        places = [pl.ds(index, SUBLANES, stride=stride) for index in range(half, stride, halves)]
        sides = [(None, block_ref[place, :] * values_ref[place, :]) for place in places]
        nodes = state_parts(state_ref, half * total, total, 3)
        _, givens = tree_sides(sides, y_rolls(), nodes)
        for place, value in zip(places, tree_values(nothing, nothing, y_rolls(), len(places), nodes, givens)):
            given_ref[place, :] = value


def read_message(ref):
    return [ref[:, quantity(number)] for number in range(QUANTITIES)]


def join_by_bit(own, other, upper):
    left = [choose(upper, b, a) for a, b in zip(own, other)]
    right = [choose(upper, a, b) for a, b in zip(own, other)]
    coefs, node = join_coefs(left[:3], right[:3])
    sides, given = join_sides(left[3:], right[3:], node)
    return coefs + sides, (node[0], node[1], given)


def own_bit(axis, bit):
    return ((lax.axis_index(axis) >> bit) & 1) == 1


def y_join_kernel(axis, bit, own_ref, other_ref, kept_ref, sent_ref, path_ref):
    joined, path = join_by_bit(read_message(own_ref), read_message(other_ref), own_bit(axis, bit))
    rows = own_ref.shape[0]
    for number, value in enumerate(joined):
        kept_ref[:, quantity(number)] = value
        for row in (0, rows // 2):
            put_traded(sent_ref, row, rows, number, value[row : row + rows // 2, :])
    for number, value in enumerate(path):
        path_ref[:, quantity(number)] = value


def y_back_kernel(halves, axis, rounds, own_ref, other_ref, *refs):
    path_refs = refs[: rounds - 1]
    given_ref, spread_ref, out_ref = refs[rounds - 1 :]
    rows = out_ref.shape[0]
    joined, path = join_by_bit(read_message(own_ref), read_message(other_ref), own_bit(axis, rounds - 1))
    _, head, tail, side_head, side_tail = joined
    before = after = (side_head + side_tail) * inverse(head + tail)
    paths = [[ref[:, quantity(number)] for number in range(3)] for ref in path_refs] + [path]
    for bit in reversed(range(rounds)):
        node = paths[bit]
        middle = middle_value(node, node[2], before, after)
        upper = own_bit(axis, bit)
        before = jnp.where(upper, middle, before)
        after = jnp.where(upper, after, middle)
    sublane = lax.broadcasted_iota(jnp.int32, (SUBLANES, LANES), 0) % halves
    ends = []
    for end in (before, after):
        value = jnp.broadcast_to(end[0:1, :], (SUBLANES, LANES))
        for half in range(1, halves):
            value = jnp.where(sublane == half, jnp.broadcast_to(end[half : half + 1, :], value.shape), value)
        ends.append(value)
    for start in range(0, rows, SUBLANES):
        part = slice(start, start + SUBLANES)
        late = slice(rows + start, rows + start + SUBLANES)
        out_ref[part, :] = given_ref[part, :] + spread_ref[part, :] * ends[0] + spread_ref[late, :] * ends[1]


def trade(value, x_step, y_step):
    width = lax.axis_size("yd")
    pairs = []
    for index in range(lax.axis_size("xg")):
        for line in range(width):
            pairs.append((index * width + line, (index ^ x_step) * width + (line ^ y_step)))
    return lax.ppermute(value, ("xg", "yd"), pairs)


def x_exchange(message, block):
    count = lax.axis_size("xg")
    held = message
    pieces = [message]
    order = [0]
    other_block = trade(block, 1, 0)
    for step in doubling(count // 2):
        received = trade(held, 2 * step + 1, 0)
        pieces.append(received)
        order += [place ^ (2 * step + 1) for place in order]
        if 4 * step < count:
            held = jnp.concatenate([held, received], axis=0)
    received = pieces[1] if len(pieces) == 2 else jnp.concatenate(pieces[1:], axis=0)
    pieces.append(trade(received, 1, 0))
    order += [place ^ 1 for place in order[1:]] + [1]
    return pieces, order, other_block


def y_exchange(kept, sent):
    rows = kept.shape[0]
    paths = []
    steps = doubling(lax.axis_size("yd"))
    for bit, step in enumerate(steps):
        received = trade(sent, 1, step)
        if bit < len(steps) - 1:
            kept, sent, path = kernel_call(
                functools.partial(y_join_kernel, "yd", bit),
                (kept, received),
                [held_f32(*kept.shape), f32(*kept.shape), held_f32(rows, 3 * LANES)],
                [],
            )
            paths.append(path)
    return [kept, received] + paths, len(steps)


def f32(*shape):
    return jax.ShapeDtypeStruct(shape, jnp.float32)


def held_f32(*shape):
    return VMEM(shape, jnp.float32)


def kernel_call(body, operands, outputs, scratch, space=VMEM, cost=500000):
    return pl.pallas_call(
        body,
        out_shape=outputs,
        in_specs=[pl.BlockSpec(memory_space=space)] * len(operands),
        out_specs=[pl.BlockSpec(memory_space=VMEM)] * len(outputs),
        scratch_shapes=scratch,
        cost_estimate=pl.CostEstimate(flops=cost, bytes_accessed=cost, transcendentals=0),
        compiler_params=pltpu.CompilerParams(vmem_limit_bytes=16 * 1024 * 1024),
    )(*operands)


def local(mobile, dispersion_x, dispersion_y, capacity, immobile, exchange_rates, rate_shares):
    shape = mobile.shape
    lines, width = shape[0] * shape[1], shape[2]
    zones = immobile.shape[0]
    halves = width // LANES
    rows = lines * halves
    assert rows == LANES

    def flat(values):
        return values.reshape(-1, LANES)

    mobile, dispersion_x, dispersion_y = flat(mobile), flat(dispersion_x), flat(dispersion_y)
    capacity, immobile = flat(capacity), flat(immobile)
    square = VMEM((rows, LANES), jnp.float32)
    x_nodes = LANES // SUBLANES - 1 + len(x_rolls(halves))
    y_nodes = halves * (rows // SUBLANES // halves - 1 + len(y_rolls()))
    message, block = kernel_call(
        functools.partial(x_forward_kernel, halves),
        tuple(
            pltpu.with_memory_space_constraint(value, pltpu.HBM)
            for value in (
                mobile, dispersion_x, dispersion_y, capacity, immobile, exchange_rates[None], rate_shares[None],
            )
        ),
        [f32(SUBLANES, rows), held_f32(2 * rows + (3 * x_nodes + 1) * SUBLANES, LANES)],
        [square] * 3
        + [VMEM((zones * rows, LANES), jnp.float32)]
        + [pltpu.SMEM((1, zones), jnp.float32)] * 2
        + [pltpu.SemaphoreType.DMA((7,))]
        + [square] * 3,
        pltpu.HBM,
    )
    def prepare(part, own):
        outputs = [held_f32(SUBLANES, 3 * LANES), held_f32(3 * LANES, rows), held_f32(2 * rows, LANES)]
        if own:
            outputs += [held_f32(3 * y_nodes * SUBLANES, LANES), held_f32(2 * rows, LANES)]
        else:
            outputs += [held_f32(SUBLANES, rows)]
        return kernel_call(functools.partial(prepare_kernel, halves, own), (part,), outputs, [], cost=10000000000)

    pieces, order, other_block = x_exchange(message, block)
    y_rows, lines_x, sums, y_state, spread = prepare(block, True)
    other_rows, other_lines, other_sums, other_message = prepare(other_block, False)
    kept, sent, values = kernel_call(
        functools.partial(x_back_kernel, halves, "xg", order, len(pieces)),
        (*pieces, lines_x, other_lines, sums, other_sums, y_rows, other_rows, other_message),
        [
            held_f32(2 * halves, QUANTITIES * LANES),
            f32(2 * halves, QUANTITIES * LANES),
            held_f32(rows, LANES),
        ],
        [],
    )
    (given,) = kernel_call(
        functools.partial(y_given_kernel, halves), (block, values, y_state), [held_f32(rows, LANES)], []
    )
    pieces, rounds = y_exchange(kept, sent)
    (updated,) = kernel_call(
        functools.partial(y_back_kernel, halves, "yd", rounds),
        (*pieces, given, spread),
        [f32(rows, LANES)],
        [],
    )
    return updated.reshape(shape)


def solution(mesh):
    field = P("yd", None, "xg")
    return jax.shard_map(
        local,
        mesh=mesh,
        in_specs=(field, field, field, field, P(None, "yd", None, "xg"), P(), P()),
        out_specs=field,
        check_vma=False,
    )
```

```python
import functools

import jax
import jax.numpy as jnp
from jax import lax
from jax.experimental import pallas as pl
from jax.experimental.pallas import tpu as pltpu
from jax.sharding import PartitionSpec as P

LANES = 128
SUBLANES = 8
QUANTITIES = 5
VMEM = pltpu.VMEM


def inverse(value):
    return 1.0 / value


def plus(first, second):
    if first is None:
        return second
    return first + second


def join_coefs(left, right):
    coupling_1, head_1, tail_1 = left
    coupling_2, head_2, tail_2 = right
    middle = plus(head_2, tail_1)
    inv = inverse(coupling_1 + coupling_2 + middle)
    weight_1 = coupling_1 * inv
    weight_2 = coupling_2 * inv
    joined = (coupling_1 * weight_2, plus(head_1, weight_1 * middle), tail_2 + weight_2 * middle)
    return joined, (weight_1, weight_2, inv)


def join_sides(left, right, node):
    head_1, tail_1 = left
    head_2, tail_2 = right
    weight_1, weight_2, inv = node
    side = plus(head_2, tail_1)
    joined = (plus(head_1, weight_1 * side), tail_2 + weight_2 * side)
    return joined, side * inv


def middle_value(node, given, before, after):
    return given + node[0] * before + node[1] * after


def ahead(value, step, axis):
    return pltpu.roll(value, value.shape[axis] - step, axis)


def behind(value, step, axis):
    return pltpu.roll(value, step, axis)


def doubling(count):
    steps = []
    step = 1
    while step < count:
        steps.append(step)
        step *= 2
    return steps


def tree_coefs(leaves, rolls):
    nodes = []
    level = leaves
    while len(level) > 1:
        following = []
        for index in range(0, len(level), 2):
            joined, node = join_coefs(level[index], level[index + 1])
            following.append(joined)
            nodes.append(node)
        level = following
    piece = level[0]
    for step, axis in rolls:
        piece, node = join_coefs(piece, tuple(ahead(part, step, axis) for part in piece))
        nodes.append(node)
    return piece, nodes


def tree_sides(leaves, rolls, nodes):
    givens = []
    level = leaves
    while len(level) > 1:
        following = []
        for index in range(0, len(level), 2):
            joined, given = join_sides(level[index], level[index + 1], nodes[len(givens)])
            following.append(joined)
            givens.append(given)
        level = following
    piece = level[0]
    for step, axis in rolls:
        other = tuple(ahead(part, step, axis) for part in piece)
        piece, given = join_sides(piece, other, nodes[len(givens)])
        givens.append(given)
    return piece, givens


def tree_values(before, after, rolls, count, nodes, givens):
    place = len(nodes)
    for step, axis in reversed(rolls):
        place -= 1
        middle = middle_value(nodes[place], givens[place], before, after)
        upper = (lax.broadcasted_iota(jnp.int32, middle.shape, axis) & step) != 0
        before = jnp.where(upper, behind(middle, step, axis), before)
        after = jnp.where(upper, behind(after, step, axis), middle)
    bounds = [before, after]
    while len(bounds) - 1 < count:
        width = len(bounds) - 1
        place -= width
        following = [bounds[0]]
        for index in range(width):
            following.append(
                middle_value(
                    nodes[place + index], givens[place + index], bounds[index], bounds[index + 1]
                )
            )
            following.append(bounds[index + 1])
        bounds = following
    return bounds[1:]


def choose(condition, first, second):
    if isinstance(condition, bool):
        return first if condition else second
    return jnp.where(condition, first, second)


def ring_bounds(slots, index):
    level = slots
    rounds = []
    bit = 0
    while len(level) > 1:
        upper = ((index >> bit) & 1) == 1
        following, nodes = [], []
        for place in range(0, len(level), 2):
            own, other = level[place], level[place + 1]
            left = [jnp.where(upper, b, a) for a, b in zip(own, other)]
            right = [jnp.where(upper, a, b) for a, b in zip(own, other)]
            coefs, node = join_coefs(left[:3], right[:3])
            sides, given = join_sides(left[3:], right[3:], node)
            nodes.append((node, given))
            following.append(coefs + sides)
        rounds.append((nodes, upper))
        level = following
        bit += 1
    _, head, tail, side_head, side_tail = level[0]
    last = (side_head + side_tail) * inverse(head + tail)
    bounds = [(last, last)]
    for nodes, upper in reversed(rounds):
        following = []
        for (node, given), (before, after) in zip(nodes, bounds):
            middle = middle_value(node, given, before, after)
            following.append((jnp.where(upper, middle, before), jnp.where(upper, after, middle)))
            following.append((jnp.where(upper, before, middle), jnp.where(upper, middle, after)))
        bounds = following
    return bounds


def capacity_weights(rates_ref, shares_ref):
    weights = []
    for zone in range(rates_ref.shape[1]):
        rate = jnp.full((SUBLANES, LANES), rates_ref[0, zone], jnp.float32)
        share = jnp.full((SUBLANES, LANES), shares_ref[0, zone], jnp.float32)
        weights.append((share * rate / (1.0 + rate))[0:1, :])
    return weights


def strided(ref, start, size, stride):
    return ref[pl.ds(start, size, stride=stride), :]


def x_rolls(halves):
    return [(step, 0) for step in doubling(SUBLANES)] + [(step, 1) for step in doubling(halves)]


def y_rolls():
    return [(step, 0) for step in doubling(SUBLANES)]


def x_forward_kernel(
    halves, mobile_hbm, faces_hbm, across_hbm, capacity_hbm, immobile_hbm, rates_hbm, shares_hbm,
    message_ref, block_ref,
    mobile_ref, faces_ref, capacity_ref, immobile_ref, rates_ref, shares_ref, arrived,
    faces_t, storage_t, source_t,
):
    rows = mobile_ref.shape[0]
    pairs = (
        (rates_hbm, rates_ref), (shares_hbm, shares_ref), (capacity_hbm, capacity_ref), (faces_hbm, faces_ref),
        (immobile_hbm, immobile_ref), (mobile_hbm, mobile_ref), (across_hbm, block_ref.at[rows : 2 * rows, :]),
    )
    copies = [pltpu.make_async_copy(pair[0], pair[1], arrived.at[place]) for place, pair in enumerate(pairs)]
    for place, copy in enumerate(copies):
        copy.start(priority=int(place in (4, 6)))
    stride = LANES // SUBLANES
    for copy in copies[:3]:
        copy.wait()
    weights = capacity_weights(rates_ref, shares_ref)
    capacity = capacity_ref[...]
    storage = 1.0 + capacity * sum(weights[1:], weights[0])
    block_ref[0:rows, :] = storage
    storage_t[...] = storage.T
    copies[3].wait()
    faces_t[...] = faces_ref[...].T
    rolls = x_rolls(halves)
    places = [pl.ds(index, SUBLANES, stride=stride) for index in range(stride)]
    piece, nodes = tree_coefs([(faces_t[place, :], None, storage_t[place, :]) for place in places], rolls)
    copies[4].wait()
    total = None
    for zone, weight in enumerate(weights):
        total = plus(total, weight * immobile_ref[zone * rows : (zone + 1) * rows, :])
    copies[5].wait()
    source_t[...] = (mobile_ref[...] + capacity * total).T
    side, givens = tree_sides([(None, source_t[place, :]) for place in places], rolls, nodes)
    start = 2 * rows
    for node, given in zip(nodes, givens):
        for part in (node[0], node[1], given):
            block_ref[start : start + SUBLANES, :] = part
            start += SUBLANES
    for row, value in enumerate(piece + side):
        message_ref[row : row + 1, :] = value[0:1, :]
        block_ref[start + row : start + row + 1, :] = value[0:1, :]
    copies[6].wait()


def ends_responses(shape):
    one, nothing = jnp.ones(shape, jnp.float32), jnp.zeros(shape, jnp.float32)
    return ((one, nothing), (nothing, one))


def prepare_kernel(halves, own, block_ref, rows_ref, lines_ref, sums_ref, *extra_refs):
    rows = lines_ref.shape[1]
    stride = LANES // SUBLANES
    rolls = x_rolls(halves)
    total = stride - 1 + len(rolls)
    nodes = state_parts(block_ref.at[2 * rows :, :], 0, total, 3)
    own_refs = extra_refs if own else ()
    if not own:
        extra_refs[0][...] = block_ref[-SUBLANES:, :]
    nothing = jnp.zeros((SUBLANES, rows), jnp.float32)
    cases = [((nothing, nothing), [node[2] for node in nodes])]
    cases += [(ends, [0.0] * total) for ends in ends_responses((SUBLANES, rows))]
    for case, (ends, givens) in enumerate(cases):
        for index, value in enumerate(tree_values(*ends, rolls, stride, nodes, givens)):
            lines_ref[pl.ds(case * LANES + index, SUBLANES, stride=stride), :] = value
    stride = rows // SUBLANES
    start = 0
    sublane = lax.broadcasted_iota(jnp.int32, (SUBLANES, LANES), 0) % halves
    tiles = None
    for half in range(halves):
        storage = [strided(block_ref, index, SUBLANES, stride) for index in range(half, stride, halves)]
        faces = [strided(block_ref, rows + index, SUBLANES, stride) for index in range(half, stride, halves)]
        piece, nodes = tree_coefs([(face, None, held) for face, held in zip(faces, storage)], y_rolls())
        for part in [part for node in nodes for part in node] if own_refs else []:
            own_refs[0][start : start + SUBLANES, :] = part
            start += SUBLANES
        values = [jnp.broadcast_to(value[0:1, :], value.shape) for value in piece]
        tiles = [jnp.where(sublane == half, new, old) for new, old in zip(values, tiles or values)]
        for case, ends in enumerate(ends_responses((SUBLANES, LANES))):
            values = tree_values(*ends, y_rolls(), len(storage), nodes, [0.0] * len(nodes))
            for index, (value, held) in enumerate(zip(values, storage)):
                place = pl.ds(case * rows + index * halves + half, SUBLANES, stride=stride)
                sums_ref[place, :] = value * held
                if own_refs:
                    own_refs[1][place, :] = value
    for number, tile in enumerate(tiles):
        rows_ref[:, quantity(number)] = tile


def state_parts(ref, first, total, parts, pitch=3):
    return [
        tuple(
            ref[(pitch * place + part) * SUBLANES : (pitch * place + part + 1) * SUBLANES, :]
            for part in range(parts)
        )
        for place in range(first, first + total)
    ]


def message_slots(refs, height, pitch, quantity_rows, skips):
    blocks = [(ref, start) for ref in refs for start in range(0, ref.shape[0], height)]
    slots = []
    for (ref, start), skip in zip(blocks, skips):
        rows = [start + quantity * pitch + skip for quantity in range(QUANTITIES)]
        slots.append(tuple(ref[row : row + quantity_rows, :] for row in rows))
    return slots


def quantity(number):
    return slice(number * LANES, (number + 1) * LANES)


def put_traded(ref, row, rows, number, value):
    ref[(row + rows // 2) % rows : (row + rows // 2) % rows + value.shape[0], quantity(number)] = value


def along_line(bound, halves, rows):
    value = jnp.broadcast_to(bound, (SUBLANES, rows))
    lane = lax.broadcasted_iota(jnp.int32, value.shape, 1)
    for step in doubling(halves):
        value = jnp.where((lane & step) != 0, behind(value, step, 1), value)
    return value[0:1, :]


def x_back_kernel(halves, axis, order, pieces, *refs):
    lines_refs, sums_refs, rows_refs = (refs[pieces + 2 * pair : pieces + 2 * pair + 2] for pair in range(3))
    last_ref, kept_ref, sent_ref, values_ref = refs[pieces + 6 :]
    slots = message_slots([*refs[:pieces], last_ref], SUBLANES, 1, 1, [0] * len(order))
    slots = [slots[order.index(place)] for place in range(len(order))]
    bounds = ring_bounds(slots, lax.axis_index(axis))
    rows = values_ref.shape[0]

    height = 2 * halves
    first = lax.broadcasted_iota(jnp.int32, (SUBLANES, LANES), 0) < halves

    def put(number, own, other):
        kept_ref[:, quantity(number)] = jnp.where(first, own, other)[0:height, :]
        sent_ref[:, quantity(number)] = jnp.where(first, other, own)[0:height, :]

    for number in range(3):
        put(number, *(ref[:, quantity(number)] for ref in rows_refs))
    sides = []
    for block in range(2):
        lines_ref, sums_ref = lines_refs[block], sums_refs[block]
        before, after = (along_line(bound, halves, rows) for bound in bounds[block])
        values = lines_ref[0:LANES, :] + lines_ref[LANES : 2 * LANES, :] * before + lines_ref[2 * LANES :, :] * after
        values = values.T
        if block == 0:
            values_ref[...] = values
        for end in range(2):
            parts = (values * sums_ref[end * rows : (end + 1) * rows, :]).reshape(-1, SUBLANES, LANES)
            side = jnp.sum(parts, axis=0)
            for step in doubling(SUBLANES // halves):
                side = side + behind(side, step * halves, 0)
            sides.append(side)
    for end in range(2):
        put(3 + end, sides[end], sides[2 + end])


def y_given_kernel(halves, block_ref, values_ref, state_ref, given_ref):
    rows = values_ref.shape[0]
    stride = rows // SUBLANES
    total = stride // halves - 1 + len(y_rolls())
    nothing = jnp.zeros((SUBLANES, LANES), jnp.float32)
    for half in range(halves):
        places = [pl.ds(index, SUBLANES, stride=stride) for index in range(half, stride, halves)]
        sides = [(None, block_ref[place, :] * values_ref[place, :]) for place in places]
        nodes = state_parts(state_ref, half * total, total, 3)
        _, givens = tree_sides(sides, y_rolls(), nodes)
        for place, value in zip(places, tree_values(nothing, nothing, y_rolls(), len(places), nodes, givens)):
            given_ref[place, :] = value


def read_message(ref):
    return [ref[:, quantity(number)] for number in range(QUANTITIES)]


def join_by_bit(own, other, upper):
    left = [choose(upper, b, a) for a, b in zip(own, other)]
    right = [choose(upper, a, b) for a, b in zip(own, other)]
    coefs, node = join_coefs(left[:3], right[:3])
    sides, given = join_sides(left[3:], right[3:], node)
    return coefs + sides, (node[0], node[1], given)


def own_bit(axis, bit):
    return ((lax.axis_index(axis) >> bit) & 1) == 1


def y_join_kernel(axis, bit, own_ref, other_ref, kept_ref, sent_ref, path_ref):
    joined, path = join_by_bit(read_message(own_ref), read_message(other_ref), own_bit(axis, bit))
    rows = own_ref.shape[0]
    for number, value in enumerate(joined):
        kept_ref[:, quantity(number)] = value
        for row in (0, rows // 2):
            put_traded(sent_ref, row, rows, number, value[row : row + rows // 2, :])
    for number, value in enumerate(path):
        path_ref[:, quantity(number)] = value


def y_back_kernel(halves, axis, rounds, own_ref, other_ref, *refs):
    path_refs = refs[: rounds - 1]
    given_ref, spread_ref, out_ref = refs[rounds - 1 :]
    rows = out_ref.shape[0]
    joined, path = join_by_bit(read_message(own_ref), read_message(other_ref), own_bit(axis, rounds - 1))
    _, head, tail, side_head, side_tail = joined
    before = after = (side_head + side_tail) * inverse(head + tail)
    paths = [[ref[:, quantity(number)] for number in range(3)] for ref in path_refs] + [path]
    for bit in reversed(range(rounds)):
        node = paths[bit]
        middle = middle_value(node, node[2], before, after)
        upper = own_bit(axis, bit)
        before = jnp.where(upper, middle, before)
        after = jnp.where(upper, after, middle)
    sublane = lax.broadcasted_iota(jnp.int32, (SUBLANES, LANES), 0) % halves
    ends = []
    for end in (before, after):
        value = jnp.broadcast_to(end[0:1, :], (SUBLANES, LANES))
        for half in range(1, halves):
            value = jnp.where(sublane == half, jnp.broadcast_to(end[half : half + 1, :], value.shape), value)
        ends.append(value)
    for start in range(0, rows, SUBLANES):
        part = slice(start, start + SUBLANES)
        late = slice(rows + start, rows + start + SUBLANES)
        out_ref[part, :] = given_ref[part, :] + spread_ref[part, :] * ends[0] + spread_ref[late, :] * ends[1]


def trade(value, x_step, y_step):
    width = lax.axis_size("yd")
    pairs = []
    for index in range(lax.axis_size("xg")):
        for line in range(width):
            pairs.append((index * width + line, (index ^ x_step) * width + (line ^ y_step)))
    return lax.ppermute(value, ("xg", "yd"), pairs)


def x_exchange(message, block):
    count = lax.axis_size("xg")
    held = message
    pieces = [message]
    order = [0]
    other_block = trade(block, 1, 0)
    for step in doubling(count // 2):
        received = trade(held, 2 * step + 1, 0)
        pieces.append(received)
        order += [place ^ (2 * step + 1) for place in order]
        if 4 * step < count:
            held = jnp.concatenate([held, received], axis=0)
    received = pieces[1] if len(pieces) == 2 else jnp.concatenate(pieces[1:], axis=0)
    pieces.append(trade(received, 1, 0))
    order += [place ^ 1 for place in order[1:]] + [1]
    return pieces, order, other_block


def y_exchange(kept, sent):
    rows = kept.shape[0]
    paths = []
    steps = doubling(lax.axis_size("yd"))
    for bit, step in enumerate(steps):
        received = trade(sent, 1, step)
        if bit < len(steps) - 1:
            kept, sent, path = kernel_call(
                functools.partial(y_join_kernel, "yd", bit),
                (kept, received),
                [held_f32(*kept.shape), f32(*kept.shape), held_f32(rows, 3 * LANES)],
                [],
            )
            paths.append(path)
    return [kept, received] + paths, len(steps)


def f32(*shape):
    return jax.ShapeDtypeStruct(shape, jnp.float32)


def held_f32(*shape):
    return VMEM(shape, jnp.float32)


def kernel_call(body, operands, outputs, scratch, space=VMEM, cost=500000):
    return pl.pallas_call(
        body,
        out_shape=outputs,
        in_specs=[pl.BlockSpec(memory_space=space)] * len(operands),
        out_specs=[pl.BlockSpec(memory_space=VMEM)] * len(outputs),
        scratch_shapes=scratch,
        cost_estimate=pl.CostEstimate(flops=cost, bytes_accessed=cost, transcendentals=0),
        compiler_params=pltpu.CompilerParams(vmem_limit_bytes=16 * 1024 * 1024),
    )(*operands)


def local(mobile, dispersion_x, dispersion_y, capacity, immobile, exchange_rates, rate_shares):
    shape = mobile.shape
    lines, width = shape[0] * shape[1], shape[2]
    zones = immobile.shape[0]
    halves = width // LANES
    rows = lines * halves
    assert rows == LANES

    def flat(values):
        return values.reshape(-1, LANES)

    mobile, dispersion_x, dispersion_y = flat(mobile), flat(dispersion_x), flat(dispersion_y)
    capacity, immobile = flat(capacity), flat(immobile)
    square = VMEM((rows, LANES), jnp.float32)
    x_nodes = LANES // SUBLANES - 1 + len(x_rolls(halves))
    y_nodes = halves * (rows // SUBLANES // halves - 1 + len(y_rolls()))
    message, block = kernel_call(
        functools.partial(x_forward_kernel, halves),
        tuple(
            pltpu.with_memory_space_constraint(value, pltpu.HBM)
            for value in (
                mobile, dispersion_x, dispersion_y, capacity, immobile, exchange_rates[None], rate_shares[None],
            )
        ),
        [f32(SUBLANES, rows), held_f32(2 * rows + (3 * x_nodes + 1) * SUBLANES, LANES)],
        [square] * 3
        + [VMEM((zones * rows, LANES), jnp.float32)]
        + [pltpu.SMEM((1, zones), jnp.float32)] * 2
        + [pltpu.SemaphoreType.DMA((7,))]
        + [square] * 3,
        pltpu.HBM,
    )
    def prepare(part, own):
        outputs = [held_f32(SUBLANES, 3 * LANES), held_f32(3 * LANES, rows), held_f32(2 * rows, LANES)]
        if own:
            outputs += [held_f32(3 * y_nodes * SUBLANES, LANES), held_f32(2 * rows, LANES)]
        else:
            outputs += [held_f32(SUBLANES, rows)]
        return kernel_call(functools.partial(prepare_kernel, halves, own), (part,), outputs, [], cost=10000000000)

    pieces, order, other_block = x_exchange(message, block)
    y_rows, lines_x, sums, y_state, spread = prepare(block, True)
    other_rows, other_lines, other_sums, other_message = prepare(other_block, False)
    kept, sent, values = kernel_call(
        functools.partial(x_back_kernel, halves, "xg", order, len(pieces)),
        (*pieces, lines_x, other_lines, sums, other_sums, y_rows, other_rows, other_message),
        [
            held_f32(2 * halves, QUANTITIES * LANES),
            f32(2 * halves, QUANTITIES * LANES),
            held_f32(rows, LANES),
        ],
        [],
    )
    (given,) = kernel_call(
        functools.partial(y_given_kernel, halves), (block, values, y_state), [held_f32(rows, LANES)], []
    )
    pieces, rounds = y_exchange(kept, sent)
    (updated,) = kernel_call(
        functools.partial(y_back_kernel, halves, "yd", rounds),
        (*pieces, given, spread),
        [f32(rows, LANES)],
        [],
    )
    return updated.reshape(shape)


def solution(mesh):
    field = P("yd", None, "xg")
    return jax.shard_map(
        local,
        mesh=mesh,
        in_specs=(field, field, field, field, P(None, "yd", None, "xg"), P(), P()),
        out_specs=field,
        check_vma=False,
    )
```

```python
import functools

import jax
import jax.numpy as jnp
from jax import lax
from jax.experimental import pallas as pl
from jax.experimental.pallas import tpu as pltpu
from jax.sharding import PartitionSpec as P

LANES = 128
SUBLANES = 8
QUANTITIES = 5
VMEM = pltpu.VMEM


def inverse(value):
    return 1.0 / value


def plus(first, second):
    if first is None:
        return second
    return first + second


def join_coefs(left, right):
    coupling_1, head_1, tail_1 = left
    coupling_2, head_2, tail_2 = right
    middle = plus(head_2, tail_1)
    inv = inverse(coupling_1 + coupling_2 + middle)
    weight_1 = coupling_1 * inv
    weight_2 = coupling_2 * inv
    joined = (coupling_1 * weight_2, plus(head_1, weight_1 * middle), tail_2 + weight_2 * middle)
    return joined, (weight_1, weight_2, inv)


def join_sides(left, right, node):
    head_1, tail_1 = left
    head_2, tail_2 = right
    weight_1, weight_2, inv = node
    side = plus(head_2, tail_1)
    joined = (plus(head_1, weight_1 * side), tail_2 + weight_2 * side)
    return joined, side * inv


def middle_value(node, given, before, after):
    return given + node[0] * before + node[1] * after


def ahead(value, step, axis):
    return pltpu.roll(value, value.shape[axis] - step, axis)


def behind(value, step, axis):
    return pltpu.roll(value, step, axis)


def doubling(count):
    steps = []
    step = 1
    while step < count:
        steps.append(step)
        step *= 2
    return steps


def tree_coefs(leaves, rolls):
    nodes = []
    level = leaves
    while len(level) > 1:
        following = []
        for index in range(0, len(level), 2):
            joined, node = join_coefs(level[index], level[index + 1])
            following.append(joined)
            nodes.append(node)
        level = following
    piece = level[0]
    for step, axis in rolls:
        piece, node = join_coefs(piece, tuple(ahead(part, step, axis) for part in piece))
        nodes.append(node)
    return piece, nodes


def tree_sides(leaves, rolls, nodes):
    givens = []
    level = leaves
    while len(level) > 1:
        following = []
        for index in range(0, len(level), 2):
            joined, given = join_sides(level[index], level[index + 1], nodes[len(givens)])
            following.append(joined)
            givens.append(given)
        level = following
    piece = level[0]
    for step, axis in rolls:
        other = tuple(ahead(part, step, axis) for part in piece)
        piece, given = join_sides(piece, other, nodes[len(givens)])
        givens.append(given)
    return piece, givens


def join_all(left, right):
    coefs, node = join_coefs(left[:3], right[:3])
    sides, given = join_sides(left[3:], right[3:], node)
    return coefs + sides, (node[0], node[1], given)


def tree_all(leaves, rolls):
    nodes = []
    level = leaves
    while len(level) > 1:
        pairs = [join_all(level[index], level[index + 1]) for index in range(0, len(level), 2)]
        nodes += [node for _, node in pairs]
        level = [joined for joined, _ in pairs]
    piece = level[0]
    count = SUBLANES
    level = [piece] + [tuple(ahead(part, step, 0) for part in piece) for step in range(1, count)]
    while len(level) > 1:
        pairs = [join_all(level[index], level[index + 1]) for index in range(0, len(level), 2)]
        nodes.append(pairs[0][1])
        level = [joined for joined, _ in pairs]
    piece = level[0]
    for step, axis in rolls[len(doubling(count)) :]:
        piece, node = join_all(piece, tuple(ahead(part, step, axis) for part in piece))
        nodes.append(node)
    return piece, nodes


def tree_values(before, after, rolls, count, nodes, givens):
    place = len(nodes)
    for step, axis in reversed(rolls):
        place -= 1
        middle = middle_value(nodes[place], givens[place], before, after)
        upper = (lax.broadcasted_iota(jnp.int32, middle.shape, axis) & step) != 0
        before = jnp.where(upper, behind(middle, step, axis), before)
        after = jnp.where(upper, behind(after, step, axis), middle)
    bounds = [before, after]
    while len(bounds) - 1 < count:
        width = len(bounds) - 1
        place -= width
        following = [bounds[0]]
        for index in range(width):
            following.append(
                middle_value(
                    nodes[place + index], givens[place + index], bounds[index], bounds[index + 1]
                )
            )
            following.append(bounds[index + 1])
        bounds = following
    return bounds[1:]


def choose(condition, first, second):
    if isinstance(condition, bool):
        return first if condition else second
    return jnp.where(condition, first, second)


def ring_bounds(slots, index):
    level = slots
    rounds = []
    bit = 0
    while len(level) > 1:
        upper = ((index >> bit) & 1) == 1
        following, nodes = [], []
        for place in range(0, len(level), 2):
            own, other = level[place], level[place + 1]
            left = [jnp.where(upper, b, a) for a, b in zip(own, other)]
            right = [jnp.where(upper, a, b) for a, b in zip(own, other)]
            coefs, node = join_coefs(left[:3], right[:3])
            sides, given = join_sides(left[3:], right[3:], node)
            nodes.append((node, given))
            following.append(coefs + sides)
        rounds.append((nodes, upper))
        level = following
        bit += 1
    _, head, tail, side_head, side_tail = level[0]
    last = (side_head + side_tail) * inverse(head + tail)
    bounds = [(last, last)]
    for nodes, upper in reversed(rounds):
        following = []
        for (node, given), (before, after) in zip(nodes, bounds):
            middle = middle_value(node, given, before, after)
            following.append((jnp.where(upper, middle, before), jnp.where(upper, after, middle)))
            following.append((jnp.where(upper, before, middle), jnp.where(upper, middle, after)))
        bounds = following
    return bounds


def capacity_weights(rates_ref, shares_ref):
    weights = []
    for zone in range(rates_ref.shape[1]):
        rate = jnp.full((SUBLANES, LANES), rates_ref[0, zone], jnp.float32)
        share = jnp.full((SUBLANES, LANES), shares_ref[0, zone], jnp.float32)
        weights.append((share * rate / (1.0 + rate))[0:1, :])
    return weights


def strided(ref, start, size, stride):
    return ref[pl.ds(start, size, stride=stride), :]


def x_rolls(halves):
    return [(step, 0) for step in doubling(SUBLANES)] + [(step, 1) for step in doubling(halves)]


def y_rolls():
    return [(step, 0) for step in doubling(SUBLANES)]


def x_forward_kernel(
    halves, mobile_hbm, faces_hbm, across_hbm, capacity_hbm, immobile_hbm, rates_hbm, shares_hbm,
    message_ref, block_ref,
    mobile_ref, faces_ref, capacity_ref, immobile_ref, rates_ref, shares_ref, arrived,
    faces_t, storage_t, source_t,
):
    rows = mobile_ref.shape[0]
    pairs = (
        (rates_hbm, rates_ref), (shares_hbm, shares_ref), (capacity_hbm, capacity_ref), (faces_hbm, faces_ref),
        (immobile_hbm, immobile_ref), (mobile_hbm, mobile_ref), (across_hbm, block_ref.at[rows : 2 * rows, :]),
    )
    copies = [pltpu.make_async_copy(pair[0], pair[1], arrived.at[place]) for place, pair in enumerate(pairs)]
    for place, copy in enumerate(copies):
        copy.start(priority=int(place in (4, 6)))
    stride = LANES // SUBLANES
    for copy in copies[:3]:
        copy.wait()
    weights = capacity_weights(rates_ref, shares_ref)
    capacity = capacity_ref[...]
    storage = 1.0 + capacity * sum(weights[1:], weights[0])
    block_ref[0:rows, :] = storage
    storage_t[...] = storage.T
    copies[3].wait()
    faces_t[...] = faces_ref[...].T
    copies[4].wait()
    total = None
    for zone, weight in enumerate(weights):
        total = plus(total, weight * immobile_ref[zone * rows : (zone + 1) * rows, :])
    copies[5].wait()
    source_t[...] = (mobile_ref[...] + capacity * total).T
    leaves = []
    for index in range(stride):
        face, held, source = (strided(ref, index, SUBLANES, stride) for ref in (faces_t, storage_t, source_t))
        leaves.append((face, None, held, None, source))
    piece, nodes = tree_all(leaves, x_rolls(halves))
    start = 2 * rows
    for part in [part for node in nodes for part in node]:
        block_ref[start : start + SUBLANES, :] = part
        start += SUBLANES
    for row, value in enumerate(piece):
        message_ref[row : row + 1, :] = value[0:1, :]
        block_ref[start + row : start + row + 1, :] = value[0:1, :]
    copies[6].wait()


def ends_responses(shape):
    one, nothing = jnp.ones(shape, jnp.float32), jnp.zeros(shape, jnp.float32)
    return ((one, nothing), (nothing, one))


def prepare_kernel(halves, own, block_ref, rows_ref, lines_ref, sums_ref, *extra_refs):
    rows = lines_ref.shape[1]
    stride = LANES // SUBLANES
    rolls = x_rolls(halves)
    total = stride - 1 + len(rolls)
    nodes = state_parts(block_ref.at[2 * rows :, :], 0, total, 3)
    own_refs = extra_refs if own else ()
    if not own:
        extra_refs[0][...] = block_ref[-SUBLANES:, :]
    nothing = jnp.zeros((SUBLANES, rows), jnp.float32)
    cases = [((nothing, nothing), [node[2] for node in nodes])]
    cases += [(ends, [0.0] * total) for ends in ends_responses((SUBLANES, rows))]
    for case, (ends, givens) in enumerate(cases):
        for index, value in enumerate(tree_values(*ends, rolls, stride, nodes, givens)):
            lines_ref[pl.ds(case * LANES + index, SUBLANES, stride=stride), :] = value
    stride = rows // SUBLANES
    start = 0
    sublane = lax.broadcasted_iota(jnp.int32, (SUBLANES, LANES), 0) % halves
    tiles = None
    for half in range(halves):
        storage = [strided(block_ref, index, SUBLANES, stride) for index in range(half, stride, halves)]
        faces = [strided(block_ref, rows + index, SUBLANES, stride) for index in range(half, stride, halves)]
        piece, nodes = tree_coefs([(face, None, held) for face, held in zip(faces, storage)], y_rolls())
        for part in [part for node in nodes for part in node] if own_refs else []:
            own_refs[0][start : start + SUBLANES, :] = part
            start += SUBLANES
        values = [jnp.broadcast_to(value[0:1, :], value.shape) for value in piece]
        tiles = [jnp.where(sublane == half, new, old) for new, old in zip(values, tiles or values)]
        for case, ends in enumerate(ends_responses((SUBLANES, LANES))):
            values = tree_values(*ends, y_rolls(), len(storage), nodes, [0.0] * len(nodes))
            for index, (value, held) in enumerate(zip(values, storage)):
                place = pl.ds(case * rows + index * halves + half, SUBLANES, stride=stride)
                sums_ref[place, :] = value * held
                if own_refs:
                    own_refs[1][place, :] = value
    for number, tile in enumerate(tiles):
        rows_ref[:, quantity(number)] = tile


def state_parts(ref, first, total, parts, pitch=3):
    return [
        tuple(
            ref[(pitch * place + part) * SUBLANES : (pitch * place + part + 1) * SUBLANES, :]
            for part in range(parts)
        )
        for place in range(first, first + total)
    ]


def message_slots(refs, height, pitch, quantity_rows, skips):
    blocks = [(ref, start) for ref in refs for start in range(0, ref.shape[0], height)]
    slots = []
    for (ref, start), skip in zip(blocks, skips):
        rows = [start + quantity * pitch + skip for quantity in range(QUANTITIES)]
        slots.append(tuple(ref[row : row + quantity_rows, :] for row in rows))
    return slots


def quantity(number):
    return slice(number * LANES, (number + 1) * LANES)


def put_traded(ref, row, rows, number, value):
    ref[(row + rows // 2) % rows : (row + rows // 2) % rows + value.shape[0], quantity(number)] = value


def along_line(bound, halves, rows):
    value = jnp.broadcast_to(bound, (SUBLANES, rows))
    lane = lax.broadcasted_iota(jnp.int32, value.shape, 1)
    for step in doubling(halves):
        value = jnp.where((lane & step) != 0, behind(value, step, 1), value)
    return value[0:1, :]


def x_back_kernel(halves, axis, order, pieces, *refs):
    lines_refs, sums_refs, rows_refs = (refs[pieces + 2 * pair : pieces + 2 * pair + 2] for pair in range(3))
    last_ref, kept_ref, sent_ref, values_ref = refs[pieces + 6 :]
    slots = message_slots([*refs[:pieces], last_ref], SUBLANES, 1, 1, [0] * len(order))
    slots = [slots[order.index(place)] for place in range(len(order))]
    bounds = ring_bounds(slots, lax.axis_index(axis))
    rows = values_ref.shape[0]

    height = 2 * halves
    first = lax.broadcasted_iota(jnp.int32, (SUBLANES, LANES), 0) < halves

    def put(number, own, other):
        kept_ref[:, quantity(number)] = jnp.where(first, own, other)[0:height, :]
        sent_ref[:, quantity(number)] = jnp.where(first, other, own)[0:height, :]

    for number in range(3):
        put(number, *(ref[:, quantity(number)] for ref in rows_refs))
    sides = []
    for block in range(2):
        lines_ref, sums_ref = lines_refs[block], sums_refs[block]
        before, after = (along_line(bound, halves, rows) for bound in bounds[block])
        values = lines_ref[0:LANES, :] + lines_ref[LANES : 2 * LANES, :] * before + lines_ref[2 * LANES :, :] * after
        values = values.T
        if block == 0:
            values_ref[...] = values
        for end in range(2):
            parts = (values * sums_ref[end * rows : (end + 1) * rows, :]).reshape(-1, SUBLANES, LANES)
            side = jnp.sum(parts, axis=0)
            sides.append(sum([behind(side, step, 0) for step in range(halves, SUBLANES, halves)], side))
    for end in range(2):
        put(3 + end, sides[end], sides[2 + end])


def y_given_kernel(halves, block_ref, values_ref, state_ref, given_ref):
    rows = values_ref.shape[0]
    stride = rows // SUBLANES
    total = stride // halves - 1 + len(y_rolls())
    nothing = jnp.zeros((SUBLANES, LANES), jnp.float32)
    for half in range(halves):
        places = [pl.ds(index, SUBLANES, stride=stride) for index in range(half, stride, halves)]
        sides = [(None, block_ref[place, :] * values_ref[place, :]) for place in places]
        nodes = state_parts(state_ref, half * total, total, 3)
        _, givens = tree_sides(sides, y_rolls(), nodes)
        for place, value in zip(places, tree_values(nothing, nothing, y_rolls(), len(places), nodes, givens)):
            given_ref[place, :] = value


def read_message(ref):
    return [ref[:, quantity(number)] for number in range(QUANTITIES)]


def join_by_bit(own, other, upper):
    left = [choose(upper, b, a) for a, b in zip(own, other)]
    right = [choose(upper, a, b) for a, b in zip(own, other)]
    coefs, node = join_coefs(left[:3], right[:3])
    sides, given = join_sides(left[3:], right[3:], node)
    return coefs + sides, (node[0], node[1], given)


def own_bit(axis, bit):
    return ((lax.axis_index(axis) >> bit) & 1) == 1


def y_join_kernel(axis, bit, own_ref, other_ref, kept_ref, sent_ref, path_ref):
    joined, path = join_by_bit(read_message(own_ref), read_message(other_ref), own_bit(axis, bit))
    rows = own_ref.shape[0]
    for number, value in enumerate(joined):
        kept_ref[:, quantity(number)] = value
        for row in (0, rows // 2):
            put_traded(sent_ref, row, rows, number, value[row : row + rows // 2, :])
    for number, value in enumerate(path):
        path_ref[:, quantity(number)] = value


def y_back_kernel(halves, axis, rounds, own_ref, other_ref, *refs):
    path_refs = refs[: rounds - 1]
    given_ref, spread_ref, out_ref = refs[rounds - 1 :]
    rows = out_ref.shape[0]
    joined, path = join_by_bit(read_message(own_ref), read_message(other_ref), own_bit(axis, rounds - 1))
    _, head, tail, side_head, side_tail = joined
    before = after = (side_head + side_tail) * inverse(head + tail)
    paths = [[ref[:, quantity(number)] for number in range(3)] for ref in path_refs] + [path]
    for bit in reversed(range(rounds)):
        node = paths[bit]
        middle = middle_value(node, node[2], before, after)
        upper = own_bit(axis, bit)
        before = jnp.where(upper, middle, before)
        after = jnp.where(upper, after, middle)
    sublane = lax.broadcasted_iota(jnp.int32, (SUBLANES, LANES), 0) % halves
    ends = []
    for end in (before, after):
        value = jnp.broadcast_to(end[0:1, :], (SUBLANES, LANES))
        for half in range(1, halves):
            value = jnp.where(sublane == half, jnp.broadcast_to(end[half : half + 1, :], value.shape), value)
        ends.append(value)
    for start in range(0, rows, SUBLANES):
        part = slice(start, start + SUBLANES)
        late = slice(rows + start, rows + start + SUBLANES)
        out_ref[part, :] = given_ref[part, :] + spread_ref[part, :] * ends[0] + spread_ref[late, :] * ends[1]


def trade(value, x_step, y_step):
    width = lax.axis_size("yd")
    pairs = []
    for index in range(lax.axis_size("xg")):
        for line in range(width):
            pairs.append((index * width + line, (index ^ x_step) * width + (line ^ y_step)))
    return lax.ppermute(value, ("xg", "yd"), pairs)


def x_exchange(message, block):
    count = lax.axis_size("xg")
    held = message
    pieces = [message]
    order = [0]
    other_block = trade(block, 1, 0)
    for step in doubling(count // 2):
        received = trade(held, 2 * step + 1, 0)
        pieces.append(received)
        order += [place ^ (2 * step + 1) for place in order]
        if 4 * step < count:
            held = jnp.concatenate([held, received], axis=0)
    received = pieces[1] if len(pieces) == 2 else jnp.concatenate(pieces[1:], axis=0)
    pieces.append(trade(received, 1, 0))
    order += [place ^ 1 for place in order[1:]] + [1]
    return pieces, order, other_block


def y_exchange(kept, sent):
    rows = kept.shape[0]
    paths = []
    steps = doubling(lax.axis_size("yd"))
    for bit, step in enumerate(steps):
        received = trade(sent, 1, step)
        if bit < len(steps) - 1:
            kept, sent, path = kernel_call(
                functools.partial(y_join_kernel, "yd", bit),
                (kept, received),
                [held_f32(*kept.shape), f32(*kept.shape), held_f32(rows, 3 * LANES)],
                [],
            )
            paths.append(path)
    return [kept, received] + paths, len(steps)


def f32(*shape):
    return jax.ShapeDtypeStruct(shape, jnp.float32)


def held_f32(*shape):
    return VMEM(shape, jnp.float32)


def kernel_call(body, operands, outputs, scratch, space=VMEM, cost=500000):
    return pl.pallas_call(
        body,
        out_shape=outputs,
        in_specs=[pl.BlockSpec(memory_space=space)] * len(operands),
        out_specs=[pl.BlockSpec(memory_space=VMEM)] * len(outputs),
        scratch_shapes=scratch,
        cost_estimate=pl.CostEstimate(flops=cost, bytes_accessed=cost, transcendentals=0),
        compiler_params=pltpu.CompilerParams(vmem_limit_bytes=16 * 1024 * 1024),
    )(*operands)


def local(mobile, dispersion_x, dispersion_y, capacity, immobile, exchange_rates, rate_shares):
    shape = mobile.shape
    lines, width = shape[0] * shape[1], shape[2]
    zones = immobile.shape[0]
    halves = width // LANES
    rows = lines * halves
    assert rows == LANES

    def flat(values):
        return values.reshape(-1, LANES)

    mobile, dispersion_x, dispersion_y = flat(mobile), flat(dispersion_x), flat(dispersion_y)
    capacity, immobile = flat(capacity), flat(immobile)
    square = VMEM((rows, LANES), jnp.float32)
    x_nodes = LANES // SUBLANES - 1 + len(x_rolls(halves))
    y_nodes = halves * (rows // SUBLANES // halves - 1 + len(y_rolls()))
    message, block = kernel_call(
        functools.partial(x_forward_kernel, halves),
        tuple(
            pltpu.with_memory_space_constraint(value, pltpu.HBM)
            for value in (
                mobile, dispersion_x, dispersion_y, capacity, immobile, exchange_rates[None], rate_shares[None],
            )
        ),
        [f32(SUBLANES, rows), held_f32(2 * rows + (3 * x_nodes + 1) * SUBLANES, LANES)],
        [square] * 3
        + [VMEM((zones * rows, LANES), jnp.float32)]
        + [pltpu.SMEM((1, zones), jnp.float32)] * 2
        + [pltpu.SemaphoreType.DMA((7,))]
        + [square] * 3,
        pltpu.HBM,
    )
    def prepare(part, own):
        outputs = [held_f32(SUBLANES, 3 * LANES), held_f32(3 * LANES, rows), held_f32(2 * rows, LANES)]
        if own:
            outputs += [held_f32(3 * y_nodes * SUBLANES, LANES), held_f32(2 * rows, LANES)]
        else:
            outputs += [held_f32(SUBLANES, rows)]
        return kernel_call(functools.partial(prepare_kernel, halves, own), (part,), outputs, [], cost=10000000000)

    pieces, order, other_block = x_exchange(message, block)
    y_rows, lines_x, sums, y_state, spread = prepare(block, True)
    other_rows, other_lines, other_sums, other_message = prepare(other_block, False)
    kept, sent, values = kernel_call(
        functools.partial(x_back_kernel, halves, "xg", order, len(pieces)),
        (*pieces, lines_x, other_lines, sums, other_sums, y_rows, other_rows, other_message),
        [
            held_f32(2 * halves, QUANTITIES * LANES),
            f32(2 * halves, QUANTITIES * LANES),
            held_f32(rows, LANES),
        ],
        [],
    )
    (given,) = kernel_call(
        functools.partial(y_given_kernel, halves), (block, values, y_state), [held_f32(rows, LANES)], []
    )
    pieces, rounds = y_exchange(kept, sent)
    (updated,) = kernel_call(
        functools.partial(y_back_kernel, halves, "yd", rounds),
        (*pieces, given, spread),
        [f32(rows, LANES)],
        [],
    )
    return updated.reshape(shape)


def solution(mesh):
    field = P("yd", None, "xg")
    return jax.shard_map(
        local,
        mesh=mesh,
        in_specs=(field, field, field, field, P(None, "yd", None, "xg"), P(), P()),
        out_specs=field,
        check_vma=False,
    )
```

```python
import functools

import jax
import jax.numpy as jnp
from jax import lax
from jax.experimental import pallas as pl
from jax.experimental.pallas import tpu as pltpu
from jax.sharding import PartitionSpec as P

LANES = 128
SUBLANES = 8
QUANTITIES = 5
VMEM = pltpu.VMEM


def inverse(value):
    return 1.0 / value


def plus(first, second):
    if first is None:
        return second
    return first + second


def join_coefs(left, right):
    coupling_1, head_1, tail_1 = left
    coupling_2, head_2, tail_2 = right
    middle = plus(head_2, tail_1)
    inv = inverse(coupling_1 + coupling_2 + middle)
    weight_1 = coupling_1 * inv
    weight_2 = coupling_2 * inv
    joined = (coupling_1 * weight_2, plus(head_1, weight_1 * middle), tail_2 + weight_2 * middle)
    return joined, (weight_1, weight_2, inv)


def join_sides(left, right, node):
    head_1, tail_1 = left
    head_2, tail_2 = right
    weight_1, weight_2, inv = node
    side = plus(head_2, tail_1)
    joined = (plus(head_1, weight_1 * side), tail_2 + weight_2 * side)
    return joined, side * inv


def middle_value(node, given, before, after):
    return given + node[0] * before + node[1] * after


def ahead(value, step, axis):
    return pltpu.roll(value, value.shape[axis] - step, axis)


def behind(value, step, axis):
    return pltpu.roll(value, step, axis)


def doubling(count):
    steps = []
    step = 1
    while step < count:
        steps.append(step)
        step *= 2
    return steps


def tree_coefs(leaves, rolls):
    nodes = []
    level = leaves
    while len(level) > 1:
        following = []
        for index in range(0, len(level), 2):
            joined, node = join_coefs(level[index], level[index + 1])
            following.append(joined)
            nodes.append(node)
        level = following
    piece = level[0]
    for step, axis in rolls:
        piece, node = join_coefs(piece, tuple(ahead(part, step, axis) for part in piece))
        nodes.append(node)
    return piece, nodes


def tree_sides(leaves, rolls, nodes):
    givens = []
    level = leaves
    while len(level) > 1:
        following = []
        for index in range(0, len(level), 2):
            joined, given = join_sides(level[index], level[index + 1], nodes[len(givens)])
            following.append(joined)
            givens.append(given)
        level = following
    piece = level[0]
    for step, axis in rolls:
        other = tuple(ahead(part, step, axis) for part in piece)
        piece, given = join_sides(piece, other, nodes[len(givens)])
        givens.append(given)
    return piece, givens


def join_all(left, right):
    coefs, node = join_coefs(left[:3], right[:3])
    sides, given = join_sides(left[3:], right[3:], node)
    return coefs + sides, (node[0], node[1], given)


def tree_all(leaves, rolls):
    nodes = []
    level = leaves
    while len(level) > 1:
        pairs = [join_all(level[index], level[index + 1]) for index in range(0, len(level), 2)]
        nodes += [node for _, node in pairs]
        level = [joined for joined, _ in pairs]
    piece = level[0]
    count = SUBLANES
    level = [piece] + [tuple(ahead(part, step, 0) for part in piece) for step in range(1, count)]
    while len(level) > 1:
        pairs = [join_all(level[index], level[index + 1]) for index in range(0, len(level), 2)]
        nodes.append(pairs[0][1])
        level = [joined for joined, _ in pairs]
    piece = level[0]
    for step, axis in rolls[len(doubling(count)) :]:
        piece, node = join_all(piece, tuple(ahead(part, step, axis) for part in piece))
        nodes.append(node)
    return piece, nodes


def tree_values(before, after, rolls, count, nodes, givens):
    place = len(nodes)
    for step, axis in reversed(rolls):
        place -= 1
        middle = middle_value(nodes[place], givens[place], before, after)
        upper = (lax.broadcasted_iota(jnp.int32, middle.shape, axis) & step) != 0
        before = jnp.where(upper, behind(middle, step, axis), before)
        after = jnp.where(upper, behind(after, step, axis), middle)
    bounds = [before, after]
    while len(bounds) - 1 < count:
        width = len(bounds) - 1
        place -= width
        following = [bounds[0]]
        for index in range(width):
            following.append(
                middle_value(
                    nodes[place + index], givens[place + index], bounds[index], bounds[index + 1]
                )
            )
            following.append(bounds[index + 1])
        bounds = following
    return bounds[1:]


def choose(condition, first, second):
    if isinstance(condition, bool):
        return first if condition else second
    return jnp.where(condition, first, second)


def ring_bounds(slots, index):
    level = slots
    rounds = []
    bit = 0
    while len(level) > 1:
        upper = ((index >> bit) & 1) == 1
        following, nodes = [], []
        for place in range(0, len(level), 2):
            own, other = level[place], level[place + 1]
            left = [jnp.where(upper, b, a) for a, b in zip(own, other)]
            right = [jnp.where(upper, a, b) for a, b in zip(own, other)]
            coefs, node = join_coefs(left[:3], right[:3])
            sides, given = join_sides(left[3:], right[3:], node)
            nodes.append((node, given))
            following.append(coefs + sides)
        rounds.append((nodes, upper))
        level = following
        bit += 1
    _, head, tail, side_head, side_tail = level[0]
    last = (side_head + side_tail) * inverse(head + tail)
    bounds = [(last, last)]
    for nodes, upper in reversed(rounds):
        following = []
        for (node, given), (before, after) in zip(nodes, bounds):
            middle = middle_value(node, given, before, after)
            following.append((jnp.where(upper, middle, before), jnp.where(upper, after, middle)))
            following.append((jnp.where(upper, before, middle), jnp.where(upper, middle, after)))
        bounds = following
    return bounds


def capacity_weights(rates_ref, shares_ref):
    weights = []
    for zone in range(rates_ref.shape[1]):
        rate = jnp.full((SUBLANES, LANES), rates_ref[0, zone], jnp.float32)
        share = jnp.full((SUBLANES, LANES), shares_ref[0, zone], jnp.float32)
        weights.append((share * rate / (1.0 + rate))[0:1, :])
    return weights


def strided(ref, start, size, stride):
    return ref[pl.ds(start, size, stride=stride), :]


def x_rolls(halves):
    return [(step, 0) for step in doubling(SUBLANES)] + [(step, 1) for step in doubling(halves)]


def y_rolls():
    return [(step, 0) for step in doubling(SUBLANES)]


def x_forward_kernel(
    halves, mobile_hbm, faces_hbm, across_hbm, capacity_hbm, immobile_hbm, rates_hbm, shares_hbm,
    message_ref, block_ref,
    mobile_ref, faces_ref, capacity_ref, immobile_ref, rates_ref, shares_ref, arrived,
    faces_t, storage_t, source_t,
):
    rows = mobile_ref.shape[0]
    pairs = (
        (rates_hbm, rates_ref), (shares_hbm, shares_ref), (capacity_hbm, capacity_ref), (faces_hbm, faces_ref),
        (immobile_hbm, immobile_ref), (mobile_hbm, mobile_ref), (across_hbm, block_ref.at[rows : 2 * rows, :]),
    )
    copies = [pltpu.make_async_copy(pair[0], pair[1], arrived.at[place]) for place, pair in enumerate(pairs)]
    for place, copy in enumerate(copies):
        copy.start(priority=int(place in (4, 6)))
    stride = LANES // SUBLANES
    for copy in copies[:3]:
        copy.wait()
    weights = capacity_weights(rates_ref, shares_ref)
    capacity = capacity_ref[...]
    storage = 1.0 + capacity * sum(weights[1:], weights[0])
    block_ref[0:rows, :] = storage
    storage_t[...] = storage.T
    copies[3].wait()
    faces_t[...] = faces_ref[...].T
    copies[4].wait()
    total = None
    for zone, weight in enumerate(weights):
        total = plus(total, weight * immobile_ref[zone * rows : (zone + 1) * rows, :])
    copies[5].wait()
    source_t[...] = (mobile_ref[...] + capacity * total).T
    leaves = []
    for index in range(stride):
        face, held, source = (strided(ref, index, SUBLANES, stride) for ref in (faces_t, storage_t, source_t))
        leaves.append((face, None, held, None, source))
    piece, nodes = tree_all(leaves, x_rolls(halves))
    start = 2 * rows
    for part in [part for node in nodes for part in node]:
        block_ref[start : start + SUBLANES, :] = part
        start += SUBLANES
    for row, value in enumerate(piece):
        message_ref[row : row + 1, :] = value[0:1, :]
        block_ref[start + row : start + row + 1, :] = value[0:1, :]
    copies[6].wait()


def ends_responses(shape):
    one, nothing = jnp.ones(shape, jnp.float32), jnp.zeros(shape, jnp.float32)
    return ((one, nothing), (nothing, one))


def prepare_kernel(halves, own, block_ref, rows_ref, lines_ref, sums_ref, *extra_refs):
    rows = lines_ref.shape[1]
    stride = LANES // SUBLANES
    rolls = x_rolls(halves)
    total = stride - 1 + len(rolls)
    nodes = state_parts(block_ref.at[2 * rows :, :], 0, total, 3)
    own_refs = extra_refs if own else ()
    if not own:
        extra_refs[0][...] = block_ref[-SUBLANES:, :]
    nothing = jnp.zeros((SUBLANES, rows), jnp.float32)
    cases = [((nothing, nothing), [node[2] for node in nodes])]
    cases += [(ends, [0.0] * total) for ends in ends_responses((SUBLANES, rows))]
    for case, (ends, givens) in enumerate(cases):
        for index, value in enumerate(tree_values(*ends, rolls, stride, nodes, givens)):
            lines_ref[pl.ds(case * LANES + index, SUBLANES, stride=stride), :] = value
    stride = rows // SUBLANES
    start = 0
    sublane = lax.broadcasted_iota(jnp.int32, (SUBLANES, LANES), 0) % halves
    tiles = None
    for half in range(halves):
        storage = [strided(block_ref, index, SUBLANES, stride) for index in range(half, stride, halves)]
        faces = [strided(block_ref, rows + index, SUBLANES, stride) for index in range(half, stride, halves)]
        piece, nodes = tree_coefs([(face, None, held) for face, held in zip(faces, storage)], y_rolls())
        for part in [part for node in nodes for part in node] if own_refs else []:
            own_refs[0][start : start + SUBLANES, :] = part
            start += SUBLANES
        values = [jnp.broadcast_to(value[0:1, :], value.shape) for value in piece]
        tiles = [jnp.where(sublane == half, new, old) for new, old in zip(values, tiles or values)]
        for case, ends in enumerate(ends_responses((SUBLANES, LANES))):
            values = tree_values(*ends, y_rolls(), len(storage), nodes, [0.0] * len(nodes))
            for index, (value, held) in enumerate(zip(values, storage)):
                place = pl.ds(case * rows + index * halves + half, SUBLANES, stride=stride)
                sums_ref[place, :] = value * held
                if own_refs:
                    own_refs[1][place, :] = value
    for number, tile in enumerate(tiles):
        rows_ref[:, quantity(number)] = tile


def state_parts(ref, first, total, parts, pitch=3):
    return [
        tuple(
            ref[(pitch * place + part) * SUBLANES : (pitch * place + part + 1) * SUBLANES, :]
            for part in range(parts)
        )
        for place in range(first, first + total)
    ]


def message_slots(refs, height, pitch, quantity_rows, skips):
    blocks = [(ref, start) for ref in refs for start in range(0, ref.shape[0], height)]
    slots = []
    for (ref, start), skip in zip(blocks, skips):
        rows = [start + quantity * pitch + skip for quantity in range(QUANTITIES)]
        slots.append(tuple(ref[row : row + quantity_rows, :] for row in rows))
    return slots


def quantity(number):
    return slice(number * LANES, (number + 1) * LANES)


def put_traded(ref, row, rows, number, value):
    ref[(row + rows // 2) % rows : (row + rows // 2) % rows + value.shape[0], quantity(number)] = value


def along_line(bound, halves, rows):
    value = jnp.broadcast_to(bound, (SUBLANES, rows))
    lane = lax.broadcasted_iota(jnp.int32, value.shape, 1)
    for step in doubling(halves):
        value = jnp.where((lane & step) != 0, behind(value, step, 1), value)
    return value[0:1, :]


def x_back_kernel(halves, axis, order, pieces, *refs):
    lines_refs, sums_refs, rows_refs = (refs[pieces + 2 * pair : pieces + 2 * pair + 2] for pair in range(3))
    last_ref, kept_ref, sent_ref, values_ref = refs[pieces + 6 :]
    slots = message_slots([*refs[:pieces], last_ref], SUBLANES, 1, 1, [0] * len(order))
    slots = [slots[order.index(place)] for place in range(len(order))]
    bounds = ring_bounds(slots, lax.axis_index(axis))
    rows = values_ref.shape[0]

    height = 2 * halves
    first = lax.broadcasted_iota(jnp.int32, (SUBLANES, LANES), 0) < halves

    def put(number, own, other):
        kept_ref[:, quantity(number)] = jnp.where(first, own, other)[0:height, :]
        sent_ref[:, quantity(number)] = jnp.where(first, other, own)[0:height, :]

    for number in range(3):
        put(number, *(ref[:, quantity(number)] for ref in rows_refs))
    sides = []
    for block in range(2):
        lines_ref, sums_ref = lines_refs[block], sums_refs[block]
        before, after = (along_line(bound, halves, rows) for bound in bounds[block])
        values = lines_ref[0:LANES, :] + lines_ref[LANES : 2 * LANES, :] * before + lines_ref[2 * LANES :, :] * after
        values = values.T
        if block == 0:
            values_ref[...] = values
        for end in range(2):
            parts = (values * sums_ref[end * rows : (end + 1) * rows, :]).reshape(-1, SUBLANES, LANES)
            side = jnp.sum(parts, axis=0)
            sides.append(sum([behind(side, step, 0) for step in range(halves, SUBLANES, halves)], side))
    for end in range(2):
        put(3 + end, sides[end], sides[2 + end])


def y_given_kernel(halves, block_ref, values_ref, state_ref, given_ref):
    rows = values_ref.shape[0]
    stride = rows // SUBLANES
    total = stride // halves - 1 + len(y_rolls())
    nothing = jnp.zeros((SUBLANES, LANES), jnp.float32)
    for half in range(halves):
        places = [pl.ds(index, SUBLANES, stride=stride) for index in range(half, stride, halves)]
        sides = [(None, block_ref[place, :] * values_ref[place, :]) for place in places]
        nodes = state_parts(state_ref, half * total, total, 3)
        _, givens = tree_sides(sides, y_rolls(), nodes)
        for place, value in zip(places, tree_values(nothing, nothing, y_rolls(), len(places), nodes, givens)):
            given_ref[place, :] = value


def read_message(ref):
    return [ref[:, quantity(number)] for number in range(QUANTITIES)]


def join_by_bit(own, other, upper):
    left = [choose(upper, b, a) for a, b in zip(own, other)]
    right = [choose(upper, a, b) for a, b in zip(own, other)]
    coefs, node = join_coefs(left[:3], right[:3])
    sides, given = join_sides(left[3:], right[3:], node)
    return coefs + sides, (node[0], node[1], given)


def own_bit(axis, bit):
    return ((lax.axis_index(axis) >> bit) & 1) == 1


def y_join_kernel(axis, bit, own_ref, other_ref, kept_ref, sent_ref, path_ref):
    joined, path = join_by_bit(read_message(own_ref), read_message(other_ref), own_bit(axis, bit))
    rows = own_ref.shape[0]
    for number, value in enumerate(joined):
        kept_ref[:, quantity(number)] = value
        for row in (0, rows // 2):
            put_traded(sent_ref, row, rows, number, value[row : row + rows // 2, :])
    for number, value in enumerate(path):
        path_ref[:, quantity(number)] = value


def y_back_kernel(halves, axis, rounds, own_ref, other_ref, *refs):
    path_refs = refs[: rounds - 1]
    given_ref, spread_ref, out_hbm, out_ref, gone = refs[rounds - 1 :]
    rows = out_ref.shape[0]
    joined, path = join_by_bit(read_message(own_ref), read_message(other_ref), own_bit(axis, rounds - 1))
    _, head, tail, side_head, side_tail = joined
    before = after = (side_head + side_tail) * inverse(head + tail)
    paths = [[ref[:, quantity(number)] for number in range(3)] for ref in path_refs] + [path]
    for bit in reversed(range(rounds)):
        node = paths[bit]
        middle = middle_value(node, node[2], before, after)
        upper = own_bit(axis, bit)
        before = jnp.where(upper, middle, before)
        after = jnp.where(upper, after, middle)
    sublane = lax.broadcasted_iota(jnp.int32, (SUBLANES, LANES), 0) % halves
    ends = []
    for end in (before, after):
        value = jnp.broadcast_to(end[0:1, :], (SUBLANES, LANES))
        for half in range(1, halves):
            value = jnp.where(sublane == half, jnp.broadcast_to(end[half : half + 1, :], value.shape), value)
        ends.append(value)
    for start in range(0, rows, SUBLANES):
        part = slice(start, start + SUBLANES)
        late = slice(rows + start, rows + start + SUBLANES)
        out_ref[part, :] = given_ref[part, :] + spread_ref[part, :] * ends[0] + spread_ref[late, :] * ends[1]
    copy = pltpu.make_async_copy(out_ref, out_hbm, gone)
    copy.start()
    copy.wait()


def trade(value, x_step, y_step):
    width = lax.axis_size("yd")
    pairs = []
    for index in range(lax.axis_size("xg")):
        for line in range(width):
            pairs.append((index * width + line, (index ^ x_step) * width + (line ^ y_step)))
    return lax.ppermute(value, ("xg", "yd"), pairs)


def x_exchange(message, block):
    count = lax.axis_size("xg")
    held = message
    pieces = [message]
    order = [0]
    other_block = trade(block, 1, 0)
    for step in doubling(count // 2):
        received = trade(held, 2 * step + 1, 0)
        pieces.append(received)
        order += [place ^ (2 * step + 1) for place in order]
        if 4 * step < count:
            held = jnp.concatenate([held, received], axis=0)
    received = pieces[1] if len(pieces) == 2 else jnp.concatenate(pieces[1:], axis=0)
    pieces.append(trade(received, 1, 0))
    order += [place ^ 1 for place in order[1:]] + [1]
    return pieces, order, other_block


def y_exchange(kept, sent):
    rows = kept.shape[0]
    paths = []
    steps = doubling(lax.axis_size("yd"))
    for bit, step in enumerate(steps):
        received = trade(sent, 1, step)
        if bit < len(steps) - 1:
            kept, sent, path = kernel_call(
                functools.partial(y_join_kernel, "yd", bit),
                (kept, received),
                [held_f32(*kept.shape), f32(*kept.shape), held_f32(rows, 3 * LANES)],
                [],
            )
            paths.append(path)
    return [kept, received] + paths, len(steps)


def f32(*shape):
    return jax.ShapeDtypeStruct(shape, jnp.float32)


def held_f32(*shape):
    return VMEM(shape, jnp.float32)


def kernel_call(body, operands, outputs, scratch, space=VMEM, cost=500000, out_space=VMEM):
    return pl.pallas_call(
        body,
        out_shape=outputs,
        in_specs=[pl.BlockSpec(memory_space=space)] * len(operands),
        out_specs=[pl.BlockSpec(memory_space=out_space)] * len(outputs),
        scratch_shapes=scratch,
        cost_estimate=pl.CostEstimate(flops=cost, bytes_accessed=cost, transcendentals=0),
        compiler_params=pltpu.CompilerParams(vmem_limit_bytes=16 * 1024 * 1024),
    )(*operands)


def local(mobile, dispersion_x, dispersion_y, capacity, immobile, exchange_rates, rate_shares):
    shape = mobile.shape
    lines, width = shape[0] * shape[1], shape[2]
    zones = immobile.shape[0]
    halves = width // LANES
    rows = lines * halves
    assert rows == LANES

    def flat(values):
        return values.reshape(-1, LANES)

    mobile, dispersion_x, dispersion_y = flat(mobile), flat(dispersion_x), flat(dispersion_y)
    capacity, immobile = flat(capacity), flat(immobile)
    square = VMEM((rows, LANES), jnp.float32)
    x_nodes = LANES // SUBLANES - 1 + len(x_rolls(halves))
    y_nodes = halves * (rows // SUBLANES // halves - 1 + len(y_rolls()))
    message, block = kernel_call(
        functools.partial(x_forward_kernel, halves),
        tuple(
            pltpu.with_memory_space_constraint(value, pltpu.HBM)
            for value in (
                mobile, dispersion_x, dispersion_y, capacity, immobile, exchange_rates[None], rate_shares[None],
            )
        ),
        [f32(SUBLANES, rows), held_f32(2 * rows + (3 * x_nodes + 1) * SUBLANES, LANES)],
        [square] * 3
        + [VMEM((zones * rows, LANES), jnp.float32)]
        + [pltpu.SMEM((1, zones), jnp.float32)] * 2
        + [pltpu.SemaphoreType.DMA((7,))]
        + [square] * 3,
        pltpu.HBM,
    )
    def prepare(part, own):
        outputs = [held_f32(SUBLANES, 3 * LANES), held_f32(3 * LANES, rows), held_f32(2 * rows, LANES)]
        if own:
            outputs += [held_f32(3 * y_nodes * SUBLANES, LANES), held_f32(2 * rows, LANES)]
        else:
            outputs += [held_f32(SUBLANES, rows)]
        return kernel_call(functools.partial(prepare_kernel, halves, own), (part,), outputs, [], cost=10000000000)

    pieces, order, other_block = x_exchange(message, block)
    y_rows, lines_x, sums, y_state, spread = prepare(block, True)
    other_rows, other_lines, other_sums, other_message = prepare(other_block, False)
    kept, sent, values = kernel_call(
        functools.partial(x_back_kernel, halves, "xg", order, len(pieces)),
        (*pieces, lines_x, other_lines, sums, other_sums, y_rows, other_rows, other_message),
        [
            held_f32(2 * halves, QUANTITIES * LANES),
            f32(2 * halves, QUANTITIES * LANES),
            held_f32(rows, LANES),
        ],
        [],
    )
    (given,) = kernel_call(
        functools.partial(y_given_kernel, halves), (block, values, y_state), [held_f32(rows, LANES)], []
    )
    pieces, rounds = y_exchange(kept, sent)
    (updated,) = kernel_call(
        functools.partial(y_back_kernel, halves, "yd", rounds),
        (*pieces, given, spread),
        [f32(rows, LANES)],
        [square, pltpu.SemaphoreType.DMA],
        out_space=pltpu.HBM,
    )
    return updated.reshape(shape)


def solution(mesh):
    field = P("yd", None, "xg")
    return jax.shard_map(
        local,
        mesh=mesh,
        in_specs=(field, field, field, field, P(None, "yd", None, "xg"), P(), P()),
        out_specs=field,
        check_vma=False,
    )
```

```python
import functools

import jax
import jax.numpy as jnp
from jax import lax
from jax.experimental import pallas as pl
from jax.experimental.pallas import tpu as pltpu
from jax.sharding import PartitionSpec as P

LANES = 128
SUBLANES = 8
QUANTITIES = 5
VMEM = pltpu.VMEM


def inverse(value):
    return 1.0 / value


def plus(first, second):
    if first is None:
        return second
    return first + second


def join_coefs(left, right):
    coupling_1, head_1, tail_1 = left
    coupling_2, head_2, tail_2 = right
    middle = plus(head_2, tail_1)
    inv = inverse(coupling_1 + coupling_2 + middle)
    weight_1 = coupling_1 * inv
    weight_2 = coupling_2 * inv
    joined = (coupling_1 * weight_2, plus(head_1, weight_1 * middle), tail_2 + weight_2 * middle)
    return joined, (weight_1, weight_2, inv)


def join_sides(left, right, node):
    head_1, tail_1 = left
    head_2, tail_2 = right
    weight_1, weight_2, inv = node
    side = plus(head_2, tail_1)
    joined = (plus(head_1, weight_1 * side), tail_2 + weight_2 * side)
    return joined, side * inv


def middle_value(node, given, before, after):
    return given + node[0] * before + node[1] * after


def ahead(value, step, axis):
    return pltpu.roll(value, value.shape[axis] - step, axis)


def behind(value, step, axis):
    return pltpu.roll(value, step, axis)


def doubling(count):
    steps = []
    step = 1
    while step < count:
        steps.append(step)
        step *= 2
    return steps


def tree_coefs(leaves, rolls):
    nodes = []
    level = leaves
    while len(level) > 1:
        following = []
        for index in range(0, len(level), 2):
            joined, node = join_coefs(level[index], level[index + 1])
            following.append(joined)
            nodes.append(node)
        level = following
    piece = level[0]
    for step, axis in rolls:
        piece, node = join_coefs(piece, tuple(ahead(part, step, axis) for part in piece))
        nodes.append(node)
    return piece, nodes


def tree_sides(leaves, rolls, nodes):
    givens = []
    level = leaves
    while len(level) > 1:
        following = []
        for index in range(0, len(level), 2):
            joined, given = join_sides(level[index], level[index + 1], nodes[len(givens)])
            following.append(joined)
            givens.append(given)
        level = following
    piece = level[0]
    for step, axis in rolls:
        other = tuple(ahead(part, step, axis) for part in piece)
        piece, given = join_sides(piece, other, nodes[len(givens)])
        givens.append(given)
    return piece, givens


def join_all(left, right):
    coefs, node = join_coefs(left[:3], right[:3])
    sides, given = join_sides(left[3:], right[3:], node)
    return coefs + sides, (node[0], node[1], given)


def tree_all(leaves, rolls):
    nodes = []
    level = leaves
    while len(level) > 1:
        pairs = [join_all(level[index], level[index + 1]) for index in range(0, len(level), 2)]
        nodes += [node for _, node in pairs]
        level = [joined for joined, _ in pairs]
    piece = level[0]
    count = SUBLANES
    level = [piece] + [tuple(ahead(part, step, 0) for part in piece) for step in range(1, count)]
    while len(level) > 1:
        pairs = [join_all(level[index], level[index + 1]) for index in range(0, len(level), 2)]
        nodes.append(pairs[0][1])
        level = [joined for joined, _ in pairs]
    piece = level[0]
    for step, axis in rolls[len(doubling(count)) :]:
        piece, node = join_all(piece, tuple(ahead(part, step, axis) for part in piece))
        nodes.append(node)
    return piece, nodes


def tree_values(before, after, rolls, count, nodes, givens):
    place = len(nodes)
    for step, axis in reversed(rolls):
        place -= 1
        middle = middle_value(nodes[place], givens[place], before, after)
        upper = (lax.broadcasted_iota(jnp.int32, middle.shape, axis) & step) != 0
        before = jnp.where(upper, behind(middle, step, axis), before)
        after = jnp.where(upper, behind(after, step, axis), middle)
    bounds = [before, after]
    while len(bounds) - 1 < count:
        width = len(bounds) - 1
        place -= width
        following = [bounds[0]]
        for index in range(width):
            following.append(
                middle_value(
                    nodes[place + index], givens[place + index], bounds[index], bounds[index + 1]
                )
            )
            following.append(bounds[index + 1])
        bounds = following
    return bounds[1:]


def choose(condition, first, second):
    if isinstance(condition, bool):
        return first if condition else second
    return jnp.where(condition, first, second)


def ring_bounds(slots, index):
    level = slots
    rounds = []
    bit = 0
    while len(level) > 1:
        upper = ((index >> bit) & 1) == 1
        following, nodes = [], []
        for place in range(0, len(level), 2):
            own, other = level[place], level[place + 1]
            left = [jnp.where(upper, b, a) for a, b in zip(own, other)]
            right = [jnp.where(upper, a, b) for a, b in zip(own, other)]
            coefs, node = join_coefs(left[:3], right[:3])
            sides, given = join_sides(left[3:], right[3:], node)
            nodes.append((node, given))
            following.append(coefs + sides)
        rounds.append((nodes, upper))
        level = following
        bit += 1
    _, head, tail, side_head, side_tail = level[0]
    last = (side_head + side_tail) * inverse(head + tail)
    bounds = [(last, last)]
    for nodes, upper in reversed(rounds):
        following = []
        for (node, given), (before, after) in zip(nodes, bounds):
            middle = middle_value(node, given, before, after)
            following.append((jnp.where(upper, middle, before), jnp.where(upper, after, middle)))
            following.append((jnp.where(upper, before, middle), jnp.where(upper, middle, after)))
        bounds = following
    return bounds


def capacity_weights(rates_ref, shares_ref):
    weights = []
    for zone in range(rates_ref.shape[1]):
        rate = jnp.full((SUBLANES, LANES), rates_ref[0, zone], jnp.float32)
        share = jnp.full((SUBLANES, LANES), shares_ref[0, zone], jnp.float32)
        weights.append((share * rate / (1.0 + rate))[0:1, :])
    return weights


def strided(ref, start, size, stride):
    return ref[pl.ds(start, size, stride=stride), :]


def x_rolls(halves):
    return [(step, 0) for step in doubling(SUBLANES)] + [(step, 1) for step in doubling(halves)]


def y_rolls():
    return [(step, 0) for step in doubling(SUBLANES)]


def x_forward_kernel(
    halves, mobile_hbm, faces_hbm, across_hbm, capacity_hbm, immobile_hbm, rates_hbm, shares_hbm,
    message_ref, block_ref,
    mobile_ref, faces_ref, capacity_ref, immobile_ref, rates_ref, shares_ref, arrived,
    faces_t, storage_t, source_t,
):
    rows = mobile_ref.shape[0]
    pairs = (
        (rates_hbm, rates_ref), (shares_hbm, shares_ref), (capacity_hbm, capacity_ref), (faces_hbm, faces_ref),
        (immobile_hbm, immobile_ref), (mobile_hbm, mobile_ref), (across_hbm, block_ref.at[rows : 2 * rows, :]),
    )
    copies = [pltpu.make_async_copy(pair[0], pair[1], arrived.at[place]) for place, pair in enumerate(pairs)]
    for place, copy in enumerate(copies):
        copy.start(priority=int(place in (4, 6)))
    stride = LANES // SUBLANES
    for copy in copies[:3]:
        copy.wait()
    weights = capacity_weights(rates_ref, shares_ref)
    capacity = capacity_ref[...]
    storage = 1.0 + capacity * sum(weights[1:], weights[0])
    block_ref[0:rows, :] = storage
    storage_t[...] = storage.T
    copies[3].wait()
    faces_t[...] = faces_ref[...].T
    copies[4].wait()
    total = None
    for zone, weight in enumerate(weights):
        total = plus(total, weight * immobile_ref[zone * rows : (zone + 1) * rows, :])
    copies[5].wait()
    source_t[...] = (mobile_ref[...] + capacity * total).T
    leaves = []
    for index in range(stride):
        face, held, source = (strided(ref, index, SUBLANES, stride) for ref in (faces_t, storage_t, source_t))
        leaves.append((face, None, held, None, source))
    piece, nodes = tree_all(leaves, x_rolls(halves))
    start = 2 * rows
    for part in [part for node in nodes for part in node]:
        block_ref[start : start + SUBLANES, :] = part
        start += SUBLANES
    for row, value in enumerate(piece):
        message_ref[row : row + 1, :] = value[0:1, :]
        block_ref[start + row : start + row + 1, :] = value[0:1, :]
    copies[6].wait()


def ends_responses(shape):
    one, nothing = jnp.ones(shape, jnp.float32), jnp.zeros(shape, jnp.float32)
    return ((one, nothing), (nothing, one))


def prepare_kernel(halves, own, block_ref, rows_ref, lines_ref, sums_ref, *extra_refs):
    rows = lines_ref.shape[1]
    stride = LANES // SUBLANES
    rolls = x_rolls(halves)
    total = stride - 1 + len(rolls)
    nodes = state_parts(block_ref.at[2 * rows :, :], 0, total, 3)
    own_refs = extra_refs if own else ()
    if not own:
        extra_refs[0][...] = block_ref[-SUBLANES:, :]
    nothing = jnp.zeros((SUBLANES, rows), jnp.float32)
    cases = [((nothing, nothing), [node[2] for node in nodes])]
    cases += [(ends, [0.0] * total) for ends in ends_responses((SUBLANES, rows))]
    for case, (ends, givens) in enumerate(cases):
        for index, value in enumerate(tree_values(*ends, rolls, stride, nodes, givens)):
            lines_ref[pl.ds(case * LANES + index, SUBLANES, stride=stride), :] = value
    stride = rows // SUBLANES
    start = 0
    sublane = lax.broadcasted_iota(jnp.int32, (SUBLANES, LANES), 0) % halves
    tiles = None
    for half in range(halves):
        storage = [strided(block_ref, index, SUBLANES, stride) for index in range(half, stride, halves)]
        faces = [strided(block_ref, rows + index, SUBLANES, stride) for index in range(half, stride, halves)]
        piece, nodes = tree_coefs([(face, None, held) for face, held in zip(faces, storage)], y_rolls())
        for part in [part for node in nodes for part in node] if own_refs else []:
            own_refs[0][start : start + SUBLANES, :] = part
            start += SUBLANES
        values = [jnp.broadcast_to(value[0:1, :], value.shape) for value in piece]
        tiles = [jnp.where(sublane == half, new, old) for new, old in zip(values, tiles or values)]
        for case, ends in enumerate(ends_responses((SUBLANES, LANES))):
            values = tree_values(*ends, y_rolls(), len(storage), nodes, [0.0] * len(nodes))
            for index, (value, held) in enumerate(zip(values, storage)):
                place = pl.ds(case * rows + index * halves + half, SUBLANES, stride=stride)
                sums_ref[place, :] = value * held
                if own_refs:
                    own_refs[1][place, :] = value
    for number, tile in enumerate(tiles):
        rows_ref[:, quantity(number)] = tile


def state_parts(ref, first, total, parts, pitch=3):
    return [
        tuple(
            ref[(pitch * place + part) * SUBLANES : (pitch * place + part + 1) * SUBLANES, :]
            for part in range(parts)
        )
        for place in range(first, first + total)
    ]


def message_slots(refs, height, pitch, quantity_rows, skips):
    blocks = [(ref, start) for ref in refs for start in range(0, ref.shape[0], height)]
    slots = []
    for (ref, start), skip in zip(blocks, skips):
        rows = [start + quantity * pitch + skip for quantity in range(QUANTITIES)]
        slots.append(tuple(ref[row : row + quantity_rows, :] for row in rows))
    return slots


def quantity(number):
    return slice(number * LANES, (number + 1) * LANES)


def along_line(bound, halves, rows):
    value = jnp.broadcast_to(bound, (SUBLANES, rows))
    lane = lax.broadcasted_iota(jnp.int32, value.shape, 1)
    for step in doubling(halves):
        value = jnp.where((lane & step) != 0, behind(value, step, 1), value)
    return value[0:1, :]


def x_back_kernel(halves, axis, order, pieces, *refs):
    lines_refs, sums_refs, rows_refs = (refs[pieces + 2 * pair : pieces + 2 * pair + 2] for pair in range(3))
    last_ref, kept_ref, sent_ref, values_ref = refs[pieces + 6 :]
    slots = message_slots([*refs[:pieces], last_ref], SUBLANES, 1, 1, [0] * len(order))
    slots = [slots[order.index(place)] for place in range(len(order))]
    bounds = ring_bounds(slots, lax.axis_index(axis))
    rows = values_ref.shape[0]

    height = 2 * halves
    first = lax.broadcasted_iota(jnp.int32, (SUBLANES, LANES), 0) < halves

    def put(number, own, other):
        kept_ref[:, quantity(number)] = jnp.where(first, own, other)[0:height, :]
        sent_ref[:, quantity(number)] = jnp.where(first, other, own)[0:height, :]

    for number in range(3):
        put(number, *(ref[:, quantity(number)] for ref in rows_refs))
    sides = []
    for block in range(2):
        lines_ref, sums_ref = lines_refs[block], sums_refs[block]
        before, after = (along_line(bound, halves, rows) for bound in bounds[block])
        values = lines_ref[0:LANES, :] + lines_ref[LANES : 2 * LANES, :] * before + lines_ref[2 * LANES :, :] * after
        values = values.T
        if block == 0:
            values_ref[...] = values
        for end in range(2):
            parts = (values * sums_ref[end * rows : (end + 1) * rows, :]).reshape(-1, SUBLANES, LANES)
            side = jnp.sum(parts, axis=0)
            sides.append(sum([behind(side, step, 0) for step in range(halves, SUBLANES, halves)], side))
    for end in range(2):
        put(3 + end, sides[end], sides[2 + end])


def y_given_kernel(halves, block_ref, values_ref, state_ref, given_ref):
    rows = values_ref.shape[0]
    stride = rows // SUBLANES
    total = stride // halves - 1 + len(y_rolls())
    nothing = jnp.zeros((SUBLANES, LANES), jnp.float32)
    for half in range(halves):
        places = [pl.ds(index, SUBLANES, stride=stride) for index in range(half, stride, halves)]
        sides = [(None, block_ref[place, :] * values_ref[place, :]) for place in places]
        nodes = state_parts(state_ref, half * total, total, 3)
        _, givens = tree_sides(sides, y_rolls(), nodes)
        for place, value in zip(places, tree_values(nothing, nothing, y_rolls(), len(places), nodes, givens)):
            given_ref[place, :] = value


def read_message(ref, rows=None):
    return [ref[0:rows, quantity(number)] for number in range(QUANTITIES)]


def join_by_bit(own, other, upper):
    left = [choose(upper, b, a) for a, b in zip(own, other)]
    right = [choose(upper, a, b) for a, b in zip(own, other)]
    coefs, node = join_coefs(left[:3], right[:3])
    sides, given = join_sides(left[3:], right[3:], node)
    return coefs + sides, (node[0], node[1], given)


def own_bit(axis, bit):
    return ((lax.axis_index(axis) >> bit) & 1) == 1


def y_join_kernel(axis, bit, own_ref, other_ref, kept_ref, sent_ref, path_ref):
    joined, path = join_by_bit(read_message(own_ref), read_message(other_ref), own_bit(axis, bit))
    half = own_ref.shape[0] // 2
    for number, value in enumerate(joined):
        kept_ref[:, quantity(number)] = value
        sent_ref[0:half, quantity(number)] = value[half:, :]
        if sent_ref.shape[0] > half:
            sent_ref[half:, quantity(number)] = value[0:half, :]
    for number, value in enumerate(path):
        path_ref[:, quantity(number)] = value


def y_back_kernel(halves, axis, rounds, own_ref, other_ref, *refs):
    path_refs = refs[: rounds - 1]
    given_ref, spread_ref, out_ref = refs[rounds - 1 :]
    rows = out_ref.shape[0]
    own, other = (read_message(ref, halves) for ref in (own_ref, other_ref))
    joined, path = join_by_bit(own, other, own_bit(axis, rounds - 1))
    _, head, tail, side_head, side_tail = joined
    before = after = (side_head + side_tail) * inverse(head + tail)
    paths = [[ref[0:halves, quantity(number)] for number in range(3)] for ref in path_refs] + [path]
    for bit in reversed(range(rounds)):
        node = paths[bit]
        middle = middle_value(node, node[2], before, after)
        upper = own_bit(axis, bit)
        before = jnp.where(upper, middle, before)
        after = jnp.where(upper, after, middle)
    sublane = lax.broadcasted_iota(jnp.int32, (SUBLANES, LANES), 0) % halves
    ends = []
    for end in (before, after):
        value = jnp.broadcast_to(end[0:1, :], (SUBLANES, LANES))
        for half in range(1, halves):
            value = jnp.where(sublane == half, jnp.broadcast_to(end[half : half + 1, :], value.shape), value)
        ends.append(value)
    for start in range(0, rows, SUBLANES):
        part = slice(start, start + SUBLANES)
        late = slice(rows + start, rows + start + SUBLANES)
        out_ref[part, :] = given_ref[part, :] + spread_ref[part, :] * ends[0] + spread_ref[late, :] * ends[1]


def trade(value, x_step, y_step):
    width = lax.axis_size("yd")
    pairs = []
    for index in range(lax.axis_size("xg")):
        for line in range(width):
            pairs.append((index * width + line, (index ^ x_step) * width + (line ^ y_step)))
    return lax.ppermute(value, ("xg", "yd"), pairs)


def x_exchange(message, block):
    count = lax.axis_size("xg")
    held = message
    pieces = [message]
    order = [0]
    other_block = trade(block, 1, 0)
    for step in doubling(count // 2):
        received = trade(held, 2 * step + 1, 0)
        pieces.append(received)
        order += [place ^ (2 * step + 1) for place in order]
        if 4 * step < count:
            held = jnp.concatenate([held, received], axis=0)
    received = pieces[1] if len(pieces) == 2 else jnp.concatenate(pieces[1:], axis=0)
    pieces.append(trade(received, 1, 0))
    order += [place ^ 1 for place in order[1:]] + [1]
    return pieces, order, other_block


def y_exchange(kept, sent):
    rows = kept.shape[0]
    paths = []
    steps = doubling(lax.axis_size("yd"))
    for bit, step in enumerate(steps):
        received = trade(sent, 1, step)
        if bit < len(steps) - 1:
            kept, sent, path = kernel_call(
                functools.partial(y_join_kernel, "yd", bit),
                (kept, received),
                [held_f32(*kept.shape), f32(rows // 2 if bit == len(steps) - 2 else rows, kept.shape[1]), held_f32(rows, 3 * LANES)],
                [],
            )
            paths.append(path)
    return [kept, received] + paths, len(steps)


def f32(*shape):
    return jax.ShapeDtypeStruct(shape, jnp.float32)


def held_f32(*shape):
    return VMEM(shape, jnp.float32)


def kernel_call(body, operands, outputs, scratch, space=VMEM, cost=500000):
    return pl.pallas_call(
        body,
        out_shape=outputs,
        in_specs=[pl.BlockSpec(memory_space=space)] * len(operands),
        out_specs=[pl.BlockSpec(memory_space=VMEM)] * len(outputs),
        scratch_shapes=scratch,
        cost_estimate=pl.CostEstimate(flops=cost, bytes_accessed=cost, transcendentals=0),
        compiler_params=pltpu.CompilerParams(vmem_limit_bytes=16 * 1024 * 1024),
    )(*operands)


def local(mobile, dispersion_x, dispersion_y, capacity, immobile, exchange_rates, rate_shares):
    shape = mobile.shape
    lines, width = shape[0] * shape[1], shape[2]
    zones = immobile.shape[0]
    halves = width // LANES
    rows = lines * halves
    assert rows == LANES

    def flat(values):
        return values.reshape(-1, LANES)

    mobile, dispersion_x, dispersion_y = flat(mobile), flat(dispersion_x), flat(dispersion_y)
    capacity, immobile = flat(capacity), flat(immobile)
    square = VMEM((rows, LANES), jnp.float32)
    x_nodes = LANES // SUBLANES - 1 + len(x_rolls(halves))
    y_nodes = halves * (rows // SUBLANES // halves - 1 + len(y_rolls()))
    message, block = kernel_call(
        functools.partial(x_forward_kernel, halves),
        tuple(
            pltpu.with_memory_space_constraint(value, pltpu.HBM)
            for value in (
                mobile, dispersion_x, dispersion_y, capacity, immobile, exchange_rates[None], rate_shares[None],
            )
        ),
        [f32(SUBLANES, rows), held_f32(2 * rows + (3 * x_nodes + 1) * SUBLANES, LANES)],
        [square] * 3
        + [VMEM((zones * rows, LANES), jnp.float32)]
        + [pltpu.SMEM((1, zones), jnp.float32)] * 2
        + [pltpu.SemaphoreType.DMA((7,))]
        + [square] * 3,
        pltpu.HBM,
    )
    def prepare(part, own):
        outputs = [held_f32(SUBLANES, 3 * LANES), held_f32(3 * LANES, rows), held_f32(2 * rows, LANES)]
        if own:
            outputs += [held_f32(3 * y_nodes * SUBLANES, LANES), held_f32(2 * rows, LANES)]
        else:
            outputs += [held_f32(SUBLANES, rows)]
        return kernel_call(functools.partial(prepare_kernel, halves, own), (part,), outputs, [], cost=10000000000)

    pieces, order, other_block = x_exchange(message, block)
    y_rows, lines_x, sums, y_state, spread = prepare(block, True)
    other_rows, other_lines, other_sums, other_message = prepare(other_block, False)
    kept, sent, values = kernel_call(
        functools.partial(x_back_kernel, halves, "xg", order, len(pieces)),
        (*pieces, lines_x, other_lines, sums, other_sums, y_rows, other_rows, other_message),
        [
            held_f32(2 * halves, QUANTITIES * LANES),
            f32(2 * halves, QUANTITIES * LANES),
            held_f32(rows, LANES),
        ],
        [],
    )
    (given,) = kernel_call(
        functools.partial(y_given_kernel, halves), (block, values, y_state), [held_f32(rows, LANES)], []
    )
    pieces, rounds = y_exchange(kept, sent)
    (updated,) = kernel_call(
        functools.partial(y_back_kernel, halves, "yd", rounds),
        (*pieces, given, spread),
        [f32(rows, LANES)],
        [],
    )
    return updated.reshape(shape)


def solution(mesh):
    field = P("yd", None, "xg")
    return jax.shard_map(
        local,
        mesh=mesh,
        in_specs=(field, field, field, field, P(None, "yd", None, "xg"), P(), P()),
        out_specs=field,
        check_vma=False,
    )
```

```python
import functools

import jax
import jax.numpy as jnp
from jax import lax
from jax.experimental import pallas as pl
from jax.experimental.pallas import tpu as pltpu
from jax.sharding import PartitionSpec as P

LANES = 128
SUBLANES = 8
QUANTITIES = 5
VMEM = pltpu.VMEM


def inverse(value):
    return 1.0 / value


def plus(first, second):
    if first is None:
        return second
    return first + second


def join_coefs(left, right):
    coupling_1, head_1, tail_1 = left
    coupling_2, head_2, tail_2 = right
    middle = plus(head_2, tail_1)
    inv = inverse(coupling_1 + coupling_2 + middle)
    weight_1 = coupling_1 * inv
    weight_2 = coupling_2 * inv
    joined = (coupling_1 * weight_2, plus(head_1, weight_1 * middle), tail_2 + weight_2 * middle)
    return joined, (weight_1, weight_2, inv)


def join_sides(left, right, node):
    head_1, tail_1 = left
    head_2, tail_2 = right
    weight_1, weight_2, inv = node
    side = plus(head_2, tail_1)
    joined = (plus(head_1, weight_1 * side), tail_2 + weight_2 * side)
    return joined, side * inv


def middle_value(node, given, before, after):
    return given + node[0] * before + node[1] * after


def ahead(value, step, axis):
    return pltpu.roll(value, value.shape[axis] - step, axis)


def behind(value, step, axis):
    return pltpu.roll(value, step, axis)


def doubling(count):
    steps = []
    step = 1
    while step < count:
        steps.append(step)
        step *= 2
    return steps


def tree_coefs(leaves, rolls):
    nodes = []
    level = leaves
    while len(level) > 1:
        following = []
        for index in range(0, len(level), 2):
            joined, node = join_coefs(level[index], level[index + 1])
            following.append(joined)
            nodes.append(node)
        level = following
    piece = level[0]
    for step, axis in rolls:
        piece, node = join_coefs(piece, tuple(ahead(part, step, axis) for part in piece))
        nodes.append(node)
    return piece, nodes


def tree_sides(leaves, rolls, nodes):
    givens = []
    level = leaves
    while len(level) > 1:
        following = []
        for index in range(0, len(level), 2):
            joined, given = join_sides(level[index], level[index + 1], nodes[len(givens)])
            following.append(joined)
            givens.append(given)
        level = following
    piece = level[0]
    for step, axis in rolls:
        other = tuple(ahead(part, step, axis) for part in piece)
        piece, given = join_sides(piece, other, nodes[len(givens)])
        givens.append(given)
    return piece, givens


def join_all(left, right):
    coefs, node = join_coefs(left[:3], right[:3])
    sides, given = join_sides(left[3:], right[3:], node)
    return coefs + sides, (node[0], node[1], given)


def tree_all(leaves, rolls):
    nodes = []
    level = leaves
    while len(level) > 1:
        pairs = [join_all(level[index], level[index + 1]) for index in range(0, len(level), 2)]
        nodes += [node for _, node in pairs]
        level = [joined for joined, _ in pairs]
    piece = level[0]
    count = SUBLANES
    level = [piece] + [tuple(ahead(part, step, 0) for part in piece) for step in range(1, count)]
    while len(level) > 1:
        pairs = [join_all(level[index], level[index + 1]) for index in range(0, len(level), 2)]
        nodes.append(pairs[0][1])
        level = [joined for joined, _ in pairs]
    piece = level[0]
    for step, axis in rolls[len(doubling(count)) :]:
        piece, node = join_all(piece, tuple(ahead(part, step, axis) for part in piece))
        nodes.append(node)
    return piece, nodes


def tree_values(before, after, rolls, count, nodes, givens):
    place = len(nodes)
    for step, axis in reversed(rolls):
        place -= 1
        middle = middle_value(nodes[place], givens[place], before, after)
        upper = (lax.broadcasted_iota(jnp.int32, middle.shape, axis) & step) != 0
        before = jnp.where(upper, behind(middle, step, axis), before)
        after = jnp.where(upper, behind(after, step, axis), middle)
    bounds = [before, after]
    while len(bounds) - 1 < count:
        width = len(bounds) - 1
        place -= width
        following = [bounds[0]]
        for index in range(width):
            following.append(
                middle_value(
                    nodes[place + index], givens[place + index], bounds[index], bounds[index + 1]
                )
            )
            following.append(bounds[index + 1])
        bounds = following
    return bounds[1:]


def choose(condition, first, second):
    if isinstance(condition, bool):
        return first if condition else second
    return jnp.where(condition, first, second)


def ring_bounds(slots, index):
    level = slots
    rounds = []
    bit = 0
    while len(level) > 1:
        upper = ((index >> bit) & 1) == 1
        following, nodes = [], []
        for place in range(0, len(level), 2):
            own, other = level[place], level[place + 1]
            left = [jnp.where(upper, b, a) for a, b in zip(own, other)]
            right = [jnp.where(upper, a, b) for a, b in zip(own, other)]
            coefs, node = join_coefs(left[:3], right[:3])
            sides, given = join_sides(left[3:], right[3:], node)
            nodes.append((node, given))
            following.append(coefs + sides)
        rounds.append((nodes, upper))
        level = following
        bit += 1
    _, head, tail, side_head, side_tail = level[0]
    last = (side_head + side_tail) * inverse(head + tail)
    bounds = [(last, last)]
    for nodes, upper in reversed(rounds):
        following = []
        for (node, given), (before, after) in zip(nodes, bounds):
            middle = middle_value(node, given, before, after)
            following.append((jnp.where(upper, middle, before), jnp.where(upper, after, middle)))
            following.append((jnp.where(upper, before, middle), jnp.where(upper, middle, after)))
        bounds = following
    return bounds


def capacity_weights(rates_ref, shares_ref):
    weights = []
    for zone in range(rates_ref.shape[1]):
        rate = jnp.full((SUBLANES, LANES), rates_ref[0, zone], jnp.float32)
        share = jnp.full((SUBLANES, LANES), shares_ref[0, zone], jnp.float32)
        weights.append((share * rate / (1.0 + rate))[0:1, :])
    return weights


def strided(ref, start, size, stride):
    return ref[pl.ds(start, size, stride=stride), :]


def x_rolls(halves):
    return [(step, 0) for step in doubling(SUBLANES)] + [(step, 1) for step in doubling(halves)]


def y_rolls():
    return [(step, 0) for step in doubling(SUBLANES)]


def x_forward_kernel(
    halves, mobile_hbm, faces_hbm, across_hbm, capacity_hbm, immobile_hbm, rates_hbm, shares_hbm,
    message_ref, block_ref,
    mobile_ref, faces_ref, capacity_ref, immobile_ref, rates_ref, shares_ref, arrived,
    faces_t, storage_t, source_t,
):
    rows = mobile_ref.shape[0]
    pairs = (
        (rates_hbm, rates_ref), (shares_hbm, shares_ref), (capacity_hbm, capacity_ref), (faces_hbm, faces_ref),
        (immobile_hbm, immobile_ref), (mobile_hbm, mobile_ref), (across_hbm, block_ref.at[rows : 2 * rows, :]),
    )
    copies = [pltpu.make_async_copy(pair[0], pair[1], arrived.at[place]) for place, pair in enumerate(pairs)]
    for place, copy in enumerate(copies):
        copy.start(priority=int(place in (4, 6)))
    stride = LANES // SUBLANES
    for copy in copies[:3]:
        copy.wait()
    weights = capacity_weights(rates_ref, shares_ref)
    capacity = capacity_ref[...]
    storage = 1.0 + capacity * sum(weights[1:], weights[0])
    block_ref[0:rows, :] = storage
    storage_t[0:LANES, :] = storage.T
    copies[3].wait()
    faces_t[0:LANES, :] = faces_ref[...].T
    copies[4].wait()
    total = None
    for zone, weight in enumerate(weights):
        total = plus(total, weight * immobile_ref[zone * rows : (zone + 1) * rows, :])
    copies[5].wait()
    source_t[0:LANES, :] = (mobile_ref[...] + capacity * total).T
    leaves = []
    for index in range(stride):
        face, held, source = (strided(ref, index, SUBLANES, stride) for ref in (faces_t, storage_t, source_t))
        leaves.append((face, None, held, None, source))
    piece, nodes = tree_all(leaves, x_rolls(halves))
    start = 2 * rows
    for part in [part for node in nodes for part in node]:
        block_ref[start : start + SUBLANES, :] = part
        start += SUBLANES
    for row, value in enumerate(piece):
        message_ref[row : row + 1, :] = value[0:1, :]
        block_ref[start + row : start + row + 1, :] = value[0:1, :]
    copies[6].wait()


def ends_responses(shape):
    one, nothing = jnp.ones(shape, jnp.float32), jnp.zeros(shape, jnp.float32)
    return ((one, nothing), (nothing, one))


def prepare_kernel(halves, own, block_ref, rows_ref, lines_ref, sums_ref, *extra_refs):
    rows = lines_ref.shape[1]
    stride = LANES // SUBLANES
    rolls = x_rolls(halves)
    total = stride - 1 + len(rolls)
    nodes = state_parts(block_ref.at[2 * rows :, :], 0, total, 3)
    own_refs = extra_refs if own else ()
    if not own:
        extra_refs[0][...] = block_ref[-SUBLANES:, :]
    nothing = jnp.zeros((SUBLANES, rows), jnp.float32)
    cases = [((nothing, nothing), [node[2] for node in nodes])]
    cases += [(ends, [0.0] * total) for ends in ends_responses((SUBLANES, rows))]
    for case, (ends, givens) in enumerate(cases):
        for index, value in enumerate(tree_values(*ends, rolls, stride, nodes, givens)):
            lines_ref[pl.ds(case * LANES + index, SUBLANES, stride=stride), :] = value
    stride = rows // SUBLANES
    start = 0
    sublane = lax.broadcasted_iota(jnp.int32, (SUBLANES, LANES), 0) % halves
    tiles = None
    for half in range(halves):
        storage = [strided(block_ref, index, SUBLANES, stride) for index in range(half, stride, halves)]
        faces = [strided(block_ref, rows + index, SUBLANES, stride) for index in range(half, stride, halves)]
        piece, nodes = tree_coefs([(face, None, held) for face, held in zip(faces, storage)], y_rolls())
        for part in [part for node in nodes for part in node] if own_refs else []:
            own_refs[0][start : start + SUBLANES, :] = part
            start += SUBLANES
        values = [jnp.broadcast_to(value[0:1, :], value.shape) for value in piece]
        tiles = [jnp.where(sublane == half, new, old) for new, old in zip(values, tiles or values)]
        for case, ends in enumerate(ends_responses((SUBLANES, LANES))):
            values = tree_values(*ends, y_rolls(), len(storage), nodes, [0.0] * len(nodes))
            for index, (value, held) in enumerate(zip(values, storage)):
                place = pl.ds(case * rows + index * halves + half, SUBLANES, stride=stride)
                sums_ref[place, :] = value * held
                if own_refs:
                    own_refs[1][place, :] = value
    for number, tile in enumerate(tiles):
        rows_ref[:, quantity(number)] = tile


def state_parts(ref, first, total, parts, pitch=3):
    return [
        tuple(
            ref[(pitch * place + part) * SUBLANES : (pitch * place + part + 1) * SUBLANES, :]
            for part in range(parts)
        )
        for place in range(first, first + total)
    ]


def message_slots(refs, height, pitch, quantity_rows, skips):
    blocks = [(ref, start) for ref in refs for start in range(0, ref.shape[0], height)]
    slots = []
    for (ref, start), skip in zip(blocks, skips):
        rows = [start + quantity * pitch + skip for quantity in range(QUANTITIES)]
        slots.append(tuple(ref[row : row + quantity_rows, :] for row in rows))
    return slots


def quantity(number):
    return slice(number * LANES, (number + 1) * LANES)


def along_line(bound, halves, rows):
    value = jnp.broadcast_to(bound, (SUBLANES, rows))
    lane = lax.broadcasted_iota(jnp.int32, value.shape, 1)
    for step in doubling(halves):
        value = jnp.where((lane & step) != 0, behind(value, step, 1), value)
    return value[0:1, :]


def x_back_kernel(halves, axis, order, pieces, *refs):
    lines_refs, sums_refs, rows_refs = (refs[pieces + 2 * pair : pieces + 2 * pair + 2] for pair in range(3))
    last_ref, kept_ref, sent_ref, values_ref = refs[pieces + 6 :]
    slots = message_slots([*refs[:pieces], last_ref], SUBLANES, 1, 1, [0] * len(order))
    slots = [slots[order.index(place)] for place in range(len(order))]
    bounds = ring_bounds(slots, lax.axis_index(axis))
    rows = lines_refs[0].shape[1]

    height = 2 * halves
    first = lax.broadcasted_iota(jnp.int32, (SUBLANES, LANES), 0) < halves

    def put(number, own, other):
        kept_ref[:, quantity(number)] = jnp.where(first, own, other)[0:height, :]
        sent_ref[:, quantity(number)] = jnp.where(first, other, own)[0:height, :]

    for number in range(3):
        put(number, *(ref[:, quantity(number)] for ref in rows_refs))
    sides = []
    for block in range(2):
        lines_ref, sums_ref = lines_refs[block], sums_refs[block]
        before, after = (along_line(bound, halves, rows) for bound in bounds[block])
        values = lines_ref[0:LANES, :] + lines_ref[LANES : 2 * LANES, :] * before + lines_ref[2 * LANES : 3 * LANES, :] * after
        values = values.T
        if block == 0:
            values_ref[0:rows, :] = values
        for end in range(2):
            parts = (values * sums_ref[end * rows : (end + 1) * rows, :]).reshape(-1, SUBLANES, LANES)
            side = jnp.sum(parts, axis=0)
            sides.append(sum([behind(side, step, 0) for step in range(halves, SUBLANES, halves)], side))
    for end in range(2):
        put(3 + end, sides[end], sides[2 + end])


def y_given_kernel(halves, rows, block_ref, values_ref, state_ref, given_ref):
    stride = rows // SUBLANES
    total = stride // halves - 1 + len(y_rolls())
    nothing = jnp.zeros((SUBLANES, LANES), jnp.float32)
    for half in range(halves):
        places = [pl.ds(index, SUBLANES, stride=stride) for index in range(half, stride, halves)]
        sides = [(None, block_ref[place, :] * values_ref[place, :]) for place in places]
        nodes = state_parts(state_ref, half * total, total, 3)
        _, givens = tree_sides(sides, y_rolls(), nodes)
        for place, value in zip(places, tree_values(nothing, nothing, y_rolls(), len(places), nodes, givens)):
            given_ref[place, :] = value


def read_message(ref, rows=None):
    return [ref[0:rows, quantity(number)] for number in range(QUANTITIES)]


def join_by_bit(own, other, upper):
    left = [choose(upper, b, a) for a, b in zip(own, other)]
    right = [choose(upper, a, b) for a, b in zip(own, other)]
    coefs, node = join_coefs(left[:3], right[:3])
    sides, given = join_sides(left[3:], right[3:], node)
    return coefs + sides, (node[0], node[1], given)


def own_bit(axis, bit):
    return ((lax.axis_index(axis) >> bit) & 1) == 1


def y_join_kernel(axis, bit, own_ref, other_ref, kept_ref, sent_ref, path_ref):
    joined, path = join_by_bit(read_message(own_ref), read_message(other_ref), own_bit(axis, bit))
    half = own_ref.shape[0] // 2
    for number, value in enumerate(joined):
        kept_ref[:, quantity(number)] = value
        sent_ref[0:half, quantity(number)] = value[half:, :]
        if sent_ref.shape[0] > half:
            sent_ref[half:, quantity(number)] = value[0:half, :]
    for number, value in enumerate(path):
        path_ref[:, quantity(number)] = value


def y_back_kernel(halves, axis, rounds, own_ref, other_ref, *refs):
    path_refs = refs[: rounds - 1]
    given_ref, spread_ref, out_ref = refs[rounds - 1 :]
    rows = out_ref.shape[0]
    own, other = (read_message(ref, halves) for ref in (own_ref, other_ref))
    joined, path = join_by_bit(own, other, own_bit(axis, rounds - 1))
    _, head, tail, side_head, side_tail = joined
    before = after = (side_head + side_tail) * inverse(head + tail)
    paths = [[ref[0:halves, quantity(number)] for number in range(3)] for ref in path_refs] + [path]
    for bit in reversed(range(rounds)):
        node = paths[bit]
        middle = middle_value(node, node[2], before, after)
        upper = own_bit(axis, bit)
        before = jnp.where(upper, middle, before)
        after = jnp.where(upper, after, middle)
    sublane = lax.broadcasted_iota(jnp.int32, (SUBLANES, LANES), 0) % halves
    ends = []
    for end in (before, after):
        value = jnp.broadcast_to(end[0:1, :], (SUBLANES, LANES))
        for half in range(1, halves):
            value = jnp.where(sublane == half, jnp.broadcast_to(end[half : half + 1, :], value.shape), value)
        ends.append(value)
    for start in range(0, rows, SUBLANES):
        part = slice(start, start + SUBLANES)
        late = slice(rows + start, rows + start + SUBLANES)
        out_ref[part, :] = given_ref[part, :] + spread_ref[part, :] * ends[0] + spread_ref[late, :] * ends[1]


def trade(value, x_step, y_step):
    width = lax.axis_size("yd")
    pairs = []
    for index in range(lax.axis_size("xg")):
        for line in range(width):
            pairs.append((index * width + line, (index ^ x_step) * width + (line ^ y_step)))
    return lax.ppermute(value, ("xg", "yd"), pairs)


def x_exchange(message, block):
    count = lax.axis_size("xg")
    held = message
    pieces = [message]
    order = [0]
    other_block = trade(block, 1, 0)
    for step in doubling(count // 2):
        received = trade(held, 2 * step + 1, 0)
        pieces.append(received)
        order += [place ^ (2 * step + 1) for place in order]
        if 4 * step < count:
            held = jnp.concatenate([held, received], axis=0)
    received = pieces[1] if len(pieces) == 2 else jnp.concatenate(pieces[1:], axis=0)
    pieces.append(trade(received, 1, 0))
    order += [place ^ 1 for place in order[1:]] + [1]
    return pieces, order, other_block


def y_exchange(kept, sent):
    rows = kept.shape[0]
    paths = []
    steps = doubling(lax.axis_size("yd"))
    for bit, step in enumerate(steps):
        received = trade(sent, 1, step)
        if bit < len(steps) - 1:
            kept, sent, path = kernel_call(
                functools.partial(y_join_kernel, "yd", bit),
                (kept, received),
                [held_f32(*kept.shape), f32(rows // 2 if bit == len(steps) - 2 else rows, kept.shape[1]), held_f32(rows, 3 * LANES)],
                [],
            )
            paths.append(path)
    return [kept, received] + paths, len(steps)


def f32(*shape):
    return jax.ShapeDtypeStruct(shape, jnp.float32)


def held_f32(*shape):
    return VMEM(shape, jnp.float32)


def kernel_call(body, operands, outputs, scratch, space=VMEM, cost=500000):
    return pl.pallas_call(
        body,
        out_shape=outputs,
        in_specs=[pl.BlockSpec(memory_space=space)] * len(operands),
        out_specs=[pl.BlockSpec(memory_space=VMEM)] * len(outputs),
        scratch_shapes=scratch,
        cost_estimate=pl.CostEstimate(flops=cost, bytes_accessed=cost, transcendentals=0),
        compiler_params=pltpu.CompilerParams(vmem_limit_bytes=16 * 1024 * 1024),
    )(*operands)


def local(mobile, dispersion_x, dispersion_y, capacity, immobile, exchange_rates, rate_shares):
    shape = mobile.shape
    lines, width = shape[0] * shape[1], shape[2]
    zones = immobile.shape[0]
    halves = width // LANES
    rows = lines * halves
    assert rows == LANES

    def flat(values):
        return values.reshape(-1, LANES)

    mobile, dispersion_x, dispersion_y = flat(mobile), flat(dispersion_x), flat(dispersion_y)
    capacity, immobile = flat(capacity), flat(immobile)
    square = VMEM((rows, LANES), jnp.float32)
    spare = max(rows, LANES) // SUBLANES
    x_nodes = LANES // SUBLANES - 1 + len(x_rolls(halves))
    y_nodes = halves * (rows // SUBLANES // halves - 1 + len(y_rolls()))
    message, block = kernel_call(
        functools.partial(x_forward_kernel, halves),
        tuple(
            pltpu.with_memory_space_constraint(value, pltpu.HBM)
            for value in (
                mobile, dispersion_x, dispersion_y, capacity, immobile, exchange_rates[None], rate_shares[None],
            )
        ),
        [f32(SUBLANES, rows), held_f32(2 * rows + (3 * x_nodes + 1) * SUBLANES, LANES)],
        [square] * 3
        + [VMEM((zones * rows, LANES), jnp.float32)]
        + [pltpu.SMEM((1, zones), jnp.float32)] * 2
        + [pltpu.SemaphoreType.DMA((7,))]
        + [VMEM((LANES + LANES // SUBLANES, rows), jnp.float32)] * 3,
        pltpu.HBM,
    )
    def prepare(part, own):
        outputs = [held_f32(SUBLANES, 3 * LANES), held_f32(3 * LANES + spare, rows), held_f32(2 * rows + spare, LANES)]
        if own:
            outputs += [held_f32(3 * y_nodes * SUBLANES, LANES), held_f32(2 * rows + spare, LANES)]
        else:
            outputs += [held_f32(SUBLANES, rows)]
        return kernel_call(functools.partial(prepare_kernel, halves, own), (part,), outputs, [], cost=10000000000)

    pieces, order, other_block = x_exchange(message, block)
    y_rows, lines_x, sums, y_state, spread = prepare(block, True)
    other_rows, other_lines, other_sums, other_message = prepare(other_block, False)
    kept, sent, values = kernel_call(
        functools.partial(x_back_kernel, halves, "xg", order, len(pieces)),
        (*pieces, lines_x, other_lines, sums, other_sums, y_rows, other_rows, other_message),
        [
            held_f32(2 * halves, QUANTITIES * LANES),
            f32(2 * halves, QUANTITIES * LANES),
            held_f32(rows + spare, LANES),
        ],
        [],
    )
    (given,) = kernel_call(
        functools.partial(y_given_kernel, halves, rows), (block, values, y_state), [held_f32(rows + spare, LANES)], []
    )
    pieces, rounds = y_exchange(kept, sent)
    (updated,) = kernel_call(
        functools.partial(y_back_kernel, halves, "yd", rounds),
        (*pieces, given, spread),
        [f32(rows, LANES)],
        [],
    )
    return updated.reshape(shape)


def solution(mesh):
    field = P("yd", None, "xg")
    return jax.shard_map(
        local,
        mesh=mesh,
        in_specs=(field, field, field, field, P(None, "yd", None, "xg"), P(), P()),
        out_specs=field,
        check_vma=False,
    )
```

```python
import functools

import jax
import jax.numpy as jnp
from jax import lax
from jax.experimental import pallas as pl
from jax.experimental.pallas import tpu as pltpu
from jax.sharding import PartitionSpec as P

LANES = 128
SUBLANES = 8
QUANTITIES = 5
VMEM = pltpu.VMEM


def inverse(value):
    return 1.0 / value


def plus(first, second):
    if first is None:
        return second
    return first + second


def join_coefs(left, right):
    coupling_1, head_1, tail_1 = left
    coupling_2, head_2, tail_2 = right
    middle = plus(head_2, tail_1)
    inv = inverse(coupling_1 + coupling_2 + middle)
    weight_1 = coupling_1 * inv
    weight_2 = coupling_2 * inv
    joined = (coupling_1 * weight_2, plus(head_1, weight_1 * middle), tail_2 + weight_2 * middle)
    return joined, (weight_1, weight_2, inv)


def join_sides(left, right, node):
    head_1, tail_1 = left
    head_2, tail_2 = right
    weight_1, weight_2, inv = node
    side = plus(head_2, tail_1)
    joined = (plus(head_1, weight_1 * side), tail_2 + weight_2 * side)
    return joined, side * inv


def middle_value(node, given, before, after):
    return given + node[0] * before + node[1] * after


def ahead(value, step, axis):
    return pltpu.roll(value, value.shape[axis] - step, axis)


def behind(value, step, axis):
    return pltpu.roll(value, step, axis)


def doubling(count):
    steps = []
    step = 1
    while step < count:
        steps.append(step)
        step *= 2
    return steps


def tree_coefs(leaves, rolls):
    nodes = []
    level = leaves
    while len(level) > 1:
        following = []
        for index in range(0, len(level), 2):
            joined, node = join_coefs(level[index], level[index + 1])
            following.append(joined)
            nodes.append(node)
        level = following
    piece = level[0]
    for step, axis in rolls:
        piece, node = join_coefs(piece, tuple(ahead(part, step, axis) for part in piece))
        nodes.append(node)
    return piece, nodes


def tree_sides(leaves, rolls, nodes):
    givens = []
    level = leaves
    while len(level) > 1:
        following = []
        for index in range(0, len(level), 2):
            joined, given = join_sides(level[index], level[index + 1], nodes[len(givens)])
            following.append(joined)
            givens.append(given)
        level = following
    piece = level[0]
    for step, axis in rolls:
        other = tuple(ahead(part, step, axis) for part in piece)
        piece, given = join_sides(piece, other, nodes[len(givens)])
        givens.append(given)
    return piece, givens


def join_all(left, right):
    coefs, node = join_coefs(left[:3], right[:3])
    sides, given = join_sides(left[3:], right[3:], node)
    return coefs + sides, (node[0], node[1], given)


def tree_all(leaves, rolls):
    nodes = []
    level = leaves
    while len(level) > 1:
        pairs = [join_all(level[index], level[index + 1]) for index in range(0, len(level), 2)]
        nodes += [node for _, node in pairs]
        level = [joined for joined, _ in pairs]
    piece = level[0]
    count = SUBLANES
    level = [piece] + [tuple(ahead(part, step, 0) for part in piece) for step in range(1, count)]
    while len(level) > 1:
        pairs = [join_all(level[index], level[index + 1]) for index in range(0, len(level), 2)]
        nodes.append(pairs[0][1])
        level = [joined for joined, _ in pairs]
    piece = level[0]
    for step, axis in rolls[len(doubling(count)) :]:
        piece, node = join_all(piece, tuple(ahead(part, step, axis) for part in piece))
        nodes.append(node)
    return piece, nodes


def tree_values(before, after, rolls, count, nodes, givens):
    place = len(nodes)
    for step, axis in reversed(rolls):
        place -= 1
        middle = middle_value(nodes[place], givens[place], before, after)
        upper = (lax.broadcasted_iota(jnp.int32, middle.shape, axis) & step) != 0
        before = jnp.where(upper, behind(middle, step, axis), before)
        after = jnp.where(upper, behind(after, step, axis), middle)
    bounds = [before, after]
    while len(bounds) - 1 < count:
        width = len(bounds) - 1
        place -= width
        following = [bounds[0]]
        for index in range(width):
            following.append(
                middle_value(
                    nodes[place + index], givens[place + index], bounds[index], bounds[index + 1]
                )
            )
            following.append(bounds[index + 1])
        bounds = following
    return bounds[1:]


def choose(condition, first, second):
    if isinstance(condition, bool):
        return first if condition else second
    return jnp.where(condition, first, second)


def ring_bounds(slots, index):
    level = slots
    rounds = []
    bit = 0
    while len(level) > 1:
        upper = ((index >> bit) & 1) == 1
        following, nodes = [], []
        for place in range(0, len(level), 2):
            own, other = level[place], level[place + 1]
            left = [jnp.where(upper, b, a) for a, b in zip(own, other)]
            right = [jnp.where(upper, a, b) for a, b in zip(own, other)]
            coefs, node = join_coefs(left[:3], right[:3])
            sides, given = join_sides(left[3:], right[3:], node)
            nodes.append((node, given))
            following.append(coefs + sides)
        rounds.append((nodes, upper))
        level = following
        bit += 1
    _, head, tail, side_head, side_tail = level[0]
    last = (side_head + side_tail) * inverse(head + tail)
    bounds = [(last, last)]
    for nodes, upper in reversed(rounds):
        following = []
        for (node, given), (before, after) in zip(nodes, bounds):
            middle = middle_value(node, given, before, after)
            following.append((jnp.where(upper, middle, before), jnp.where(upper, after, middle)))
            following.append((jnp.where(upper, before, middle), jnp.where(upper, middle, after)))
        bounds = following
    return bounds


def capacity_weights(rates_ref, shares_ref):
    weights = []
    for zone in range(rates_ref.shape[1]):
        rate = jnp.full((SUBLANES, LANES), rates_ref[0, zone], jnp.float32)
        share = jnp.full((SUBLANES, LANES), shares_ref[0, zone], jnp.float32)
        weights.append((share * rate / (1.0 + rate))[0:1, :])
    return weights


def strided(ref, start, size, stride):
    return ref[pl.ds(start, size, stride=stride), :]


def x_rolls(halves):
    return [(step, 0) for step in doubling(SUBLANES)] + [(step, 1) for step in doubling(halves)]


def y_rolls():
    return [(step, 0) for step in doubling(SUBLANES)]


def x_forward_kernel(
    halves, mobile_hbm, faces_hbm, across_hbm, capacity_hbm, immobile_hbm, rates_hbm, shares_hbm,
    message_ref, block_ref,
    mobile_ref, faces_ref, capacity_ref, immobile_ref, rates_ref, shares_ref, arrived,
    faces_t, storage_t, source_t,
):
    rows = mobile_ref.shape[0]
    pairs = (
        (faces_hbm, faces_ref), (capacity_hbm, capacity_ref), (rates_hbm, rates_ref), (shares_hbm, shares_ref),
        (immobile_hbm, immobile_ref), (mobile_hbm, mobile_ref), (across_hbm, block_ref.at[rows : 2 * rows, :]),
    )
    copies = [pltpu.make_async_copy(pair[0], pair[1], arrived.at[place]) for place, pair in enumerate(pairs)]
    for place, copy in enumerate(copies):
        copy.start(priority=int(place in (4, 6)))
    stride = LANES // SUBLANES
    copies[0].wait()
    faces_t[0:LANES, :] = faces_ref[...].T
    for copy in copies[1:4]:
        copy.wait()
    weights = capacity_weights(rates_ref, shares_ref)
    capacity = capacity_ref[...]
    storage = 1.0 + capacity * sum(weights[1:], weights[0])
    block_ref[0:rows, :] = storage
    storage_t[0:LANES, :] = storage.T
    copies[4].wait()
    total = None
    for zone, weight in enumerate(weights):
        total = plus(total, weight * immobile_ref[zone * rows : (zone + 1) * rows, :])
    copies[5].wait()
    source_t[0:LANES, :] = (mobile_ref[...] + capacity * total).T
    leaves = []
    for index in range(stride):
        face, held, source = (strided(ref, index, SUBLANES, stride) for ref in (faces_t, storage_t, source_t))
        leaves.append((face, None, held, None, source))
    piece, nodes = tree_all(leaves, x_rolls(halves))
    start = 2 * rows
    for part in [part for node in nodes for part in node]:
        block_ref[start : start + SUBLANES, :] = part
        start += SUBLANES
    for row, value in enumerate(piece):
        message_ref[row : row + 1, :] = value[0:1, :]
        block_ref[start + row : start + row + 1, :] = value[0:1, :]
    copies[6].wait()


def ends_responses(shape):
    one, nothing = jnp.ones(shape, jnp.float32), jnp.zeros(shape, jnp.float32)
    return ((one, nothing), (nothing, one))


def prepare_kernel(halves, own, block_ref, rows_ref, lines_ref, sums_ref, *extra_refs):
    rows = lines_ref.shape[1]
    stride = LANES // SUBLANES
    rolls = x_rolls(halves)
    total = stride - 1 + len(rolls)
    nodes = state_parts(block_ref.at[2 * rows :, :], 0, total, 3)
    own_refs = extra_refs if own else ()
    if not own:
        extra_refs[0][...] = block_ref[-SUBLANES:, :]
    nothing = jnp.zeros((SUBLANES, rows), jnp.float32)
    cases = [((nothing, nothing), [node[2] for node in nodes])]
    cases += [(ends, [0.0] * total) for ends in ends_responses((SUBLANES, rows))]
    for case, (ends, givens) in enumerate(cases):
        for index, value in enumerate(tree_values(*ends, rolls, stride, nodes, givens)):
            lines_ref[pl.ds(case * LANES + index, SUBLANES, stride=stride), :] = value
    stride = rows // SUBLANES
    start = 0
    sublane = lax.broadcasted_iota(jnp.int32, (SUBLANES, LANES), 0) % halves
    tiles = None
    for half in range(halves):
        storage = [strided(block_ref, index, SUBLANES, stride) for index in range(half, stride, halves)]
        faces = [strided(block_ref, rows + index, SUBLANES, stride) for index in range(half, stride, halves)]
        piece, nodes = tree_coefs([(face, None, held) for face, held in zip(faces, storage)], y_rolls())
        for part in [part for node in nodes for part in node] if own_refs else []:
            own_refs[0][start : start + SUBLANES, :] = part
            start += SUBLANES
        values = [jnp.broadcast_to(value[0:1, :], value.shape) for value in piece]
        tiles = [jnp.where(sublane == half, new, old) for new, old in zip(values, tiles or values)]
        for case, ends in enumerate(ends_responses((SUBLANES, LANES))):
            values = tree_values(*ends, y_rolls(), len(storage), nodes, [0.0] * len(nodes))
            for index, (value, held) in enumerate(zip(values, storage)):
                place = pl.ds(case * rows + index * halves + half, SUBLANES, stride=stride)
                sums_ref[place, :] = value * held
                if own_refs:
                    own_refs[1][place, :] = value
    for number, tile in enumerate(tiles):
        rows_ref[:, quantity(number)] = tile


def state_parts(ref, first, total, parts, pitch=3):
    return [
        tuple(
            ref[(pitch * place + part) * SUBLANES : (pitch * place + part + 1) * SUBLANES, :]
            for part in range(parts)
        )
        for place in range(first, first + total)
    ]


def message_slots(refs, height, pitch, quantity_rows, skips):
    blocks = [(ref, start) for ref in refs for start in range(0, ref.shape[0], height)]
    slots = []
    for (ref, start), skip in zip(blocks, skips):
        rows = [start + quantity * pitch + skip for quantity in range(QUANTITIES)]
        slots.append(tuple(ref[row : row + quantity_rows, :] for row in rows))
    return slots


def quantity(number):
    return slice(number * LANES, (number + 1) * LANES)


def along_line(bound, halves, rows):
    value = jnp.broadcast_to(bound, (SUBLANES, rows))
    lane = lax.broadcasted_iota(jnp.int32, value.shape, 1)
    for step in doubling(halves):
        value = jnp.where((lane & step) != 0, behind(value, step, 1), value)
    return value[0:1, :]


def x_back_kernel(halves, axis, order, pieces, *refs):
    lines_refs, sums_refs, rows_refs = (refs[pieces + 2 * pair : pieces + 2 * pair + 2] for pair in range(3))
    last_ref, kept_ref, sent_ref, values_ref = refs[pieces + 6 :]
    slots = message_slots([*refs[:pieces], last_ref], SUBLANES, 1, 1, [0] * len(order))
    slots = [slots[order.index(place)] for place in range(len(order))]
    bounds = ring_bounds(slots, lax.axis_index(axis))
    rows = lines_refs[0].shape[1]

    height = 2 * halves
    first = lax.broadcasted_iota(jnp.int32, (SUBLANES, LANES), 0) < halves

    def put(number, own, other):
        kept_ref[:, quantity(number)] = jnp.where(first, own, other)[0:height, :]
        sent_ref[:, quantity(number)] = jnp.where(first, other, own)[0:height, :]

    for number in range(3):
        put(number, *(ref[:, quantity(number)] for ref in rows_refs))
    sides = []
    for block in range(2):
        lines_ref, sums_ref = lines_refs[block], sums_refs[block]
        before, after = (along_line(bound, halves, rows) for bound in bounds[block])
        values = lines_ref[0:LANES, :] + lines_ref[LANES : 2 * LANES, :] * before + lines_ref[2 * LANES : 3 * LANES, :] * after
        values = values.T
        if block == 0:
            values_ref[0:rows, :] = values
        for end in range(2):
            parts = (values * sums_ref[end * rows : (end + 1) * rows, :]).reshape(-1, SUBLANES, LANES)
            side = jnp.sum(parts, axis=0)
            sides.append(sum([behind(side, step, 0) for step in range(halves, SUBLANES, halves)], side))
    for end in range(2):
        put(3 + end, sides[end], sides[2 + end])


def y_given_kernel(halves, rows, block_ref, values_ref, state_ref, given_ref):
    stride = rows // SUBLANES
    total = stride // halves - 1 + len(y_rolls())
    nothing = jnp.zeros((SUBLANES, LANES), jnp.float32)
    for half in range(halves):
        places = [pl.ds(index, SUBLANES, stride=stride) for index in range(half, stride, halves)]
        sides = [(None, block_ref[place, :] * values_ref[place, :]) for place in places]
        nodes = state_parts(state_ref, half * total, total, 3)
        _, givens = tree_sides(sides, y_rolls(), nodes)
        for place, value in zip(places, tree_values(nothing, nothing, y_rolls(), len(places), nodes, givens)):
            given_ref[place, :] = value


def read_message(ref, rows=None):
    return [ref[0:rows, quantity(number)] for number in range(QUANTITIES)]


def join_by_bit(own, other, upper):
    left = [choose(upper, b, a) for a, b in zip(own, other)]
    right = [choose(upper, a, b) for a, b in zip(own, other)]
    coefs, node = join_coefs(left[:3], right[:3])
    sides, given = join_sides(left[3:], right[3:], node)
    return coefs + sides, (node[0], node[1], given)


def own_bit(axis, bit):
    return ((lax.axis_index(axis) >> bit) & 1) == 1


def y_join_kernel(axis, bit, own_ref, other_ref, kept_ref, sent_ref, path_ref):
    joined, path = join_by_bit(read_message(own_ref), read_message(other_ref), own_bit(axis, bit))
    half = own_ref.shape[0] // 2
    for number, value in enumerate(joined):
        kept_ref[:, quantity(number)] = value
        sent_ref[0:half, quantity(number)] = value[half:, :]
        if sent_ref.shape[0] > half:
            sent_ref[half:, quantity(number)] = value[0:half, :]
    for number, value in enumerate(path):
        path_ref[:, quantity(number)] = value


def y_back_kernel(halves, axis, rounds, own_ref, other_ref, *refs):
    path_refs = refs[: rounds - 1]
    given_ref, spread_ref, out_ref = refs[rounds - 1 :]
    rows = out_ref.shape[0]
    own, other = (read_message(ref, halves) for ref in (own_ref, other_ref))
    joined, path = join_by_bit(own, other, own_bit(axis, rounds - 1))
    _, head, tail, side_head, side_tail = joined
    before = after = (side_head + side_tail) * inverse(head + tail)
    paths = [[ref[0:halves, quantity(number)] for number in range(3)] for ref in path_refs] + [path]
    for bit in reversed(range(rounds)):
        node = paths[bit]
        middle = middle_value(node, node[2], before, after)
        upper = own_bit(axis, bit)
        before = jnp.where(upper, middle, before)
        after = jnp.where(upper, after, middle)
    sublane = lax.broadcasted_iota(jnp.int32, (SUBLANES, LANES), 0) % halves
    ends = []
    for end in (before, after):
        value = jnp.broadcast_to(end[0:1, :], (SUBLANES, LANES))
        for half in range(1, halves):
            value = jnp.where(sublane == half, jnp.broadcast_to(end[half : half + 1, :], value.shape), value)
        ends.append(value)
    for start in range(0, rows, SUBLANES):
        part = slice(start, start + SUBLANES)
        late = slice(rows + start, rows + start + SUBLANES)
        out_ref[part, :] = given_ref[part, :] + spread_ref[part, :] * ends[0] + spread_ref[late, :] * ends[1]


def trade(value, x_step, y_step):
    width = lax.axis_size("yd")
    pairs = []
    for index in range(lax.axis_size("xg")):
        for line in range(width):
            pairs.append((index * width + line, (index ^ x_step) * width + (line ^ y_step)))
    return lax.ppermute(value, ("xg", "yd"), pairs)


def x_exchange(message, block):
    count = lax.axis_size("xg")
    held = message
    pieces = [message]
    order = [0]
    other_block = trade(block, 1, 0)
    for step in doubling(count // 2):
        received = trade(held, 2 * step + 1, 0)
        pieces.append(received)
        order += [place ^ (2 * step + 1) for place in order]
        if 4 * step < count:
            held = jnp.concatenate([held, received], axis=0)
    received = pieces[1] if len(pieces) == 2 else jnp.concatenate(pieces[1:], axis=0)
    pieces.append(trade(received, 1, 0))
    order += [place ^ 1 for place in order[1:]] + [1]
    return pieces, order, other_block


def y_exchange(kept, sent):
    rows = kept.shape[0]
    paths = []
    steps = doubling(lax.axis_size("yd"))
    for bit, step in enumerate(steps):
        received = trade(sent, 1, step)
        if bit < len(steps) - 1:
            kept, sent, path = kernel_call(
                functools.partial(y_join_kernel, "yd", bit),
                (kept, received),
                [held_f32(*kept.shape), f32(rows // 2 if bit == len(steps) - 2 else rows, kept.shape[1]), held_f32(rows, 3 * LANES)],
                [],
            )
            paths.append(path)
    return [kept, received] + paths, len(steps)


def f32(*shape):
    return jax.ShapeDtypeStruct(shape, jnp.float32)


def held_f32(*shape):
    return VMEM(shape, jnp.float32)


def kernel_call(body, operands, outputs, scratch, space=VMEM, cost=500000):
    return pl.pallas_call(
        body,
        out_shape=outputs,
        in_specs=[pl.BlockSpec(memory_space=space)] * len(operands),
        out_specs=[pl.BlockSpec(memory_space=VMEM)] * len(outputs),
        scratch_shapes=scratch,
        cost_estimate=pl.CostEstimate(flops=cost, bytes_accessed=cost, transcendentals=0),
        compiler_params=pltpu.CompilerParams(vmem_limit_bytes=16 * 1024 * 1024),
    )(*operands)


def local(mobile, dispersion_x, dispersion_y, capacity, immobile, exchange_rates, rate_shares):
    shape = mobile.shape
    lines, width = shape[0] * shape[1], shape[2]
    zones = immobile.shape[0]
    halves = width // LANES
    rows = lines * halves
    assert rows == LANES

    def flat(values):
        return values.reshape(-1, LANES)

    mobile, dispersion_x, dispersion_y = flat(mobile), flat(dispersion_x), flat(dispersion_y)
    capacity, immobile = flat(capacity), flat(immobile)
    square = VMEM((rows, LANES), jnp.float32)
    spare = max(rows, LANES) // SUBLANES
    x_nodes = LANES // SUBLANES - 1 + len(x_rolls(halves))
    y_nodes = halves * (rows // SUBLANES // halves - 1 + len(y_rolls()))
    message, block = kernel_call(
        functools.partial(x_forward_kernel, halves),
        tuple(
            pltpu.with_memory_space_constraint(value, pltpu.HBM)
            for value in (
                mobile, dispersion_x, dispersion_y, capacity, immobile, exchange_rates[None], rate_shares[None],
            )
        ),
        [f32(SUBLANES, rows), held_f32(2 * rows + (3 * x_nodes + 1) * SUBLANES, LANES)],
        [square] * 3
        + [VMEM((zones * rows, LANES), jnp.float32)]
        + [pltpu.SMEM((1, zones), jnp.float32)] * 2
        + [pltpu.SemaphoreType.DMA((7,))]
        + [VMEM((LANES + LANES // SUBLANES, rows), jnp.float32)] * 3,
        pltpu.HBM,
    )
    def prepare(part, own):
        outputs = [held_f32(SUBLANES, 3 * LANES), held_f32(3 * LANES + spare, rows), held_f32(2 * rows + spare, LANES)]
        if own:
            outputs += [held_f32(3 * y_nodes * SUBLANES, LANES), held_f32(2 * rows + spare, LANES)]
        else:
            outputs += [held_f32(SUBLANES, rows)]
        return kernel_call(functools.partial(prepare_kernel, halves, own), (part,), outputs, [], cost=10000000000)

    pieces, order, other_block = x_exchange(message, block)
    y_rows, lines_x, sums, y_state, spread = prepare(block, True)
    other_rows, other_lines, other_sums, other_message = prepare(other_block, False)
    kept, sent, values = kernel_call(
        functools.partial(x_back_kernel, halves, "xg", order, len(pieces)),
        (*pieces, lines_x, other_lines, sums, other_sums, y_rows, other_rows, other_message),
        [
            held_f32(2 * halves, QUANTITIES * LANES),
            f32(2 * halves, QUANTITIES * LANES),
            held_f32(rows + spare, LANES),
        ],
        [],
    )
    (given,) = kernel_call(
        functools.partial(y_given_kernel, halves, rows), (block, values, y_state), [held_f32(rows + spare, LANES)], []
    )
    pieces, rounds = y_exchange(kept, sent)
    (updated,) = kernel_call(
        functools.partial(y_back_kernel, halves, "yd", rounds),
        (*pieces, given, spread),
        [f32(rows, LANES)],
        [],
    )
    return updated.reshape(shape)


def solution(mesh):
    field = P("yd", None, "xg")
    return jax.shard_map(
        local,
        mesh=mesh,
        in_specs=(field, field, field, field, P(None, "yd", None, "xg"), P(), P()),
        out_specs=field,
        check_vma=False,
    )
```

```python
import functools

import jax
import jax.numpy as jnp
from jax import lax
from jax.experimental import pallas as pl
from jax.experimental.pallas import tpu as pltpu
from jax.sharding import PartitionSpec as P

LANES = 128
SUBLANES = 8
QUANTITIES = 5
VMEM = pltpu.VMEM


def inverse(value):
    return 1.0 / value


def plus(first, second):
    if first is None:
        return second
    return first + second


def join_coefs(left, right):
    coupling_1, head_1, tail_1 = left
    coupling_2, head_2, tail_2 = right
    middle = plus(head_2, tail_1)
    inv = inverse(coupling_1 + coupling_2 + middle)
    weight_1 = coupling_1 * inv
    weight_2 = coupling_2 * inv
    joined = (coupling_1 * weight_2, plus(head_1, weight_1 * middle), tail_2 + weight_2 * middle)
    return joined, (weight_1, weight_2, inv)


def join_sides(left, right, node):
    head_1, tail_1 = left
    head_2, tail_2 = right
    weight_1, weight_2, inv = node
    side = plus(head_2, tail_1)
    joined = (plus(head_1, weight_1 * side), tail_2 + weight_2 * side)
    return joined, side * inv


def middle_value(node, given, before, after):
    return given + node[0] * before + node[1] * after


def ahead(value, step, axis):
    return pltpu.roll(value, value.shape[axis] - step, axis)


def behind(value, step, axis):
    return pltpu.roll(value, step, axis)


def doubling(count):
    steps = []
    step = 1
    while step < count:
        steps.append(step)
        step *= 2
    return steps


def tree_coefs(leaves, rolls):
    nodes = []
    level = leaves
    while len(level) > 1:
        following = []
        for index in range(0, len(level), 2):
            joined, node = join_coefs(level[index], level[index + 1])
            following.append(joined)
            nodes.append(node)
        level = following
    piece = level[0]
    for step, axis in rolls:
        piece, node = join_coefs(piece, tuple(ahead(part, step, axis) for part in piece))
        nodes.append(node)
    return piece, nodes


def tree_sides(leaves, rolls, nodes):
    givens = []
    level = leaves
    while len(level) > 1:
        following = []
        for index in range(0, len(level), 2):
            joined, given = join_sides(level[index], level[index + 1], nodes[len(givens)])
            following.append(joined)
            givens.append(given)
        level = following
    piece = level[0]
    for step, axis in rolls:
        other = tuple(ahead(part, step, axis) for part in piece)
        piece, given = join_sides(piece, other, nodes[len(givens)])
        givens.append(given)
    return piece, givens


def join_all(left, right):
    coefs, node = join_coefs(left[:3], right[:3])
    sides, given = join_sides(left[3:], right[3:], node)
    return coefs + sides, (node[0], node[1], given)


def tree_all(leaves, rolls):
    nodes = []
    level = leaves
    while len(level) > 1:
        pairs = [join_all(level[index], level[index + 1]) for index in range(0, len(level), 2)]
        nodes += [node for _, node in pairs]
        level = [joined for joined, _ in pairs]
    piece = level[0]
    count = SUBLANES
    level = [piece] + [tuple(ahead(part, step, 0) for part in piece) for step in range(1, count)]
    while len(level) > 1:
        pairs = [join_all(level[index], level[index + 1]) for index in range(0, len(level), 2)]
        nodes.append(pairs[0][1])
        level = [joined for joined, _ in pairs]
    piece = level[0]
    for step, axis in rolls[len(doubling(count)) :]:
        piece, node = join_all(piece, tuple(ahead(part, step, axis) for part in piece))
        nodes.append(node)
    return piece, nodes


def tree_values(before, after, rolls, count, nodes, givens):
    place = len(nodes)
    for step, axis in reversed(rolls):
        place -= 1
        middle = middle_value(nodes[place], givens[place], before, after)
        upper = (lax.broadcasted_iota(jnp.int32, middle.shape, axis) & step) != 0
        before = jnp.where(upper, behind(middle, step, axis), before)
        after = jnp.where(upper, behind(after, step, axis), middle)
    bounds = [before, after]
    while len(bounds) - 1 < count:
        width = len(bounds) - 1
        place -= width
        following = [bounds[0]]
        for index in range(width):
            following.append(
                middle_value(
                    nodes[place + index], givens[place + index], bounds[index], bounds[index + 1]
                )
            )
            following.append(bounds[index + 1])
        bounds = following
    return bounds[1:]


def choose(condition, first, second):
    if isinstance(condition, bool):
        return first if condition else second
    return jnp.where(condition, first, second)


def ring_bounds(slots, index):
    level = slots
    rounds = []
    bit = 0
    while len(level) > 1:
        upper = ((index >> bit) & 1) == 1
        following, nodes = [], []
        for place in range(0, len(level), 2):
            own, other = level[place], level[place + 1]
            left = [jnp.where(upper, b, a) for a, b in zip(own, other)]
            right = [jnp.where(upper, a, b) for a, b in zip(own, other)]
            coefs, node = join_coefs(left[:3], right[:3])
            sides, given = join_sides(left[3:], right[3:], node)
            nodes.append((node, given))
            following.append(coefs + sides)
        rounds.append((nodes, upper))
        level = following
        bit += 1
    _, head, tail, side_head, side_tail = level[0]
    last = (side_head + side_tail) * inverse(head + tail)
    bounds = [(last, last)]
    for nodes, upper in reversed(rounds):
        following = []
        for (node, given), (before, after) in zip(nodes, bounds):
            middle = middle_value(node, given, before, after)
            following.append((jnp.where(upper, middle, before), jnp.where(upper, after, middle)))
            following.append((jnp.where(upper, before, middle), jnp.where(upper, middle, after)))
        bounds = following
    return bounds


def capacity_weights(rates_ref, shares_ref):
    weights = []
    for zone in range(rates_ref.shape[1]):
        rate = jnp.full((SUBLANES, LANES), rates_ref[0, zone], jnp.float32)
        share = jnp.full((SUBLANES, LANES), shares_ref[0, zone], jnp.float32)
        weights.append((share * rate / (1.0 + rate))[0:1, :])
    return weights


def strided(ref, start, size, stride):
    return ref[pl.ds(start, size, stride=stride), :]


def x_rolls(halves):
    return [(step, 0) for step in doubling(SUBLANES)] + [(step, 1) for step in doubling(halves)]


def y_rolls():
    return [(step, 0) for step in doubling(SUBLANES)]


def x_forward_kernel(
    halves, mobile_hbm, faces_hbm, across_hbm, capacity_hbm, immobile_hbm, rates_hbm, shares_hbm,
    message_ref, block_ref,
    mobile_ref, faces_ref, capacity_ref, immobile_ref, rates_ref, shares_ref, arrived,
    faces_t, storage_t, source_t,
):
    rows = mobile_ref.shape[0]
    pairs = (
        (rates_hbm, rates_ref), (shares_hbm, shares_ref), (capacity_hbm, capacity_ref), (faces_hbm, faces_ref),
        (immobile_hbm, immobile_ref), (mobile_hbm, mobile_ref), (across_hbm, block_ref.at[rows : 2 * rows, :]),
    )
    copies = [pltpu.make_async_copy(pair[0], pair[1], arrived.at[place]) for place, pair in enumerate(pairs)]
    for place, copy in enumerate(copies):
        copy.start(priority=int(place in (4, 6)))
    stride = LANES // SUBLANES
    for copy in copies[:3]:
        copy.wait()
    weights = capacity_weights(rates_ref, shares_ref)
    capacity = capacity_ref[...]
    storage = 1.0 + capacity * sum(weights[1:], weights[0])
    block_ref[0:rows, :] = storage
    storage_t[0:LANES, :] = storage.T
    copies[3].wait()
    faces_t[0:LANES, :] = faces_ref[...].T
    copies[4].wait()
    total = None
    for zone, weight in enumerate(weights):
        total = plus(total, weight * immobile_ref[zone * rows : (zone + 1) * rows, :])
    copies[5].wait()
    source_t[0:LANES, :] = (mobile_ref[...] + capacity * total).T
    leaves = []
    for index in range(stride):
        face, held, source = (strided(ref, index, SUBLANES, stride) for ref in (faces_t, storage_t, source_t))
        leaves.append((face, None, held, None, source))
    piece, nodes = tree_all(leaves, x_rolls(halves))
    start = 2 * rows
    for part in [part for node in nodes for part in node]:
        block_ref[start : start + SUBLANES, :] = part
        start += SUBLANES
    for row, value in enumerate(piece):
        message_ref[row : row + 1, :] = value[0:1, :]
        block_ref[start + row : start + row + 1, :] = value[0:1, :]
    copies[6].wait()


def ends_responses(shape):
    one, nothing = jnp.ones(shape, jnp.float32), jnp.zeros(shape, jnp.float32)
    return ((one, nothing), (nothing, one))


def summed(halves, value):
    side = jnp.sum(value.reshape(-1, SUBLANES, LANES), axis=0)
    return sum([behind(side, step, 0) for step in range(halves, SUBLANES, halves)], side)


def prepare_kernel(halves, own, block_ref, rows_ref, natural_ref, response_ref, *extra_refs):
    rows = extra_refs[-2].shape[1]
    stride = LANES // SUBLANES
    rolls = x_rolls(halves)
    total = stride - 1 + len(rolls)
    nodes = state_parts(block_ref.at[2 * rows :, :], 0, total, 3)
    *extra_refs, lines_ref, sums_ref = extra_refs
    own_refs = extra_refs if own else ()
    if not own:
        extra_refs[0][...] = block_ref[-SUBLANES:, :]
    nothing = jnp.zeros((SUBLANES, rows), jnp.float32)
    cases = [((nothing, nothing), [node[2] for node in nodes])]
    cases += [(ends, [0.0] * total) for ends in ends_responses((SUBLANES, rows))]
    for case, (ends, givens) in enumerate(cases):
        for index, value in enumerate(tree_values(*ends, rolls, stride, nodes, givens)):
            lines_ref[pl.ds(case * LANES + index, SUBLANES, stride=stride), :] = value
    stride = rows // SUBLANES
    start = 0
    sublane = lax.broadcasted_iota(jnp.int32, (SUBLANES, LANES), 0) % halves
    tiles = None
    for half in range(halves):
        storage = [strided(block_ref, index, SUBLANES, stride) for index in range(half, stride, halves)]
        faces = [strided(block_ref, rows + index, SUBLANES, stride) for index in range(half, stride, halves)]
        piece, nodes = tree_coefs([(face, None, held) for face, held in zip(faces, storage)], y_rolls())
        for part in [part for node in nodes for part in node] if own_refs else []:
            own_refs[0][start : start + SUBLANES, :] = part
            start += SUBLANES
        values = [jnp.broadcast_to(value[0:1, :], value.shape) for value in piece]
        tiles = [jnp.where(sublane == half, new, old) for new, old in zip(values, tiles or values)]
        for case, ends in enumerate(ends_responses((SUBLANES, LANES))):
            values = tree_values(*ends, y_rolls(), len(storage), nodes, [0.0] * len(nodes))
            for index, (value, held) in enumerate(zip(values, storage)):
                place = pl.ds(case * rows + index * halves + half, SUBLANES, stride=stride)
                sums_ref[place, :] = value * held
                if own_refs:
                    own_refs[1][place, :] = value
    for case in range(3):
        natural_ref[case * rows : (case + 1) * rows, :] = lines_ref[case * LANES : (case + 1) * LANES, :].T
    for end in range(2):
        weight = sums_ref[end * rows : (end + 1) * rows, :]
        tiles.append(summed(halves, weight * natural_ref[0:rows, :]))
        for case in range(2):
            place = (2 * end + case) * rows
            response_ref[place : place + rows, :] = weight * natural_ref[(case + 1) * rows : (case + 2) * rows, :]
    for number, tile in enumerate(tiles):
        rows_ref[:, quantity(number)] = tile


def state_parts(ref, first, total, parts, pitch=3):
    return [
        tuple(
            ref[(pitch * place + part) * SUBLANES : (pitch * place + part + 1) * SUBLANES, :]
            for part in range(parts)
        )
        for place in range(first, first + total)
    ]


def message_slots(refs, height, pitch, quantity_rows, skips):
    blocks = [(ref, start) for ref in refs for start in range(0, ref.shape[0], height)]
    slots = []
    for (ref, start), skip in zip(blocks, skips):
        rows = [start + quantity * pitch + skip for quantity in range(QUANTITIES)]
        slots.append(tuple(ref[row : row + quantity_rows, :] for row in rows))
    return slots


def quantity(number):
    return slice(number * LANES, (number + 1) * LANES)


def along_line(bound, halves, rows):
    value = jnp.broadcast_to(bound, (SUBLANES, rows))
    lane = lax.broadcasted_iota(jnp.int32, value.shape, 1)
    for step in doubling(halves):
        value = jnp.where((lane & step) != 0, behind(value, step, 1), value)
    return value[0:1, :]


def x_back_kernel(halves, axis, order, pieces, *refs):
    natural_refs, response_refs, rows_refs = (refs[pieces + 2 * pair : pieces + 2 * pair + 2] for pair in range(3))
    last_ref, kept_ref, sent_ref, values_ref = refs[pieces + 6 :]
    slots = message_slots([*refs[:pieces], last_ref], SUBLANES, 1, 1, [0] * len(order))
    slots = [slots[order.index(place)] for place in range(len(order))]
    bounds = ring_bounds(slots, lax.axis_index(axis))
    rows = natural_refs[0].shape[0] // 3

    height = 2 * halves
    first = lax.broadcasted_iota(jnp.int32, (SUBLANES, LANES), 0) < halves

    def put(number, own, other):
        kept_ref[:, quantity(number)] = jnp.where(first, own, other)[0:height, :]
        sent_ref[:, quantity(number)] = jnp.where(first, other, own)[0:height, :]

    for number in range(3):
        put(number, *(ref[:, quantity(number)] for ref in rows_refs))
    row = lax.broadcasted_iota(jnp.int32, (SUBLANES, rows), 0)
    ends = jnp.zeros((SUBLANES, rows), jnp.float32)
    for place, bound in enumerate([bound for block in range(2) for bound in bounds[block]]):
        ends = jnp.where(row == place, along_line(bound, halves, rows), ends)
    columns = ends.T
    sides = []
    for block in range(2):
        before, after = (
            jnp.broadcast_to(columns[:, 2 * block + end : 2 * block + end + 1], (rows, LANES)) for end in range(2)
        )
        if block == 0:
            natural = [natural_refs[0][case * rows : (case + 1) * rows, :] for case in range(3)]
            values_ref[0:rows, :] = natural[0] + natural[1] * before + natural[2] * after
        for end in range(2):
            first_part, last_part = (
                response_refs[block][(2 * end + case) * rows : (2 * end + case + 1) * rows, :] for case in range(2)
            )
            side = summed(halves, first_part * before + last_part * after)
            sides.append(side + rows_refs[block][:, quantity(3 + end)])
    for end in range(2):
        put(3 + end, sides[end], sides[2 + end])


def y_given_kernel(halves, rows, block_ref, values_ref, state_ref, given_ref):
    stride = rows // SUBLANES
    total = stride // halves - 1 + len(y_rolls())
    nothing = jnp.zeros((SUBLANES, LANES), jnp.float32)
    for half in range(halves):
        places = [pl.ds(index, SUBLANES, stride=stride) for index in range(half, stride, halves)]
        sides = [(None, block_ref[place, :] * values_ref[place, :]) for place in places]
        nodes = state_parts(state_ref, half * total, total, 3)
        _, givens = tree_sides(sides, y_rolls(), nodes)
        for place, value in zip(places, tree_values(nothing, nothing, y_rolls(), len(places), nodes, givens)):
            given_ref[place, :] = value


def read_message(ref, rows=None):
    return [ref[0:rows, quantity(number)] for number in range(QUANTITIES)]


def join_by_bit(own, other, upper):
    left = [choose(upper, b, a) for a, b in zip(own, other)]
    right = [choose(upper, a, b) for a, b in zip(own, other)]
    coefs, node = join_coefs(left[:3], right[:3])
    sides, given = join_sides(left[3:], right[3:], node)
    return coefs + sides, (node[0], node[1], given)


def own_bit(axis, bit):
    return ((lax.axis_index(axis) >> bit) & 1) == 1


def y_join_kernel(axis, bit, own_ref, other_ref, kept_ref, sent_ref, path_ref):
    joined, path = join_by_bit(read_message(own_ref), read_message(other_ref), own_bit(axis, bit))
    half = own_ref.shape[0] // 2
    for number, value in enumerate(joined):
        kept_ref[:, quantity(number)] = value
        sent_ref[0:half, quantity(number)] = value[half:, :]
        if sent_ref.shape[0] > half:
            sent_ref[half:, quantity(number)] = value[0:half, :]
    for number, value in enumerate(path):
        path_ref[:, quantity(number)] = value


def y_back_kernel(halves, axis, rounds, own_ref, other_ref, *refs):
    path_refs = refs[: rounds - 1]
    given_ref, spread_ref, out_ref = refs[rounds - 1 :]
    rows = out_ref.shape[0]
    own, other = (read_message(ref, halves) for ref in (own_ref, other_ref))
    joined, path = join_by_bit(own, other, own_bit(axis, rounds - 1))
    _, head, tail, side_head, side_tail = joined
    before = after = (side_head + side_tail) * inverse(head + tail)
    paths = [[ref[0:halves, quantity(number)] for number in range(3)] for ref in path_refs] + [path]
    for bit in reversed(range(rounds)):
        node = paths[bit]
        middle = middle_value(node, node[2], before, after)
        upper = own_bit(axis, bit)
        before = jnp.where(upper, middle, before)
        after = jnp.where(upper, after, middle)
    sublane = lax.broadcasted_iota(jnp.int32, (SUBLANES, LANES), 0) % halves
    ends = []
    for end in (before, after):
        value = jnp.broadcast_to(end[0:1, :], (SUBLANES, LANES))
        for half in range(1, halves):
            value = jnp.where(sublane == half, jnp.broadcast_to(end[half : half + 1, :], value.shape), value)
        ends.append(value)
    for start in range(0, rows, SUBLANES):
        part = slice(start, start + SUBLANES)
        late = slice(rows + start, rows + start + SUBLANES)
        out_ref[part, :] = given_ref[part, :] + spread_ref[part, :] * ends[0] + spread_ref[late, :] * ends[1]


def trade(value, x_step, y_step):
    width = lax.axis_size("yd")
    pairs = []
    for index in range(lax.axis_size("xg")):
        for line in range(width):
            pairs.append((index * width + line, (index ^ x_step) * width + (line ^ y_step)))
    return lax.ppermute(value, ("xg", "yd"), pairs)


def x_exchange(message, block):
    count = lax.axis_size("xg")
    held = message
    pieces = [message]
    order = [0]
    other_block = trade(block, 1, 0)
    for step in doubling(count // 2):
        received = trade(held, 2 * step + 1, 0)
        pieces.append(received)
        order += [place ^ (2 * step + 1) for place in order]
        if 4 * step < count:
            held = jnp.concatenate([held, received], axis=0)
    received = pieces[1] if len(pieces) == 2 else jnp.concatenate(pieces[1:], axis=0)
    pieces.append(trade(received, 1, 0))
    order += [place ^ 1 for place in order[1:]] + [1]
    return pieces, order, other_block


def y_exchange(kept, sent):
    rows = kept.shape[0]
    paths = []
    steps = doubling(lax.axis_size("yd"))
    for bit, step in enumerate(steps):
        received = trade(sent, 1, step)
        if bit < len(steps) - 1:
            kept, sent, path = kernel_call(
                functools.partial(y_join_kernel, "yd", bit),
                (kept, received),
                [held_f32(*kept.shape), f32(rows // 2 if bit == len(steps) - 2 else rows, kept.shape[1]), held_f32(rows, 3 * LANES)],
                [],
            )
            paths.append(path)
    return [kept, received] + paths, len(steps)


def f32(*shape):
    return jax.ShapeDtypeStruct(shape, jnp.float32)


def held_f32(*shape):
    return VMEM(shape, jnp.float32)


def kernel_call(body, operands, outputs, scratch, space=VMEM, cost=500000):
    return pl.pallas_call(
        body,
        out_shape=outputs,
        in_specs=[pl.BlockSpec(memory_space=space)] * len(operands),
        out_specs=[pl.BlockSpec(memory_space=VMEM)] * len(outputs),
        scratch_shapes=scratch,
        cost_estimate=pl.CostEstimate(flops=cost, bytes_accessed=cost, transcendentals=0),
        compiler_params=pltpu.CompilerParams(vmem_limit_bytes=16 * 1024 * 1024),
    )(*operands)


def local(mobile, dispersion_x, dispersion_y, capacity, immobile, exchange_rates, rate_shares):
    shape = mobile.shape
    lines, width = shape[0] * shape[1], shape[2]
    zones = immobile.shape[0]
    halves = width // LANES
    rows = lines * halves
    assert rows == LANES

    def flat(values):
        return values.reshape(-1, LANES)

    mobile, dispersion_x, dispersion_y = flat(mobile), flat(dispersion_x), flat(dispersion_y)
    capacity, immobile = flat(capacity), flat(immobile)
    square = VMEM((rows, LANES), jnp.float32)
    spare = max(rows, LANES) // SUBLANES
    x_nodes = LANES // SUBLANES - 1 + len(x_rolls(halves))
    y_nodes = halves * (rows // SUBLANES // halves - 1 + len(y_rolls()))
    message, block = kernel_call(
        functools.partial(x_forward_kernel, halves),
        tuple(
            pltpu.with_memory_space_constraint(value, pltpu.HBM)
            for value in (
                mobile, dispersion_x, dispersion_y, capacity, immobile, exchange_rates[None], rate_shares[None],
            )
        ),
        [f32(SUBLANES, rows), held_f32(2 * rows + (3 * x_nodes + 1) * SUBLANES, LANES)],
        [square] * 3
        + [VMEM((zones * rows, LANES), jnp.float32)]
        + [pltpu.SMEM((1, zones), jnp.float32)] * 2
        + [pltpu.SemaphoreType.DMA((7,))]
        + [VMEM((LANES + LANES // SUBLANES, rows), jnp.float32)] * 3,
        pltpu.HBM,
    )
    def prepare(part, own):
        outputs = [held_f32(SUBLANES, QUANTITIES * LANES), held_f32(3 * rows, LANES), held_f32(4 * rows, LANES)]
        if own:
            outputs += [held_f32(3 * y_nodes * SUBLANES, LANES), held_f32(2 * rows + spare, LANES)]
        else:
            outputs += [held_f32(SUBLANES, rows)]
        scratch = [VMEM((3 * LANES + spare, rows), jnp.float32), VMEM((2 * rows + spare, LANES), jnp.float32)]
        return kernel_call(functools.partial(prepare_kernel, halves, own), (part,), outputs, scratch, cost=10000000000)

    pieces, order, other_block = x_exchange(message, block)
    y_rows, lines_x, sums, y_state, spread = prepare(block, True)
    other_rows, other_lines, other_sums, other_message = prepare(other_block, False)
    kept, sent, values = kernel_call(
        functools.partial(x_back_kernel, halves, "xg", order, len(pieces)),
        (*pieces, lines_x, other_lines, sums, other_sums, y_rows, other_rows, other_message),
        [
            held_f32(2 * halves, QUANTITIES * LANES),
            f32(2 * halves, QUANTITIES * LANES),
            held_f32(rows + spare, LANES),
        ],
        [],
    )
    (given,) = kernel_call(
        functools.partial(y_given_kernel, halves, rows), (block, values, y_state), [held_f32(rows + spare, LANES)], []
    )
    pieces, rounds = y_exchange(kept, sent)
    (updated,) = kernel_call(
        functools.partial(y_back_kernel, halves, "yd", rounds),
        (*pieces, given, spread),
        [f32(rows, LANES)],
        [],
    )
    return updated.reshape(shape)


def solution(mesh):
    field = P("yd", None, "xg")
    return jax.shard_map(
        local,
        mesh=mesh,
        in_specs=(field, field, field, field, P(None, "yd", None, "xg"), P(), P()),
        out_specs=field,
        check_vma=False,
    )
```

```python
import functools

import jax
import jax.numpy as jnp
from jax import lax
from jax.experimental import pallas as pl
from jax.experimental.pallas import tpu as pltpu
from jax.sharding import PartitionSpec as P

LANES = 128
SUBLANES = 8
QUANTITIES = 5
VMEM = pltpu.VMEM


def inverse(value):
    return 1.0 / value


def plus(first, second):
    if first is None:
        return second
    return first + second


def join_coefs(left, right):
    coupling_1, head_1, tail_1 = left
    coupling_2, head_2, tail_2 = right
    middle = plus(head_2, tail_1)
    inv = inverse(coupling_1 + coupling_2 + middle)
    weight_1 = coupling_1 * inv
    weight_2 = coupling_2 * inv
    joined = (coupling_1 * weight_2, plus(head_1, weight_1 * middle), tail_2 + weight_2 * middle)
    return joined, (weight_1, weight_2, inv)


def join_sides(left, right, node):
    head_1, tail_1 = left
    head_2, tail_2 = right
    weight_1, weight_2, inv = node
    side = plus(head_2, tail_1)
    joined = (plus(head_1, weight_1 * side), tail_2 + weight_2 * side)
    return joined, side * inv


def middle_value(node, given, before, after):
    return given + node[0] * before + node[1] * after


def ahead(value, step, axis):
    return pltpu.roll(value, value.shape[axis] - step, axis)


def behind(value, step, axis):
    return pltpu.roll(value, step, axis)


def doubling(count):
    steps = []
    step = 1
    while step < count:
        steps.append(step)
        step *= 2
    return steps


def tree_coefs(leaves, rolls):
    nodes = []
    level = leaves
    while len(level) > 1:
        following = []
        for index in range(0, len(level), 2):
            joined, node = join_coefs(level[index], level[index + 1])
            following.append(joined)
            nodes.append(node)
        level = following
    piece = level[0]
    for step, axis in rolls:
        piece, node = join_coefs(piece, tuple(ahead(part, step, axis) for part in piece))
        nodes.append(node)
    return piece, nodes


def tree_sides(leaves, rolls, nodes):
    givens = []
    level = leaves
    while len(level) > 1:
        following = []
        for index in range(0, len(level), 2):
            joined, given = join_sides(level[index], level[index + 1], nodes[len(givens)])
            following.append(joined)
            givens.append(given)
        level = following
    piece = level[0]
    for step, axis in rolls:
        other = tuple(ahead(part, step, axis) for part in piece)
        piece, given = join_sides(piece, other, nodes[len(givens)])
        givens.append(given)
    return piece, givens


def join_all(left, right):
    coefs, node = join_coefs(left[:3], right[:3])
    sides, given = join_sides(left[3:], right[3:], node)
    return coefs + sides, (node[0], node[1], given)


def tree_all(leaves, rolls):
    nodes = []
    level = leaves
    while len(level) > 1:
        pairs = [join_all(level[index], level[index + 1]) for index in range(0, len(level), 2)]
        nodes += [node for _, node in pairs]
        level = [joined for joined, _ in pairs]
    piece = level[0]
    count = SUBLANES
    level = [piece] + [tuple(ahead(part, step, 0) for part in piece) for step in range(1, count)]
    while len(level) > 1:
        pairs = [join_all(level[index], level[index + 1]) for index in range(0, len(level), 2)]
        nodes.append(pairs[0][1])
        level = [joined for joined, _ in pairs]
    piece = level[0]
    for step, axis in rolls[len(doubling(count)) :]:
        piece, node = join_all(piece, tuple(ahead(part, step, axis) for part in piece))
        nodes.append(node)
    return piece, nodes


def tree_values(before, after, rolls, count, nodes, givens):
    place = len(nodes)
    for step, axis in reversed(rolls):
        place -= 1
        middle = middle_value(nodes[place], givens[place], before, after)
        upper = (lax.broadcasted_iota(jnp.int32, middle.shape, axis) & step) != 0
        before = jnp.where(upper, behind(middle, step, axis), before)
        after = jnp.where(upper, behind(after, step, axis), middle)
    bounds = [before, after]
    while len(bounds) - 1 < count:
        width = len(bounds) - 1
        place -= width
        following = [bounds[0]]
        for index in range(width):
            following.append(
                middle_value(
                    nodes[place + index], givens[place + index], bounds[index], bounds[index + 1]
                )
            )
            following.append(bounds[index + 1])
        bounds = following
    return bounds[1:]


def choose(condition, first, second):
    if isinstance(condition, bool):
        return first if condition else second
    return jnp.where(condition, first, second)


def ring_bounds(slots, index):
    level = slots
    rounds = []
    bit = 0
    while len(level) > 1:
        upper = ((index >> bit) & 1) == 1
        following, nodes = [], []
        for place in range(0, len(level), 2):
            own, other = level[place], level[place + 1]
            left = [jnp.where(upper, b, a) for a, b in zip(own, other)]
            right = [jnp.where(upper, a, b) for a, b in zip(own, other)]
            coefs, node = join_coefs(left[:3], right[:3])
            sides, given = join_sides(left[3:], right[3:], node)
            nodes.append((node, given))
            following.append(coefs + sides)
        rounds.append((nodes, upper))
        level = following
        bit += 1
    _, head, tail, side_head, side_tail = level[0]
    last = (side_head + side_tail) * inverse(head + tail)
    bounds = [(last, last)]
    for nodes, upper in reversed(rounds):
        following = []
        for (node, given), (before, after) in zip(nodes, bounds):
            middle = middle_value(node, given, before, after)
            following.append((jnp.where(upper, middle, before), jnp.where(upper, after, middle)))
            following.append((jnp.where(upper, before, middle), jnp.where(upper, middle, after)))
        bounds = following
    return bounds


def capacity_weights(rates_ref, shares_ref):
    weights = []
    for zone in range(rates_ref.shape[1]):
        rate = jnp.full((SUBLANES, LANES), rates_ref[0, zone], jnp.float32)
        share = jnp.full((SUBLANES, LANES), shares_ref[0, zone], jnp.float32)
        weights.append((share * rate / (1.0 + rate))[0:1, :])
    return weights


def strided(ref, start, size, stride):
    return ref[pl.ds(start, size, stride=stride), :]


def x_rolls(halves):
    return [(step, 0) for step in doubling(SUBLANES)] + [(step, 1) for step in doubling(halves)]


def y_rolls():
    return [(step, 0) for step in doubling(SUBLANES)]


def x_forward_kernel(
    halves, mobile_hbm, faces_hbm, across_hbm, capacity_hbm, immobile_hbm, rates_hbm, shares_hbm,
    message_ref, block_ref,
    mobile_ref, faces_ref, capacity_ref, immobile_ref, rates_ref, shares_ref, arrived,
    faces_t, storage_t, source_t,
):
    rows = mobile_ref.shape[0]
    zones = [slice(start, start + rows) for start in range(0, immobile_ref.shape[0], rows)]
    pairs = (
        (rates_hbm, rates_ref), (shares_hbm, shares_ref), (capacity_hbm, capacity_ref), (faces_hbm, faces_ref),
        (mobile_hbm, mobile_ref),
        *((immobile_hbm.at[zone, :], immobile_ref.at[zone, :]) for zone in zones),
        (across_hbm, block_ref.at[rows : 2 * rows, :]),
    )
    copies = [pltpu.make_async_copy(pair[0], pair[1], arrived.at[place]) for place, pair in enumerate(pairs)]
    for copy in copies:
        copy.start()
    stride = LANES // SUBLANES
    for copy in copies[:3]:
        copy.wait()
    weights = capacity_weights(rates_ref, shares_ref)
    capacity = capacity_ref[...]
    storage = 1.0 + capacity * sum(weights[1:], weights[0])
    block_ref[0:rows, :] = storage
    storage_t[0:LANES, :] = storage.T
    copies[3].wait()
    faces_t[0:LANES, :] = faces_ref[...].T
    copies[4].wait()
    total = None
    for copy, weight, zone in zip(copies[5:], weights, zones):
        copy.wait()
        total = plus(total, weight * immobile_ref[zone, :])
    source_t[0:LANES, :] = (mobile_ref[...] + capacity * total).T
    leaves = []
    for index in range(stride):
        face, held, source = (strided(ref, index, SUBLANES, stride) for ref in (faces_t, storage_t, source_t))
        leaves.append((face, None, held, None, source))
    piece, nodes = tree_all(leaves, x_rolls(halves))
    start = 2 * rows
    for part in [part for node in nodes for part in node]:
        block_ref[start : start + SUBLANES, :] = part
        start += SUBLANES
    for row, value in enumerate(piece):
        message_ref[row : row + 1, :] = value[0:1, :]
        block_ref[start + row : start + row + 1, :] = value[0:1, :]
    copies[-1].wait()


def ends_responses(shape):
    one, nothing = jnp.ones(shape, jnp.float32), jnp.zeros(shape, jnp.float32)
    return ((one, nothing), (nothing, one))


def prepare_kernel(halves, own, block_ref, rows_ref, lines_ref, sums_ref, *extra_refs):
    rows = lines_ref.shape[1]
    stride = LANES // SUBLANES
    rolls = x_rolls(halves)
    total = stride - 1 + len(rolls)
    nodes = state_parts(block_ref.at[2 * rows :, :], 0, total, 3)
    own_refs = extra_refs if own else ()
    if not own:
        extra_refs[0][...] = block_ref[-SUBLANES:, :]
    nothing = jnp.zeros((SUBLANES, rows), jnp.float32)
    cases = [((nothing, nothing), [node[2] for node in nodes])]
    cases += [(ends, [0.0] * total) for ends in ends_responses((SUBLANES, rows))]
    for case, (ends, givens) in enumerate(cases):
        for index, value in enumerate(tree_values(*ends, rolls, stride, nodes, givens)):
            lines_ref[pl.ds(case * LANES + index, SUBLANES, stride=stride), :] = value
    stride = rows // SUBLANES
    start = 0
    sublane = lax.broadcasted_iota(jnp.int32, (SUBLANES, LANES), 0) % halves
    tiles = None
    for half in range(halves):
        storage = [strided(block_ref, index, SUBLANES, stride) for index in range(half, stride, halves)]
        faces = [strided(block_ref, rows + index, SUBLANES, stride) for index in range(half, stride, halves)]
        piece, nodes = tree_coefs([(face, None, held) for face, held in zip(faces, storage)], y_rolls())
        for part in [part for node in nodes for part in node] if own_refs else []:
            own_refs[0][start : start + SUBLANES, :] = part
            start += SUBLANES
        values = [jnp.broadcast_to(value[0:1, :], value.shape) for value in piece]
        tiles = [jnp.where(sublane == half, new, old) for new, old in zip(values, tiles or values)]
        for case, ends in enumerate(ends_responses((SUBLANES, LANES))):
            values = tree_values(*ends, y_rolls(), len(storage), nodes, [0.0] * len(nodes))
            for index, (value, held) in enumerate(zip(values, storage)):
                place = pl.ds(case * rows + index * halves + half, SUBLANES, stride=stride)
                sums_ref[place, :] = value * held
                if own_refs:
                    own_refs[1][place, :] = value
    for number, tile in enumerate(tiles):
        rows_ref[:, quantity(number)] = tile


def state_parts(ref, first, total, parts, pitch=3):
    return [
        tuple(
            ref[(pitch * place + part) * SUBLANES : (pitch * place + part + 1) * SUBLANES, :]
            for part in range(parts)
        )
        for place in range(first, first + total)
    ]


def message_slots(refs, height, pitch, quantity_rows, skips):
    blocks = [(ref, start) for ref in refs for start in range(0, ref.shape[0], height)]
    slots = []
    for (ref, start), skip in zip(blocks, skips):
        rows = [start + quantity * pitch + skip for quantity in range(QUANTITIES)]
        slots.append(tuple(ref[row : row + quantity_rows, :] for row in rows))
    return slots


def quantity(number):
    return slice(number * LANES, (number + 1) * LANES)


def along_line(bound, halves, rows):
    value = jnp.broadcast_to(bound, (SUBLANES, rows))
    lane = lax.broadcasted_iota(jnp.int32, value.shape, 1)
    for step in doubling(halves):
        value = jnp.where((lane & step) != 0, behind(value, step, 1), value)
    return value[0:1, :]


def x_back_kernel(halves, axis, order, pieces, *refs):
    lines_refs, sums_refs, rows_refs = (refs[pieces + 2 * pair : pieces + 2 * pair + 2] for pair in range(3))
    last_ref, kept_ref, sent_ref, values_ref = refs[pieces + 6 :]
    slots = message_slots([*refs[:pieces], last_ref], SUBLANES, 1, 1, [0] * len(order))
    slots = [slots[order.index(place)] for place in range(len(order))]
    bounds = ring_bounds(slots, lax.axis_index(axis))
    rows = lines_refs[0].shape[1]

    height = 2 * halves
    first = lax.broadcasted_iota(jnp.int32, (SUBLANES, LANES), 0) < halves

    def put(number, own, other):
        kept_ref[:, quantity(number)] = jnp.where(first, own, other)[0:height, :]
        sent_ref[:, quantity(number)] = jnp.where(first, other, own)[0:height, :]

    for number in range(3):
        put(number, *(ref[:, quantity(number)] for ref in rows_refs))
    sides = []
    for block in range(2):
        lines_ref, sums_ref = lines_refs[block], sums_refs[block]
        before, after = (along_line(bound, halves, rows) for bound in bounds[block])
        values = lines_ref[0:LANES, :] + lines_ref[LANES : 2 * LANES, :] * before + lines_ref[2 * LANES : 3 * LANES, :] * after
        values = values.T
        if block == 0:
            values_ref[0:rows, :] = values
        for end in range(2):
            parts = (values * sums_ref[end * rows : (end + 1) * rows, :]).reshape(-1, SUBLANES, LANES)
            side = jnp.sum(parts, axis=0)
            sides.append(sum([behind(side, step, 0) for step in range(halves, SUBLANES, halves)], side))
    for end in range(2):
        put(3 + end, sides[end], sides[2 + end])


def y_given_kernel(halves, rows, block_ref, values_ref, state_ref, given_ref):
    stride = rows // SUBLANES
    total = stride // halves - 1 + len(y_rolls())
    nothing = jnp.zeros((SUBLANES, LANES), jnp.float32)
    for half in range(halves):
        places = [pl.ds(index, SUBLANES, stride=stride) for index in range(half, stride, halves)]
        sides = [(None, block_ref[place, :] * values_ref[place, :]) for place in places]
        nodes = state_parts(state_ref, half * total, total, 3)
        _, givens = tree_sides(sides, y_rolls(), nodes)
        for place, value in zip(places, tree_values(nothing, nothing, y_rolls(), len(places), nodes, givens)):
            given_ref[place, :] = value


def read_message(ref, rows=None):
    return [ref[0:rows, quantity(number)] for number in range(QUANTITIES)]


def join_by_bit(own, other, upper):
    left = [choose(upper, b, a) for a, b in zip(own, other)]
    right = [choose(upper, a, b) for a, b in zip(own, other)]
    coefs, node = join_coefs(left[:3], right[:3])
    sides, given = join_sides(left[3:], right[3:], node)
    return coefs + sides, (node[0], node[1], given)


def own_bit(axis, bit):
    return ((lax.axis_index(axis) >> bit) & 1) == 1


def y_join_kernel(axis, bit, own_ref, other_ref, kept_ref, sent_ref, path_ref):
    joined, path = join_by_bit(read_message(own_ref), read_message(other_ref), own_bit(axis, bit))
    half = own_ref.shape[0] // 2
    for number, value in enumerate(joined):
        kept_ref[:, quantity(number)] = value
        sent_ref[0:half, quantity(number)] = value[half:, :]
        if sent_ref.shape[0] > half:
            sent_ref[half:, quantity(number)] = value[0:half, :]
    for number, value in enumerate(path):
        path_ref[:, quantity(number)] = value


def y_back_kernel(halves, axis, rounds, own_ref, other_ref, *refs):
    path_refs = refs[: rounds - 1]
    given_ref, spread_ref, out_ref = refs[rounds - 1 :]
    rows = out_ref.shape[0]
    own, other = (read_message(ref, halves) for ref in (own_ref, other_ref))
    joined, path = join_by_bit(own, other, own_bit(axis, rounds - 1))
    _, head, tail, side_head, side_tail = joined
    before = after = (side_head + side_tail) * inverse(head + tail)
    paths = [[ref[0:halves, quantity(number)] for number in range(3)] for ref in path_refs] + [path]
    for bit in reversed(range(rounds)):
        node = paths[bit]
        middle = middle_value(node, node[2], before, after)
        upper = own_bit(axis, bit)
        before = jnp.where(upper, middle, before)
        after = jnp.where(upper, after, middle)
    sublane = lax.broadcasted_iota(jnp.int32, (SUBLANES, LANES), 0) % halves
    ends = []
    for end in (before, after):
        value = jnp.broadcast_to(end[0:1, :], (SUBLANES, LANES))
        for half in range(1, halves):
            value = jnp.where(sublane == half, jnp.broadcast_to(end[half : half + 1, :], value.shape), value)
        ends.append(value)
    for start in range(0, rows, SUBLANES):
        part = slice(start, start + SUBLANES)
        late = slice(rows + start, rows + start + SUBLANES)
        out_ref[part, :] = given_ref[part, :] + spread_ref[part, :] * ends[0] + spread_ref[late, :] * ends[1]


def trade(value, x_step, y_step):
    width = lax.axis_size("yd")
    pairs = []
    for index in range(lax.axis_size("xg")):
        for line in range(width):
            pairs.append((index * width + line, (index ^ x_step) * width + (line ^ y_step)))
    return lax.ppermute(value, ("xg", "yd"), pairs)


def x_exchange(message, block):
    count = lax.axis_size("xg")
    held = message
    pieces = [message]
    order = [0]
    other_block = trade(block, 1, 0)
    for step in doubling(count // 2):
        received = trade(held, 2 * step + 1, 0)
        pieces.append(received)
        order += [place ^ (2 * step + 1) for place in order]
        if 4 * step < count:
            held = jnp.concatenate([held, received], axis=0)
    received = pieces[1] if len(pieces) == 2 else jnp.concatenate(pieces[1:], axis=0)
    pieces.append(trade(received, 1, 0))
    order += [place ^ 1 for place in order[1:]] + [1]
    return pieces, order, other_block


def y_exchange(kept, sent):
    rows = kept.shape[0]
    paths = []
    steps = doubling(lax.axis_size("yd"))
    for bit, step in enumerate(steps):
        received = trade(sent, 1, step)
        if bit < len(steps) - 1:
            kept, sent, path = kernel_call(
                functools.partial(y_join_kernel, "yd", bit),
                (kept, received),
                [held_f32(*kept.shape), f32(rows // 2 if bit == len(steps) - 2 else rows, kept.shape[1]), held_f32(rows, 3 * LANES)],
                [],
            )
            paths.append(path)
    return [kept, received] + paths, len(steps)


def f32(*shape):
    return jax.ShapeDtypeStruct(shape, jnp.float32)


def held_f32(*shape):
    return VMEM(shape, jnp.float32)


def kernel_call(body, operands, outputs, scratch, space=VMEM, cost=500000):
    return pl.pallas_call(
        body,
        out_shape=outputs,
        in_specs=[pl.BlockSpec(memory_space=space)] * len(operands),
        out_specs=[pl.BlockSpec(memory_space=VMEM)] * len(outputs),
        scratch_shapes=scratch,
        cost_estimate=pl.CostEstimate(flops=cost, bytes_accessed=cost, transcendentals=0),
        compiler_params=pltpu.CompilerParams(vmem_limit_bytes=16 * 1024 * 1024),
    )(*operands)


def local(mobile, dispersion_x, dispersion_y, capacity, immobile, exchange_rates, rate_shares):
    shape = mobile.shape
    lines, width = shape[0] * shape[1], shape[2]
    zones = immobile.shape[0]
    halves = width // LANES
    rows = lines * halves
    assert rows == LANES

    def flat(values):
        return values.reshape(-1, LANES)

    mobile, dispersion_x, dispersion_y = flat(mobile), flat(dispersion_x), flat(dispersion_y)
    capacity, immobile = flat(capacity), flat(immobile)
    square = VMEM((rows, LANES), jnp.float32)
    spare = max(rows, LANES) // SUBLANES
    x_nodes = LANES // SUBLANES - 1 + len(x_rolls(halves))
    y_nodes = halves * (rows // SUBLANES // halves - 1 + len(y_rolls()))
    message, block = kernel_call(
        functools.partial(x_forward_kernel, halves),
        tuple(
            pltpu.with_memory_space_constraint(value, pltpu.HBM)
            for value in (
                mobile, dispersion_x, dispersion_y, capacity, immobile, exchange_rates[None], rate_shares[None],
            )
        ),
        [f32(SUBLANES, rows), held_f32(2 * rows + (3 * x_nodes + 1) * SUBLANES, LANES)],
        [square] * 3
        + [VMEM((zones * rows, LANES), jnp.float32)]
        + [pltpu.SMEM((1, zones), jnp.float32)] * 2
        + [pltpu.SemaphoreType.DMA((6 + zones,))]
        + [VMEM((LANES + LANES // SUBLANES, rows), jnp.float32)] * 3,
        pltpu.HBM,
    )
    def prepare(part, own):
        outputs = [held_f32(SUBLANES, 3 * LANES), held_f32(3 * LANES + spare, rows), held_f32(2 * rows + spare, LANES)]
        if own:
            outputs += [held_f32(3 * y_nodes * SUBLANES, LANES), held_f32(2 * rows + spare, LANES)]
        else:
            outputs += [held_f32(SUBLANES, rows)]
        return kernel_call(functools.partial(prepare_kernel, halves, own), (part,), outputs, [], cost=10000000000)

    pieces, order, other_block = x_exchange(message, block)
    y_rows, lines_x, sums, y_state, spread = prepare(block, True)
    other_rows, other_lines, other_sums, other_message = prepare(other_block, False)
    kept, sent, values = kernel_call(
        functools.partial(x_back_kernel, halves, "xg", order, len(pieces)),
        (*pieces, lines_x, other_lines, sums, other_sums, y_rows, other_rows, other_message),
        [
            held_f32(2 * halves, QUANTITIES * LANES),
            f32(2 * halves, QUANTITIES * LANES),
            held_f32(rows + spare, LANES),
        ],
        [],
    )
    (given,) = kernel_call(
        functools.partial(y_given_kernel, halves, rows), (block, values, y_state), [held_f32(rows + spare, LANES)], []
    )
    pieces, rounds = y_exchange(kept, sent)
    (updated,) = kernel_call(
        functools.partial(y_back_kernel, halves, "yd", rounds),
        (*pieces, given, spread),
        [f32(rows, LANES)],
        [],
    )
    return updated.reshape(shape)


def solution(mesh):
    field = P("yd", None, "xg")
    return jax.shard_map(
        local,
        mesh=mesh,
        in_specs=(field, field, field, field, P(None, "yd", None, "xg"), P(), P()),
        out_specs=field,
        check_vma=False,
    )
```

```python
import functools

import jax
import jax.numpy as jnp
from jax import lax
from jax.experimental import pallas as pl
from jax.experimental.pallas import tpu as pltpu
from jax.sharding import PartitionSpec as P

LANES = 128
SUBLANES = 8
QUANTITIES = 5
VMEM = pltpu.VMEM


def inverse(value):
    return 1.0 / value


def plus(first, second):
    if first is None:
        return second
    return first + second


def join_coefs(left, right):
    coupling_1, head_1, tail_1 = left
    coupling_2, head_2, tail_2 = right
    middle = plus(head_2, tail_1)
    inv = inverse(coupling_1 + coupling_2 + middle)
    weight_1 = coupling_1 * inv
    weight_2 = coupling_2 * inv
    joined = (coupling_1 * weight_2, plus(head_1, weight_1 * middle), tail_2 + weight_2 * middle)
    return joined, (weight_1, weight_2, inv)


def join_sides(left, right, node):
    head_1, tail_1 = left
    head_2, tail_2 = right
    weight_1, weight_2, inv = node
    side = plus(head_2, tail_1)
    joined = (plus(head_1, weight_1 * side), tail_2 + weight_2 * side)
    return joined, side * inv


def middle_value(node, given, before, after):
    return given + node[0] * before + node[1] * after


def ahead(value, step, axis):
    return pltpu.roll(value, value.shape[axis] - step, axis)


def behind(value, step, axis):
    return pltpu.roll(value, step, axis)


def doubling(count):
    steps = []
    step = 1
    while step < count:
        steps.append(step)
        step *= 2
    return steps


def tree_coefs(leaves, rolls):
    nodes = []
    level = leaves
    while len(level) > 1:
        following = []
        for index in range(0, len(level), 2):
            joined, node = join_coefs(level[index], level[index + 1])
            following.append(joined)
            nodes.append(node)
        level = following
    piece = level[0]
    for step, axis in rolls:
        piece, node = join_coefs(piece, tuple(ahead(part, step, axis) for part in piece))
        nodes.append(node)
    return piece, nodes


def tree_sides(leaves, rolls, nodes):
    givens = []
    level = leaves
    while len(level) > 1:
        following = []
        for index in range(0, len(level), 2):
            joined, given = join_sides(level[index], level[index + 1], nodes[len(givens)])
            following.append(joined)
            givens.append(given)
        level = following
    piece = level[0]
    for step, axis in rolls:
        other = tuple(ahead(part, step, axis) for part in piece)
        piece, given = join_sides(piece, other, nodes[len(givens)])
        givens.append(given)
    return piece, givens


def join_all(left, right):
    coefs, node = join_coefs(left[:3], right[:3])
    sides, given = join_sides(left[3:], right[3:], node)
    return coefs + sides, (node[0], node[1], given)


def tree_all(leaves, rolls):
    nodes = []
    level = leaves
    while len(level) > 1:
        pairs = [join_all(level[index], level[index + 1]) for index in range(0, len(level), 2)]
        nodes += [node for _, node in pairs]
        level = [joined for joined, _ in pairs]
    piece = level[0]
    count = SUBLANES
    level = [piece] + [tuple(ahead(part, step, 0) for part in piece) for step in range(1, count)]
    while len(level) > 1:
        pairs = [join_all(level[index], level[index + 1]) for index in range(0, len(level), 2)]
        nodes.append(pairs[0][1])
        level = [joined for joined, _ in pairs]
    piece = level[0]
    for step, axis in rolls[len(doubling(count)) :]:
        piece, node = join_all(piece, tuple(ahead(part, step, axis) for part in piece))
        nodes.append(node)
    return piece, nodes


def tree_values(before, after, rolls, count, nodes, givens):
    place = len(nodes)
    for step, axis in reversed(rolls):
        place -= 1
        middle = middle_value(nodes[place], givens[place], before, after)
        upper = (lax.broadcasted_iota(jnp.int32, middle.shape, axis) & step) != 0
        before = jnp.where(upper, behind(middle, step, axis), before)
        after = jnp.where(upper, behind(after, step, axis), middle)
    bounds = [before, after]
    while len(bounds) - 1 < count:
        width = len(bounds) - 1
        place -= width
        following = [bounds[0]]
        for index in range(width):
            following.append(
                middle_value(
                    nodes[place + index], givens[place + index], bounds[index], bounds[index + 1]
                )
            )
            following.append(bounds[index + 1])
        bounds = following
    return bounds[1:]


def choose(condition, first, second):
    if isinstance(condition, bool):
        return first if condition else second
    return jnp.where(condition, first, second)


def ring_bounds(slots, index):
    level = slots
    rounds = []
    bit = 0
    while len(level) > 1:
        upper = ((index >> bit) & 1) == 1
        following, nodes = [], []
        for place in range(0, len(level), 2):
            own, other = level[place], level[place + 1]
            left = [jnp.where(upper, b, a) for a, b in zip(own, other)]
            right = [jnp.where(upper, a, b) for a, b in zip(own, other)]
            coefs, node = join_coefs(left[:3], right[:3])
            sides, given = join_sides(left[3:], right[3:], node)
            nodes.append((node, given))
            following.append(coefs + sides)
        rounds.append((nodes, upper))
        level = following
        bit += 1
    _, head, tail, side_head, side_tail = level[0]
    last = (side_head + side_tail) * inverse(head + tail)
    bounds = [(last, last)]
    for nodes, upper in reversed(rounds):
        following = []
        for (node, given), (before, after) in zip(nodes, bounds):
            middle = middle_value(node, given, before, after)
            following.append((jnp.where(upper, middle, before), jnp.where(upper, after, middle)))
            following.append((jnp.where(upper, before, middle), jnp.where(upper, middle, after)))
        bounds = following
    return bounds


def capacity_weights(rates_ref, shares_ref):
    weights = []
    for zone in range(rates_ref.shape[1]):
        rate = jnp.full((SUBLANES, LANES), rates_ref[0, zone], jnp.float32)
        share = jnp.full((SUBLANES, LANES), shares_ref[0, zone], jnp.float32)
        weights.append((share * rate / (1.0 + rate))[0:1, :])
    return weights


def strided(ref, start, size, stride):
    return ref[pl.ds(start, size, stride=stride), :]


def x_rolls(halves):
    return [(step, 0) for step in doubling(SUBLANES)] + [(step, 1) for step in doubling(halves)]


def y_rolls():
    return [(step, 0) for step in doubling(SUBLANES)]


def put_line(block_ref, rows, number, value):
    start = 2 * rows + number * LANES
    block_ref[start : start + LANES, :] = value.T


def line_leaves(block_ref, rows):
    stride = LANES // SUBLANES
    leaves = []
    for index in range(stride):
        starts = [2 * rows + number * LANES + index for number in range(3)]
        face, held, source = (strided(block_ref, start, SUBLANES, stride) for start in starts)
        leaves.append((face, None, held, None, source))
    return leaves


def x_forward_kernel(
    halves, mobile_hbm, faces_hbm, across_hbm, capacity_hbm, immobile_hbm, rates_hbm, shares_hbm,
    message_ref, block_ref,
    mobile_ref, faces_ref, capacity_ref, immobile_ref, rates_ref, shares_ref, arrived,
):
    rows = mobile_ref.shape[0]
    pairs = (
        (rates_hbm, rates_ref), (shares_hbm, shares_ref), (capacity_hbm, capacity_ref), (faces_hbm, faces_ref),
        (immobile_hbm, immobile_ref), (mobile_hbm, mobile_ref), (across_hbm, block_ref.at[rows : 2 * rows, :]),
    )
    copies = [pltpu.make_async_copy(pair[0], pair[1], arrived.at[place]) for place, pair in enumerate(pairs)]
    for place, copy in enumerate(copies):
        copy.start(priority=int(place in (4, 6)))
    stride = LANES // SUBLANES
    for copy in copies[:3]:
        copy.wait()
    weights = capacity_weights(rates_ref, shares_ref)
    capacity = capacity_ref[...]
    storage = 1.0 + capacity * sum(weights[1:], weights[0])
    block_ref[0:rows, :] = storage
    put_line(block_ref, rows, 1, storage)
    copies[3].wait()
    put_line(block_ref, rows, 0, faces_ref[...])
    copies[4].wait()
    total = None
    for zone, weight in enumerate(weights):
        total = plus(total, weight * immobile_ref[zone * rows : (zone + 1) * rows, :])
    copies[5].wait()
    put_line(block_ref, rows, 2, mobile_ref[...] + capacity * total)
    piece, _ = tree_all(line_leaves(block_ref, rows), x_rolls(halves))
    last = block_ref.shape[0] - SUBLANES
    for row, value in enumerate(piece):
        message_ref[row : row + 1, :] = value[0:1, :]
        block_ref[last + row : last + row + 1, :] = value[0:1, :]
    copies[6].wait()


def ends_responses(shape):
    one, nothing = jnp.ones(shape, jnp.float32), jnp.zeros(shape, jnp.float32)
    return ((one, nothing), (nothing, one))


def prepare_kernel(halves, own, block_ref, rows_ref, lines_ref, sums_ref, *extra_refs):
    rows = lines_ref.shape[1]
    stride = LANES // SUBLANES
    rolls = x_rolls(halves)
    total = stride - 1 + len(rolls)
    _, nodes = tree_all(line_leaves(block_ref, rows), rolls)
    own_refs = extra_refs if own else ()
    if not own:
        extra_refs[0][...] = block_ref[-SUBLANES:, :]
    nothing = jnp.zeros((SUBLANES, rows), jnp.float32)
    cases = [((nothing, nothing), [node[2] for node in nodes])]
    cases += [(ends, [0.0] * total) for ends in ends_responses((SUBLANES, rows))]
    for case, (ends, givens) in enumerate(cases):
        for index, value in enumerate(tree_values(*ends, rolls, stride, nodes, givens)):
            lines_ref[pl.ds(case * LANES + index, SUBLANES, stride=stride), :] = value
    stride = rows // SUBLANES
    start = 0
    sublane = lax.broadcasted_iota(jnp.int32, (SUBLANES, LANES), 0) % halves
    tiles = None
    for half in range(halves):
        storage = [strided(block_ref, index, SUBLANES, stride) for index in range(half, stride, halves)]
        faces = [strided(block_ref, rows + index, SUBLANES, stride) for index in range(half, stride, halves)]
        piece, nodes = tree_coefs([(face, None, held) for face, held in zip(faces, storage)], y_rolls())
        for part in [part for node in nodes for part in node] if own_refs else []:
            own_refs[0][start : start + SUBLANES, :] = part
            start += SUBLANES
        values = [jnp.broadcast_to(value[0:1, :], value.shape) for value in piece]
        tiles = [jnp.where(sublane == half, new, old) for new, old in zip(values, tiles or values)]
        for case, ends in enumerate(ends_responses((SUBLANES, LANES))):
            values = tree_values(*ends, y_rolls(), len(storage), nodes, [0.0] * len(nodes))
            for index, (value, held) in enumerate(zip(values, storage)):
                place = pl.ds(case * rows + index * halves + half, SUBLANES, stride=stride)
                sums_ref[place, :] = value * held
                if own_refs:
                    own_refs[1][place, :] = value
    for number, tile in enumerate(tiles):
        rows_ref[:, quantity(number)] = tile


def state_parts(ref, first, total, parts, pitch=3):
    return [
        tuple(
            ref[(pitch * place + part) * SUBLANES : (pitch * place + part + 1) * SUBLANES, :]
            for part in range(parts)
        )
        for place in range(first, first + total)
    ]


def message_slots(refs, height, pitch, quantity_rows, skips):
    blocks = [(ref, start) for ref in refs for start in range(0, ref.shape[0], height)]
    slots = []
    for (ref, start), skip in zip(blocks, skips):
        rows = [start + quantity * pitch + skip for quantity in range(QUANTITIES)]
        slots.append(tuple(ref[row : row + quantity_rows, :] for row in rows))
    return slots


def quantity(number):
    return slice(number * LANES, (number + 1) * LANES)


def along_line(bound, halves, rows):
    value = jnp.broadcast_to(bound, (SUBLANES, rows))
    lane = lax.broadcasted_iota(jnp.int32, value.shape, 1)
    for step in doubling(halves):
        value = jnp.where((lane & step) != 0, behind(value, step, 1), value)
    return value[0:1, :]


def x_back_kernel(halves, axis, order, pieces, *refs):
    lines_refs, sums_refs, rows_refs = (refs[pieces + 2 * pair : pieces + 2 * pair + 2] for pair in range(3))
    last_ref, kept_ref, sent_ref, values_ref = refs[pieces + 6 :]
    slots = message_slots([*refs[:pieces], last_ref], SUBLANES, 1, 1, [0] * len(order))
    slots = [slots[order.index(place)] for place in range(len(order))]
    bounds = ring_bounds(slots, lax.axis_index(axis))
    rows = lines_refs[0].shape[1]

    height = 2 * halves
    first = lax.broadcasted_iota(jnp.int32, (SUBLANES, LANES), 0) < halves

    def put(number, own, other):
        kept_ref[:, quantity(number)] = jnp.where(first, own, other)[0:height, :]
        sent_ref[:, quantity(number)] = jnp.where(first, other, own)[0:height, :]

    for number in range(3):
        put(number, *(ref[:, quantity(number)] for ref in rows_refs))
    sides = []
    for block in range(2):
        lines_ref, sums_ref = lines_refs[block], sums_refs[block]
        before, after = (along_line(bound, halves, rows) for bound in bounds[block])
        values = lines_ref[0:LANES, :] + lines_ref[LANES : 2 * LANES, :] * before + lines_ref[2 * LANES : 3 * LANES, :] * after
        values = values.T
        if block == 0:
            values_ref[0:rows, :] = values
        for end in range(2):
            parts = (values * sums_ref[end * rows : (end + 1) * rows, :]).reshape(-1, SUBLANES, LANES)
            side = jnp.sum(parts, axis=0)
            sides.append(sum([behind(side, step, 0) for step in range(halves, SUBLANES, halves)], side))
    for end in range(2):
        put(3 + end, sides[end], sides[2 + end])


def y_given_kernel(halves, rows, block_ref, values_ref, state_ref, given_ref):
    stride = rows // SUBLANES
    total = stride // halves - 1 + len(y_rolls())
    nothing = jnp.zeros((SUBLANES, LANES), jnp.float32)
    for half in range(halves):
        places = [pl.ds(index, SUBLANES, stride=stride) for index in range(half, stride, halves)]
        sides = [(None, block_ref[place, :] * values_ref[place, :]) for place in places]
        nodes = state_parts(state_ref, half * total, total, 3)
        _, givens = tree_sides(sides, y_rolls(), nodes)
        for place, value in zip(places, tree_values(nothing, nothing, y_rolls(), len(places), nodes, givens)):
            given_ref[place, :] = value


def read_message(ref, rows=None):
    return [ref[0:rows, quantity(number)] for number in range(QUANTITIES)]


def join_by_bit(own, other, upper):
    left = [choose(upper, b, a) for a, b in zip(own, other)]
    right = [choose(upper, a, b) for a, b in zip(own, other)]
    coefs, node = join_coefs(left[:3], right[:3])
    sides, given = join_sides(left[3:], right[3:], node)
    return coefs + sides, (node[0], node[1], given)


def own_bit(axis, bit):
    return ((lax.axis_index(axis) >> bit) & 1) == 1


def y_join_kernel(axis, bit, own_ref, other_ref, kept_ref, sent_ref, path_ref):
    joined, path = join_by_bit(read_message(own_ref), read_message(other_ref), own_bit(axis, bit))
    half = own_ref.shape[0] // 2
    for number, value in enumerate(joined):
        kept_ref[:, quantity(number)] = value
        sent_ref[0:half, quantity(number)] = value[half:, :]
        if sent_ref.shape[0] > half:
            sent_ref[half:, quantity(number)] = value[0:half, :]
    for number, value in enumerate(path):
        path_ref[:, quantity(number)] = value


def y_back_kernel(halves, axis, rounds, own_ref, other_ref, *refs):
    path_refs = refs[: rounds - 1]
    given_ref, spread_ref, out_ref = refs[rounds - 1 :]
    rows = out_ref.shape[0]
    own, other = (read_message(ref, halves) for ref in (own_ref, other_ref))
    joined, path = join_by_bit(own, other, own_bit(axis, rounds - 1))
    _, head, tail, side_head, side_tail = joined
    before = after = (side_head + side_tail) * inverse(head + tail)
    paths = [[ref[0:halves, quantity(number)] for number in range(3)] for ref in path_refs] + [path]
    for bit in reversed(range(rounds)):
        node = paths[bit]
        middle = middle_value(node, node[2], before, after)
        upper = own_bit(axis, bit)
        before = jnp.where(upper, middle, before)
        after = jnp.where(upper, after, middle)
    sublane = lax.broadcasted_iota(jnp.int32, (SUBLANES, LANES), 0) % halves
    ends = []
    for end in (before, after):
        value = jnp.broadcast_to(end[0:1, :], (SUBLANES, LANES))
        for half in range(1, halves):
            value = jnp.where(sublane == half, jnp.broadcast_to(end[half : half + 1, :], value.shape), value)
        ends.append(value)
    for start in range(0, rows, SUBLANES):
        part = slice(start, start + SUBLANES)
        late = slice(rows + start, rows + start + SUBLANES)
        out_ref[part, :] = given_ref[part, :] + spread_ref[part, :] * ends[0] + spread_ref[late, :] * ends[1]


def trade(value, x_step, y_step):
    width = lax.axis_size("yd")
    pairs = []
    for index in range(lax.axis_size("xg")):
        for line in range(width):
            pairs.append((index * width + line, (index ^ x_step) * width + (line ^ y_step)))
    return lax.ppermute(value, ("xg", "yd"), pairs)


def x_exchange(message, block):
    count = lax.axis_size("xg")
    held = message
    pieces = [message]
    order = [0]
    other_block = trade(block, 1, 0)
    for step in doubling(count // 2):
        received = trade(held, 2 * step + 1, 0)
        pieces.append(received)
        order += [place ^ (2 * step + 1) for place in order]
        if 4 * step < count:
            held = jnp.concatenate([held, received], axis=0)
    received = pieces[1] if len(pieces) == 2 else jnp.concatenate(pieces[1:], axis=0)
    pieces.append(trade(received, 1, 0))
    order += [place ^ 1 for place in order[1:]] + [1]
    return pieces, order, other_block


def y_exchange(kept, sent):
    rows = kept.shape[0]
    paths = []
    steps = doubling(lax.axis_size("yd"))
    for bit, step in enumerate(steps):
        received = trade(sent, 1, step)
        if bit < len(steps) - 1:
            kept, sent, path = kernel_call(
                functools.partial(y_join_kernel, "yd", bit),
                (kept, received),
                [held_f32(*kept.shape), f32(rows // 2 if bit == len(steps) - 2 else rows, kept.shape[1]), held_f32(rows, 3 * LANES)],
                [],
            )
            paths.append(path)
    return [kept, received] + paths, len(steps)


def f32(*shape):
    return jax.ShapeDtypeStruct(shape, jnp.float32)


def held_f32(*shape):
    return VMEM(shape, jnp.float32)


def kernel_call(body, operands, outputs, scratch, space=VMEM, cost=500000):
    return pl.pallas_call(
        body,
        out_shape=outputs,
        in_specs=[pl.BlockSpec(memory_space=space)] * len(operands),
        out_specs=[pl.BlockSpec(memory_space=VMEM)] * len(outputs),
        scratch_shapes=scratch,
        cost_estimate=pl.CostEstimate(flops=cost, bytes_accessed=cost, transcendentals=0),
        compiler_params=pltpu.CompilerParams(vmem_limit_bytes=16 * 1024 * 1024),
    )(*operands)


def local(mobile, dispersion_x, dispersion_y, capacity, immobile, exchange_rates, rate_shares):
    shape = mobile.shape
    lines, width = shape[0] * shape[1], shape[2]
    zones = immobile.shape[0]
    halves = width // LANES
    rows = lines * halves
    assert rows == LANES

    def flat(values):
        return values.reshape(-1, LANES)

    mobile, dispersion_x, dispersion_y = flat(mobile), flat(dispersion_x), flat(dispersion_y)
    capacity, immobile = flat(capacity), flat(immobile)
    square = VMEM((rows, LANES), jnp.float32)
    spare = max(rows, LANES) // SUBLANES
    y_nodes = halves * (rows // SUBLANES // halves - 1 + len(y_rolls()))
    message, block = kernel_call(
        functools.partial(x_forward_kernel, halves),
        tuple(
            pltpu.with_memory_space_constraint(value, pltpu.HBM)
            for value in (
                mobile, dispersion_x, dispersion_y, capacity, immobile, exchange_rates[None], rate_shares[None],
            )
        ),
        [f32(SUBLANES, rows), held_f32(2 * rows + 3 * LANES + spare + SUBLANES, LANES)],
        [square] * 3
        + [VMEM((zones * rows, LANES), jnp.float32)]
        + [pltpu.SMEM((1, zones), jnp.float32)] * 2
        + [pltpu.SemaphoreType.DMA((7,))],
        pltpu.HBM,
    )
    def prepare(part, own):
        outputs = [held_f32(SUBLANES, 3 * LANES), held_f32(3 * LANES + spare, rows), held_f32(2 * rows + spare, LANES)]
        if own:
            outputs += [held_f32(3 * y_nodes * SUBLANES, LANES), held_f32(2 * rows + spare, LANES)]
        else:
            outputs += [held_f32(SUBLANES, rows)]
        return kernel_call(functools.partial(prepare_kernel, halves, own), (part,), outputs, [], cost=10000000000)

    pieces, order, other_block = x_exchange(message, block)
    y_rows, lines_x, sums, y_state, spread = prepare(block, True)
    other_rows, other_lines, other_sums, other_message = prepare(other_block, False)
    kept, sent, values = kernel_call(
        functools.partial(x_back_kernel, halves, "xg", order, len(pieces)),
        (*pieces, lines_x, other_lines, sums, other_sums, y_rows, other_rows, other_message),
        [
            held_f32(2 * halves, QUANTITIES * LANES),
            f32(2 * halves, QUANTITIES * LANES),
            held_f32(rows + spare, LANES),
        ],
        [],
    )
    (given,) = kernel_call(
        functools.partial(y_given_kernel, halves, rows), (block, values, y_state), [held_f32(rows + spare, LANES)], []
    )
    pieces, rounds = y_exchange(kept, sent)
    (updated,) = kernel_call(
        functools.partial(y_back_kernel, halves, "yd", rounds),
        (*pieces, given, spread),
        [f32(rows, LANES)],
        [],
    )
    return updated.reshape(shape)


def solution(mesh):
    field = P("yd", None, "xg")
    return jax.shard_map(
        local,
        mesh=mesh,
        in_specs=(field, field, field, field, P(None, "yd", None, "xg"), P(), P()),
        out_specs=field,
        check_vma=False,
    )
```
